32 devices in a mesh: shard: 2 (over y), context: 4 (over z), tensor: 4 (over x, core).
Axes of the slice: x: 2, y: 2, z: 4, core: 2. Of those that a mesh axis runs over, the one named last changes fastest.
Arguments:
- states: bfloat16 [4, 1536, 1536], P('shard', 'context'), may hold values from -6 to 6
- segments: int32 [4, 1536], P('shard', 'context'), may hold values from 0 to 12, as said below
- routes: int32 [4, 1536, 8], P('shard', 'context'), may hold values from 0 to 15, all different within a row
- gates: float32 [4, 1536, 8], P('shard', 'context'), may hold values from 0.06 to 0.2
- valid: int32 [4, 1536], P('shard', 'context'), may hold values from 0 to 1, as said below
- teacher: bfloat16 [4, 1536, 1536], P('shard', 'context'), may hold values from -18 to 18
- attn_gain: float32 [1536], P('shard'), may hold values from 0.5 to 1.5
- w_query: bfloat16 [1536, 1536], P('shard', 'tensor'), may hold values from -0.15625 to 0.15625
- key_matrix: bfloat16 [1536, 512], P('shard', 'tensor'), may hold values from -0.15625 to 0.15625
- value_matrix: bfloat16 [1536, 512], P('shard', 'tensor'), may hold values from -0.15625 to 0.15625
- w_out: bfloat16 [1536, 1536], P('tensor', 'shard'), may hold values from -0.875 to 0.875
- moe_gain: float32 [1536], P('shard'), may hold values from 0.5 to 1.5
- w_gate: bfloat16 [16, 1536, 512], P(None, 'shard', 'tensor'), may hold values from -0.15625 to 0.15625
- w_up: bfloat16 [16, 1536, 512], P(None, 'shard', 'tensor'), may hold values from -0.15625 to 0.15625
- w_down: bfloat16 [16, 512, 1536], P(None, 'tensor', 'shard'), may hold values from -1 to 1
Outputs:
- loss: float32 [], replicated
- output: bfloat16 [4, 1536, 1536], P('shard', 'context')
- grad_states: float32 [4, 1536, 1536], P('shard', 'context')
- grad_attn_gain: float32 [1536], P('shard')
- grad_query: float32 [1536, 1536], P('shard', 'tensor')
- grad_key: float32 [1536, 512], P('shard', 'tensor')
- grad_value: float32 [1536, 512], P('shard', 'tensor')
- grad_out: float32 [1536, 1536], P('tensor', 'shard')
- grad_moe_gain: float32 [1536], P('shard')
- grad_gate: float32 [16, 1536, 512], P(None, 'shard', 'tensor')
- grad_up: float32 [16, 1536, 512], P(None, 'shard', 'tensor')
- grad_down: float32 [16, 512, 1536], P(None, 'tensor', 'shard')
The draws below stay inside these ranges and needn't reach their ends.
Inputs may be any that keep to these rules, and one draw needn't show every extreme that they name: `segments`: in each tree segment numbers never fall; 0 is the trunk and starts the tree; segment 3b + 1 (b = 0 to 3) is a branch followed by its two leaves 3b + 2 and 3b + 3; every number appears. The first token of each tree is valid. `routes`: each row names 8 different experts.
All inputs are finite; a program needn't handle non-finite values.
Results may differ from the reference program's by a relative error of at most 0.035.
Values may be sent and summed in bfloat16 or wider, within the bound.
A program may use at most 256 MiB of HBM per device.

```python
import math
import jax
import jax.numpy as jnp
from jax import lax

MODEL_WIDTH = 1536
QUERY_HEADS = 24
KEY_VALUE_HEADS = 8
HEAD_SIZE = 64
FF = 512
TOP = 8
EXPERTS = 16
TREE_TOK = 1536
TREES = 4


def draw_segments(key, part):
    key = jax.random.fold_in(key, 11)
    positions = jnp.arange(TREE_TOK, dtype=jnp.int32)

    def one_tree(tree_key):
        first_key, second_key = jax.random.split(tree_key)
        trunk_end = TREE_TOK // 2 - jax.random.randint(first_key, (1,), 0, TREE_TOK // 8 + 1, dtype=jnp.int32)
        others = jax.random.permutation(second_key, TREE_TOK // 2 - 1)[:11].astype(jnp.int32) + TREE_TOK // 2 + 1
        cuts = jnp.concatenate([trunk_end, others])
        return jnp.sum((positions[:, None] >= cuts[None, :]).astype(jnp.int32), axis=1).astype(jnp.int32)
    return jax.vmap(one_tree)(jax.random.split(key, TREES))


def draw_valid(key, part):
    key = jax.random.fold_in(key, 23)
    positions = jnp.arange(TREE_TOK, dtype=jnp.int32)
    overall = jnp.arange(TREES, dtype=jnp.int32)[:, None] * TREE_TOK + positions[None, :]
    span = TREES * TREE_TOK
    picks = jax.random.randint(key, (TREES, TREE_TOK), 0, 8 * span, dtype=jnp.int32)
    chosen = (picks < span + 7 * overall) | (positions[None, :] == 0)
    return chosen.astype(jnp.int32)


def draw_teacher(key, part):
    key = jax.random.fold_in(key, 37)
    overall = (jnp.arange(TREES, dtype=jnp.float32)[:, None] * TREE_TOK + jnp.arange(TREE_TOK, dtype=jnp.float32)[None, :]) / (TREES * TREE_TOK)
    base = jnp.clip(jax.random.normal(key, (TREES, TREE_TOK, MODEL_WIDTH), jnp.float32), -3.0, 3.0)
    rising = 1.0 + 5.0 * overall
    return (base * rising[:, :, None]).astype(jnp.bfloat16)


def steps_of(stream_key, extent, cuts, least, top_value):
    def one(dim, shards_of):
        steps = jax.random.uniform(jax.random.fold_in(jax.random.fold_in(stream_key, 6), dim), (shards_of,), jnp.float32, least / len(cuts), top_value / len(cuts))
        return jnp.repeat(jnp.exp(steps), extent[dim] // shards_of).reshape((-1,) + (1,) * (len(extent) - dim - 1))

    factor_of = one(*cuts[0])
    for cut in cuts[1:]:
        factor_of = factor_of * one(*cut)
    return factor_of


def different_ones(rng, rows, amount, top, lift):
    ranking = jax.random.permutation(jax.random.fold_in(rng, 1), amount)
    favour = ranking
    for power in range(3):
        favour = favour * favour // amount
    favour = favour * lift // amount
    lots = jax.random.randint(jax.random.fold_in(rng, 2), (rows, amount), 0, 4096) + favour
    holders = jax.random.permutation(jax.random.fold_in(rng, 3), rows)[jnp.arange(amount) % rows]
    lots = jnp.where(jnp.arange(rows)[:, None] == holders[None, :], 1 << 14, lots)
    priority = lots * amount + jnp.arange(amount)
    return lax.top_k(priority.astype(jnp.int32), top)[1].astype(jnp.int32)


def scatter_about(rng, extent, scale, bound, cuts=(), kind=jnp.bfloat16):
    array = jax.random.normal(rng, extent, jnp.float32) * scale
    if len(cuts) > 0:
        array = steps_of(rng, extent, cuts, -0.22, 0.18) * array
    return jnp.clip(array, min=-bound, max=bound).astype(kind)


def setup_inputs(seed: int = 0) -> dict:
    seeds = jax.random.split(jax.random.key(seed), 16)
    states = scatter_about(seeds[0], (TREES, TREE_TOK, MODEL_WIDTH), 1.0, 6.0, ((0, 2), (1, 4)))
    segments = draw_segments(jax.random.fold_in(seeds[15], 71), 0)
    routes = different_ones(seeds[2], TREES * TREE_TOK, EXPERTS, TOP, 4096).reshape((TREES, TREE_TOK, TOP))
    gates = jnp.clip(jnp.exp(math.log(0.2) - 1.2039728 * jax.random.uniform(seeds[3], (TREES, TREE_TOK, TOP), jnp.float32) ** steps_of(seeds[3], (TREES, TREE_TOK, TOP), ((0, 2), (1, 4)), -0.2, 0.2)), 0.06, 0.2)
    valid = draw_valid(jax.random.fold_in(seeds[15], 71), 0)
    teacher = draw_teacher(jax.random.fold_in(seeds[15], 71), 0)
    attn_gain = jnp.clip(1.0 + 0.1 * jax.random.normal(seeds[6], (MODEL_WIDTH,), jnp.float32), 0.5, 1.5)
    w_query = scatter_about(seeds[7], (MODEL_WIDTH, QUERY_HEADS * HEAD_SIZE), MODEL_WIDTH ** -0.5, 0.15625, ((0, 2), (1, 4)))
    key_matrix = scatter_about(seeds[8], (MODEL_WIDTH, KEY_VALUE_HEADS * HEAD_SIZE), MODEL_WIDTH ** -0.5, 0.15625, ((0, 2), (1, 4)))
    value_matrix = scatter_about(seeds[9], (MODEL_WIDTH, KEY_VALUE_HEADS * HEAD_SIZE), MODEL_WIDTH ** -0.5, 0.15625, ((0, 2), (1, 4)))
    w_out = scatter_about(seeds[10], (QUERY_HEADS * HEAD_SIZE, MODEL_WIDTH), (QUERY_HEADS * HEAD_SIZE // 32) ** -0.5, 0.875, ((0, 4), (1, 2)))
    moe_gain = jnp.clip(1.0 + 0.1 * jax.random.normal(seeds[11], (MODEL_WIDTH,), jnp.float32), 0.5, 1.5)
    w_gate = scatter_about(seeds[12], (EXPERTS, MODEL_WIDTH, FF), MODEL_WIDTH ** -0.5, 0.15625, ((1, 2), (2, 4)))
    w_up = scatter_about(seeds[13], (EXPERTS, MODEL_WIDTH, FF), MODEL_WIDTH ** -0.5, 0.15625, ((1, 2), (2, 4)))
    w_down = scatter_about(seeds[14], (EXPERTS, FF, MODEL_WIDTH), (FF // 16) ** -0.5, 1.0, ((1, 4), (2, 2)))
    return {"states": states, "segments": segments, "routes": routes, "gates": gates, "valid": valid, "teacher": teacher, "attn_gain": attn_gain, "w_query": w_query, "key_matrix": key_matrix, "value_matrix": value_matrix, "w_out": w_out, "moe_gain": moe_gain, "w_gate": w_gate, "w_up": w_up, "w_down": w_down}


PRECISE = lax.Precision.HIGHEST

@jax.custom_vjp
def low(v):
    return lax.optimization_barrier(v.astype(jnp.bfloat16)).astype(jnp.float32)

@jax.custom_vjp
def low_back(v):
    return v

def low_keep(v):
    return (low(v), None)

def low_pass(kept, grad):
    return (grad,)

def back_keep(v):
    return (v, None)

def back_low(kept, grad):
    return (low(grad),)
low.defvjp(low_keep, low_pass)
low_back.defvjp(back_keep, back_low)

def both_ways(values):
    return low_back(low(values))

def product(left, right):
    return jnp.dot(left, right, precision=PRECISE, preferred_element_type=jnp.float32)

def normalize(values, scales):
    return values * lax.rsqrt(lax.optimization_barrier(jnp.mean(values * values, axis=-1, keepdims=True)) + 1e-05) * scales

def visible(key_segment, query_segment):
    return (key_segment == 0) | (key_segment == query_segment) | (key_segment % 3 == 1) & (query_segment > key_segment) & (query_segment <= key_segment + 2)

def tree_attention(queries, keys_all, values_all, segment):
    total = queries.shape[0]
    block_rows = math.gcd(512, total)
    head_groups = KEY_VALUE_HEADS
    query_per_key = QUERY_HEADS // KEY_VALUE_HEADS
    query_heads = queries.reshape(total // block_rows, block_rows, head_groups, query_per_key, HEAD_SIZE)
    key_heads = keys_all.reshape(total, head_groups, HEAD_SIZE)
    value_heads = values_all.reshape(total, head_groups, HEAD_SIZE)
    positions = jnp.arange(total, dtype=jnp.int32)

    def one_block(packed):
        block_queries, block_index = packed
        query_pos = block_index * block_rows + jnp.arange(block_rows, dtype=jnp.int32)
        query_seg = lax.dynamic_slice_in_dim(segment, block_index * block_rows, block_rows)
        scores = jnp.einsum('qgjd,kgd->gjqk', block_queries, key_heads, precision=PRECISE) * 0.125
        scores = low_back(scores)
        allowed = (positions[None, :] <= query_pos[:, None]) & visible(segment[None, :], query_seg[:, None])
        scores = jnp.where(allowed, scores, -1e+30)
        shifted = scores - lax.optimization_barrier(jnp.max(scores, axis=-1, keepdims=True))
        expo = jnp.exp(shifted)
        weights = expo / lax.optimization_barrier(jnp.sum(expo, axis=-1, keepdims=True))
        return jnp.einsum('gjqk,kgd->qgjd', weights, value_heads, precision=PRECISE)
    block_ids = jnp.arange(total // block_rows, dtype=jnp.int32)
    outputs = lax.map(jax.checkpoint(one_block), (query_heads, block_ids))
    return outputs.reshape(total, QUERY_HEADS * HEAD_SIZE)

def reference(states, segments, routes, gates, valid, teacher, attn_gain, w_query, key_matrix, value_matrix, w_out, moe_gain, w_gate, w_up, w_down):
    expert_ids = jnp.arange(EXPERTS, dtype=jnp.int32)
    combine = lax.optimization_barrier(jnp.sum(gates.astype(jnp.float32)[..., None] * (routes[..., None] == expert_ids).astype(jnp.float32), axis=-2)).reshape(-1, EXPERTS)
    valid_f = valid.astype(jnp.float32).reshape(-1)
    teacher_f = teacher.astype(jnp.float32).reshape(-1, MODEL_WIDTH)

    def forward(flat, attn_scale, query_w, key_w, value_w, out_w, moe_scale, gate_w, up_w, down_w):
        normed = low(normalize(flat, attn_scale))
        queries = both_ways(product(normed, query_w))
        keys_all = both_ways(product(normed, key_w))
        values_all = both_ways(product(normed, value_w))
        pieces = []
        for tree in range(TREES):
            lo_row = tree * TREE_TOK
            pieces.append(tree_attention(queries[lo_row:lo_row + TREE_TOK], keys_all[lo_row:lo_row + TREE_TOK], values_all[lo_row:lo_row + TREE_TOK], segments[tree]))
        attended = both_ways(jnp.concatenate(pieces, axis=0))
        branch = low_back(product(attended, out_w))
        hidden_state = flat + branch
        normed_two = low(normalize(hidden_state, moe_scale))

        def expert_step(running, packed):
            gate_e, up_e, down_e, weight_e = packed
            pre_gate = low_back(product(normed_two, gate_e))
            pre_up = low_back(product(normed_two, up_e))
            middle = low(pre_gate * jax.nn.sigmoid(pre_gate) * pre_up)
            expert_out = low_back(product(middle, down_e))
            return (running + weight_e[:, None] * expert_out, None)
        moe, _ = lax.scan(jax.checkpoint(expert_step), jnp.zeros_like(flat), (gate_w, up_w, down_w, combine.T))
        result = hidden_state + moe
        counted = jnp.sum(valid_f)
        error = result - teacher_f
        loss = jnp.sum(valid_f[:, None] * error * error) / (counted * MODEL_WIDTH)
        return (loss, result)
    primals = (states.astype(jnp.float32).reshape(-1, MODEL_WIDTH), attn_gain.astype(jnp.float32), w_query.astype(jnp.float32), key_matrix.astype(jnp.float32), value_matrix.astype(jnp.float32), w_out.astype(jnp.float32), moe_gain.astype(jnp.float32), w_gate.astype(jnp.float32), w_up.astype(jnp.float32), w_down.astype(jnp.float32))
    loss, pull, result = jax.vjp(forward, *primals, has_aux=True)
    grads = pull(jnp.asarray(TREES * TREE_TOK * MODEL_WIDTH / 2, dtype=jnp.float32))
    return (loss, result.reshape(TREES, TREE_TOK, MODEL_WIDTH).astype(jnp.bfloat16), grads[0].reshape(TREES, TREE_TOK, MODEL_WIDTH), grads[1], grads[2], grads[3], grads[4], grads[5], grads[6], grads[7], grads[8], grads[9])
```

```python
import math

import jax
import jax.numpy as jnp
from jax import lax
from jax.experimental import pallas as pl
from jax.experimental.pallas import tpu as pltpu
from jax.sharding import PartitionSpec as P

HEAD = 64
EPS = 1e-05
BF = jnp.bfloat16
F32 = jnp.float32
VMEM_LIMIT = 56 * 1024 * 1024


def matmul(left, right):
    return jnp.dot(left, right, preferred_element_type=F32)


def contract_first(left, right):
    return lax.dot_general(left, right, (((0,), (0,)), ((), ())), preferred_element_type=F32)


def contract_last(left, right):
    return lax.dot_general(left, right, (((1,), (1,)), ((), ())), preferred_element_type=F32)


def attention_forward_kernel(
    place, q_ref, kv_ref, last_ref, seg_ref, o_ref, lse_ref, bias, tops, norms, sums
):
    rows = q_ref.shape[0]
    width = kv_ref.shape[2] // 2
    total = kv_ref.shape[1]
    heads = q_ref.shape[1] // HEAD
    per_group = q_ref.shape[1] // width
    block = bias.shape[1]
    tops[...] = jnp.full_like(tops, -1e30)
    norms[...] = jnp.zeros_like(norms)
    sums[...] = jnp.zeros_like(sums)

    @pl.loop(0, total // block)
    def _(index):
        begin = pl.multiple_of(index * block, block)
        key_pos = begin + lax.broadcasted_iota(jnp.int32, (rows, block), 1)
        query_pos = place[0] * rows + lax.broadcasted_iota(jnp.int32, (rows, block), 0)
        allowed = (key_pos <= query_pos) & (seg_ref[...] <= last_ref[0, :, pl.ds(begin, block)])
        bias[...] = jnp.where(allowed, 0.0, -2e30)
        for head in range(heads):
            group = head // per_group
            cols = slice(head * HEAD, (head + 1) * HEAD)
            keys = kv_ref[0, pl.ds(begin, block), group * HEAD : (group + 1) * HEAD]
            values = kv_ref[
                0, pl.ds(begin, block), width + group * HEAD : width + (group + 1) * HEAD
            ]
            scores = contract_last(q_ref[:, cols], keys) * 0.125 + bias[...]
            old = tops[:, head : head + 1]
            top = jnp.maximum(old, jnp.max(scores, axis=1, keepdims=True))
            weights = jnp.exp(scores - top)
            shrink = jnp.exp(old - top)
            tops[:, head : head + 1] = top
            norms[:, head : head + 1] = norms[:, head : head + 1] * shrink + jnp.sum(
                weights, axis=1, keepdims=True
            )
            sums[:, cols] = sums[:, cols] * shrink + matmul(weights.astype(BF), values)

    for head in range(heads):
        cols = slice(head * HEAD, (head + 1) * HEAD)
        o_ref[:, cols] = (sums[:, cols] / norms[:, head : head + 1]).astype(BF)
    lse = tops[...] + jnp.log(norms[...] + jnp.where(norms[...] == 0.0, 1.0, 0.0))
    lse_ref[0] = lse.T[: lse_ref.shape[1]]


def attention_forward(place, q, kv, last_row, seg_col):
    trees, total, both = kv.shape
    rows = q.shape[0] // trees
    cols = q.shape[1]
    block = math.gcd(total, 1536)
    return pl.pallas_call(
        attention_forward_kernel,
        out_shape=(
            jax.ShapeDtypeStruct(q.shape, BF),
            jax.ShapeDtypeStruct((trees, 8, rows), F32),
        ),
        grid_spec=pltpu.PrefetchScalarGridSpec(
            num_scalar_prefetch=1,
            grid=(trees,),
            in_specs=[
                pl.BlockSpec((rows, cols), lambda t, s: (t, 0)),
                pl.BlockSpec((1, total, both), lambda t, s: (t, 0, 0)),
                pl.BlockSpec((1, 1, total), lambda t, s: (t, 0, 0)),
                pl.BlockSpec((rows, 1), lambda t, s: (t, 0)),
            ],
            out_specs=[
                pl.BlockSpec((rows, cols), lambda t, s: (t, 0)),
                pl.BlockSpec((1, 8, rows), lambda t, s: (t, 0, 0)),
            ],
            scratch_shapes=[
                pltpu.VMEM((rows, block), F32),
                pltpu.VMEM((rows, 128), F32),
                pltpu.VMEM((rows, 128), F32),
                pltpu.VMEM((rows, cols), F32),
            ],
        ),
        compiler_params=pltpu.CompilerParams(vmem_limit_bytes=VMEM_LIMIT),
        name="attention_forward",
    )(place, q, kv, last_row, seg_col)


def attention_backward_kernel(
    place, q_ref, do_ref, o_ref, lse_ref, kv_ref, last_ref, seg_ref, dq_ref, dkv_ref, bias, deltas, sums
):
    rows = q_ref.shape[0]
    width = kv_ref.shape[2] // 2
    total = kv_ref.shape[1]
    heads = q_ref.shape[1] // HEAD
    per_group = q_ref.shape[1] // width
    block = bias.shape[0]
    sums[...] = jnp.zeros_like(sums)
    for head in range(heads):
        cols = slice(head * HEAD, (head + 1) * HEAD)
        product = do_ref[:, cols].astype(F32) * o_ref[:, cols].astype(F32)
        deltas[head] = lax.dot_general(
            jnp.ones((8, HEAD), F32),
            product,
            (((1,), (1,)), ((), ())),
            precision=lax.Precision.HIGHEST,
            preferred_element_type=F32,
        )

    @pl.loop(0, total // block)
    def _(index):
        begin = pl.multiple_of(index * block, block)
        span = pl.ds(begin, block)
        key_pos = begin + lax.broadcasted_iota(jnp.int32, (block, rows), 0)
        query_pos = place[0] * rows + lax.broadcasted_iota(jnp.int32, (block, rows), 1)
        allowed = (key_pos <= query_pos) & (seg_ref[0] <= last_ref[span, :])
        bias[...] = jnp.where(allowed, 0.0, -2e30)
        for group in range(heads // per_group):
            keys = kv_ref[0, span, group * HEAD : (group + 1) * HEAD]
            values = kv_ref[0, span, width + group * HEAD : width + (group + 1) * HEAD]
            dk = jnp.zeros((block, HEAD), F32)
            dv = jnp.zeros((block, HEAD), F32)
            for head in range(group * per_group, (group + 1) * per_group):
                cols = slice(head * HEAD, (head + 1) * HEAD)
                queries = q_ref[:, cols]
                grads = do_ref[:, cols]
                scores = contract_last(keys, queries) * 0.125 + bias[...]
                probs = jnp.exp(scores - lse_ref[0, head : head + 1, :])
                grad_probs = contract_last(values, grads)
                grad_scores = (probs * (grad_probs - deltas[head, 0:1, :])).astype(BF)
                dv = dv + matmul(probs.astype(BF), grads)
                dk = dk + matmul(grad_scores, queries)
                sums[:, cols] += contract_first(grad_scores, keys)
            dkv_ref[0, span, group * HEAD : (group + 1) * HEAD] = (dk * 0.125).astype(BF)
            dkv_ref[0, span, width + group * HEAD : width + (group + 1) * HEAD] = dv.astype(BF)

    dq_ref[...] = (sums[...] * 0.125).astype(BF)


def attention_backward(place, q, do, o, lse, kv, last_col, seg_row):
    trees, total, both = kv.shape
    rows = q.shape[0] // trees
    cols = q.shape[1]
    block = math.gcd(total, 768)
    by_tree = pl.BlockSpec((rows, cols), lambda t, s: (t, 0))
    return pl.pallas_call(
        attention_backward_kernel,
        out_shape=(
            jax.ShapeDtypeStruct(q.shape, BF),
            jax.ShapeDtypeStruct(kv.shape, BF),
        ),
        grid_spec=pltpu.PrefetchScalarGridSpec(
            num_scalar_prefetch=1,
            grid=(trees,),
            in_specs=[
                by_tree,
                by_tree,
                by_tree,
                pl.BlockSpec((1, 8, rows), lambda t, s: (t, 0, 0)),
                pl.BlockSpec((1, total, both), lambda t, s: (t, 0, 0)),
                pl.BlockSpec((total, 1), lambda t, s: (t, 0)),
                pl.BlockSpec((1, 1, rows), lambda t, s: (t, 0, 0)),
            ],
            out_specs=[
                by_tree,
                pl.BlockSpec((1, total, both), lambda t, s: (t, 0, 0)),
            ],
            scratch_shapes=[
                pltpu.VMEM((block, rows), F32),
                pltpu.VMEM((q.shape[1] // HEAD, 8, rows), F32),
                pltpu.VMEM((rows, cols), F32),
            ],
        ),
        compiler_params=pltpu.CompilerParams(vmem_limit_bytes=VMEM_LIMIT),
        name="attention_backward",
    )(place, q, do, o, lse, kv, last_col, seg_row)


def stage_weights(step, split, gate_refs, up_refs, down_refs, wide, tall):
    half, ff = gate_refs[0].shape[1], gate_refs[0].shape[2]
    for a in range(2):
        for part, refs in ((0, gate_refs), (1, up_refs)):
            cols = pl.ds((2 * a + part) * ff, ff)
            wide[0:half, cols] = refs[0][a]

            @pl.when(step < split)
            def _(refs=refs, cols=cols, a=a):
                wide[half : 2 * half, cols] = refs[1][a]

            @pl.when(step >= split)
            def _(refs=refs, cols=cols, a=a):
                wide[half : 2 * half, cols] = refs[2][a]

        rows = pl.ds(a * ff, ff)
        tall[rows, 0:half] = down_refs[0][a]

        @pl.when(step < split)
        def _(rows=rows, a=a):
            tall[rows, half : 2 * half] = down_refs[1][a]

        @pl.when(step >= split)
        def _(rows=rows, a=a):
            tall[rows, half : 2 * half] = down_refs[2][a]


def column(block, index):
    lane = lax.broadcasted_iota(jnp.int32, block.shape, 1)
    return jnp.sum(jnp.where(lane == index, block, 0.0), axis=1, keepdims=True)


def experts_forward_kernel(
    parity, n_ref, c_ref, g0, g1, g2, u0, u1, u2, d0, d1, d2, pre_ref, cm_ref, m_ref, wide, tall, acc
):
    step = pl.program_id(0)
    steps = pl.num_programs(0)
    split = steps // 2
    ff = g0.shape[2]
    pair = lax.rem(parity[0] * split + step, steps)
    stage_weights(step, split, (g0, g1, g2), (u0, u1, u2), (d0, d1, d2), wide, tall)
    tile = 256

    @pl.when(step == 0)
    def _():
        acc[...] = jnp.zeros_like(acc)

    @pl.loop(0, n_ref.shape[0] // tile)
    def _(index):
        rows = pl.ds(pl.multiple_of(index * tile, tile), tile)
        hidden = matmul(n_ref[rows, :], wide[...])
        pre_ref[0, rows, :] = hidden.astype(BF)
        pieces = []
        for a in range(2):
            gate = hidden[:, 2 * a * ff : (2 * a + 1) * ff]
            up = hidden[:, (2 * a + 1) * ff : (2 * a + 2) * ff]
            weight = column(c_ref[rows, :], 2 * pair + a)
            pieces.append((weight * (gate * jax.nn.sigmoid(gate) * up)).astype(BF))
        middle = jnp.concatenate(pieces, axis=1)
        cm_ref[0, rows, :] = middle
        acc[rows, :] += matmul(middle, tall[...])

    @pl.when(step == steps - 1)
    def _():
        m_ref[...] = acc[...].astype(BF)


def weight_specs(steps, half, ff):
    split = steps // 2

    def own(i, s):
        return (lax.rem(s[0] * split + i, steps), 0, 0)

    def first(i, s):
        return (jnp.minimum(i, split - 1), 0, 0)

    def second(i, s):
        return (jnp.maximum(i - split, 0), 0, 0)

    wide = [pl.BlockSpec((2, half, ff), f) for f in (own, first, second)]
    tall = [pl.BlockSpec((2, ff, half), f) for f in (own, first, second)]
    return wide + wide + tall, own


def experts_forward(parity, normed, combine, gates, ups, downs):
    tokens, width = normed.shape
    experts, half, ff = gates[0].shape
    steps = experts // 2
    specs, _ = weight_specs(steps, half, ff)
    return pl.pallas_call(
        experts_forward_kernel,
        out_shape=(
            jax.ShapeDtypeStruct((steps, tokens, 4 * ff), BF),
            jax.ShapeDtypeStruct((steps, tokens, 2 * ff), BF),
            jax.ShapeDtypeStruct((tokens, width), BF),
        ),
        grid_spec=pltpu.PrefetchScalarGridSpec(
            num_scalar_prefetch=1,
            grid=(steps,),
            in_specs=[
                pl.BlockSpec((tokens, width), lambda i, s: (0, 0)),
                pl.BlockSpec((tokens, experts), lambda i, s: (0, 0)),
            ]
            + specs,
            out_specs=[
                pl.BlockSpec((1, tokens, 4 * ff), lambda i, s: (i, 0, 0)),
                pl.BlockSpec((1, tokens, 2 * ff), lambda i, s: (i, 0, 0)),
                pl.BlockSpec((tokens, width), lambda i, s: (0, 0)),
            ],
            scratch_shapes=[
                pltpu.VMEM((width, 4 * ff), BF),
                pltpu.VMEM((2 * ff, width), BF),
                pltpu.VMEM((tokens, width), F32),
            ],
        ),
        compiler_params=pltpu.CompilerParams(vmem_limit_bytes=VMEM_LIMIT),
        name="experts_forward",
    )(parity, normed, combine, *gates, *ups, *downs)


def experts_backward_kernel(
    parity, n_ref, gy_ref, c_ref, g0, g1, g2, u0, u1, u2, d0, d1, d2, pre_ref, cm_ref,
    gg_own, gg_far, gu_own, gu_far, gd_own, gd_far, dn_ref, wide, tall, acc, grads
):
    step = pl.program_id(0)
    steps = pl.num_programs(0)
    split = steps // 2
    half, ff = g0.shape[1], g0.shape[2]
    pair = lax.rem(parity[0] * split + step, steps)
    stage_weights(step, split, (g0, g1, g2), (u0, u1, u2), (d0, d1, d2), wide, tall)
    tile = 256

    @pl.when(step == 0)
    def _():
        acc[...] = jnp.zeros_like(acc)

    @pl.loop(0, gy_ref.shape[0] // tile)
    def _(index):
        rows = pl.ds(pl.multiple_of(index * tile, tile), tile)
        grad_middle = contract_last(gy_ref[rows, :], tall[...])
        for a in range(2):
            gate = pre_ref[0, rows, 2 * a * ff : (2 * a + 1) * ff].astype(F32)
            up = pre_ref[0, rows, (2 * a + 1) * ff : (2 * a + 2) * ff].astype(F32)
            weight = column(c_ref[rows, :], 2 * pair + a)
            gm = weight * grad_middle[:, a * ff : (a + 1) * ff]
            sig = jax.nn.sigmoid(gate)
            grads[rows, 2 * a * ff : (2 * a + 1) * ff] = (
                gm * up * (sig + gate * sig * (1.0 - sig))
            ).astype(BF)
            grads[rows, (2 * a + 1) * ff : (2 * a + 2) * ff] = (gm * gate * sig).astype(BF)
        acc[rows, :] += contract_last(grads[rows, :], wide[...])

    for part, gate_out, up_out in ((0, gg_own, gu_own), (1, gg_far, gu_far)):

        @pl.loop(0, half // tile)
        def _(index, part=part, gate_out=gate_out, up_out=up_out):
            begin = pl.multiple_of(index * tile, tile)
            block = matmul(n_ref[pl.ds(part * half + begin, tile), :], grads[...]).astype(BF)
            for a in range(2):
                gate_out[a, pl.ds(begin, tile), :] = block[:, 2 * a * ff : (2 * a + 1) * ff]
                up_out[a, pl.ds(begin, tile), :] = block[:, (2 * a + 1) * ff : (2 * a + 2) * ff]

    middle = cm_ref[0].T
    for part, out in ((0, gd_own), (1, gd_far)):
        block = matmul(middle, gy_ref[:, part * half : (part + 1) * half]).astype(BF)
        for a in range(2):
            out[a] = block[a * ff : (a + 1) * ff]

    @pl.when(step == steps - 1)
    def _():
        dn_ref[...] = acc[...].astype(BF)


def experts_backward(parity, normed_t, grad_y, combine, gates, ups, downs, pre, middle):
    tokens, width = grad_y.shape
    experts, half, ff = gates[0].shape
    steps = experts // 2
    specs, own = weight_specs(steps, half, ff)
    wide_shape = jax.ShapeDtypeStruct((experts, half, ff), BF)
    tall_shape = jax.ShapeDtypeStruct((experts, ff, half), BF)
    return pl.pallas_call(
        experts_backward_kernel,
        out_shape=(wide_shape,) * 4
        + (tall_shape,) * 2
        + (jax.ShapeDtypeStruct((tokens, width), BF),),
        grid_spec=pltpu.PrefetchScalarGridSpec(
            num_scalar_prefetch=1,
            grid=(steps,),
            in_specs=[
                pl.BlockSpec((width, tokens), lambda i, s: (0, 0)),
                pl.BlockSpec((tokens, width), lambda i, s: (0, 0)),
                pl.BlockSpec((tokens, experts), lambda i, s: (0, 0)),
            ]
            + specs
            + [
                pl.BlockSpec((1, tokens, 4 * ff), lambda i, s: (i, 0, 0)),
                pl.BlockSpec((1, tokens, 2 * ff), lambda i, s: (i, 0, 0)),
            ],
            out_specs=[pl.BlockSpec((2, half, ff), own)] * 4
            + [pl.BlockSpec((2, ff, half), own)] * 2
            + [pl.BlockSpec((tokens, width), lambda i, s: (0, 0))],
            scratch_shapes=[
                pltpu.VMEM((width, 4 * ff), BF),
                pltpu.VMEM((2 * ff, width), BF),
                pltpu.VMEM((tokens, width), F32),
                pltpu.VMEM((tokens, 4 * ff), BF),
            ],
        ),
        compiler_params=pltpu.CompilerParams(vmem_limit_bytes=VMEM_LIMIT),
        name="experts_backward",
    )(parity, normed_t, grad_y, combine, *gates, *ups, *downs, pre, middle)


def norm_forward(values, scale):
    inverse = lax.rsqrt(jnp.mean(values * values, axis=-1, keepdims=True) + EPS)
    return values * inverse * scale, inverse


def norm_backward(values, inverse, scale, grad):
    scaled = grad * scale
    along = jnp.mean(scaled * values, axis=-1, keepdims=True)
    grad_values = inverse * scaled - values * (inverse * inverse * inverse * along)
    grad_scale = jnp.sum(grad * values * inverse, axis=0)
    return grad_values, grad_scale


def local(
    states, segments, routes, gates, valid, teacher, attn_gain, w_query, key_matrix, value_matrix,
    w_out, moe_gain, w_gate, w_up, w_down,
):
    shard = lax.axis_index("shard")
    context = lax.axis_index("context")
    shards = lax.axis_size("shard")
    contexts = lax.axis_size("context")
    trees, rows, width = states.shape
    tokens = trees * rows
    half = width // 2
    experts = w_gate.shape[0]
    swap = [(a, shards - 1 - a) for a in range(shards)]
    pairs = [(a, a + 1 - 2 * (a % 2)) for a in range(contexts)]
    parity = lax.rem(context, 2)
    place = jnp.reshape(context, (1,)).astype(jnp.int32)
    side = jnp.reshape(parity, (1,)).astype(jnp.int32)

    def over_shard(value):
        return lax.ppermute(value, "shard", swap)

    def turned(value):
        return jnp.where(shard == 0, value, jnp.concatenate([value[:, half:], value[:, :half]], 1))

    qkv_own = jnp.concatenate([w_query, key_matrix, value_matrix], axis=1)
    qkv_w = jnp.concatenate([qkv_own, over_shard(qkv_own)], axis=0)
    gains_own = jnp.stack([attn_gain, moe_gain])
    gains = jnp.concatenate([gains_own, over_shard(gains_own)], axis=1)
    out_w = jnp.concatenate([w_out, over_shard(w_out)], axis=1)
    attn_scale, moe_scale = gains[0], gains[1]

    def both_ways(weights):
        mine = lax.dynamic_slice_in_dim(weights, parity * (experts // 2), experts // 2, 0)
        direct = over_shard(mine)
        relayed = lax.ppermute(direct, "context", pairs)
        return (weights, direct, relayed)

    gate_ws, up_ws, down_ws = both_ways(w_gate), both_ways(w_up), both_ways(w_down)

    valid_total = lax.psum(jnp.sum(valid.astype(F32)), ("shard", "context"))
    segments_all = lax.all_gather(segments, "context", axis=1, tiled=True)
    last = jnp.where(
        segments_all == 0,
        1 << 20,
        jnp.where(segments_all % 3 == 1, segments_all + 2, segments_all),
    )

    x = turned(states.reshape(tokens, width)).astype(F32)
    normed, inverse_one = norm_forward(x, attn_scale)
    normed = normed.astype(BF)
    qkv = matmul(normed, qkv_w).astype(BF)
    query_cols = w_query.shape[1]
    both = qkv.shape[1] - query_cols
    q = qkv[:, :query_cols]
    kv = lax.all_gather(
        qkv[:, query_cols:].reshape(trees, rows, both), "context", axis=1, tiled=True
    )
    total = kv.shape[1]
    attended, lse = attention_forward(
        place, q, kv, last.reshape(trees, 1, total), segments.reshape(tokens, 1)
    )
    branch = lax.psum(matmul(attended, out_w).astype(BF), "tensor").astype(F32)
    hidden = x + branch
    normed_two, inverse_two = norm_forward(hidden, moe_scale)
    normed_two = normed_two.astype(BF)

    expert_ids = jnp.arange(experts, dtype=jnp.int32)
    combine = jnp.sum(
        gates.reshape(tokens, -1)[..., None]
        * (routes.reshape(tokens, -1)[..., None] == expert_ids).astype(F32),
        axis=1,
    )
    pre, middle, moe_part = experts_forward(
        side, normed_two, combine, gate_ws, up_ws, down_ws
    )
    moe = lax.psum(moe_part, "tensor").astype(F32)
    result = hidden + moe
    mask = valid.reshape(tokens, 1).astype(F32)
    error = result - turned(teacher.reshape(tokens, width)).astype(F32)
    square = lax.psum(jnp.sum(mask * error * error), ("shard", "context"))
    loss = square / (valid_total * width)
    token_total = tokens * shards * contexts
    grad_y = token_total / valid_total * mask * error

    grads = experts_backward(
        side, normed_two.T, grad_y.astype(BF), combine, gate_ws, up_ws, down_ws, pre, middle
    )
    gg_own, gg_far, gu_own, gu_far, gd_own, gd_far, dn_part = grads

    def reduced(own, far):
        pair = own.astype(F32) + over_shard(far).astype(F32)
        return lax.psum(pair.astype(BF), "context").astype(F32)

    final_gate = reduced(gg_own, gg_far)
    final_up = reduced(gu_own, gu_far)
    final_down = reduced(gd_own, gd_far)

    grad_normed_two = lax.psum(dn_part, "tensor").astype(F32)
    grad_hidden_norm, grad_moe_scale = norm_backward(
        hidden, inverse_two, moe_scale, grad_normed_two
    )
    grad_hidden = grad_y + grad_hidden_norm
    grad_branch = grad_hidden.astype(BF)
    grad_out_w = contract_first(attended, grad_branch).astype(BF)
    grad_attended = contract_last(grad_branch, out_w).astype(BF)
    grad_q, grad_kv_all = attention_backward(
        place, q, grad_attended, attended, lse, kv, last.reshape(trees * total, 1),
        segments.reshape(trees, 1, rows),
    )
    grad_kv = lax.psum_scatter(grad_kv_all, "context", scatter_dimension=1, tiled=True)
    grad_qkv = jnp.concatenate([grad_q, grad_kv.reshape(tokens, both)], axis=1)
    grad_qkv_w = contract_first(normed, grad_qkv).astype(BF)
    grad_normed = lax.psum(contract_last(grad_qkv, qkv_w).astype(BF), "tensor").astype(F32)
    grad_inputs_norm, grad_attn_scale = norm_backward(x, inverse_one, attn_scale, grad_normed)
    grad_inputs = grad_hidden + grad_inputs_norm

    final_out = reduced(grad_out_w[:, :half], grad_out_w[:, half:])
    final_qkv = reduced(grad_qkv_w[:half], grad_qkv_w[half:])
    grad_scales = jnp.stack([grad_attn_scale, grad_moe_scale])
    final_scales = lax.psum(
        grad_scales[:, :half] + over_shard(grad_scales[:, half:]), "context"
    )
    kv_cols = key_matrix.shape[1]
    return (
        loss,
        turned(result).reshape(trees, rows, width).astype(BF),
        turned(grad_inputs).reshape(trees, rows, width),
        final_scales[0],
        final_qkv[:, :query_cols],
        final_qkv[:, query_cols : query_cols + kv_cols],
        final_qkv[:, query_cols + kv_cols :],
        final_out,
        final_scales[1],
        final_gate,
        final_up,
        final_down,
    )


def solution(mesh):
    return jax.shard_map(
        local,
        mesh=mesh,
        in_specs=(
            P("shard", "context", None),
            P("shard", "context"),
            P("shard", "context", None),
            P("shard", "context", None),
            P("shard", "context"),
            P("shard", "context", None),
            P("shard"),
            P("shard", "tensor"),
            P("shard", "tensor"),
            P("shard", "tensor"),
            P("tensor", "shard"),
            P("shard"),
            P(None, "shard", "tensor"),
            P(None, "shard", "tensor"),
            P(None, "tensor", "shard"),
        ),
        out_specs=(
            P(),
            P("shard", "context", None),
            P("shard", "context", None),
            P("shard"),
            P("shard", "tensor"),
            P("shard", "tensor"),
            P("shard", "tensor"),
            P("tensor", "shard"),
            P("shard"),
            P(None, "shard", "tensor"),
            P(None, "shard", "tensor"),
            P(None, "tensor", "shard"),
        ),
        check_vma=False,
    )
```

```python
import math

import jax
import jax.numpy as jnp
from jax import lax
from jax.experimental import pallas as pl
from jax.experimental.pallas import tpu as pltpu
from jax.sharding import PartitionSpec as P

HEAD = 64
EPS = 1e-05
BF = jnp.bfloat16
F32 = jnp.float32
MESH = pl.DeviceIdType.MESH
VMEM_LIMIT = 56 * 1024 * 1024


def matmul(left, right):
    return jnp.dot(left, right, preferred_element_type=F32)


def contract_first(left, right):
    return lax.dot_general(left, right, (((0,), (0,)), ((), ())), preferred_element_type=F32)


def contract_last(left, right):
    return lax.dot_general(left, right, (((1,), (1,)), ((), ())), preferred_element_type=F32)


def attention_forward_kernel(
    place, q_ref, kv_ref, last_ref, seg_ref, o_ref, lse_ref, bias, tops, norms, sums
):
    rows = q_ref.shape[0]
    width = kv_ref.shape[2] // 2
    total = kv_ref.shape[1]
    heads = q_ref.shape[1] // HEAD
    per_group = q_ref.shape[1] // width
    block = bias.shape[1]
    tops[...] = jnp.full_like(tops, -1e30)
    norms[...] = jnp.zeros_like(norms)
    sums[...] = jnp.zeros_like(sums)

    @pl.loop(0, total // block)
    def _(index):
        begin = pl.multiple_of(index * block, block)
        key_pos = begin + lax.broadcasted_iota(jnp.int32, (rows, block), 1)
        query_pos = place[0] * rows + lax.broadcasted_iota(jnp.int32, (rows, block), 0)
        allowed = (key_pos <= query_pos) & (seg_ref[...] <= last_ref[0, :, pl.ds(begin, block)])
        bias[...] = jnp.where(allowed, 0.0, -2e30)
        for head in range(heads):
            group = head // per_group
            cols = slice(head * HEAD, (head + 1) * HEAD)
            keys = kv_ref[0, pl.ds(begin, block), group * HEAD : (group + 1) * HEAD]
            values = kv_ref[
                0, pl.ds(begin, block), width + group * HEAD : width + (group + 1) * HEAD
            ]
            scores = contract_last(q_ref[:, cols], keys) * 0.125 + bias[...]
            old = tops[:, head : head + 1]
            top = jnp.maximum(old, jnp.max(scores, axis=1, keepdims=True))
            weights = jnp.exp(scores - top)
            shrink = jnp.exp(old - top)
            tops[:, head : head + 1] = top
            norms[:, head : head + 1] = norms[:, head : head + 1] * shrink + jnp.sum(
                weights, axis=1, keepdims=True
            )
            sums[:, cols] = sums[:, cols] * shrink + matmul(weights.astype(BF), values)

    for head in range(heads):
        cols = slice(head * HEAD, (head + 1) * HEAD)
        o_ref[:, cols] = (sums[:, cols] / norms[:, head : head + 1]).astype(BF)
    lse = tops[...] + jnp.log(norms[...] + jnp.where(norms[...] == 0.0, 1.0, 0.0))
    lse_ref[0] = lse.T[: lse_ref.shape[1]]


def attention_forward(place, q, kv, last_row, seg_col):
    trees, total, both = kv.shape
    rows = q.shape[0] // trees
    cols = q.shape[1]
    block = math.gcd(total, 1536)
    return pl.pallas_call(
        attention_forward_kernel,
        out_shape=(
            jax.ShapeDtypeStruct(q.shape, BF),
            jax.ShapeDtypeStruct((trees, 8, rows), F32),
        ),
        grid_spec=pltpu.PrefetchScalarGridSpec(
            num_scalar_prefetch=1,
            grid=(trees,),
            in_specs=[
                pl.BlockSpec((rows, cols), lambda t, s: (t, 0)),
                pl.BlockSpec((1, total, both), lambda t, s: (t, 0, 0)),
                pl.BlockSpec((1, 1, total), lambda t, s: (t, 0, 0)),
                pl.BlockSpec((rows, 1), lambda t, s: (t, 0)),
            ],
            out_specs=[
                pl.BlockSpec((rows, cols), lambda t, s: (t, 0)),
                pl.BlockSpec((1, 8, rows), lambda t, s: (t, 0, 0)),
            ],
            scratch_shapes=[
                pltpu.VMEM((rows, block), F32),
                pltpu.VMEM((rows, 128), F32),
                pltpu.VMEM((rows, 128), F32),
                pltpu.VMEM((rows, cols), F32),
            ],
        ),
        compiler_params=pltpu.CompilerParams(vmem_limit_bytes=VMEM_LIMIT),
        name="attention_forward",
    )(place, q, kv, last_row, seg_col)


def attention_backward_kernel(
    place, q_ref, do_ref, o_ref, lse_ref, kv_ref, last_ref, seg_ref, dq_ref, dkv_ref, bias, deltas, sums
):
    rows = q_ref.shape[0]
    width = kv_ref.shape[2] // 2
    total = kv_ref.shape[1]
    heads = q_ref.shape[1] // HEAD
    per_group = q_ref.shape[1] // width
    block = bias.shape[0]
    sums[...] = jnp.zeros_like(sums)
    for head in range(heads):
        cols = slice(head * HEAD, (head + 1) * HEAD)
        product = do_ref[:, cols].astype(F32) * o_ref[:, cols].astype(F32)
        deltas[head] = lax.dot_general(
            jnp.ones((8, HEAD), F32),
            product,
            (((1,), (1,)), ((), ())),
            precision=lax.Precision.HIGHEST,
            preferred_element_type=F32,
        )

    @pl.loop(0, total // block)
    def _(index):
        begin = pl.multiple_of(index * block, block)
        span = pl.ds(begin, block)
        key_pos = begin + lax.broadcasted_iota(jnp.int32, (block, rows), 0)
        query_pos = place[0] * rows + lax.broadcasted_iota(jnp.int32, (block, rows), 1)
        allowed = (key_pos <= query_pos) & (seg_ref[0] <= last_ref[span, :])
        bias[...] = jnp.where(allowed, 0.0, -2e30)
        for group in range(heads // per_group):
            keys = kv_ref[0, span, group * HEAD : (group + 1) * HEAD]
            values = kv_ref[0, span, width + group * HEAD : width + (group + 1) * HEAD]
            dk = jnp.zeros((block, HEAD), F32)
            dv = jnp.zeros((block, HEAD), F32)
            for head in range(group * per_group, (group + 1) * per_group):
                cols = slice(head * HEAD, (head + 1) * HEAD)
                queries = q_ref[:, cols]
                grads = do_ref[:, cols]
                scores = contract_last(keys, queries) * 0.125 + bias[...]
                probs = jnp.exp(scores - lse_ref[0, head : head + 1, :])
                grad_probs = contract_last(values, grads)
                grad_scores = (probs * (grad_probs - deltas[head, 0:1, :])).astype(BF)
                dv = dv + matmul(probs.astype(BF), grads)
                dk = dk + matmul(grad_scores, queries)
                sums[:, cols] += contract_first(grad_scores, keys)
            dkv_ref[0, span, group * HEAD : (group + 1) * HEAD] = (dk * 0.125).astype(BF)
            dkv_ref[0, span, width + group * HEAD : width + (group + 1) * HEAD] = dv.astype(BF)

    dq_ref[...] = (sums[...] * 0.125).astype(BF)


def attention_backward(place, q, do, o, lse, kv, last_col, seg_row):
    trees, total, both = kv.shape
    rows = q.shape[0] // trees
    cols = q.shape[1]
    block = math.gcd(total, 768)
    by_tree = pl.BlockSpec((rows, cols), lambda t, s: (t, 0))
    return pl.pallas_call(
        attention_backward_kernel,
        out_shape=(
            jax.ShapeDtypeStruct(q.shape, BF),
            jax.ShapeDtypeStruct(kv.shape, BF),
        ),
        grid_spec=pltpu.PrefetchScalarGridSpec(
            num_scalar_prefetch=1,
            grid=(trees,),
            in_specs=[
                by_tree,
                by_tree,
                by_tree,
                pl.BlockSpec((1, 8, rows), lambda t, s: (t, 0, 0)),
                pl.BlockSpec((1, total, both), lambda t, s: (t, 0, 0)),
                pl.BlockSpec((total, 1), lambda t, s: (t, 0)),
                pl.BlockSpec((1, 1, rows), lambda t, s: (t, 0, 0)),
            ],
            out_specs=[
                by_tree,
                pl.BlockSpec((1, total, both), lambda t, s: (t, 0, 0)),
            ],
            scratch_shapes=[
                pltpu.VMEM((block, rows), F32),
                pltpu.VMEM((q.shape[1] // HEAD, 8, rows), F32),
                pltpu.VMEM((rows, cols), F32),
            ],
        ),
        compiler_params=pltpu.CompilerParams(vmem_limit_bytes=VMEM_LIMIT),
        name="attention_backward",
    )(place, q, do, o, lse, kv, last_col, seg_row)


def stage_weights(step, split, gate_refs, up_refs, down_refs, wide, tall):
    half, ff = gate_refs[0].shape[1], gate_refs[0].shape[2]
    for a in range(2):
        for part, refs in ((0, gate_refs), (1, up_refs)):
            cols = pl.ds((2 * a + part) * ff, ff)
            wide[0:half, cols] = refs[0][a]

            @pl.when(step < split)
            def _(refs=refs, cols=cols, a=a):
                wide[half : 2 * half, cols] = refs[1][a]

            @pl.when(step >= split)
            def _(refs=refs, cols=cols, a=a):
                wide[half : 2 * half, cols] = refs[2][a]

        rows = pl.ds(a * ff, ff)
        tall[rows, 0:half] = down_refs[0][a]

        @pl.when(step < split)
        def _(rows=rows, a=a):
            tall[rows, half : 2 * half] = down_refs[1][a]

        @pl.when(step >= split)
        def _(rows=rows, a=a):
            tall[rows, half : 2 * half] = down_refs[2][a]


def column(block, index):
    lane = lax.broadcasted_iota(jnp.int32, block.shape, 1)
    return jnp.sum(jnp.where(lane == index, block, 0.0), axis=1, keepdims=True)


def experts_forward_kernel(
    parity, n_ref, c_ref, g0, g1, g2, u0, u1, u2, d0, d1, d2, pre_ref, cm_ref, m_ref, wide, tall, acc
):
    step = pl.program_id(0)
    steps = pl.num_programs(0)
    split = steps // 2
    ff = g0.shape[2]
    pair = lax.rem(parity[0] * split + step, steps)
    stage_weights(step, split, (g0, g1, g2), (u0, u1, u2), (d0, d1, d2), wide, tall)
    tile = 256

    @pl.when(step == 0)
    def _():
        acc[...] = jnp.zeros_like(acc)

    @pl.loop(0, n_ref.shape[0] // tile)
    def _(index):
        rows = pl.ds(pl.multiple_of(index * tile, tile), tile)
        hidden = matmul(n_ref[rows, :], wide[...])
        pre_ref[0, rows, :] = hidden.astype(BF)
        pieces = []
        for a in range(2):
            gate = hidden[:, 2 * a * ff : (2 * a + 1) * ff]
            up = hidden[:, (2 * a + 1) * ff : (2 * a + 2) * ff]
            weight = column(c_ref[rows, :], 2 * pair + a)
            pieces.append((weight * (gate * jax.nn.sigmoid(gate) * up)).astype(BF))
        middle = jnp.concatenate(pieces, axis=1)
        cm_ref[0, rows, :] = middle
        acc[rows, :] += matmul(middle, tall[...])

    @pl.when(step == steps - 1)
    def _():
        m_ref[...] = acc[...].astype(BF)


def weight_specs(steps, half, ff):
    split = steps // 2

    def own(i, s):
        return (lax.rem(s[0] * split + i, steps), 0, 0)

    def first(i, s):
        return (jnp.minimum(i, split - 1), 0, 0)

    def second(i, s):
        return (jnp.maximum(i - split, 0), 0, 0)

    wide = [pl.BlockSpec((2, half, ff), f) for f in (own, first, second)]
    tall = [pl.BlockSpec((2, ff, half), f) for f in (own, first, second)]
    return wide + wide + tall, own


def experts_forward(parity, normed, combine, gates, ups, downs):
    tokens, width = normed.shape
    experts, half, ff = gates[0].shape
    steps = experts // 2
    specs, _ = weight_specs(steps, half, ff)
    return pl.pallas_call(
        experts_forward_kernel,
        out_shape=(
            jax.ShapeDtypeStruct((steps, tokens, 4 * ff), BF),
            jax.ShapeDtypeStruct((steps, tokens, 2 * ff), BF),
            jax.ShapeDtypeStruct((tokens, width), BF),
        ),
        grid_spec=pltpu.PrefetchScalarGridSpec(
            num_scalar_prefetch=1,
            grid=(steps,),
            in_specs=[
                pl.BlockSpec((tokens, width), lambda i, s: (0, 0)),
                pl.BlockSpec((tokens, experts), lambda i, s: (0, 0)),
            ]
            + specs,
            out_specs=[
                pl.BlockSpec((1, tokens, 4 * ff), lambda i, s: (i, 0, 0)),
                pl.BlockSpec((1, tokens, 2 * ff), lambda i, s: (i, 0, 0)),
                pl.BlockSpec((tokens, width), lambda i, s: (0, 0)),
            ],
            scratch_shapes=[
                pltpu.VMEM((width, 4 * ff), BF),
                pltpu.VMEM((2 * ff, width), BF),
                pltpu.VMEM((tokens, width), F32),
            ],
        ),
        compiler_params=pltpu.CompilerParams(vmem_limit_bytes=VMEM_LIMIT),
        name="experts_forward",
    )(parity, normed, combine, *gates, *ups, *downs)


def experts_backward_kernel(
    parity, gy_ref, c_ref, g0, g1, g2, u0, u1, u2, d0, d1, d2, pre_ref, grads_ref, dn_ref, wide, tall, acc
):
    step = pl.program_id(0)
    steps = pl.num_programs(0)
    split = steps // 2
    ff = g0.shape[2]
    pair = lax.rem(parity[0] * split + step, steps)
    stage_weights(step, split, (g0, g1, g2), (u0, u1, u2), (d0, d1, d2), wide, tall)
    tile = 256

    @pl.when(step == 0)
    def _():
        acc[...] = jnp.zeros_like(acc)

    @pl.loop(0, gy_ref.shape[0] // tile)
    def _(index):
        rows = pl.ds(pl.multiple_of(index * tile, tile), tile)
        grad_middle = contract_last(gy_ref[rows, :], tall[...])
        for a in range(2):
            gate = pre_ref[0, rows, 2 * a * ff : (2 * a + 1) * ff].astype(F32)
            up = pre_ref[0, rows, (2 * a + 1) * ff : (2 * a + 2) * ff].astype(F32)
            weight = column(c_ref[rows, :], 2 * pair + a)
            gm = weight * grad_middle[:, a * ff : (a + 1) * ff]
            sig = jax.nn.sigmoid(gate)
            grads_ref[0, rows, 2 * a * ff : (2 * a + 1) * ff] = (
                gm * up * (sig + gate * sig * (1.0 - sig))
            ).astype(BF)
            grads_ref[0, rows, (2 * a + 1) * ff : (2 * a + 2) * ff] = (gm * gate * sig).astype(BF)
        acc[rows, :] += contract_last(grads_ref[0, rows, :], wide[...])

    @pl.when(step == steps - 1)
    def _():
        dn_ref[...] = acc[...].astype(BF)


def experts_backward(parity, grad_y, combine, gates, ups, downs, pre):
    tokens, width = grad_y.shape
    experts, half, ff = gates[0].shape
    steps = experts // 2
    specs, _ = weight_specs(steps, half, ff)
    return pl.pallas_call(
        experts_backward_kernel,
        out_shape=(
            jax.ShapeDtypeStruct((steps, tokens, 4 * ff), BF),
            jax.ShapeDtypeStruct((tokens, width), BF),
        ),
        grid_spec=pltpu.PrefetchScalarGridSpec(
            num_scalar_prefetch=1,
            grid=(steps,),
            in_specs=[
                pl.BlockSpec((tokens, width), lambda i, s: (0, 0)),
                pl.BlockSpec((tokens, experts), lambda i, s: (0, 0)),
            ]
            + specs
            + [pl.BlockSpec((1, tokens, 4 * ff), lambda i, s: (i, 0, 0))],
            out_specs=[
                pl.BlockSpec((1, tokens, 4 * ff), lambda i, s: (i, 0, 0)),
                pl.BlockSpec((tokens, width), lambda i, s: (0, 0)),
            ],
            scratch_shapes=[
                pltpu.VMEM((width, 4 * ff), BF),
                pltpu.VMEM((2 * ff, width), BF),
                pltpu.VMEM((tokens, width), F32),
            ],
        ),
        compiler_params=pltpu.CompilerParams(vmem_limit_bytes=VMEM_LIMIT),
        name="experts_backward",
    )(parity, grad_y, combine, *gates, *ups, *downs, pre)


def expert_weights_kernel(parity, n_ref, gy_ref, grads_ref, cm_ref, own_ref, far_ref):
    half, ff = own_ref.shape[1], own_ref.shape[2]
    tile = 256
    for part, out in ((0, own_ref), (1, far_ref)):

        @pl.loop(0, half // tile)
        def _(index, part=part, out=out):
            begin = pl.multiple_of(index * tile, tile)
            rows = pl.ds(part * half + begin, tile)
            block = matmul(n_ref[rows, :], grads_ref[0]).astype(BF)
            for c in range(4):
                out[c, pl.ds(begin, tile), :] = block[:, c * ff : (c + 1) * ff]
            block = matmul(gy_ref[rows, :], cm_ref[0]).astype(BF)
            for c in range(2):
                out[4 + c, pl.ds(begin, tile), :] = block[:, c * ff : (c + 1) * ff]


def expert_weights(parity, normed_t, grad_y_t, grads, middle):
    width, tokens = normed_t.shape
    steps, _, four = grads.shape
    ff, half = four // 4, width // 2
    slabs = jax.ShapeDtypeStruct((steps * 6, half, ff), BF)
    place = pl.BlockSpec(
        (6, half, ff), lambda i, s: (lax.rem(s[0] * (steps // 2) + i, steps), 0, 0)
    )
    return pl.pallas_call(
        expert_weights_kernel,
        out_shape=(slabs, slabs),
        grid_spec=pltpu.PrefetchScalarGridSpec(
            num_scalar_prefetch=1,
            grid=(steps,),
            in_specs=[
                pl.BlockSpec((width, tokens), lambda i, s: (0, 0)),
                pl.BlockSpec((width, tokens), lambda i, s: (0, 0)),
                pl.BlockSpec((1, tokens, 4 * ff), lambda i, s: (i, 0, 0)),
                pl.BlockSpec((1, tokens, 2 * ff), lambda i, s: (i, 0, 0)),
            ],
            out_specs=[place, place],
        ),
        compiler_params=pltpu.CompilerParams(vmem_limit_bytes=VMEM_LIMIT),
        name="expert_weights",
    )(parity, normed_t, grad_y_t, grads, middle)


def reduce_kernel(
    contexts, owns, fars, outs, own, far, up, down,
    own_sem, ysend, yrecv, usend, urecv, dsend, drecv, out_sem,
):
    units, unit = own.shape[0], own.shape[1]
    ahead = 6
    i = lax.axis_index("context")
    shard = lax.axis_index("shard")
    has_left, has_right = i > 0, i < contexts - 1
    right = {"context": lax.rem(i + 1, contexts)}
    left = {"context": lax.rem(i + contexts - 1, contexts)}
    other = {"shard": 1 - shard}

    barrier = pltpu.get_barrier_semaphore()
    pl.semaphore_signal(barrier, inc=1, device_id=other, device_id_type=MESH)

    @pl.when(has_left)
    def _():
        pl.semaphore_signal(barrier, inc=1, device_id=left, device_id_type=MESH)

    @pl.when(has_right)
    def _():
        pl.semaphore_signal(barrier, inc=1, device_id=right, device_id_type=MESH)

    pl.semaphore_wait(barrier, 1 + has_left.astype(jnp.int32) + has_right.astype(jnp.int32))

    firsts = []
    total = 0
    for ref in owns:
        firsts.append((total, total + ref.shape[0] // unit))
        total += ref.shape[0] // unit

    def each_source(k, act):
        for (begin, end), o, f, r in zip(firsts, owns, fars, outs):

            @pl.when((k >= begin) & (k < end))
            def _(begin=begin, o=o, f=f, r=r):
                act(pl.ds((k - begin) * unit, unit), o, f, r)

    def exchange(k, f, span):
        return pltpu.make_async_remote_copy(
            f.at[span], far.at[k], ysend.at[k], yrecv.at[k], device_id=other, device_id_type=MESH
        )

    def load(k, o, span):
        return pltpu.make_async_copy(o.at[span], own.at[k], own_sem.at[k])

    def store(k, r, span):
        return pltpu.make_async_copy(far.at[k], r.at[span], out_sem.at[k])

    def upward(k, src):
        return pltpu.make_async_remote_copy(
            src.at[k], up.at[k], usend.at[k], urecv.at[k], device_id=right, device_id_type=MESH
        )

    def downward(k, src):
        return pltpu.make_async_remote_copy(
            src.at[k], down.at[k], dsend.at[k], drecv.at[k], device_id=left, device_id_type=MESH
        )

    def begin_unit(k):
        def act(span, o, f, r):
            exchange(k, f, span).start()
            load(k, o, span).start()

        each_source(k, act)

    @pl.loop(0, ahead)
    def _(k):
        begin_unit(k)

    @pl.loop(0, units + contexts - 1)
    def _(k):
        @pl.when(k + ahead < units)
        def _():
            begin_unit(k + ahead)

        @pl.when(k < units)
        def _():
            exchange(k, fars[0], pl.ds(0, unit)).wait_recv()
            load(k, owns[0], pl.ds(0, unit)).wait()
            own[k] = (own[k].astype(F32) + far[k].astype(F32)).astype(BF)

            @pl.when(i == 0)
            def _():
                upward(k, own).start()

            @pl.when(i == contexts - 1)
            def _():
                downward(k, own).start()

        u = k - i

        @pl.when(has_left & (u >= 0) & (u < units))
        def _():
            upward(u, up).wait_recv()
            up[u] = (up[u].astype(F32) + own[u].astype(F32)).astype(BF)

            @pl.when(has_right)
            def _():
                upward(u, up).start()

        d = k - (contexts - 1 - i)

        @pl.when(has_right & (d >= 0) & (d < units))
        def _():
            downward(d, down).wait_recv()
            down[d] = (down[d].astype(F32) + own[d].astype(F32)).astype(BF)

            @pl.when(has_left)
            def _():
                downward(d, down).start()

        e = k - jnp.maximum(i, contexts - 1 - i)

        @pl.when((e >= 0) & (e < units))
        def _():
            @pl.when(i == 0)
            def _():
                far[e] = down[e]

            @pl.when(i == contexts - 1)
            def _():
                far[e] = up[e]

            @pl.when(has_left & has_right)
            def _():
                far[e] = (
                    up[e].astype(F32) + (down[e].astype(F32) - own[e].astype(F32))
                ).astype(BF)

            each_source(e, lambda span, o, f, r: store(e, r, span).start())

    @pl.loop(0, units)
    def _(k):
        exchange(k, fars[0], pl.ds(0, unit)).wait_send()
        store(k, outs[0], pl.ds(0, unit)).wait()

        @pl.when(has_right)
        def _():
            upward(k, up).wait_send()

        @pl.when(has_left)
        def _():
            downward(k, down).wait_send()


def reduce_gradients(contexts, owns, fars):
    count = len(owns)
    unit = 2
    slabs = sum(ref.shape[0] for ref in owns)
    units = slabs // unit
    buffer = pltpu.VMEM((units, unit) + owns[0].shape[1:], BF)

    def kernel(*refs):
        reduce_kernel(
            contexts, refs[:count], refs[count : 2 * count], refs[2 * count : 3 * count],
            *refs[3 * count :],
        )

    anywhere = pl.BlockSpec(memory_space=pl.ANY)
    return pl.pallas_call(
        kernel,
        out_shape=tuple(jax.ShapeDtypeStruct(ref.shape, BF) for ref in owns),
        in_specs=[anywhere] * (2 * count),
        out_specs=(anywhere,) * count,
        scratch_shapes=[buffer] * 4 + [pltpu.SemaphoreType.DMA((units,))] * 8,
        compiler_params=pltpu.CompilerParams(
            collective_id=1, has_side_effects=True, vmem_limit_bytes=VMEM_LIMIT
        ),
        name="reduce_gradients",
    )(*owns, *fars)


def unpack_kernel(slabs_ref, gate_ref, up_ref, down_ref):
    for a in range(2):
        gate_ref[a] = slabs_ref[2 * a].astype(F32)
        up_ref[a] = slabs_ref[2 * a + 1].astype(F32)
        down_ref[a] = slabs_ref[4 + a].astype(F32).T


def unpack(slabs):
    count, half, ff = slabs.shape
    steps = count // 6
    wide = jax.ShapeDtypeStruct((2 * steps, half, ff), F32)
    tall = jax.ShapeDtypeStruct((2 * steps, ff, half), F32)
    return pl.pallas_call(
        unpack_kernel,
        out_shape=(wide, wide, tall),
        grid=(steps,),
        in_specs=[pl.BlockSpec((6, half, ff), lambda i: (i, 0, 0))],
        out_specs=[pl.BlockSpec((2, half, ff), lambda i: (i, 0, 0))] * 2
        + [pl.BlockSpec((2, ff, half), lambda i: (i, 0, 0))],
        compiler_params=pltpu.CompilerParams(vmem_limit_bytes=VMEM_LIMIT),
        name="unpack",
    )(slabs)


def to_slabs(value, ff):
    rows, cols = value.shape
    split = value.reshape(2, rows // 2, cols // ff, ff).transpose(0, 2, 1, 3)
    return split[0], split[1]


def from_slabs(slabs):
    count, rows, ff = slabs.shape
    return slabs.transpose(1, 0, 2).reshape(rows, count * ff)


def norm_forward(values, scale):
    inverse = lax.rsqrt(jnp.mean(values * values, axis=-1, keepdims=True) + EPS)
    return values * inverse * scale, inverse


def norm_backward(values, inverse, scale, grad):
    scaled = grad * scale
    along = jnp.mean(scaled * values, axis=-1, keepdims=True)
    grad_values = inverse * scaled - values * (inverse * inverse * inverse * along)
    grad_scale = jnp.sum(grad * values * inverse, axis=0)
    return grad_values, grad_scale


def local(
    states, segments, routes, gates, valid, teacher, attn_gain, w_query, key_matrix, value_matrix,
    w_out, moe_gain, w_gate, w_up, w_down,
):
    shard = lax.axis_index("shard")
    context = lax.axis_index("context")
    shards = lax.axis_size("shard")
    contexts = lax.axis_size("context")
    trees, rows, width = states.shape
    tokens = trees * rows
    half = width // 2
    experts = w_gate.shape[0]
    swap = [(a, shards - 1 - a) for a in range(shards)]
    pairs = [(a, a + 1 - 2 * (a % 2)) for a in range(contexts)]
    parity = lax.rem(context, 2)
    place = jnp.reshape(context, (1,)).astype(jnp.int32)
    side = jnp.reshape(parity, (1,)).astype(jnp.int32)

    def over_shard(value):
        return lax.ppermute(value, "shard", swap)

    def turned(value):
        return jnp.where(shard == 0, value, jnp.concatenate([value[:, half:], value[:, :half]], 1))

    qkv_own = jnp.concatenate([w_query, key_matrix, value_matrix], axis=1)
    qkv_w = jnp.concatenate([qkv_own, over_shard(qkv_own)], axis=0)
    gains_own = jnp.stack([attn_gain, moe_gain])
    gains = jnp.concatenate([gains_own, over_shard(gains_own)], axis=1)
    out_w = jnp.concatenate([w_out, over_shard(w_out)], axis=1)
    attn_scale, moe_scale = gains[0], gains[1]

    def both_ways(weights):
        mine = lax.dynamic_slice_in_dim(weights, parity * (experts // 2), experts // 2, 0)
        direct = over_shard(mine)
        relayed = lax.ppermute(direct, "context", pairs)
        return (weights, direct, relayed)

    gate_ws, up_ws, down_ws = both_ways(w_gate), both_ways(w_up), both_ways(w_down)

    valid_total = lax.psum(jnp.sum(valid.astype(F32)), ("shard", "context"))
    segments_all = lax.all_gather(segments, "context", axis=1, tiled=True)
    last = jnp.where(
        segments_all == 0,
        1 << 20,
        jnp.where(segments_all % 3 == 1, segments_all + 2, segments_all),
    )

    x = turned(states.reshape(tokens, width)).astype(F32)
    normed, inverse_one = norm_forward(x, attn_scale)
    normed = normed.astype(BF)
    qkv = matmul(normed, qkv_w).astype(BF)
    query_cols = w_query.shape[1]
    both = qkv.shape[1] - query_cols
    q = qkv[:, :query_cols]
    kv = lax.all_gather(
        qkv[:, query_cols:].reshape(trees, rows, both), "context", axis=1, tiled=True
    )
    total = kv.shape[1]
    attended, lse = attention_forward(
        place, q, kv, last.reshape(trees, 1, total), segments.reshape(tokens, 1)
    )
    branch = lax.psum(matmul(attended, out_w).astype(BF), "tensor").astype(F32)
    hidden = x + branch
    normed_two, inverse_two = norm_forward(hidden, moe_scale)
    normed_two = normed_two.astype(BF)

    expert_ids = jnp.arange(experts, dtype=jnp.int32)
    combine = jnp.sum(
        gates.reshape(tokens, -1)[..., None]
        * (routes.reshape(tokens, -1)[..., None] == expert_ids).astype(F32),
        axis=1,
    )
    pre, middle, moe_part = experts_forward(
        side, normed_two, combine, gate_ws, up_ws, down_ws
    )
    moe = lax.psum(moe_part, "tensor").astype(F32)
    result = hidden + moe
    mask = valid.reshape(tokens, 1).astype(F32)
    error = result - turned(teacher.reshape(tokens, width)).astype(F32)
    square = lax.psum(jnp.sum(mask * error * error), ("shard", "context"))
    loss = square / (valid_total * width)
    token_total = tokens * shards * contexts
    grad_y = token_total / valid_total * mask * error

    grad_y_low = grad_y.astype(BF)
    expert_grads, dn_part = experts_backward(
        side, grad_y_low, combine, gate_ws, up_ws, down_ws, pre
    )
    own_experts, far_experts = expert_weights(
        side, normed_two.T, grad_y_low.T, expert_grads, middle
    )

    grad_normed_two = lax.psum(dn_part, "tensor").astype(F32)
    grad_hidden_norm, grad_moe_scale = norm_backward(
        hidden, inverse_two, moe_scale, grad_normed_two
    )
    grad_hidden = grad_y + grad_hidden_norm
    grad_branch = grad_hidden.astype(BF)
    grad_out_w = contract_first(grad_branch, attended).astype(BF)
    grad_attended = contract_last(grad_branch, out_w).astype(BF)
    grad_q, grad_kv_all = attention_backward(
        place, q, grad_attended, attended, lse, kv, last.reshape(trees * total, 1),
        segments.reshape(trees, 1, rows),
    )
    grad_kv = lax.psum_scatter(grad_kv_all, "context", scatter_dimension=1, tiled=True)
    grad_qkv = jnp.concatenate([grad_q, grad_kv.reshape(tokens, both)], axis=1)
    grad_qkv_w = contract_first(normed, grad_qkv).astype(BF)
    grad_normed = lax.psum(contract_last(grad_qkv, qkv_w).astype(BF), "tensor").astype(F32)
    grad_inputs_norm, grad_attn_scale = norm_backward(x, inverse_one, attn_scale, grad_normed)
    grad_inputs = grad_hidden + grad_inputs_norm

    ff = w_gate.shape[2]
    own_qkv, far_qkv = to_slabs(grad_qkv_w, ff)
    own_out, far_out = to_slabs(grad_out_w, ff)
    own_attn = jnp.concatenate([own_qkv, own_out])
    far_attn = jnp.concatenate([far_qkv, far_out])
    sum_experts, sum_attn = reduce_gradients(
        contexts, (own_experts, own_attn), (far_experts, far_attn)
    )
    final_gate, final_up, final_down = unpack(sum_experts)
    final_qkv = from_slabs(sum_attn[: own_qkv.shape[0]]).astype(F32)
    final_out = from_slabs(sum_attn[own_qkv.shape[0] :]).astype(F32).T
    grad_scales = jnp.stack([grad_attn_scale, grad_moe_scale])
    final_scales = lax.psum(
        grad_scales[:, :half] + over_shard(grad_scales[:, half:]), "context"
    )
    kv_cols = key_matrix.shape[1]
    return (
        loss,
        turned(result).reshape(trees, rows, width).astype(BF),
        turned(grad_inputs).reshape(trees, rows, width),
        final_scales[0],
        final_qkv[:, :query_cols],
        final_qkv[:, query_cols : query_cols + kv_cols],
        final_qkv[:, query_cols + kv_cols :],
        final_out,
        final_scales[1],
        final_gate,
        final_up,
        final_down,
    )


def solution(mesh):
    return jax.shard_map(
        local,
        mesh=mesh,
        in_specs=(
            P("shard", "context", None),
            P("shard", "context"),
            P("shard", "context", None),
            P("shard", "context", None),
            P("shard", "context"),
            P("shard", "context", None),
            P("shard"),
            P("shard", "tensor"),
            P("shard", "tensor"),
            P("shard", "tensor"),
            P("tensor", "shard"),
            P("shard"),
            P(None, "shard", "tensor"),
            P(None, "shard", "tensor"),
            P(None, "tensor", "shard"),
        ),
        out_specs=(
            P(),
            P("shard", "context", None),
            P("shard", "context", None),
            P("shard"),
            P("shard", "tensor"),
            P("shard", "tensor"),
            P("shard", "tensor"),
            P("tensor", "shard"),
            P("shard"),
            P(None, "shard", "tensor"),
            P(None, "shard", "tensor"),
            P(None, "tensor", "shard"),
        ),
        check_vma=False,
    )
```

```python
import functools
import math

import jax
import jax.numpy as jnp
from jax import lax
from jax.experimental import pallas as pl
from jax.experimental.pallas import tpu as pltpu
from jax.sharding import PartitionSpec as P

HEAD = 64
EPS = 1e-05
BF = jnp.bfloat16
F32 = jnp.float32
MESH = pl.DeviceIdType.MESH
VMEM_LIMIT = 56 * 1024 * 1024
UNIT = 2
COST = pl.CostEstimate(flops=1, bytes_accessed=1, transcendentals=0)


def matmul(left, right):
    return jnp.dot(left, right, preferred_element_type=F32)


def contract_first(left, right):
    return lax.dot_general(left, right, (((0,), (0,)), ((), ())), preferred_element_type=F32)


def contract_last(left, right):
    return lax.dot_general(left, right, (((1,), (1,)), ((), ())), preferred_element_type=F32)


def attention_forward_kernel(
    place, q_ref, kv_ref, last_ref, seg_ref, wo_ref, wf_ref, o_ref, lse_ref, a_ref,
    bias, tops, norms, sums,
):
    rows = q_ref.shape[0]
    width = kv_ref.shape[2] // 2
    total = kv_ref.shape[1]
    heads = q_ref.shape[1] // HEAD
    per_group = q_ref.shape[1] // width
    block = bias.shape[1]
    tops[...] = jnp.full_like(tops, -1e30)
    norms[...] = jnp.zeros_like(norms)
    sums[...] = jnp.zeros_like(sums)

    @pl.loop(0, total // block)
    def _(index):
        begin = pl.multiple_of(index * block, block)
        key_pos = begin + lax.broadcasted_iota(jnp.int32, (rows, block), 1)
        query_pos = place[0] * rows + lax.broadcasted_iota(jnp.int32, (rows, block), 0)
        allowed = (key_pos <= query_pos) & (seg_ref[...] <= last_ref[0, :, pl.ds(begin, block)])
        bias[...] = jnp.where(allowed, 0.0, -2e30)
        for head in range(heads):
            group = head // per_group
            cols = slice(head * HEAD, (head + 1) * HEAD)
            keys = kv_ref[0, pl.ds(begin, block), group * HEAD : (group + 1) * HEAD]
            values = kv_ref[
                0, pl.ds(begin, block), width + group * HEAD : width + (group + 1) * HEAD
            ]
            scores = contract_last(q_ref[:, cols], keys) * 0.125 + bias[...]
            old = tops[:, head : head + 1]
            top = jnp.maximum(old, jnp.max(scores, axis=1, keepdims=True))
            weights = jnp.exp(scores - top)
            shrink = jnp.exp(old - top)
            tops[:, head : head + 1] = top
            norms[:, head : head + 1] = norms[:, head : head + 1] * shrink + jnp.sum(
                weights, axis=1, keepdims=True
            )
            sums[:, cols] = sums[:, cols] * shrink + matmul(weights.astype(BF), values)

    for head in range(heads):
        cols = slice(head * HEAD, (head + 1) * HEAD)
        o_ref[:, cols] = (sums[:, cols] / norms[:, head : head + 1]).astype(BF)
    lse = tops[...] + jnp.log(norms[...] + jnp.where(norms[...] == 0.0, 1.0, 0.0))
    lse_ref[0] = lse.T[: lse_ref.shape[1]]
    half = wo_ref.shape[1]
    a_ref[:, :half] = matmul(o_ref[...], wo_ref[...]).astype(BF)
    a_ref[:, half:] = matmul(o_ref[...], wf_ref[...]).astype(BF)


def attention_forward(place, q, kv, last_row, seg_col, out_own, out_far):
    half = out_own.shape[1]
    trees, total, both = kv.shape
    rows = q.shape[0] // trees
    cols = q.shape[1]
    block = math.gcd(total, 1536)
    return pl.pallas_call(
        attention_forward_kernel,
        out_shape=(
            jax.ShapeDtypeStruct(q.shape, BF),
            jax.ShapeDtypeStruct((trees, 8, rows), F32),
            jax.ShapeDtypeStruct((q.shape[0], 2 * half), BF),
        ),
        grid_spec=pltpu.PrefetchScalarGridSpec(
            num_scalar_prefetch=1,
            grid=(trees,),
            in_specs=[
                pl.BlockSpec((rows, cols), lambda t, s: (t, 0)),
                pl.BlockSpec((1, total, both), lambda t, s: (t, 0, 0)),
                pl.BlockSpec((1, 1, total), lambda t, s: (t, 0, 0)),
                pl.BlockSpec((rows, 1), lambda t, s: (t, 0)),
                pl.BlockSpec((cols, half), lambda t, s: (0, 0)),
                pl.BlockSpec((cols, half), lambda t, s: (0, 0)),
            ],
            out_specs=[
                pl.BlockSpec((rows, cols), lambda t, s: (t, 0)),
                pl.BlockSpec((1, 8, rows), lambda t, s: (t, 0, 0)),
                pl.BlockSpec((rows, 2 * half), lambda t, s: (t, 0)),
            ],
            scratch_shapes=[
                pltpu.VMEM((rows, block), F32),
                pltpu.VMEM((rows, 128), F32),
                pltpu.VMEM((rows, 128), F32),
                pltpu.VMEM((rows, cols), F32),
            ],
        ),
        compiler_params=pltpu.CompilerParams(vmem_limit_bytes=VMEM_LIMIT),
        cost_estimate=COST,
        name="attention_forward",
    )(place, q, kv, last_row, seg_col, out_own, out_far)


def attention_backward_kernel(
    place, q_ref, do_ref, o_ref, lse_ref, kv_ref, last_ref, seg_ref, dq_ref, dkv_ref, bias, deltas, sums
):
    rows = q_ref.shape[0]
    width = kv_ref.shape[2] // 2
    total = kv_ref.shape[1]
    heads = q_ref.shape[1] // HEAD
    per_group = q_ref.shape[1] // width
    block = bias.shape[0]
    sums[...] = jnp.zeros_like(sums)
    for head in range(heads):
        cols = slice(head * HEAD, (head + 1) * HEAD)
        product = do_ref[:, cols].astype(F32) * o_ref[:, cols].astype(F32)
        deltas[head] = lax.dot_general(
            jnp.ones((8, HEAD), F32),
            product,
            (((1,), (1,)), ((), ())),
            precision=lax.Precision.HIGHEST,
            preferred_element_type=F32,
        )

    @pl.loop(0, total // block)
    def _(index):
        begin = pl.multiple_of(index * block, block)
        span = pl.ds(begin, block)
        key_pos = begin + lax.broadcasted_iota(jnp.int32, (block, rows), 0)
        query_pos = place[0] * rows + lax.broadcasted_iota(jnp.int32, (block, rows), 1)
        allowed = (key_pos <= query_pos) & (seg_ref[0] <= last_ref[span, :])
        bias[...] = jnp.where(allowed, 0.0, -2e30)
        for group in range(heads // per_group):
            keys = kv_ref[0, span, group * HEAD : (group + 1) * HEAD]
            values = kv_ref[0, span, width + group * HEAD : width + (group + 1) * HEAD]
            dk = jnp.zeros((block, HEAD), F32)
            dv = jnp.zeros((block, HEAD), F32)
            for head in range(group * per_group, (group + 1) * per_group):
                cols = slice(head * HEAD, (head + 1) * HEAD)
                queries = q_ref[:, cols]
                grads = do_ref[:, cols]
                scores = contract_last(keys, queries) * 0.125 + bias[...]
                probs = jnp.exp(scores - lse_ref[0, head : head + 1, :])
                grad_probs = contract_last(values, grads)
                grad_scores = (probs * (grad_probs - deltas[head, 0:1, :])).astype(BF)
                dv = dv + matmul(probs.astype(BF), grads)
                dk = dk + matmul(grad_scores, queries)
                sums[:, cols] += contract_first(grad_scores, keys)
            dkv_ref[0, span, group * HEAD : (group + 1) * HEAD] = (dk * 0.125).astype(BF)
            dkv_ref[0, span, width + group * HEAD : width + (group + 1) * HEAD] = dv.astype(BF)

    dq_ref[...] = (sums[...] * 0.125).astype(BF)


def attention_backward(place, q, do, o, lse, kv, last_col, seg_row):
    trees, total, both = kv.shape
    rows = q.shape[0] // trees
    cols = q.shape[1]
    block = math.gcd(total, 768)
    by_tree = pl.BlockSpec((rows, cols), lambda t, s: (t, 0))
    return pl.pallas_call(
        attention_backward_kernel,
        out_shape=(
            jax.ShapeDtypeStruct(q.shape, BF),
            jax.ShapeDtypeStruct(kv.shape, BF),
        ),
        grid_spec=pltpu.PrefetchScalarGridSpec(
            num_scalar_prefetch=1,
            grid=(trees,),
            in_specs=[
                by_tree,
                by_tree,
                by_tree,
                pl.BlockSpec((1, 8, rows), lambda t, s: (t, 0, 0)),
                pl.BlockSpec((1, total, both), lambda t, s: (t, 0, 0)),
                pl.BlockSpec((total, 1), lambda t, s: (t, 0)),
                pl.BlockSpec((1, 1, rows), lambda t, s: (t, 0, 0)),
            ],
            out_specs=[
                by_tree,
                pl.BlockSpec((1, total, both), lambda t, s: (t, 0, 0)),
            ],
            scratch_shapes=[
                pltpu.VMEM((block, rows), F32),
                pltpu.VMEM((q.shape[1] // HEAD, 8, rows), F32),
                pltpu.VMEM((rows, cols), F32),
            ],
        ),
        compiler_params=pltpu.CompilerParams(vmem_limit_bytes=VMEM_LIMIT),
        cost_estimate=COST,
        name="attention_backward",
    )(place, q, do, o, lse, kv, last_col, seg_row)


def stage_weights(step, split, gate_refs, up_refs, down_refs, wide, tall):
    half, ff = gate_refs[0].shape[1], gate_refs[0].shape[2]
    for a in range(2):
        for part, refs in ((0, gate_refs), (1, up_refs)):
            cols = pl.ds((2 * a + part) * ff, ff)
            wide[0:half, cols] = refs[0][a]

            @pl.when(step < split)
            def _(refs=refs, cols=cols, a=a):
                wide[half : 2 * half, cols] = refs[1][a]

            @pl.when(step >= split)
            def _(refs=refs, cols=cols, a=a):
                wide[half : 2 * half, cols] = refs[2][a]

        rows = pl.ds(a * ff, ff)
        tall[rows, 0:half] = down_refs[0][a]

        @pl.when(step < split)
        def _(rows=rows, a=a):
            tall[rows, half : 2 * half] = down_refs[1][a]

        @pl.when(step >= split)
        def _(rows=rows, a=a):
            tall[rows, half : 2 * half] = down_refs[2][a]


def column(block, index):
    lane = lax.broadcasted_iota(jnp.int32, block.shape, 1)
    return jnp.sum(jnp.where(lane == index, block, 0.0), axis=1, keepdims=True)


def experts_forward_kernel(
    first, steps, parity, n_ref, c_ref, g0, g1, u0, u1, d0, d1, *refs
):
    if first:
        held_ref, (pre_ref, cm_ref, m_ref, wide, tall, acc) = None, refs
    else:
        held_ref, (pre_ref, cm_ref, m_ref, wide, tall, acc) = refs[0], refs[3:]
    step = pl.program_id(0)
    ff = g0.shape[2]
    split = steps // 2
    pair = lax.rem(parity[0] * split + step + (0 if first else split), steps)
    half = g0.shape[1]
    for a in range(2):
        for part, refs in ((0, (g0, g1)), (1, (u0, u1))):
            cols = pl.ds((2 * a + part) * ff, ff)
            wide[0:half, cols] = refs[0][a]
            wide[half : 2 * half, cols] = refs[1][a]
        rows = pl.ds(a * ff, ff)
        tall[rows, 0:half] = d0[a]
        tall[rows, half : 2 * half] = d1[a]
    tile = 256

    @pl.when(step == 0)
    def _():
        acc[...] = jnp.zeros_like(acc) if first else held_ref[...]

    @pl.loop(0, n_ref.shape[0] // tile)
    def _(index):
        rows = pl.ds(pl.multiple_of(index * tile, tile), tile)
        hidden = matmul(n_ref[rows, :], wide[...])
        pre_ref[0, rows, :] = hidden.astype(BF)
        pieces = []
        for a in range(2):
            gate = hidden[:, 2 * a * ff : (2 * a + 1) * ff]
            up = hidden[:, (2 * a + 1) * ff : (2 * a + 2) * ff]
            weight = column(c_ref[rows, :], 2 * pair + a)
            pieces.append((weight * (gate * jax.nn.sigmoid(gate) * up)).astype(BF))
        middle = jnp.concatenate(pieces, axis=1)
        cm_ref[0, rows, :] = middle
        acc[rows, :] += matmul(middle, tall[...])

    @pl.when(step == split - 1)
    def _():
        m_ref[...] = acc[...].astype(m_ref.dtype)


def weight_specs(steps, half, ff):
    split = steps // 2

    def own(i, s):
        return (lax.rem(s[0] * split + i, steps), 0, 0)

    def first(i, s):
        return (jnp.minimum(i, split - 1), 0, 0)

    def second(i, s):
        return (jnp.maximum(i - split, 0), 0, 0)

    wide = [pl.BlockSpec((2, half, ff), f) for f in (own, first, second)]
    tall = [pl.BlockSpec((2, ff, half), f) for f in (own, first, second)]
    return wide + wide + tall, own


def experts_forward(parity, normed, combine, gates, ups, downs, held=None):
    tokens, width = normed.shape
    experts, half, ff = gates[0].shape
    steps = experts // 2
    split = steps // 2
    skip = 0 if held is None else split

    def own(i, s):
        return (lax.rem(s[0] * split + i + skip, steps), 0, 0)

    def plain(i, s):
        return (i, 0, 0)

    specs = [
        pl.BlockSpec(shape, f)
        for shape in ((2, half, ff), (2, half, ff), (2, ff, half))
        for f in (own, plain)
    ]
    whole = pl.BlockSpec((tokens, width), lambda i, s: (0, 0))
    anywhere = pl.BlockSpec(memory_space=pl.ANY)
    return pl.pallas_call(
        functools.partial(experts_forward_kernel, held is None, steps),
        out_shape=(
            jax.ShapeDtypeStruct((steps, tokens, 4 * ff), BF),
            jax.ShapeDtypeStruct((steps, tokens, 2 * ff), BF),
            jax.ShapeDtypeStruct((tokens, width), F32 if held is None else BF),
        ),
        grid_spec=pltpu.PrefetchScalarGridSpec(
            num_scalar_prefetch=1,
            grid=(split,),
            in_specs=[whole, pl.BlockSpec((tokens, experts), lambda i, s: (0, 0))]
            + specs
            + ([] if held is None else [whole, anywhere, anywhere]),
            out_specs=[
                pl.BlockSpec((1, tokens, 4 * ff), lambda i, s: (i + skip, 0, 0)),
                pl.BlockSpec((1, tokens, 2 * ff), lambda i, s: (i + skip, 0, 0)),
                whole,
            ],
            scratch_shapes=[
                pltpu.VMEM((width, 4 * ff), BF),
                pltpu.VMEM((2 * ff, width), BF),
                pltpu.VMEM((tokens, width), F32),
            ],
        ),
        input_output_aliases={} if held is None else {10: 0, 11: 1},
        compiler_params=pltpu.CompilerParams(vmem_limit_bytes=VMEM_LIMIT),
        cost_estimate=COST,
        name="experts_forward",
    )(parity, normed, combine, *gates, *ups, *downs, *(() if held is None else held))


def experts_backward_kernel(
    parity, gy_ref, c_ref, g0, g1, g2, u0, u1, u2, d0, d1, d2, pre_ref, grads_ref, dn_ref, wide, tall, acc
):
    step = pl.program_id(0)
    steps = pl.num_programs(0)
    split = steps // 2
    ff = g0.shape[2]
    pair = lax.rem(parity[0] * split + step, steps)
    stage_weights(step, split, (g0, g1, g2), (u0, u1, u2), (d0, d1, d2), wide, tall)
    tile = 256

    @pl.when(step == 0)
    def _():
        acc[...] = jnp.zeros_like(acc)

    @pl.loop(0, gy_ref.shape[0] // tile)
    def _(index):
        rows = pl.ds(pl.multiple_of(index * tile, tile), tile)
        grad_middle = contract_last(gy_ref[rows, :], tall[...])
        for a in range(2):
            gate = pre_ref[0, rows, 2 * a * ff : (2 * a + 1) * ff].astype(F32)
            up = pre_ref[0, rows, (2 * a + 1) * ff : (2 * a + 2) * ff].astype(F32)
            weight = column(c_ref[rows, :], 2 * pair + a)
            gm = weight * grad_middle[:, a * ff : (a + 1) * ff]
            sig = jax.nn.sigmoid(gate)
            grads_ref[0, rows, 2 * a * ff : (2 * a + 1) * ff] = (
                gm * up * (sig + gate * sig * (1.0 - sig))
            ).astype(BF)
            grads_ref[0, rows, (2 * a + 1) * ff : (2 * a + 2) * ff] = (gm * gate * sig).astype(BF)
        acc[rows, :] += contract_last(grads_ref[0, rows, :], wide[...])

    @pl.when(step == steps - 1)
    def _():
        dn_ref[...] = acc[...].astype(BF)


def experts_backward(parity, grad_y, combine, gates, ups, downs, pre):
    tokens, width = grad_y.shape
    experts, half, ff = gates[0].shape
    steps = experts // 2
    specs, _ = weight_specs(steps, half, ff)
    return pl.pallas_call(
        experts_backward_kernel,
        out_shape=(
            jax.ShapeDtypeStruct((steps, tokens, 4 * ff), BF),
            jax.ShapeDtypeStruct((tokens, width), BF),
        ),
        grid_spec=pltpu.PrefetchScalarGridSpec(
            num_scalar_prefetch=1,
            grid=(steps,),
            in_specs=[
                pl.BlockSpec((tokens, width), lambda i, s: (0, 0)),
                pl.BlockSpec((tokens, experts), lambda i, s: (0, 0)),
            ]
            + specs
            + [pl.BlockSpec((1, tokens, 4 * ff), lambda i, s: (i, 0, 0))],
            out_specs=[
                pl.BlockSpec((1, tokens, 4 * ff), lambda i, s: (i, 0, 0)),
                pl.BlockSpec((tokens, width), lambda i, s: (0, 0)),
            ],
            scratch_shapes=[
                pltpu.VMEM((width, 4 * ff), BF),
                pltpu.VMEM((2 * ff, width), BF),
                pltpu.VMEM((tokens, width), F32),
            ],
        ),
        compiler_params=pltpu.CompilerParams(vmem_limit_bytes=VMEM_LIMIT),
        cost_estimate=COST,
        name="experts_backward",
    )(parity, grad_y, combine, *gates, *ups, *downs, pre)


def expert_weights_kernel(parity, n_ref, gy_ref, grads_ref, cm_ref, own_ref, far_ref):
    half, ff = own_ref.shape[1], own_ref.shape[2]
    tile = 256
    for part, out in ((0, own_ref), (1, far_ref)):

        @pl.loop(0, half // tile)
        def _(index, part=part, out=out):
            begin = pl.multiple_of(index * tile, tile)
            rows = pl.ds(part * half + begin, tile)
            block = matmul(n_ref[rows, :], grads_ref[0]).astype(BF)
            for c in range(4):
                out[c, pl.ds(begin, tile), :] = block[:, c * ff : (c + 1) * ff]
            block = matmul(gy_ref[rows, :], cm_ref[0]).astype(BF)
            for c in range(2):
                out[4 + c, pl.ds(begin, tile), :] = block[:, c * ff : (c + 1) * ff]


def expert_weights(parity, normed_t, grad_y_t, grads, middle, begin, end):
    width, tokens = normed_t.shape
    steps, _, four = grads.shape
    ff, half = four // 4, width // 2
    slabs = jax.ShapeDtypeStruct(((end - begin) * 6, half, ff), BF)

    def held(i, s):
        return (lax.rem(begin + i + s[0] * (steps // 2), steps), 0, 0)

    return pl.pallas_call(
        expert_weights_kernel,
        out_shape=(slabs, slabs),
        grid_spec=pltpu.PrefetchScalarGridSpec(
            num_scalar_prefetch=1,
            grid=(end - begin,),
            in_specs=[
                pl.BlockSpec((width, tokens), lambda i, s: (0, 0)),
                pl.BlockSpec((width, tokens), lambda i, s: (0, 0)),
                pl.BlockSpec((1, tokens, 4 * ff), held),
                pl.BlockSpec((1, tokens, 2 * ff), held),
            ],
            out_specs=[pl.BlockSpec((6, half, ff), lambda i, s: (i, 0, 0))] * 2,
        ),
        compiler_params=pltpu.CompilerParams(vmem_limit_bytes=VMEM_LIMIT),
        cost_estimate=COST,
        name="expert_weights",
    )(parity, normed_t, grad_y_t, grads, middle)


def reduce_kernel(
    contexts, owns, fars, outs, own, far, up, down,
    own_sem, ysend, yrecv, usend, urecv, dsend, drecv, out_sem,
):
    units, unit = own.shape[0], own.shape[1]
    ahead = 6
    i = lax.axis_index("context")
    shard = lax.axis_index("shard")
    has_left, has_right = i > 0, i < contexts - 1
    right = {"context": lax.rem(i + 1, contexts)}
    left = {"context": lax.rem(i + contexts - 1, contexts)}
    other = {"shard": 1 - shard}

    barrier = pltpu.get_barrier_semaphore()
    pl.semaphore_signal(barrier, inc=1, device_id=other, device_id_type=MESH)

    @pl.when(has_left)
    def _():
        pl.semaphore_signal(barrier, inc=1, device_id=left, device_id_type=MESH)

    @pl.when(has_right)
    def _():
        pl.semaphore_signal(barrier, inc=1, device_id=right, device_id_type=MESH)

    pl.semaphore_wait(barrier, 1 + has_left.astype(jnp.int32) + has_right.astype(jnp.int32))

    firsts = []
    total = 0
    for ref in owns:
        firsts.append((total, total + ref.shape[0] // unit))
        total += ref.shape[0] // unit

    def each_source(k, act):
        for (begin, end), o, f, r in zip(firsts, owns, fars, outs):

            @pl.when((k >= begin) & (k < end))
            def _(begin=begin, o=o, f=f, r=r):
                act(pl.ds((k - begin) * unit, unit), o, f, r)

    def exchange(k, f, span):
        return pltpu.make_async_remote_copy(
            f.at[span], far.at[k], ysend.at[k], yrecv.at[k], device_id=other, device_id_type=MESH
        )

    def load(k, o, span):
        return pltpu.make_async_copy(o.at[span], own.at[k], own_sem.at[k])

    def store(k, r, span):
        return pltpu.make_async_copy(far.at[k], r.at[span], out_sem.at[k])

    def upward(k, src):
        return pltpu.make_async_remote_copy(
            src.at[k], up.at[k], usend.at[k], urecv.at[k], device_id=right, device_id_type=MESH
        )

    def downward(k, src):
        return pltpu.make_async_remote_copy(
            src.at[k], down.at[k], dsend.at[k], drecv.at[k], device_id=left, device_id_type=MESH
        )

    def begin_unit(k):
        def act(span, o, f, r):
            exchange(k, f, span).start()
            load(k, o, span).start()

        each_source(k, act)

    @pl.loop(0, ahead)
    def _(k):
        begin_unit(k)

    @pl.loop(0, units + contexts - 1)
    def _(k):
        @pl.when(k + ahead < units)
        def _():
            begin_unit(k + ahead)

        @pl.when(k < units)
        def _():
            exchange(k, fars[0], pl.ds(0, unit)).wait_recv()
            load(k, owns[0], pl.ds(0, unit)).wait()
            own[k] = (own[k].astype(F32) + far[k].astype(F32)).astype(BF)

            @pl.when(i == 0)
            def _():
                upward(k, own).start()

            @pl.when(i == contexts - 1)
            def _():
                downward(k, own).start()

        u = k - i

        @pl.when(has_left & (u >= 0) & (u < units))
        def _():
            upward(u, up).wait_recv()
            up[u] = (up[u].astype(F32) + own[u].astype(F32)).astype(BF)

            @pl.when(has_right)
            def _():
                upward(u, up).start()

        d = k - (contexts - 1 - i)

        @pl.when(has_right & (d >= 0) & (d < units))
        def _():
            downward(d, down).wait_recv()
            down[d] = (down[d].astype(F32) + own[d].astype(F32)).astype(BF)

            @pl.when(has_left)
            def _():
                downward(d, down).start()

        e = k - jnp.maximum(i, contexts - 1 - i)

        @pl.when((e >= 0) & (e < units))
        def _():
            @pl.when(i == 0)
            def _():
                far[e] = down[e]

            @pl.when(i == contexts - 1)
            def _():
                far[e] = up[e]

            @pl.when(has_left & has_right)
            def _():
                far[e] = (
                    up[e].astype(F32) + (down[e].astype(F32) - own[e].astype(F32))
                ).astype(BF)

            each_source(e, lambda span, o, f, r: store(e, r, span).start())

    @pl.loop(0, units)
    def _(k):
        exchange(k, fars[0], pl.ds(0, unit)).wait_send()
        store(k, outs[0], pl.ds(0, unit)).wait()

        @pl.when(has_right)
        def _():
            upward(k, up).wait_send()

        @pl.when(has_left)
        def _():
            downward(k, down).wait_send()


def reduce_gradients(contexts, owns, fars):
    count = len(owns)
    unit = UNIT
    slabs = sum(ref.shape[0] for ref in owns)
    units = slabs // unit
    buffer = pltpu.VMEM((units, unit) + owns[0].shape[1:], BF)

    def kernel(*refs):
        reduce_kernel(
            contexts, refs[:count], refs[count : 2 * count], refs[2 * count : 3 * count],
            *refs[3 * count :],
        )

    anywhere = pl.BlockSpec(memory_space=pl.ANY)
    return pl.pallas_call(
        kernel,
        out_shape=tuple(jax.ShapeDtypeStruct(ref.shape, BF) for ref in owns),
        in_specs=[anywhere] * (2 * count),
        out_specs=(anywhere,) * count,
        scratch_shapes=[buffer] * 4 + [pltpu.SemaphoreType.DMA((units,))] * 8,
        compiler_params=pltpu.CompilerParams(
            collective_id=1, has_side_effects=True, vmem_limit_bytes=VMEM_LIMIT
        ),
        cost_estimate=COST,
        name="reduce_gradients",
    )(*owns, *fars)


def unpack_kernel(slabs_ref, gate_ref, up_ref, down_ref):
    for a in range(2):
        gate_ref[a] = slabs_ref[2 * a].astype(F32)
        up_ref[a] = slabs_ref[2 * a + 1].astype(F32)
        down_ref[a] = slabs_ref[4 + a].astype(F32).T


def unpack(slabs):
    count, half, ff = slabs.shape
    steps = count // 6
    wide = jax.ShapeDtypeStruct((2 * steps, half, ff), F32)
    tall = jax.ShapeDtypeStruct((2 * steps, ff, half), F32)
    return pl.pallas_call(
        unpack_kernel,
        out_shape=(wide, wide, tall),
        grid=(steps,),
        in_specs=[pl.BlockSpec((6, half, ff), lambda i: (i, 0, 0))],
        out_specs=[pl.BlockSpec((2, half, ff), lambda i: (i, 0, 0))] * 2
        + [pl.BlockSpec((2, ff, half), lambda i: (i, 0, 0))],
        compiler_params=pltpu.CompilerParams(vmem_limit_bytes=VMEM_LIMIT),
        cost_estimate=COST,
        name="unpack",
    )(slabs)


def attention_weights_kernel(n_ref, da_ref, dq_ref, dkv_ref, o_ref, own_ref, far_ref):
    half, ff = own_ref.shape[1], own_ref.shape[2]
    tile = 256
    grads = jnp.concatenate([dq_ref[...], dkv_ref[...]], axis=1)
    count = grads.shape[1] // ff
    for part, out in ((0, own_ref), (1, far_ref)):

        @pl.loop(0, half // tile)
        def _(index, part=part, out=out):
            begin = pl.multiple_of(index * tile, tile)
            rows = pl.ds(part * half + begin, tile)
            block = matmul(n_ref[rows, :], grads).astype(BF)
            for c in range(count):
                out[c, pl.ds(begin, tile), :] = block[:, c * ff : (c + 1) * ff]
            block = matmul(da_ref[rows, :], o_ref[...]).astype(BF)
            for c in range(block.shape[1] // ff):
                out[count + c, pl.ds(begin, tile), :] = block[:, c * ff : (c + 1) * ff]


def attention_weights(normed_t, grad_branch_t, grad_q, grad_kv, attended, ff):
    count = (grad_q.shape[1] + grad_kv.shape[1] + attended.shape[1]) // ff
    slabs = jax.ShapeDtypeStruct((count, normed_t.shape[0] // 2, ff), BF)
    return pl.pallas_call(
        attention_weights_kernel,
        out_shape=(slabs, slabs),
        compiler_params=pltpu.CompilerParams(vmem_limit_bytes=VMEM_LIMIT),
        cost_estimate=COST,
        name="attention_weights",
    )(normed_t, grad_branch_t, grad_q, grad_kv, attended)


def unpack_attention_kernel(slabs_ref, q_ref, k_ref, v_ref, out_ref):
    ff = slabs_ref.shape[2]
    at = 0
    for ref in (q_ref, k_ref, v_ref):
        for c in range(ref.shape[1] // ff):
            ref[:, c * ff : (c + 1) * ff] = slabs_ref[at].astype(F32)
            at += 1
    for c in range(out_ref.shape[0] // ff):
        out_ref[c * ff : (c + 1) * ff, :] = slabs_ref[at].astype(F32).T
        at += 1


def unpack_attention(slabs, query_cols, key_cols):
    rows = slabs.shape[1]
    return pl.pallas_call(
        unpack_attention_kernel,
        out_shape=tuple(
            jax.ShapeDtypeStruct(shape, F32)
            for shape in (
                (rows, query_cols), (rows, key_cols), (rows, key_cols), (query_cols, rows)
            )
        ),
        compiler_params=pltpu.CompilerParams(vmem_limit_bytes=VMEM_LIMIT),
        cost_estimate=COST,
        name="unpack_attention",
    )(slabs)


def inverse_norm(near, far):
    count = near.shape[1] + far.shape[1]
    squares = jnp.sum(near * near, axis=1, keepdims=True) + jnp.sum(far * far, axis=1, keepdims=True)
    return lax.rsqrt(squares / count + EPS)


def halves(ref, rows, shard):
    half = ref.shape[1] // 2
    own = pl.ds(pl.multiple_of(shard * half, 128), half)
    far = pl.ds(pl.multiple_of((1 - shard) * half, 128), half)
    return ref[rows, own].astype(F32), ref[rows, far].astype(F32)


def put_halves(ref, rows, shard, near, far):
    half = ref.shape[1] // 2
    ref[rows, pl.ds(pl.multiple_of(shard * half, 128), half)] = near.astype(ref.dtype)
    ref[rows, pl.ds(pl.multiple_of((1 - shard) * half, 128), half)] = far.astype(ref.dtype)


def enter_kernel(place, x_ref, gain_ref, wo_ref, wf_ref, q_ref, kv_ref, nt_ref):
    half = x_ref.shape[1] // 2
    near, far = halves(x_ref, slice(None), place[1])
    inverse = inverse_norm(near, far)
    near = (near * inverse * gain_ref[:, :half]).astype(BF)
    far = (far * inverse * gain_ref[:, half:]).astype(BF)
    qkv = (matmul(near, wo_ref[...]) + matmul(far, wf_ref[...])).astype(BF)
    cols = q_ref.shape[1]
    q_ref[...] = qkv[:, :cols]
    kv_ref[...] = qkv[:, cols:]
    nt_ref[:half, :] = near.T
    nt_ref[half:, :] = far.T


def enter(place, x, gain, w_own, w_far, query_cols):
    tokens, width = x.shape
    both = w_own.shape[1] - query_cols
    tile = 256
    return pl.pallas_call(
        enter_kernel,
        out_shape=(
            jax.ShapeDtypeStruct((tokens, query_cols), BF),
            jax.ShapeDtypeStruct((tokens, both), BF),
            jax.ShapeDtypeStruct((width, tokens), BF),
        ),
        grid_spec=pltpu.PrefetchScalarGridSpec(
            num_scalar_prefetch=1,
            grid=(tokens // tile,),
            in_specs=[
                pl.BlockSpec((tile, width), lambda i, s: (i, 0)),
                pl.BlockSpec((1, width), lambda i, s: (0, 0)),
                pl.BlockSpec(w_own.shape, lambda i, s: (0, 0)),
                pl.BlockSpec(w_far.shape, lambda i, s: (0, 0)),
            ],
            out_specs=[
                pl.BlockSpec((tile, query_cols), lambda i, s: (i, 0)),
                pl.BlockSpec((tile, both), lambda i, s: (i, 0)),
                pl.BlockSpec((width, tile), lambda i, s: (0, i)),
            ],
        ),
        compiler_params=pltpu.CompilerParams(vmem_limit_bytes=VMEM_LIMIT),
        cost_estimate=COST,
        name="enter",
    )(place, x, gain, w_own, w_far)


def qkv_backward_kernel(dq_ref, dkv_ref, wo_ref, wf_ref, dn_ref):
    half = wo_ref.shape[0]
    grads = jnp.concatenate([dq_ref[...], dkv_ref[...]], axis=1)
    dn_ref[:, :half] = contract_last(grads, wo_ref[...]).astype(BF)
    dn_ref[:, half:] = contract_last(grads, wf_ref[...]).astype(BF)


def qkv_backward(grad_q, grad_kv, w_own, w_far):
    tokens = grad_q.shape[0]
    tile = 256
    return pl.pallas_call(
        qkv_backward_kernel,
        out_shape=jax.ShapeDtypeStruct((tokens, 2 * w_own.shape[0]), BF),
        grid=(tokens // tile,),
        in_specs=[
            pl.BlockSpec((tile, grad_q.shape[1]), lambda i: (i, 0)),
            pl.BlockSpec((tile, grad_kv.shape[1]), lambda i: (i, 0)),
            pl.BlockSpec(w_own.shape, lambda i: (0, 0)),
            pl.BlockSpec(w_far.shape, lambda i: (0, 0)),
        ],
        out_specs=pl.BlockSpec((tile, 2 * w_own.shape[0]), lambda i: (i, 0)),
        compiler_params=pltpu.CompilerParams(vmem_limit_bytes=VMEM_LIMIT),
        cost_estimate=COST,
        name="qkv_backward",
    )(grad_q, grad_kv, w_own, w_far)


def leave_kernel(place, x_ref, dn_ref, dh_ref, gain_ref, out_ref, scale_ref):
    half = x_ref.shape[1] // 2
    near, far = halves(x_ref, slice(None), place[1])
    inverse = inverse_norm(near, far)
    grads = dn_ref[...].astype(F32)
    near_out, far_out, near_scale, far_scale = norm_backward(
        near, far, inverse, gain_ref[...], grads
    )
    put_halves(
        out_ref, slice(None), place[1], dh_ref[:, :half] + near_out, dh_ref[:, half:] + far_out
    )

    @pl.when(pl.program_id(0) == 0)
    def _():
        scale_ref[...] = jnp.zeros_like(scale_ref)

    scale_ref[:, :half] += near_scale
    scale_ref[:, half:] += far_scale


def leave(place, x, grad_normed, grad_hidden, gain):
    tokens, width = x.shape
    tile = 256
    block = pl.BlockSpec((tile, width), lambda i, s: (i, 0))
    row = pl.BlockSpec((1, width), lambda i, s: (0, 0))
    return pl.pallas_call(
        leave_kernel,
        out_shape=(
            jax.ShapeDtypeStruct((tokens, width), F32),
            jax.ShapeDtypeStruct((1, width), F32),
        ),
        grid_spec=pltpu.PrefetchScalarGridSpec(
            num_scalar_prefetch=1,
            grid=(tokens // tile,),
            in_specs=[block, block, block, row],
            out_specs=[block, row],
        ),
        compiler_params=pltpu.CompilerParams(vmem_limit_bytes=VMEM_LIMIT),
        cost_estimate=COST,
        name="leave",
    )(place, x, grad_normed, grad_hidden, gain)


def norm_backward(near, far, inverse, gain, grads):
    half = near.shape[1]
    near_scaled = grads[:, :half] * gain[:, :half]
    far_scaled = grads[:, half:] * gain[:, half:]
    along = (
        jnp.sum(near_scaled * near, axis=1, keepdims=True)
        + jnp.sum(far_scaled * far, axis=1, keepdims=True)
    ) / (2 * half)
    cube = inverse * inverse * inverse * along
    return (
        inverse * near_scaled - near * cube,
        inverse * far_scaled - far * cube,
        jnp.sum(grads[:, :half] * near * inverse, axis=0, keepdims=True),
        jnp.sum(grads[:, half:] * far * inverse, axis=0, keepdims=True),
    )


CHUNK = 128


def sum_over_tensor(part, total, arrived, mine, other, sems, consume):
    send1, recv1, send2, recv2, send3, recv3 = sems
    t = lax.axis_index("tensor")
    low, high = lax.rem(t, 2), lax.rem(t // 2, 2)
    near = {"tensor": t + 1 - 2 * low}
    far = {"tensor": t + 2 - 4 * high}
    chunks = arrived.shape[0]
    half = chunks * CHUNK

    barrier = pltpu.get_barrier_semaphore()
    for peer in (near, far):
        pl.semaphore_signal(barrier, inc=1, device_id=peer, device_id_type=MESH)
    pl.semaphore_wait(barrier, 2)

    def rows(side, c):
        return pl.ds(pl.multiple_of(side * half + c * CHUNK, CHUNK), CHUNK)

    def give(c):
        return pltpu.make_async_remote_copy(
            part.at[rows(1 - low, c)], arrived.at[c], send1.at[c], recv1.at[c],
            device_id=near, device_id_type=MESH,
        )

    def swap(c):
        return pltpu.make_async_remote_copy(
            mine.at[c], other.at[c], send2.at[c], recv2.at[c], device_id=far, device_id_type=MESH
        )

    def back(c):
        return pltpu.make_async_remote_copy(
            total.at[rows(low, c)], total.at[rows(low, c)], send3.at[c], recv3.at[c],
            device_id=near, device_id_type=MESH,
        )

    @pl.loop(0, chunks)
    def _(c):
        give(c).start()

    @pl.loop(0, chunks)
    def _(c):
        give(c).wait_recv()
        mine[c] = (part[rows(low, c), :].astype(F32) + arrived[c].astype(F32)).astype(BF)
        swap(c).start()

    @pl.loop(0, chunks)
    def _(c):
        swap(c).wait_recv()
        total[rows(low, c), :] = (mine[c].astype(F32) + other[c].astype(F32)).astype(BF)
        back(c).start()
        consume(pl.multiple_of(low * half + c * CHUNK, CHUNK))
        back(c).wait_recv()
        consume(pl.multiple_of((1 - low) * half + c * CHUNK, CHUNK))

    @pl.loop(0, chunks)
    def _(c):
        give(c).wait_send()
        swap(c).wait_send()
        back(c).wait_send()


def sum_scratch(tokens, width):
    chunks = tokens // 2 // CHUNK
    piece = pltpu.VMEM((chunks, CHUNK, width), BF)
    return [pltpu.VMEM((tokens, width), BF)] + [piece] * 3 + [
        pltpu.SemaphoreType.DMA((chunks,))
    ] * 6


def after_attention_kernel(
    part, x_ref, gain_ref, h_ref, n_ref, nt_ref, total, arrived, mine, other, *sems
):
    half = x_ref.shape[1] // 2
    shard = lax.axis_index("shard")

    def consume(row):
        rows = pl.ds(row, CHUNK)
        near, far = halves(x_ref, rows, shard)
        near = near + total[rows, :half].astype(F32)
        far = far + total[rows, half:].astype(F32)
        h_ref[rows, :half] = near
        h_ref[rows, half:] = far
        inverse = inverse_norm(near, far)
        near = (near * inverse * gain_ref[:, :half]).astype(BF)
        far = (far * inverse * gain_ref[:, half:]).astype(BF)
        n_ref[rows, :half] = near
        n_ref[rows, half:] = far
        nt_ref[:half, rows] = near.T
        nt_ref[half:, rows] = far.T

    sum_over_tensor(part, total, arrived, mine, other, sems, consume)


def after_attention(part, x, gain):
    tokens, width = x.shape
    return pl.pallas_call(
        after_attention_kernel,
        out_shape=(
            jax.ShapeDtypeStruct((tokens, width), F32),
            jax.ShapeDtypeStruct((tokens, width), BF),
            jax.ShapeDtypeStruct((width, tokens), BF),
        ),
        scratch_shapes=sum_scratch(tokens, width),
        compiler_params=pltpu.CompilerParams(
            collective_id=2, has_side_effects=True, vmem_limit_bytes=VMEM_LIMIT
        ),
        cost_estimate=COST,
        name="after_attention",
    )(part, x, gain)


def after_experts_kernel(
    part, h_ref, teacher_ref, mask_ref, factor_ref,
    y_ref, gy_ref, low_ref, lowt_ref, square_ref, total, arrived, mine, other, *sems
):
    half = h_ref.shape[1] // 2
    shard = lax.axis_index("shard")
    square_ref[...] = jnp.zeros_like(square_ref)

    def consume(row):
        rows = pl.ds(row, CHUNK)
        mask = mask_ref[rows, :]
        factor = factor_ref[...] * mask
        near_t, far_t = halves(teacher_ref, rows, shard)
        near = h_ref[rows, :half] + total[rows, :half].astype(F32)
        far = h_ref[rows, half:] + total[rows, half:].astype(F32)
        put_halves(y_ref, rows, shard, near, far)
        for begin, error in ((0, near - near_t), (half, far - far_t)):
            span = slice(begin, begin + half)
            squares = mask * jnp.sum(error * error, axis=1, keepdims=True)
            square_ref[...] += jnp.sum(squares, axis=0, keepdims=True)
            grad = factor * error
            gy_ref[rows, span] = grad
            low = grad.astype(BF)
            low_ref[rows, span] = low
            lowt_ref[span, rows] = low.T

    sum_over_tensor(part, total, arrived, mine, other, sems, consume)


def after_experts(part, hidden, teacher, mask, factor):
    tokens, width = hidden.shape
    return pl.pallas_call(
        after_experts_kernel,
        out_shape=(
            jax.ShapeDtypeStruct((tokens, width), BF),
            jax.ShapeDtypeStruct((tokens, width), F32),
            jax.ShapeDtypeStruct((tokens, width), BF),
            jax.ShapeDtypeStruct((width, tokens), BF),
            jax.ShapeDtypeStruct((1, 1), F32),
        ),
        scratch_shapes=sum_scratch(tokens, width),
        compiler_params=pltpu.CompilerParams(
            collective_id=3, has_side_effects=True, vmem_limit_bytes=VMEM_LIMIT
        ),
        cost_estimate=COST,
        name="after_experts",
    )(part, hidden, teacher, mask, factor)


def after_backward_kernel(
    part, h_ref, gy_ref, gain_ref, wo_ref, wf_ref,
    dh_ref, dat_ref, do_ref, scale_ref, total, arrived, mine, other, *sems
):
    half = h_ref.shape[1] // 2
    scale_ref[...] = jnp.zeros_like(scale_ref)

    def consume(row):
        rows = pl.ds(row, CHUNK)
        near, far = h_ref[rows, :half], h_ref[rows, half:]
        inverse = inverse_norm(near, far)
        near_out, far_out, near_scale, far_scale = norm_backward(
            near, far, inverse, gain_ref[...], total[rows, :].astype(F32)
        )
        scale_ref[:, :half] += near_scale
        scale_ref[:, half:] += far_scale
        near = gy_ref[rows, :half] + near_out
        far = gy_ref[rows, half:] + far_out
        dh_ref[rows, :half] = near
        dh_ref[rows, half:] = far
        near = near.astype(BF)
        far = far.astype(BF)
        dat_ref[:half, rows] = near.T
        dat_ref[half:, rows] = far.T
        do_ref[rows, :] = (
            contract_last(near, wo_ref[...]) + contract_last(far, wf_ref[...])
        ).astype(BF)

    sum_over_tensor(part, total, arrived, mine, other, sems, consume)


def after_backward(part, hidden, grad_y, gain, out_own, out_far):
    tokens, width = hidden.shape
    return pl.pallas_call(
        after_backward_kernel,
        out_shape=(
            jax.ShapeDtypeStruct((tokens, width), F32),
            jax.ShapeDtypeStruct((width, tokens), BF),
            jax.ShapeDtypeStruct((tokens, out_own.shape[0]), BF),
            jax.ShapeDtypeStruct((1, width), F32),
        ),
        scratch_shapes=sum_scratch(tokens, width),
        compiler_params=pltpu.CompilerParams(
            collective_id=4, has_side_effects=True, vmem_limit_bytes=VMEM_LIMIT
        ),
        cost_estimate=COST,
        name="after_backward",
    )(part, hidden, grad_y, gain, out_own, out_far)


def local(
    states, segments, routes, gates, valid, teacher, attn_gain, w_query, key_matrix, value_matrix,
    w_out, moe_gain, w_gate, w_up, w_down,
):
    shard = lax.axis_index("shard")
    context = lax.axis_index("context")
    shards = lax.axis_size("shard")
    contexts = lax.axis_size("context")
    trees, rows, width = states.shape
    tokens = trees * rows
    half = width // 2
    experts, _, ff = w_gate.shape
    swap = [(a, shards - 1 - a) for a in range(shards)]
    pairs = [(a, a + 1 - 2 * (a % 2)) for a in range(contexts)]
    parity = lax.rem(context, 2)
    place = jnp.stack([context, shard]).astype(jnp.int32)
    side = jnp.reshape(parity, (1,)).astype(jnp.int32)

    def over_shard(value):
        return lax.ppermute(value, "shard", swap)

    def over_context(value):
        return lax.ppermute(value, "context", pairs)

    def half_of(value, axis):
        size = value.shape[axis] // 2
        return lax.dynamic_slice_in_dim(value, parity * size, size, axis)

    def both_parts(direct, axis):
        relayed = over_context(direct)
        return jnp.where(
            parity == 0,
            jnp.concatenate([direct, relayed], axis),
            jnp.concatenate([relayed, direct], axis),
        )

    def tied(*values):
        return lax.optimization_barrier(values)

    qkv_own = jnp.concatenate([w_query, key_matrix, value_matrix], axis=1)
    qkv_send, out_send = tied(half_of(qkv_own, 0), half_of(w_out, 1))
    gains_own = jnp.stack([attn_gain, moe_gain])
    gains = jnp.concatenate([gains_own, over_shard(gains_own)], axis=1)
    attn_scale, moe_scale = gains[0:1], gains[1:2]
    qkv_far = both_parts(over_shard(qkv_send), 0)
    out_direct = over_shard(out_send)
    out_far = both_parts(out_direct, 1)
    count = jnp.sum(valid.astype(jnp.int32))
    packed = jnp.concatenate([segments, jnp.broadcast_to(count, (1, rows))])
    packed_all = lax.all_gather(packed, "context", axis=1, tiled=True)
    gate_send, up_send, down_send, packed_all, _ = tied(
        half_of(w_gate, 0), half_of(w_up, 0), half_of(w_down, 0), packed_all, out_direct
    )
    gate_direct, up_direct, down_direct = (
        over_shard(gate_send), over_shard(up_send), over_shard(down_send)
    )
    segments_all = packed_all[:trees]
    last = jnp.where(
        segments_all == 0,
        1 << 20,
        jnp.where(segments_all % 3 == 1, segments_all + 2, segments_all),
    )
    total = segments_all.shape[1]
    x = states.reshape(tokens, width)
    x, last = tied(x, last)
    valid_total = jnp.sum(packed_all[trees:, ::rows], keepdims=True).astype(F32)
    valid_total = valid_total + over_shard(valid_total)

    query_cols = w_query.shape[1]
    q, kv_own, normed_t = enter(place, x, attn_scale, qkv_own, qkv_far, query_cols)
    both = kv_own.shape[1]
    kv_own, out_far = tied(kv_own, out_far)
    kv = lax.all_gather(kv_own.reshape(trees, rows, both), "context", axis=1, tiled=True)
    kv, gate_direct = tied(kv, gate_direct)
    gate_relayed = over_context(gate_direct)
    attended, lse, branch_part = attention_forward(
        place, q, kv, last.reshape(trees, 1, total), segments.reshape(tokens, 1), w_out, out_far
    )
    branch_part, up_direct, gate_relayed = tied(branch_part, up_direct, gate_relayed)
    up_relayed = over_context(up_direct)
    hidden, normed_two, normed_two_t = after_attention(branch_part, x, moe_scale)
    normed_two, down_direct, up_relayed = tied(normed_two, down_direct, up_relayed)
    down_relayed = over_context(down_direct)
    gate_ws = (w_gate, gate_direct, gate_relayed)
    up_ws = (w_up, up_direct, up_relayed)
    down_ws = (w_down, down_direct, down_relayed)

    expert_ids = jnp.arange(experts, dtype=jnp.int32)
    combine = jnp.sum(
        gates.reshape(tokens, -1)[..., None]
        * (routes.reshape(tokens, -1)[..., None] == expert_ids).astype(F32),
        axis=1,
    )
    pre, middle, held = experts_forward(
        side, normed_two, combine, gate_ws[:2], up_ws[:2], down_ws[:2]
    )
    pre, middle, moe_part = experts_forward(
        side, normed_two, combine, gate_ws[::2], up_ws[::2], down_ws[::2], (held, pre, middle)
    )
    token_total = tokens * shards * contexts
    result, grad_y, grad_y_low, grad_y_t, square = after_experts(
        moe_part,
        hidden,
        teacher.reshape(tokens, width),
        valid.reshape(tokens, 1).astype(F32),
        token_total / valid_total,
    )
    expert_grads, dn_part = experts_backward(
        side, grad_y_low, combine, gate_ws, up_ws, down_ws, pre
    )

    grad_hidden, grad_branch_t, grad_attended, grad_moe_scale = after_backward(
        dn_part, hidden, grad_y, moe_scale, w_out, out_far
    )
    grad_q, grad_kv_all = attention_backward(
        place, q, grad_attended, attended, lse, kv, last.reshape(trees * total, 1),
        segments.reshape(trees, 1, rows),
    )
    grad_kv = lax.psum_scatter(grad_kv_all, "context", scatter_dimension=1, tiled=True)
    grad_q, expert_grads = tied(grad_q, expert_grads)
    own_experts, far_experts = expert_weights(
        side, normed_two_t, grad_y_t, expert_grads, middle, 0, experts // 2
    )
    grad_kv, own_experts, far_experts = tied(grad_kv, own_experts, far_experts)
    grad_kv = grad_kv.reshape(tokens, both)
    dn1_part = qkv_backward(grad_q, grad_kv, qkv_own, qkv_far)
    grad_normed = lax.psum(dn1_part, "tensor")
    own_attn, far_attn = attention_weights(normed_t, grad_branch_t, grad_q, grad_kv, attended, ff)
    sum_experts, sum_attn = reduce_gradients(
        contexts, (own_experts, own_attn), (far_experts, far_attn)
    )
    grad_normed, sum_attn = lax.optimization_barrier((grad_normed, sum_attn))
    grad_inputs, grad_attn_scale = leave(place, x, grad_normed, grad_hidden, attn_scale)
    final_gate, final_up, final_down = unpack(sum_experts)
    key_cols = key_matrix.shape[1]
    final_query, final_key, final_value, final_out = unpack_attention(
        sum_attn, query_cols, key_cols
    )
    grad_scales = jnp.concatenate([grad_attn_scale, grad_moe_scale])
    tail = jnp.concatenate([grad_scales[:, :half], jnp.broadcast_to(square, (1, half))])
    tail_far = jnp.concatenate([grad_scales[:, half:], jnp.broadcast_to(square, (1, half))])
    tail = tail + over_shard(tail_far)
    hop = 1
    while hop < contexts:
        tail = tail + lax.ppermute(tail, "context", [(a, a ^ hop) for a in range(contexts)])
        hop *= 2
    return (
        tail[2, 0] / (valid_total[0, 0] * width),
        result.reshape(trees, rows, width),
        grad_inputs.reshape(trees, rows, width),
        tail[0],
        final_query,
        final_key,
        final_value,
        final_out,
        tail[1],
        final_gate,
        final_up,
        final_down,
    )


def solution(mesh):
    return jax.shard_map(
        local,
        mesh=mesh,
        in_specs=(
            P("shard", "context", None),
            P("shard", "context"),
            P("shard", "context", None),
            P("shard", "context", None),
            P("shard", "context"),
            P("shard", "context", None),
            P("shard"),
            P("shard", "tensor"),
            P("shard", "tensor"),
            P("shard", "tensor"),
            P("tensor", "shard"),
            P("shard"),
            P(None, "shard", "tensor"),
            P(None, "shard", "tensor"),
            P(None, "tensor", "shard"),
        ),
        out_specs=(
            P(),
            P("shard", "context", None),
            P("shard", "context", None),
            P("shard"),
            P("shard", "tensor"),
            P("shard", "tensor"),
            P("shard", "tensor"),
            P("tensor", "shard"),
            P("shard"),
            P(None, "shard", "tensor"),
            P(None, "shard", "tensor"),
            P(None, "tensor", "shard"),
        ),
        check_vma=False,
    )
```

```python
import functools
import math

import jax
import jax.numpy as jnp
from jax import lax
from jax.experimental import pallas as pl
from jax.experimental.pallas import tpu as pltpu
from jax.sharding import PartitionSpec as P

HEAD = 64
EPS = 1e-05
BF = jnp.bfloat16
F32 = jnp.float32
MESH = pl.DeviceIdType.MESH
VMEM_LIMIT = 56 * 1024 * 1024
UNIT = 2
COST = pl.CostEstimate(flops=1, bytes_accessed=1, transcendentals=0)


def matmul(left, right):
    return jnp.dot(left, right, preferred_element_type=F32)


def contract_first(left, right):
    return lax.dot_general(left, right, (((0,), (0,)), ((), ())), preferred_element_type=F32)


def contract_last(left, right):
    return lax.dot_general(left, right, (((1,), (1,)), ((), ())), preferred_element_type=F32)


def attention_backward_kernel(
    place, q_ref, do_ref, o_ref, lse_ref, kv_ref, last_ref, seg_ref, dq_ref, dkv_ref, bias, deltas, sums
):
    rows = q_ref.shape[0]
    width = kv_ref.shape[2] // 2
    heads = q_ref.shape[1] // HEAD
    per_group = q_ref.shape[1] // width
    sums[...] = jnp.zeros_like(sums)
    for head in range(heads):
        cols = slice(head * HEAD, (head + 1) * HEAD)
        product = do_ref[:, cols].astype(F32) * o_ref[:, cols].astype(F32)
        deltas[head] = lax.dot_general(
            jnp.ones((8, HEAD), F32),
            product,
            (((1,), (1,)), ((), ())),
            precision=lax.Precision.HIGHEST,
            preferred_element_type=F32,
        )

    @pl.loop(0, kv_ref.shape[0])
    def _(index):
        @pl.when(index > place[0])
        def _():
            dkv_ref[index] = jnp.zeros(dkv_ref.shape[1:], BF)

        @pl.when(index <= place[0])
        def _():
            span = pl.ds(pl.multiple_of(index * rows, rows), rows)
            key_pos = index * rows + lax.broadcasted_iota(jnp.int32, (rows, rows), 0)
            query_pos = place[0] * rows + lax.broadcasted_iota(jnp.int32, (rows, rows), 1)
            allowed = (key_pos <= query_pos) & (seg_ref[0] <= last_ref[span, :])
            bias[...] = jnp.where(allowed, 0.0, -2e30)
            for group in range(heads // per_group):
                keys = kv_ref[index, :, group * HEAD : (group + 1) * HEAD]
                values = kv_ref[index, :, width + group * HEAD : width + (group + 1) * HEAD]
                dk = jnp.zeros((rows, HEAD), F32)
                dv = jnp.zeros((rows, HEAD), F32)
                for head in range(group * per_group, (group + 1) * per_group):
                    cols = slice(head * HEAD, (head + 1) * HEAD)
                    queries = q_ref[:, cols]
                    grads = do_ref[:, cols]
                    scores = contract_last(keys, queries) * 0.125 + bias[...]
                    probs = jnp.exp(scores - lse_ref[0, head : head + 1, :])
                    grad_probs = contract_last(values, grads)
                    grad_scores = (probs * (grad_probs - deltas[head, 0:1, :])).astype(BF)
                    dv = dv + matmul(probs.astype(BF), grads)
                    dk = dk + matmul(grad_scores, queries)
                    sums[:, cols] += contract_first(grad_scores, keys)
                dkv_ref[index, :, group * HEAD : (group + 1) * HEAD] = (dk * 0.125).astype(BF)
                dkv_ref[index, :, width + group * HEAD : width + (group + 1) * HEAD] = dv.astype(BF)

    dq_ref[...] = (sums[...] * 0.125).astype(BF)


def attention_backward(place, q, do, o, lse, kv, last_col, seg_row):
    contexts, tokens, both = kv.shape
    trees, _, rows = seg_row.shape
    cols = q.shape[1]
    by_tree = pl.BlockSpec((rows, cols), lambda t, s: (t, 0))
    by_block = pl.BlockSpec((contexts, rows, both), lambda t, s: (0, t, 0))
    return pl.pallas_call(
        attention_backward_kernel,
        out_shape=(
            jax.ShapeDtypeStruct(q.shape, BF),
            jax.ShapeDtypeStruct(kv.shape, BF),
        ),
        grid_spec=pltpu.PrefetchScalarGridSpec(
            num_scalar_prefetch=1,
            grid=(trees,),
            in_specs=[
                by_tree,
                by_tree,
                by_tree,
                pl.BlockSpec((1, 8, rows), lambda t, s: (t, 0, 0)),
                by_block,
                pl.BlockSpec((contexts * rows, 1), lambda t, s: (t, 0)),
                pl.BlockSpec((1, 1, rows), lambda t, s: (t, 0, 0)),
            ],
            out_specs=[by_tree, by_block],
            scratch_shapes=[
                pltpu.VMEM((rows, rows), F32),
                pltpu.VMEM((q.shape[1] // HEAD, 8, rows), F32),
                pltpu.VMEM((rows, cols), F32),
            ],
        ),
        compiler_params=pltpu.CompilerParams(vmem_limit_bytes=VMEM_LIMIT),
        cost_estimate=COST,
        name="attention_backward",
    )(place, q, do, o, lse, kv, last_col, seg_row)


def stage_weights(gates, ups, downs, wide, tall):
    half, ff = gates[0].shape[1], gates[0].shape[2]
    for part in range(2):
        for a in range(2):
            features = slice(part * half, (part + 1) * half)
            wide[features, 2 * a * ff : (2 * a + 1) * ff] = gates[part][a]
            wide[features, (2 * a + 1) * ff : (2 * a + 2) * ff] = ups[part][a]
            tall[a * ff : (a + 1) * ff, features] = downs[part][a]


def column(block, index):
    lane = lax.broadcasted_iota(jnp.int32, block.shape, 1)
    return jnp.sum(jnp.where(lane == index, block, 0.0), axis=1, keepdims=True)


def experts_forward_kernel(
    n_ref, c_ref, g0, g1, u0, u1, d0, d1, pre_ref, cm_ref, m_ref, wide, tall, acc
):
    step = pl.program_id(0)
    ff = g0.shape[2]
    stage_weights((g0, g1), (u0, u1), (d0, d1), wide, tall)

    @pl.when(step == 0)
    def _():
        acc[...] = jnp.zeros_like(acc)

    hidden = matmul(n_ref[...], wide[...])
    pre_ref[0] = hidden.astype(BF)
    pieces = []
    for a in range(2):
        gate = hidden[:, 2 * a * ff : (2 * a + 1) * ff]
        up = hidden[:, (2 * a + 1) * ff : (2 * a + 2) * ff]
        weight = column(c_ref[...], 2 * step + a)
        pieces.append((weight * (gate * jax.nn.sigmoid(gate) * up)).astype(BF))
    middle = jnp.concatenate(pieces, axis=1)
    cm_ref[0] = middle
    acc[...] += matmul(middle, tall[...])

    @pl.when(step == pl.num_programs(0) - 1)
    def _():
        m_ref[...] = acc[...].astype(BF)


def expert_specs(half, ff):
    return [
        pl.BlockSpec(shape, lambda i: (i, 0, 0))
        for shape in ((2, half, ff),) * 4 + ((2, ff, half),) * 2
    ]


def experts_forward(normed, combine, gates, ups, downs):
    tokens, width = normed.shape
    experts, half, ff = gates[0].shape
    steps = experts // 2
    whole = pl.BlockSpec((tokens, width), lambda i: (0, 0))
    return pl.pallas_call(
        experts_forward_kernel,
        out_shape=(
            jax.ShapeDtypeStruct((steps, tokens, 4 * ff), BF),
            jax.ShapeDtypeStruct((steps, tokens, 2 * ff), BF),
            jax.ShapeDtypeStruct((tokens, width), BF),
        ),
        grid=(steps,),
        in_specs=[whole, pl.BlockSpec((tokens, experts), lambda i: (0, 0))]
        + expert_specs(half, ff),
        out_specs=[
            pl.BlockSpec((1, tokens, 4 * ff), lambda i: (i, 0, 0)),
            pl.BlockSpec((1, tokens, 2 * ff), lambda i: (i, 0, 0)),
            whole,
        ],
        scratch_shapes=[
            pltpu.VMEM((width, 4 * ff), BF),
            pltpu.VMEM((2 * ff, width), BF),
            pltpu.VMEM((tokens, width), F32),
        ],
        compiler_params=pltpu.CompilerParams(vmem_limit_bytes=VMEM_LIMIT),
        cost_estimate=COST,
        name="experts_forward",
    )(normed, combine, *gates, *ups, *downs)


def experts_backward_kernel(
    gy_ref, c_ref, g0, g1, u0, u1, d0, d1, pre_ref, grads_ref, dn_ref, wide, tall, acc
):
    step = pl.program_id(0)
    ff = g0.shape[2]
    stage_weights((g0, g1), (u0, u1), (d0, d1), wide, tall)

    @pl.when(step == 0)
    def _():
        acc[...] = jnp.zeros_like(acc)

    grad_middle = contract_last(gy_ref[...], tall[...])
    for a in range(2):
        gate = pre_ref[0, :, 2 * a * ff : (2 * a + 1) * ff].astype(F32)
        up = pre_ref[0, :, (2 * a + 1) * ff : (2 * a + 2) * ff].astype(F32)
        weight = column(c_ref[...], 2 * step + a)
        gm = weight * grad_middle[:, a * ff : (a + 1) * ff]
        sig = jax.nn.sigmoid(gate)
        grads_ref[0, :, 2 * a * ff : (2 * a + 1) * ff] = (
            gm * up * (sig + gate * sig * (1.0 - sig))
        ).astype(BF)
        grads_ref[0, :, (2 * a + 1) * ff : (2 * a + 2) * ff] = (gm * gate * sig).astype(BF)
    acc[...] += contract_last(grads_ref[0], wide[...])

    @pl.when(step == pl.num_programs(0) - 1)
    def _():
        dn_ref[...] = acc[...].astype(BF)


def experts_backward(grad_y, combine, gates, ups, downs, pre):
    tokens, width = grad_y.shape
    experts, half, ff = gates[0].shape
    steps = experts // 2
    whole = pl.BlockSpec((tokens, width), lambda i: (0, 0))
    by_pair = pl.BlockSpec((1, tokens, 4 * ff), lambda i: (i, 0, 0))
    return pl.pallas_call(
        experts_backward_kernel,
        out_shape=(
            jax.ShapeDtypeStruct((steps, tokens, 4 * ff), BF),
            jax.ShapeDtypeStruct((tokens, width), BF),
        ),
        grid=(steps,),
        in_specs=[whole, pl.BlockSpec((tokens, experts), lambda i: (0, 0))]
        + expert_specs(half, ff)
        + [by_pair],
        out_specs=[by_pair, whole],
        scratch_shapes=[
            pltpu.VMEM((width, 4 * ff), BF),
            pltpu.VMEM((2 * ff, width), BF),
            pltpu.VMEM((tokens, width), F32),
        ],
        compiler_params=pltpu.CompilerParams(vmem_limit_bytes=VMEM_LIMIT),
        cost_estimate=COST,
        name="experts_backward",
    )(grad_y, combine, *gates, *ups, *downs, pre)


def expert_weights_kernel(n_ref, gy_ref, grads_ref, cm_ref, own_ref, far_ref):
    half, ff = own_ref.shape[1], own_ref.shape[2]
    for part, out in ((0, own_ref), (1, far_ref)):
        rows = slice(part * half, (part + 1) * half)
        block = matmul(n_ref[rows, :], grads_ref[0]).astype(BF)
        for c in range(4):
            out[c // 2 + 2 * (c % 2)] = block[:, c * ff : (c + 1) * ff]
        block = matmul(gy_ref[rows, :], cm_ref[0]).astype(BF)
        for c in range(2):
            out[4 + c] = block[:, c * ff : (c + 1) * ff]


def expert_weights(normed_t, grad_y_t, grads, middle):
    width, tokens = normed_t.shape
    steps, _, four = grads.shape
    ff, half = four // 4, width // 2
    slabs = jax.ShapeDtypeStruct((steps * 6, half, ff), BF)
    whole = pl.BlockSpec((width, tokens), lambda i: (0, 0))
    return pl.pallas_call(
        expert_weights_kernel,
        out_shape=(slabs, slabs),
        grid=(steps,),
        in_specs=[
            whole,
            whole,
            pl.BlockSpec((1, tokens, 4 * ff), lambda i: (i, 0, 0)),
            pl.BlockSpec((1, tokens, 2 * ff), lambda i: (i, 0, 0)),
        ],
        out_specs=[pl.BlockSpec((6, half, ff), lambda i: (i, 0, 0))] * 2,
        compiler_params=pltpu.CompilerParams(vmem_limit_bytes=VMEM_LIMIT),
        cost_estimate=COST,
        name="expert_weights",
    )(normed_t, grad_y_t, grads, middle)


def reduce_kernel(
    contexts, owns, fars, outs, own, far, up, down,
    own_sem, ysend, yrecv, usend, urecv, dsend, drecv, out_sem,
):
    units, unit = own.shape[0], own.shape[1]
    ahead = 6
    i = lax.axis_index("context")
    shard = lax.axis_index("shard")
    has_left, has_right = i > 0, i < contexts - 1
    right = {"context": lax.rem(i + 1, contexts)}
    left = {"context": lax.rem(i + contexts - 1, contexts)}
    other = {"shard": 1 - shard}

    barrier = pltpu.get_barrier_semaphore()
    pl.semaphore_signal(barrier, inc=1, device_id=other, device_id_type=MESH)

    @pl.when(has_left)
    def _():
        pl.semaphore_signal(barrier, inc=1, device_id=left, device_id_type=MESH)

    @pl.when(has_right)
    def _():
        pl.semaphore_signal(barrier, inc=1, device_id=right, device_id_type=MESH)

    pl.semaphore_wait(barrier, 1 + has_left.astype(jnp.int32) + has_right.astype(jnp.int32))

    firsts = []
    total = 0
    for ref in owns:
        firsts.append((total, total + ref.shape[0] // unit))
        total += ref.shape[0] // unit

    def each_source(k, act):
        for (begin, end), o, f, r in zip(firsts, owns, fars, outs):

            @pl.when((k >= begin) & (k < end))
            def _(begin=begin, o=o, f=f, r=r):
                act(pl.ds((k - begin) * unit, unit), o, f, r)

    def exchange(k, f, span):
        return pltpu.make_async_remote_copy(
            f.at[span], far.at[k], ysend.at[k], yrecv.at[k], device_id=other, device_id_type=MESH
        )

    def load(k, o, span):
        return pltpu.make_async_copy(o.at[span], own.at[k], own_sem.at[k])

    def store(k, r, span):
        return pltpu.make_async_copy(far.at[k], r.at[span], out_sem.at[k])

    def upward(k, src):
        return pltpu.make_async_remote_copy(
            src.at[k], up.at[k], usend.at[k], urecv.at[k], device_id=right, device_id_type=MESH
        )

    def downward(k, src):
        return pltpu.make_async_remote_copy(
            src.at[k], down.at[k], dsend.at[k], drecv.at[k], device_id=left, device_id_type=MESH
        )

    def begin_unit(k):
        def act(span, o, f, r):
            exchange(k, f, span).start()
            load(k, o, span).start()

        each_source(k, act)

    @pl.loop(0, ahead)
    def _(k):
        begin_unit(k)

    @pl.loop(0, units + contexts - 1)
    def _(k):
        @pl.when(k + ahead < units)
        def _():
            begin_unit(k + ahead)

        @pl.when(k < units)
        def _():
            exchange(k, fars[0], pl.ds(0, unit)).wait_recv()
            load(k, owns[0], pl.ds(0, unit)).wait()
            own[k] = (own[k].astype(F32) + far[k].astype(F32)).astype(BF)

            @pl.when(i == 0)
            def _():
                upward(k, own).start()

            @pl.when(i == contexts - 1)
            def _():
                downward(k, own).start()

        u = k - i

        @pl.when(has_left & (u >= 0) & (u < units))
        def _():
            upward(u, up).wait_recv()
            up[u] = (up[u].astype(F32) + own[u].astype(F32)).astype(BF)

            @pl.when(has_right)
            def _():
                upward(u, up).start()

        d = k - (contexts - 1 - i)

        @pl.when(has_right & (d >= 0) & (d < units))
        def _():
            downward(d, down).wait_recv()
            down[d] = (down[d].astype(F32) + own[d].astype(F32)).astype(BF)

            @pl.when(has_left)
            def _():
                downward(d, down).start()

        e = k - jnp.maximum(i, contexts - 1 - i)

        @pl.when((e >= 0) & (e < units))
        def _():
            @pl.when(i == 0)
            def _():
                far[e] = down[e]

            @pl.when(i == contexts - 1)
            def _():
                far[e] = up[e]

            @pl.when(has_left & has_right)
            def _():
                far[e] = (
                    up[e].astype(F32) + (down[e].astype(F32) - own[e].astype(F32))
                ).astype(BF)

            each_source(e, lambda span, o, f, r: store(e, r, span).start())

    @pl.loop(0, units)
    def _(k):
        exchange(k, fars[0], pl.ds(0, unit)).wait_send()
        store(k, outs[0], pl.ds(0, unit)).wait()

        @pl.when(has_right)
        def _():
            upward(k, up).wait_send()

        @pl.when(has_left)
        def _():
            downward(k, down).wait_send()


def reduce_gradients(contexts, owns, fars):
    count = len(owns)
    unit = UNIT
    slabs = sum(ref.shape[0] for ref in owns)
    units = slabs // unit
    buffer = pltpu.VMEM((units, unit) + owns[0].shape[1:], BF)

    def kernel(*refs):
        reduce_kernel(
            contexts, refs[:count], refs[count : 2 * count], refs[2 * count : 3 * count],
            *refs[3 * count :],
        )

    anywhere = pl.BlockSpec(memory_space=pl.ANY)
    return pl.pallas_call(
        kernel,
        out_shape=tuple(jax.ShapeDtypeStruct(ref.shape, BF) for ref in owns),
        in_specs=[anywhere] * (2 * count),
        out_specs=(anywhere,) * count,
        scratch_shapes=[buffer] * 4 + [pltpu.SemaphoreType.DMA((units,))] * 8,
        compiler_params=pltpu.CompilerParams(
            collective_id=1, has_side_effects=True, vmem_limit_bytes=VMEM_LIMIT
        ),
        cost_estimate=COST,
        name="reduce_gradients",
    )(*owns, *fars)


def unpack_kernel(slabs_ref, gate_ref, up_ref, down_ref):
    for a in range(2):
        gate_ref[a] = slabs_ref[a].astype(F32)
        up_ref[a] = slabs_ref[2 + a].astype(F32)
        down_ref[a] = slabs_ref[4 + a].astype(F32).T


def unpack(slabs):
    count, half, ff = slabs.shape
    steps = count // 6
    wide = jax.ShapeDtypeStruct((2 * steps, half, ff), F32)
    tall = jax.ShapeDtypeStruct((2 * steps, ff, half), F32)
    return pl.pallas_call(
        unpack_kernel,
        out_shape=(wide, wide, tall),
        grid=(steps,),
        in_specs=[pl.BlockSpec((6, half, ff), lambda i: (i, 0, 0))],
        out_specs=[pl.BlockSpec((2, half, ff), lambda i: (i, 0, 0))] * 2
        + [pl.BlockSpec((2, ff, half), lambda i: (i, 0, 0))],
        compiler_params=pltpu.CompilerParams(vmem_limit_bytes=VMEM_LIMIT),
        cost_estimate=COST,
        name="unpack",
    )(slabs)


def attention_weights_kernel(count, *refs):
    own_ref, far_ref = refs[2 * count :]
    half, ff = own_ref.shape[1], own_ref.shape[2]
    for part, out in ((0, own_ref), (1, far_ref)):
        at = 0
        for left, right in zip(refs[:count], refs[count : 2 * count]):
            rows = slice(part * half, (part + 1) * half)
            block = matmul(left[rows, :], right[...]).astype(BF)
            for c in range(block.shape[1] // ff):
                out[at] = block[:, c * ff : (c + 1) * ff]
                at += 1


def attention_weights(lefts, rights, ff):
    count = sum(right.shape[1] for right in rights) // ff
    slabs = jax.ShapeDtypeStruct((count, lefts[0].shape[0] // 2, ff), BF)
    return pl.pallas_call(
        functools.partial(attention_weights_kernel, len(lefts)),
        out_shape=(slabs, slabs),
        compiler_params=pltpu.CompilerParams(vmem_limit_bytes=VMEM_LIMIT),
        cost_estimate=COST,
        name="attention_weights",
    )(*lefts, *rights)


def unpack_attention_kernel(first_ref, second_ref, q_ref, out_ref, k_ref, v_ref):
    ff = first_ref.shape[2]
    count = q_ref.shape[1] // ff
    for c in range(count):
        q_ref[:, c * ff : (c + 1) * ff] = first_ref[c].astype(F32)
        out_ref[c * ff : (c + 1) * ff, :] = first_ref[count + c].astype(F32).T
    count = k_ref.shape[1] // ff
    for c in range(count):
        k_ref[:, c * ff : (c + 1) * ff] = second_ref[c].astype(F32)
        v_ref[:, c * ff : (c + 1) * ff] = second_ref[count + c].astype(F32)


def unpack_attention(first, second, query_cols, key_cols):
    rows = first.shape[1]
    return pl.pallas_call(
        unpack_attention_kernel,
        out_shape=tuple(
            jax.ShapeDtypeStruct(shape, F32)
            for shape in (
                (rows, query_cols), (query_cols, rows), (rows, key_cols), (rows, key_cols)
            )
        ),
        compiler_params=pltpu.CompilerParams(vmem_limit_bytes=VMEM_LIMIT),
        cost_estimate=COST,
        name="unpack_attention",
    )(first, second)


def inverse_norm(near, far):
    count = near.shape[1] + far.shape[1]
    squares = jnp.sum(near * near, axis=1, keepdims=True) + jnp.sum(far * far, axis=1, keepdims=True)
    return lax.rsqrt(squares / count + EPS)


def halves(ref, rows, shard):
    half = ref.shape[1] // 2
    own = pl.ds(pl.multiple_of(shard * half, 128), half)
    far = pl.ds(pl.multiple_of((1 - shard) * half, 128), half)
    return ref[rows, own].astype(F32), ref[rows, far].astype(F32)


def put_halves(ref, rows, shard, near, far):
    half = ref.shape[1] // 2
    ref[rows, pl.ds(pl.multiple_of(shard * half, 128), half)] = near.astype(ref.dtype)
    ref[rows, pl.ds(pl.multiple_of((1 - shard) * half, 128), half)] = far.astype(ref.dtype)


def qkv_backward_kernel(dq_ref, dkv_ref, wo_ref, wf_ref, dn_ref):
    half = wo_ref.shape[0]
    grads = jnp.concatenate([dq_ref[...], dkv_ref[...]], axis=1)
    dn_ref[:, :half] = contract_last(grads, wo_ref[...]).astype(BF)
    dn_ref[:, half:] = contract_last(grads, wf_ref[...]).astype(BF)


def qkv_backward(grad_q, grad_kv, w_own, w_far):
    tokens = grad_q.shape[0]
    tile = 256
    return pl.pallas_call(
        qkv_backward_kernel,
        out_shape=jax.ShapeDtypeStruct((tokens, 2 * w_own.shape[0]), BF),
        grid=(tokens // tile,),
        in_specs=[
            pl.BlockSpec((tile, grad_q.shape[1]), lambda i: (i, 0)),
            pl.BlockSpec((tile, grad_kv.shape[1]), lambda i: (i, 0)),
            pl.BlockSpec(w_own.shape, lambda i: (0, 0)),
            pl.BlockSpec(w_far.shape, lambda i: (0, 0)),
        ],
        out_specs=pl.BlockSpec((tile, 2 * w_own.shape[0]), lambda i: (i, 0)),
        compiler_params=pltpu.CompilerParams(vmem_limit_bytes=VMEM_LIMIT),
        cost_estimate=COST,
        name="qkv_backward",
    )(grad_q, grad_kv, w_own, w_far)


def leave_kernel(place, x_ref, dn_ref, dh_ref, gain_ref, out_ref, scale_ref):
    half = x_ref.shape[1] // 2
    near, far = halves(x_ref, slice(None), place[1])
    inverse = inverse_norm(near, far)
    grads = dn_ref[...].astype(F32)
    near_out, far_out, near_scale, far_scale = norm_backward(
        near, far, inverse, gain_ref[...], grads
    )
    put_halves(
        out_ref, slice(None), place[1], dh_ref[:, :half] + near_out, dh_ref[:, half:] + far_out
    )

    @pl.when(pl.program_id(0) == 0)
    def _():
        scale_ref[...] = jnp.zeros_like(scale_ref)

    scale_ref[:, :half] += near_scale
    scale_ref[:, half:] += far_scale


def leave(place, x, grad_normed, grad_hidden, gain):
    tokens, width = x.shape
    tile = 256
    block = pl.BlockSpec((tile, width), lambda i, s: (i, 0))
    row = pl.BlockSpec((1, width), lambda i, s: (0, 0))
    return pl.pallas_call(
        leave_kernel,
        out_shape=(
            jax.ShapeDtypeStruct((tokens, width), F32),
            jax.ShapeDtypeStruct((1, width), F32),
        ),
        grid_spec=pltpu.PrefetchScalarGridSpec(
            num_scalar_prefetch=1,
            grid=(tokens // tile,),
            in_specs=[block, block, block, row],
            out_specs=[block, row],
        ),
        compiler_params=pltpu.CompilerParams(vmem_limit_bytes=VMEM_LIMIT),
        cost_estimate=COST,
        name="leave",
    )(place, x, grad_normed, grad_hidden, gain)


def norm_backward(near, far, inverse, gain, grads):
    half = near.shape[1]
    near_scaled = grads[:, :half] * gain[:, :half]
    far_scaled = grads[:, half:] * gain[:, half:]
    along = (
        jnp.sum(near_scaled * near, axis=1, keepdims=True)
        + jnp.sum(far_scaled * far, axis=1, keepdims=True)
    ) / (2 * half)
    cube = inverse * inverse * inverse * along
    return (
        inverse * near_scaled - near * cube,
        inverse * far_scaled - far * cube,
        jnp.sum(grads[:, :half] * near * inverse, axis=0, keepdims=True),
        jnp.sum(grads[:, half:] * far * inverse, axis=0, keepdims=True),
    )


CHUNK = 128


def tensor_peers():
    t = lax.axis_index("tensor")
    low, high = lax.rem(t, 2), lax.rem(t // 2, 2)
    return low, {"tensor": t + 1 - 2 * low}, {"tensor": t + 2 - 4 * high}


def greet(peers):
    barrier = pltpu.get_barrier_semaphore()
    for peer in peers:
        pl.semaphore_signal(barrier, inc=1, device_id=peer, device_id_type=MESH)
    pl.semaphore_wait(barrier, len(peers))


def sum_over_tensor(part, total, arrived, mine, other, sems, consume, between=lambda c: None):
    send1, recv1, send2, recv2, send3, recv3 = sems
    low, near, far = tensor_peers()
    chunks = arrived.shape[0]
    half = chunks * CHUNK

    def rows(side, c):
        return pl.ds(pl.multiple_of(side * half + c * CHUNK, CHUNK), CHUNK)

    def give(c):
        return pltpu.make_async_remote_copy(
            part.at[rows(1 - low, c)], arrived.at[c], send1.at[c], recv1.at[c],
            device_id=near, device_id_type=MESH,
        )

    def swap(c):
        return pltpu.make_async_remote_copy(
            mine.at[c], other.at[c], send2.at[c], recv2.at[c], device_id=far, device_id_type=MESH
        )

    def back(c):
        return pltpu.make_async_remote_copy(
            total.at[rows(low, c)], total.at[rows(low, c)], send3.at[c], recv3.at[c],
            device_id=near, device_id_type=MESH,
        )

    @pl.loop(0, chunks)
    def _(c):
        give(c).start()

    @pl.loop(0, chunks)
    def _(c):
        give(c).wait_recv()
        mine[c] = (part[rows(low, c), :].astype(F32) + arrived[c].astype(F32)).astype(BF)
        swap(c).start()

    @pl.loop(0, chunks)
    def _(c):
        between(c)
        swap(c).wait_recv()
        total[rows(low, c), :] = (mine[c].astype(F32) + other[c].astype(F32)).astype(BF)
        back(c).start()
        consume(pl.multiple_of(low * half + c * CHUNK, CHUNK))
        back(c).wait_recv()
        consume(pl.multiple_of((1 - low) * half + c * CHUNK, CHUNK))

    @pl.loop(0, chunks)
    def _(c):
        give(c).wait_send()
        swap(c).wait_send()
        back(c).wait_send()


def sum_scratch(tokens, width):
    chunks = tokens // 2 // CHUNK
    piece = pltpu.VMEM((chunks, CHUNK, width), BF)
    return [pltpu.VMEM((tokens, width), BF)] + [piece] * 3 + [
        pltpu.SemaphoreType.DMA((chunks,))
    ] * 6


def front_kernel(
    contexts, trees, x_ref, seg_col, packed, gains, wqkv, wout, w_gate, w_up, w_down,
    packed_all, far_gains, far_qkv, far_out, far_gate, far_up, far_down,
    q_ref, kv_all, nt_ref, o_ref, lse_ref, h_ref, n2_ref, n2t_ref,
    normed, bias, tops, norms, sums, part, total, arrived, mine, other,
    ysend, yrecv, rsend, rrecv, psend, precv, ksend, krecv, *sems
):
    i = lax.axis_index("context")
    shard = lax.axis_index("shard")
    parity = lax.rem(i, 2)
    tokens, width = x_ref.shape
    half = width // 2
    rows = tokens // trees
    heads = q_ref.shape[1] // HEAD
    kv_width = kv_all.shape[2] // 2
    per_group = q_ref.shape[1] // kv_width
    other_shard = {"shard": 1 - shard}
    partner = {"context": i + 1 - 2 * parity}
    right = {"context": lax.rem(i + 1, contexts)}
    _, near, far = tensor_peers()
    greet(
        [other_shard, near, far]
        + [{"context": lax.rem(i + c, contexts)} for c in range(1, contexts)]
    )

    def half_span(ref, axis):
        size = ref.shape[axis] // 2
        return pl.ds(pl.multiple_of(parity * size, size), size)

    quarter = w_gate.shape[0] // 4
    moves = [
        (wqkv.at[half_span(wqkv, 0)], far_qkv.at[half_span(wqkv, 0)]),
        (wout.at[:, half_span(wout, 1)], far_out.at[:, half_span(wout, 1)]),
    ]
    for c in range(2):
        for source, target in ((w_gate, far_gate), (w_up, far_up), (w_down, far_down)):
            span = pl.ds((2 * parity + c) * quarter, quarter)
            moves.append((source.at[span], target.at[span]))

    def direct(m):
        source, target = moves[m]
        return pltpu.make_async_remote_copy(
            source, target, ysend.at[m], yrecv.at[m],
            device_id=other_shard, device_id_type=MESH,
        )

    def relay(m):
        _, target = moves[m]
        return pltpu.make_async_remote_copy(
            target, target, rsend.at[m], rrecv.at[m], device_id=partner, device_id_type=MESH
        )

    def pass_on(m):
        direct(m).wait_recv()
        relay(m).start()

    count = len(moves)
    gain_copy = pltpu.make_async_remote_copy(
        gains, far_gains, ysend.at[count], yrecv.at[count],
        device_id=other_shard, device_id_type=MESH,
    )

    def tell(c, slot):
        return pltpu.make_async_remote_copy(
            packed, packed_all.at[slot], psend.at[c], precv.at[slot],
            device_id={"context": c}, device_id_type=MESH,
        )

    def lift(j):
        return pltpu.make_async_remote_copy(
            kv_all.at[j], kv_all.at[j], ksend.at[j], krecv.at[j],
            device_id=right, device_id_type=MESH,
        )

    gain_copy.start()
    for m in range(count):
        direct(m).start()

    @pl.loop(0, contexts)
    def _(c):
        @pl.when(c != i)
        def _():
            tell(c, i).start()

    packed_all[i] = packed[...]
    gain_copy.wait_recv()
    tile = 128

    @pl.loop(0, tokens // tile)
    def _(index):
        span = pl.ds(pl.multiple_of(index * tile, tile), tile)
        own_x, far_x = halves(x_ref, span, shard)
        inverse = inverse_norm(own_x, far_x)
        own_x = (own_x * inverse * gains[0:1, :]).astype(BF)
        far_x = (far_x * inverse * far_gains[0:1, :]).astype(BF)
        normed[span, :half] = own_x
        normed[span, half:] = far_x
        nt_ref[:half, span] = own_x.T
        nt_ref[half:, span] = far_x.T

    pass_on(0)
    pass_on(1)
    relay(0).wait_recv()
    qkv = matmul(normed[:, :half], wqkv[...]) + matmul(normed[:, half:], far_qkv[...])
    q_ref[...] = qkv[:, : q_ref.shape[1]].astype(BF)
    kv_all[i] = qkv[:, q_ref.shape[1] :].astype(BF)

    @pl.when(i < contexts - 1)
    def _():
        lift(i).start()

    tops[...] = jnp.full_like(tops, -1e30)
    norms[...] = jnp.zeros_like(norms)
    sums[...] = jnp.zeros_like(sums)

    @pl.loop(0, contexts)
    def _(c):
        @pl.when(c != i)
        def _():
            tell(i, c).wait_recv()

    @pl.loop(0, contexts)
    def _(d):
        @pl.when(d <= i)
        def _():
            j = i - d

            @pl.when(d > 0)
            def _():
                lift(j).wait_recv()

                @pl.when(i < contexts - 1)
                def _():
                    lift(j).start()

            @pl.loop(0, trees)
            def _(tree):
                span = pl.ds(pl.multiple_of(tree * rows, rows), rows)
                key_pos = j * rows + lax.broadcasted_iota(jnp.int32, (rows, rows), 1)
                query_pos = i * rows + lax.broadcasted_iota(jnp.int32, (rows, rows), 0)
                last = packed_all[j, pl.ds(trees + tree, 1), :]
                allowed = (key_pos <= query_pos) & (seg_col[span, :] <= last)
                bias[...] = jnp.where(allowed, 0.0, -2e30)
                for head in range(heads):
                    group = head // per_group
                    cols = slice(head * HEAD, (head + 1) * HEAD)
                    keys = kv_all[j, span, group * HEAD : (group + 1) * HEAD]
                    values = kv_all[
                        j, span, kv_width + group * HEAD : kv_width + (group + 1) * HEAD
                    ]
                    scores = contract_last(q_ref[span, cols], keys) * 0.125 + bias[...]
                    old = tops[span, head : head + 1]
                    top = jnp.maximum(old, jnp.max(scores, axis=1, keepdims=True))
                    weights = jnp.exp(scores - top)
                    shrink = jnp.exp(old - top)
                    tops[span, head : head + 1] = top
                    norms[span, head : head + 1] = norms[span, head : head + 1] * shrink + jnp.sum(
                        weights, axis=1, keepdims=True
                    )
                    sums[span, cols] = sums[span, cols] * shrink + matmul(
                        weights.astype(BF), values
                    )

        @pl.when(d == 0)
        def _():
            pass_on(2)

        @pl.when(d == min(2, contexts - 1))
        def _():
            pass_on(3)

    for head in range(heads):
        cols = slice(head * HEAD, (head + 1) * HEAD)
        o_ref[:, cols] = (sums[:, cols] / norms[:, head : head + 1]).astype(BF)
    lse = tops[...] + jnp.log(norms[...] + jnp.where(norms[...] == 0.0, 1.0, 0.0))
    for tree in range(trees):
        lse_ref[tree] = lse[tree * rows : (tree + 1) * rows].T[: lse_ref.shape[1]]
    relay(1).wait_recv()
    part[:, :half] = matmul(o_ref[...], wout[...]).astype(BF)
    part[:, half:] = matmul(o_ref[...], far_out[...]).astype(BF)

    def consume(row):
        span = pl.ds(row, CHUNK)
        own_x, far_x = halves(x_ref, span, shard)
        own_x = own_x + total[span, :half].astype(F32)
        far_x = far_x + total[span, half:].astype(F32)
        h_ref[span, :half] = own_x
        h_ref[span, half:] = far_x
        inverse = inverse_norm(own_x, far_x)
        own_x = (own_x * inverse * gains[1:2, :]).astype(BF)
        far_x = (far_x * inverse * far_gains[1:2, :]).astype(BF)
        n2_ref[span, :half] = own_x
        n2_ref[span, half:] = far_x
        n2t_ref[:half, span] = own_x.T
        n2t_ref[half:, span] = far_x.T

    def between(c):
        for at in range(2):

            @pl.when(c == at)
            def _():
                pass_on(4 + at)

    sum_over_tensor(part, total, arrived, mine, other, sems, consume, between)
    for m in range(6, count):
        pass_on(m)
    for m in range(2, count):
        relay(m).wait_recv()
    for m in range(count):
        direct(m).wait_send()
        relay(m).wait_send()
    gain_copy.wait_send()

    @pl.loop(0, contexts)
    def _(c):
        @pl.when(c != i)
        def _():
            tell(c, i).wait_send()

        @pl.when((c <= i) & (i < contexts - 1))
        def _():
            lift(c).wait_send()


def front(contexts, trees, x, seg_col, packed, gains, w_qkv, w_out, w_gate, w_up, w_down, both):
    tokens, width = x.shape
    rows = tokens // trees
    cols = w_out.shape[0]
    anywhere = pl.BlockSpec(memory_space=pl.ANY)
    local_memory = pl.BlockSpec(memory_space=pltpu.VMEM)
    shape = jax.ShapeDtypeStruct
    like = [shape(ref.shape, ref.dtype) for ref in (gains, w_qkv, w_out, w_gate, w_up, w_down)]
    dma = pltpu.SemaphoreType.DMA
    return pl.pallas_call(
        functools.partial(front_kernel, contexts, trees),
        out_shape=(
            shape((contexts,) + packed.shape, jnp.int32),
            *like,
            shape((tokens, cols), BF),
            shape((contexts, tokens, both), BF),
            shape((width, tokens), BF),
            shape((tokens, cols), BF),
            shape((trees, 8, rows), F32),
            shape((tokens, width), F32),
            shape((tokens, width), BF),
            shape((width, tokens), BF),
        ),
        in_specs=[local_memory] * 6 + [anywhere] * 3,
        out_specs=(local_memory,) * 4 + (anywhere,) * 3 + (local_memory,) * 8,
        scratch_shapes=[
            pltpu.VMEM((tokens, width), BF),
            pltpu.VMEM((rows, rows), F32),
            pltpu.VMEM((tokens, 128), F32),
            pltpu.VMEM((tokens, 128), F32),
            pltpu.VMEM((tokens, cols), F32),
            pltpu.VMEM((tokens, width), BF),
        ]
        + sum_scratch(tokens, width)[:4]
        + [dma((9,)), dma((9,)), dma((8,)), dma((8,))]
        + [dma((contexts,))] * 4
        + sum_scratch(tokens, width)[4:],
        compiler_params=pltpu.CompilerParams(
            collective_id=2, has_side_effects=True, vmem_limit_bytes=VMEM_LIMIT
        ),
        cost_estimate=COST,
        name="front",
    )(x, seg_col, packed, gains, w_qkv, w_out, w_gate, w_up, w_down)


def after_experts_kernel(
    part, h_ref, teacher_ref, mask_ref, factor_ref,
    y_ref, gy_ref, low_ref, lowt_ref, square_ref, total, arrived, mine, other, *sems
):
    half = h_ref.shape[1] // 2
    shard = lax.axis_index("shard")
    square_ref[...] = jnp.zeros_like(square_ref)

    def consume(row):
        rows = pl.ds(row, CHUNK)
        mask = mask_ref[rows, :]
        factor = factor_ref[...] * mask
        near_t, far_t = halves(teacher_ref, rows, shard)
        near = h_ref[rows, :half] + total[rows, :half].astype(F32)
        far = h_ref[rows, half:] + total[rows, half:].astype(F32)
        put_halves(y_ref, rows, shard, near, far)
        for begin, error in ((0, near - near_t), (half, far - far_t)):
            span = slice(begin, begin + half)
            squares = mask * jnp.sum(error * error, axis=1, keepdims=True)
            square_ref[...] += jnp.sum(squares, axis=0, keepdims=True)
            grad = factor * error
            gy_ref[rows, span] = grad
            low = grad.astype(BF)
            low_ref[rows, span] = low
            lowt_ref[span, rows] = low.T

    greet(tensor_peers()[1:])
    sum_over_tensor(part, total, arrived, mine, other, sems, consume)


def after_experts(part, hidden, teacher, mask, factor):
    tokens, width = hidden.shape
    return pl.pallas_call(
        after_experts_kernel,
        out_shape=(
            jax.ShapeDtypeStruct((tokens, width), BF),
            jax.ShapeDtypeStruct((tokens, width), F32),
            jax.ShapeDtypeStruct((tokens, width), BF),
            jax.ShapeDtypeStruct((width, tokens), BF),
            jax.ShapeDtypeStruct((1, 1), F32),
        ),
        scratch_shapes=sum_scratch(tokens, width),
        compiler_params=pltpu.CompilerParams(
            collective_id=3, has_side_effects=True, vmem_limit_bytes=VMEM_LIMIT
        ),
        cost_estimate=COST,
        name="after_experts",
    )(part, hidden, teacher, mask, factor)


def after_backward_kernel(
    part, h_ref, gy_ref, gain_ref, wo_ref, wf_ref,
    dh_ref, dat_ref, do_ref, scale_ref, total, arrived, mine, other, *sems
):
    half = h_ref.shape[1] // 2
    scale_ref[...] = jnp.zeros_like(scale_ref)

    def consume(row):
        rows = pl.ds(row, CHUNK)
        near, far = h_ref[rows, :half], h_ref[rows, half:]
        inverse = inverse_norm(near, far)
        near_out, far_out, near_scale, far_scale = norm_backward(
            near, far, inverse, gain_ref[...], total[rows, :].astype(F32)
        )
        scale_ref[:, :half] += near_scale
        scale_ref[:, half:] += far_scale
        near = gy_ref[rows, :half] + near_out
        far = gy_ref[rows, half:] + far_out
        dh_ref[rows, :half] = near
        dh_ref[rows, half:] = far
        near = near.astype(BF)
        far = far.astype(BF)
        dat_ref[:half, rows] = near.T
        dat_ref[half:, rows] = far.T
        do_ref[rows, :] = (
            contract_last(near, wo_ref[...]) + contract_last(far, wf_ref[...])
        ).astype(BF)

    greet(tensor_peers()[1:])
    sum_over_tensor(part, total, arrived, mine, other, sems, consume)


def after_backward(part, hidden, grad_y, gain, out_own, out_far):
    tokens, width = hidden.shape
    return pl.pallas_call(
        after_backward_kernel,
        out_shape=(
            jax.ShapeDtypeStruct((tokens, width), F32),
            jax.ShapeDtypeStruct((width, tokens), BF),
            jax.ShapeDtypeStruct((tokens, out_own.shape[0]), BF),
            jax.ShapeDtypeStruct((1, width), F32),
        ),
        scratch_shapes=sum_scratch(tokens, width),
        compiler_params=pltpu.CompilerParams(
            collective_id=4, has_side_effects=True, vmem_limit_bytes=VMEM_LIMIT
        ),
        cost_estimate=COST,
        name="after_backward",
    )(part, hidden, grad_y, gain, out_own, out_far)


def local(
    states, segments, routes, gates, valid, teacher, attn_gain, w_query, key_matrix, value_matrix,
    w_out, moe_gain, w_gate, w_up, w_down,
):
    shard = lax.axis_index("shard")
    context = lax.axis_index("context")
    shards = lax.axis_size("shard")
    contexts = lax.axis_size("context")
    trees, rows, width = states.shape
    tokens = trees * rows
    half = width // 2
    experts, _, ff = w_gate.shape
    swap = [(a, shards - 1 - a) for a in range(shards)]
    place = jnp.stack([context, shard]).astype(jnp.int32)

    def over_shard(value):
        return lax.ppermute(value, "shard", swap)

    def tied(*values):
        return lax.optimization_barrier(values)

    last = jnp.where(
        segments == 0, 1 << 20, jnp.where(segments % 3 == 1, segments + 2, segments)
    )
    count = jnp.sum(valid.astype(jnp.int32))
    packed = jnp.concatenate([segments, last, jnp.broadcast_to(count, (trees, rows))])
    packed = jnp.pad(packed, ((0, -packed.shape[0] % 8), (0, 0)))
    gains_own = jnp.pad(jnp.stack([attn_gain, moe_gain]), ((0, 6), (0, 0)))
    qkv_own = jnp.concatenate([w_query, key_matrix, value_matrix], axis=1)
    query_cols = w_query.shape[1]
    both = qkv_own.shape[1] - query_cols
    x = states.reshape(tokens, width)
    (
        packed_all, gains_far, qkv_far, out_far, gate_far, up_far, down_far,
        q, kv, normed_t, attended, lse, hidden, normed_two, normed_two_t,
    ) = front(
        contexts, trees, x, segments.reshape(tokens, 1), packed, gains_own, qkv_own, w_out,
        w_gate, w_up, w_down, both,
    )
    gains = jnp.concatenate([gains_own, gains_far], axis=1)
    attn_scale, moe_scale = gains[0:1], gains[1:2]
    valid_total = jnp.sum(packed_all[:, 2 * trees, 0]).reshape(1, 1).astype(F32)
    valid_total = valid_total + over_shard(valid_total)
    last_all = packed_all[:, trees : 2 * trees].transpose(1, 0, 2).reshape(-1, 1)
    gate_ws, up_ws, down_ws = (w_gate, gate_far), (w_up, up_far), (w_down, down_far)

    expert_ids = jnp.arange(experts, dtype=jnp.int32)
    combine = jnp.sum(
        gates.reshape(tokens, -1)[..., None]
        * (routes.reshape(tokens, -1)[..., None] == expert_ids).astype(F32),
        axis=1,
    )
    pre, middle, moe_part = experts_forward(normed_two, combine, gate_ws, up_ws, down_ws)
    token_total = tokens * shards * contexts
    result, grad_y, grad_y_low, grad_y_t, square = after_experts(
        moe_part,
        hidden,
        teacher.reshape(tokens, width),
        valid.reshape(tokens, 1).astype(F32),
        token_total / valid_total,
    )
    expert_grads, dn_part = experts_backward(
        grad_y_low, combine, gate_ws, up_ws, down_ws, pre
    )

    grad_hidden, grad_branch_t, grad_attended, grad_moe_scale = after_backward(
        dn_part, hidden, grad_y, moe_scale, w_out, out_far
    )
    grad_q, grad_kv_all = attention_backward(
        place, q, grad_attended, attended, lse, kv, last_all, segments.reshape(trees, 1, rows)
    )
    grad_kv = lax.psum_scatter(grad_kv_all, "context", scatter_dimension=0, tiled=True)
    grad_q, expert_grads = tied(grad_q, expert_grads)
    own_experts, far_experts = expert_weights(normed_two_t, grad_y_t, expert_grads, middle)
    own_first, far_first = attention_weights(
        (normed_t, grad_branch_t), (grad_q, attended), ff
    )
    grad_kv, own_experts, far_experts, own_first, far_first = tied(
        grad_kv, own_experts, far_experts, own_first, far_first
    )
    grad_kv = grad_kv.reshape(tokens, both)
    dn1_part = qkv_backward(grad_q, grad_kv, qkv_own, qkv_far)
    grad_normed = lax.psum(dn1_part, "tensor")
    own_second, far_second = attention_weights((normed_t,), (grad_kv,), ff)
    sum_experts, sum_first, sum_second = reduce_gradients(
        contexts,
        (own_experts, own_first, own_second),
        (far_experts, far_first, far_second),
    )
    grad_normed, sum_second = tied(grad_normed, sum_second)
    grad_inputs, grad_attn_scale = leave(place, x, grad_normed, grad_hidden, attn_scale)

    grad_scales = jnp.concatenate([grad_attn_scale, grad_moe_scale])
    tail = jnp.concatenate([grad_scales[:, :half], jnp.broadcast_to(square, (1, half))])
    tail_far = jnp.concatenate([grad_scales[:, half:], jnp.broadcast_to(square, (1, half))])
    tail = tail + over_shard(tail_far)
    key_cols = key_matrix.shape[1]
    final_query, final_out, final_key, final_value = unpack_attention(
        sum_first, sum_second, query_cols, key_cols
    )
    tail, sum_experts, final_query = tied(tail, sum_experts, final_query)
    final_gate, final_up, final_down = unpack(sum_experts)
    hop = 1
    while hop < contexts:
        tail = tail + lax.ppermute(tail, "context", [(a, a ^ hop) for a in range(contexts)])
        if hop == 1:
            tail, final_gate = tied(tail, final_gate)
        hop *= 2
    return (
        tail[2, 0] / (valid_total[0, 0] * width),
        result.reshape(trees, rows, width),
        grad_inputs.reshape(trees, rows, width),
        tail[0],
        final_query,
        final_key,
        final_value,
        final_out,
        tail[1],
        final_gate,
        final_up,
        final_down,
    )


def solution(mesh):
    return jax.shard_map(
        local,
        mesh=mesh,
        in_specs=(
            P("shard", "context", None),
            P("shard", "context"),
            P("shard", "context", None),
            P("shard", "context", None),
            P("shard", "context"),
            P("shard", "context", None),
            P("shard"),
            P("shard", "tensor"),
            P("shard", "tensor"),
            P("shard", "tensor"),
            P("tensor", "shard"),
            P("shard"),
            P(None, "shard", "tensor"),
            P(None, "shard", "tensor"),
            P(None, "tensor", "shard"),
        ),
        out_specs=(
            P(),
            P("shard", "context", None),
            P("shard", "context", None),
            P("shard"),
            P("shard", "tensor"),
            P("shard", "tensor"),
            P("shard", "tensor"),
            P("tensor", "shard"),
            P("shard"),
            P(None, "shard", "tensor"),
            P(None, "shard", "tensor"),
            P(None, "tensor", "shard"),
        ),
        check_vma=False,
    )
```

```python
import functools
import math

import jax
import jax.numpy as jnp
from jax import lax
from jax.experimental import pallas as pl
from jax.experimental.pallas import tpu as pltpu
from jax.sharding import PartitionSpec as P

HEAD = 64
EPS = 1e-05
BF = jnp.bfloat16
F32 = jnp.float32
MESH = pl.DeviceIdType.MESH
VMEM_LIMIT = 56 * 1024 * 1024
UNIT = 2
COST = pl.CostEstimate(flops=1, bytes_accessed=1, transcendentals=0)


def matmul(left, right):
    return jnp.dot(left, right, preferred_element_type=F32)


def contract_first(left, right):
    return lax.dot_general(left, right, (((0,), (0,)), ((), ())), preferred_element_type=F32)


def contract_last(left, right):
    return lax.dot_general(left, right, (((1,), (1,)), ((), ())), preferred_element_type=F32)


def stage_weights(gates, ups, downs, wide, tall):
    half, ff = gates[0].shape[1], gates[0].shape[2]
    for part in range(2):
        for a in range(2):
            features = slice(part * half, (part + 1) * half)
            wide[features, 2 * a * ff : (2 * a + 1) * ff] = gates[part][a]
            wide[features, (2 * a + 1) * ff : (2 * a + 2) * ff] = ups[part][a]
            tall[a * ff : (a + 1) * ff, features] = downs[part][a]


def column(block, index):
    lane = lax.broadcasted_iota(jnp.int32, block.shape, 1)
    return jnp.sum(jnp.where(lane == index, block, 0.0), axis=1, keepdims=True)


def experts_forward_kernel(
    n_ref, c_ref, g0, g1, u0, u1, d0, d1, pre_ref, cm_ref, m_ref, wide, tall, acc
):
    step = pl.program_id(0)
    ff = g0.shape[2]
    stage_weights((g0, g1), (u0, u1), (d0, d1), wide, tall)

    @pl.when(step == 0)
    def _():
        acc[...] = jnp.zeros_like(acc)

    hidden = matmul(n_ref[...], wide[...])
    pre_ref[0] = hidden.astype(BF)
    pieces = []
    for a in range(2):
        gate = hidden[:, 2 * a * ff : (2 * a + 1) * ff]
        up = hidden[:, (2 * a + 1) * ff : (2 * a + 2) * ff]
        weight = column(c_ref[...], 2 * step + a)
        pieces.append((weight * (gate * jax.nn.sigmoid(gate) * up)).astype(BF))
    middle = jnp.concatenate(pieces, axis=1)
    cm_ref[0] = middle
    acc[...] += matmul(middle, tall[...])

    @pl.when(step == pl.num_programs(0) - 1)
    def _():
        m_ref[...] = acc[...].astype(BF)


def expert_specs(half, ff):
    return [
        pl.BlockSpec(shape, lambda i: (i, 0, 0))
        for shape in ((2, half, ff),) * 4 + ((2, ff, half),) * 2
    ]


def experts_forward(normed, combine, gates, ups, downs):
    tokens, width = normed.shape
    experts, half, ff = gates[0].shape
    steps = experts // 2
    whole = pl.BlockSpec((tokens, width), lambda i: (0, 0))
    return pl.pallas_call(
        experts_forward_kernel,
        out_shape=(
            jax.ShapeDtypeStruct((steps, tokens, 4 * ff), BF),
            jax.ShapeDtypeStruct((steps, tokens, 2 * ff), BF),
            jax.ShapeDtypeStruct((tokens, width), BF),
        ),
        grid=(steps,),
        in_specs=[whole, pl.BlockSpec((tokens, experts), lambda i: (0, 0))]
        + expert_specs(half, ff),
        out_specs=[
            pl.BlockSpec((1, tokens, 4 * ff), lambda i: (i, 0, 0)),
            pl.BlockSpec((1, tokens, 2 * ff), lambda i: (i, 0, 0)),
            whole,
        ],
        scratch_shapes=[
            pltpu.VMEM((width, 4 * ff), BF),
            pltpu.VMEM((2 * ff, width), BF),
            pltpu.VMEM((tokens, width), F32),
        ],
        compiler_params=pltpu.CompilerParams(vmem_limit_bytes=VMEM_LIMIT),
        cost_estimate=COST,
        name="experts_forward",
    )(normed, combine, *gates, *ups, *downs)


def experts_backward_kernel(
    gy_ref, c_ref, g0, g1, u0, u1, d0, d1, pre_ref, grads_ref, dn_ref, wide, tall, acc
):
    step = pl.program_id(0)
    ff = g0.shape[2]
    stage_weights((g0, g1), (u0, u1), (d0, d1), wide, tall)

    @pl.when(step == 0)
    def _():
        acc[...] = jnp.zeros_like(acc)

    grad_middle = contract_last(gy_ref[...], tall[...])
    for a in range(2):
        gate = pre_ref[0, :, 2 * a * ff : (2 * a + 1) * ff].astype(F32)
        up = pre_ref[0, :, (2 * a + 1) * ff : (2 * a + 2) * ff].astype(F32)
        weight = column(c_ref[...], 2 * step + a)
        gm = weight * grad_middle[:, a * ff : (a + 1) * ff]
        sig = jax.nn.sigmoid(gate)
        grads_ref[0, :, 2 * a * ff : (2 * a + 1) * ff] = (
            gm * up * (sig + gate * sig * (1.0 - sig))
        ).astype(BF)
        grads_ref[0, :, (2 * a + 1) * ff : (2 * a + 2) * ff] = (gm * gate * sig).astype(BF)
    acc[...] += contract_last(grads_ref[0], wide[...])

    @pl.when(step == pl.num_programs(0) - 1)
    def _():
        dn_ref[...] = acc[...].astype(BF)


def experts_backward(grad_y, combine, gates, ups, downs, pre):
    tokens, width = grad_y.shape
    experts, half, ff = gates[0].shape
    steps = experts // 2
    whole = pl.BlockSpec((tokens, width), lambda i: (0, 0))
    by_pair = pl.BlockSpec((1, tokens, 4 * ff), lambda i: (i, 0, 0))
    return pl.pallas_call(
        experts_backward_kernel,
        out_shape=(
            jax.ShapeDtypeStruct((steps, tokens, 4 * ff), BF),
            jax.ShapeDtypeStruct((tokens, width), BF),
        ),
        grid=(steps,),
        in_specs=[whole, pl.BlockSpec((tokens, experts), lambda i: (0, 0))]
        + expert_specs(half, ff)
        + [by_pair],
        out_specs=[by_pair, whole],
        scratch_shapes=[
            pltpu.VMEM((width, 4 * ff), BF),
            pltpu.VMEM((2 * ff, width), BF),
            pltpu.VMEM((tokens, width), F32),
        ],
        compiler_params=pltpu.CompilerParams(vmem_limit_bytes=VMEM_LIMIT),
        cost_estimate=COST,
        name="experts_backward",
    )(grad_y, combine, *gates, *ups, *downs, pre)


def unpack_kernel(slabs_ref, gate_ref, up_ref, down_ref):
    for a in range(2):
        gate_ref[a] = slabs_ref[a].astype(F32)
        up_ref[a] = slabs_ref[2 + a].astype(F32)
        down_ref[a] = slabs_ref[4 + a].astype(F32).T


def unpack(slabs, steps):
    _, half, ff = slabs.shape
    wide = jax.ShapeDtypeStruct((2 * steps, half, ff), F32)
    tall = jax.ShapeDtypeStruct((2 * steps, ff, half), F32)
    return pl.pallas_call(
        unpack_kernel,
        out_shape=(wide, wide, tall),
        grid=(steps,),
        in_specs=[pl.BlockSpec((6, half, ff), lambda i: (i, 0, 0))],
        out_specs=[pl.BlockSpec((2, half, ff), lambda i: (i, 0, 0))] * 2
        + [pl.BlockSpec((2, ff, half), lambda i: (i, 0, 0))],
        compiler_params=pltpu.CompilerParams(vmem_limit_bytes=VMEM_LIMIT),
        cost_estimate=COST,
        name="unpack",
    )(slabs)


def unpack_attention_kernel(slabs_ref, q_ref, out_ref, k_ref, v_ref):
    ff = slabs_ref.shape[2]
    at = 0
    for ref, turn in ((q_ref, False), (out_ref, True), (k_ref, False), (v_ref, False)):
        for c in range(ref.shape[0 if turn else 1] // ff):
            value = slabs_ref[at].astype(F32)
            if turn:
                ref[c * ff : (c + 1) * ff, :] = value.T
            else:
                ref[:, c * ff : (c + 1) * ff] = value
            at += 1


def unpack_attention(slabs, query_cols, key_cols):
    total, rows, ff = slabs.shape
    count = 2 * (query_cols + key_cols) // ff
    shapes = ((rows, query_cols), (query_cols, rows), (rows, key_cols), (rows, key_cols))
    return pl.pallas_call(
        unpack_attention_kernel,
        out_shape=tuple(jax.ShapeDtypeStruct(shape, F32) for shape in shapes),
        grid=(1,),
        in_specs=[pl.BlockSpec((count, rows, ff), lambda i: (total // count - 1, 0, 0))],
        out_specs=[pl.BlockSpec(shape, lambda i: (0, 0)) for shape in shapes],
        compiler_params=pltpu.CompilerParams(vmem_limit_bytes=VMEM_LIMIT),
        cost_estimate=COST,
        name="unpack_attention",
    )(slabs)


def inverse_norm(near, far):
    count = near.shape[1] + far.shape[1]
    squares = jnp.sum(near * near, axis=1, keepdims=True) + jnp.sum(far * far, axis=1, keepdims=True)
    return lax.rsqrt(squares / count + EPS)


def halves(ref, rows, shard):
    half = ref.shape[1] // 2
    own = pl.ds(pl.multiple_of(shard * half, 128), half)
    far = pl.ds(pl.multiple_of((1 - shard) * half, 128), half)
    return ref[rows, own].astype(F32), ref[rows, far].astype(F32)


def put_halves(ref, rows, shard, near, far):
    half = ref.shape[1] // 2
    ref[rows, pl.ds(pl.multiple_of(shard * half, 128), half)] = near.astype(ref.dtype)
    ref[rows, pl.ds(pl.multiple_of((1 - shard) * half, 128), half)] = far.astype(ref.dtype)


def norm_backward(near, far, inverse, gain, grads):
    half = near.shape[1]
    near_scaled = grads[:, :half] * gain[:, :half]
    far_scaled = grads[:, half:] * gain[:, half:]
    along = (
        jnp.sum(near_scaled * near, axis=1, keepdims=True)
        + jnp.sum(far_scaled * far, axis=1, keepdims=True)
    ) / (2 * half)
    cube = inverse * inverse * inverse * along
    return (
        inverse * near_scaled - near * cube,
        inverse * far_scaled - far * cube,
        jnp.sum(grads[:, :half] * near * inverse, axis=0, keepdims=True),
        jnp.sum(grads[:, half:] * far * inverse, axis=0, keepdims=True),
    )


CHUNK = 128


def tensor_peers():
    t = lax.axis_index("tensor")
    low, high = lax.rem(t, 2), lax.rem(t // 2, 2)
    return low, {"tensor": t + 1 - 2 * low}, {"tensor": t + 2 - 4 * high}


def greet(peers):
    barrier = pltpu.get_barrier_semaphore()
    for peer in peers:
        pl.semaphore_signal(barrier, inc=1, device_id=peer, device_id_type=MESH)
    pl.semaphore_wait(barrier, len(peers))


def sum_over_tensor(part, total, arrived, mine, other, sems, consume, between=lambda c: None):
    send1, recv1, send2, recv2, send3, recv3 = sems
    low, near, far = tensor_peers()
    chunks = arrived.shape[0]
    half = chunks * CHUNK

    def rows(side, c):
        return pl.ds(pl.multiple_of(side * half + c * CHUNK, CHUNK), CHUNK)

    def give(c):
        return pltpu.make_async_remote_copy(
            part.at[rows(1 - low, c)], arrived.at[c], send1.at[c], recv1.at[c],
            device_id=near, device_id_type=MESH,
        )

    def swap(c):
        return pltpu.make_async_remote_copy(
            mine.at[c], other.at[c], send2.at[c], recv2.at[c], device_id=far, device_id_type=MESH
        )

    def back(c):
        return pltpu.make_async_remote_copy(
            total.at[rows(low, c)], total.at[rows(low, c)], send3.at[c], recv3.at[c],
            device_id=near, device_id_type=MESH,
        )

    @pl.loop(0, chunks)
    def _(c):
        give(c).start()

    @pl.loop(0, chunks)
    def _(c):
        give(c).wait_recv()
        mine[c] = (part[rows(low, c), :].astype(F32) + arrived[c].astype(F32)).astype(BF)
        swap(c).start()

    @pl.loop(0, chunks)
    def _(c):
        between(c)
        swap(c).wait_recv()
        total[rows(low, c), :] = (mine[c].astype(F32) + other[c].astype(F32)).astype(BF)
        back(c).start()
        consume(pl.multiple_of(low * half + c * CHUNK, CHUNK))
        back(c).wait_recv()
        consume(pl.multiple_of((1 - low) * half + c * CHUNK, CHUNK))

    @pl.loop(0, chunks)
    def _(c):
        give(c).wait_send()
        swap(c).wait_send()
        back(c).wait_send()


def sum_scratch(tokens, width):
    chunks = tokens // 2 // CHUNK
    piece = pltpu.VMEM((chunks, CHUNK, width), BF)
    return [pltpu.VMEM((tokens, width), BF)] + [piece] * 3 + [
        pltpu.SemaphoreType.DMA((chunks,))
    ] * 6


def front_kernel(
    contexts, trees, x_ref, seg_col, packed, gains, wqkv, wout, w_gate, w_up, w_down,
    packed_all, far_gains, far_qkv, far_out, far_gate, far_up, far_down,
    q_ref, kv_all, nt_ref, o_ref, lse_ref, h_ref, n2_ref, n2t_ref,
    normed, bias, tops, norms, sums, part, total, arrived, mine, other,
    ysend, yrecv, rsend, rrecv, psend, precv, ksend, krecv, *sems
):
    i = lax.axis_index("context")
    shard = lax.axis_index("shard")
    parity = lax.rem(i, 2)
    tokens, width = x_ref.shape
    half = width // 2
    rows = tokens // trees
    heads = q_ref.shape[1] // HEAD
    kv_width = kv_all.shape[2] // 2
    per_group = q_ref.shape[1] // kv_width
    other_shard = {"shard": 1 - shard}
    partner = {"context": i + 1 - 2 * parity}
    right = {"context": lax.rem(i + 1, contexts)}
    _, near, far = tensor_peers()
    greet(
        [other_shard, near, far]
        + [{"context": lax.rem(i + c, contexts)} for c in range(1, contexts)]
    )

    def half_span(ref, axis):
        size = ref.shape[axis] // 2
        return pl.ds(pl.multiple_of(parity * size, size), size)

    quarter = w_gate.shape[0] // 4
    moves = [
        (wqkv.at[half_span(wqkv, 0)], far_qkv.at[half_span(wqkv, 0)]),
        (wout.at[:, half_span(wout, 1)], far_out.at[:, half_span(wout, 1)]),
    ]
    for c in range(2):
        for source, target in ((w_gate, far_gate), (w_up, far_up), (w_down, far_down)):
            span = pl.ds((2 * parity + c) * quarter, quarter)
            moves.append((source.at[span], target.at[span]))

    def direct(m):
        source, target = moves[m]
        return pltpu.make_async_remote_copy(
            source, target, ysend.at[m], yrecv.at[m],
            device_id=other_shard, device_id_type=MESH,
        )

    def relay(m):
        _, target = moves[m]
        return pltpu.make_async_remote_copy(
            target, target, rsend.at[m], rrecv.at[m], device_id=partner, device_id_type=MESH
        )

    def pass_on(m):
        direct(m).wait_recv()
        relay(m).start()

    count = len(moves)
    gain_copy = pltpu.make_async_remote_copy(
        gains, far_gains, ysend.at[count], yrecv.at[count],
        device_id=other_shard, device_id_type=MESH,
    )

    def tell(c, slot):
        return pltpu.make_async_remote_copy(
            packed, packed_all.at[slot], psend.at[c], precv.at[slot],
            device_id={"context": c}, device_id_type=MESH,
        )

    def lift(j):
        return pltpu.make_async_remote_copy(
            kv_all.at[j], kv_all.at[j], ksend.at[j], krecv.at[j],
            device_id=right, device_id_type=MESH,
        )

    gain_copy.start()
    for m in range(count):
        direct(m).start()

    @pl.loop(0, contexts)
    def _(c):
        @pl.when(c != i)
        def _():
            tell(c, i).start()

    packed_all[i] = packed[...]
    gain_copy.wait_recv()
    tile = 128

    @pl.loop(0, tokens // tile)
    def _(index):
        span = pl.ds(pl.multiple_of(index * tile, tile), tile)
        own_x, far_x = halves(x_ref, span, shard)
        inverse = inverse_norm(own_x, far_x)
        own_x = (own_x * inverse * gains[0:1, :]).astype(BF)
        far_x = (far_x * inverse * far_gains[0:1, :]).astype(BF)
        normed[span, :half] = own_x
        normed[span, half:] = far_x
        nt_ref[:half, span] = own_x.T
        nt_ref[half:, span] = far_x.T

    pass_on(0)
    pass_on(1)
    relay(0).wait_recv()
    qkv = matmul(normed[:, :half], wqkv[...]) + matmul(normed[:, half:], far_qkv[...])
    q_ref[...] = qkv[:, : q_ref.shape[1]].astype(BF)
    kv_all[i] = qkv[:, q_ref.shape[1] :].astype(BF)

    @pl.when(i < contexts - 1)
    def _():
        lift(i).start()

    tops[...] = jnp.full_like(tops, -1e30)
    norms[...] = jnp.zeros_like(norms)
    sums[...] = jnp.zeros_like(sums)

    @pl.loop(0, contexts)
    def _(c):
        @pl.when(c != i)
        def _():
            tell(i, c).wait_recv()

    @pl.loop(0, contexts)
    def _(d):
        @pl.when(d <= i)
        def _():
            j = i - d

            @pl.when(d > 0)
            def _():
                lift(j).wait_recv()

                @pl.when(i < contexts - 1)
                def _():
                    lift(j).start()

            @pl.loop(0, trees)
            def _(tree):
                span = pl.ds(pl.multiple_of(tree * rows, rows), rows)
                key_pos = j * rows + lax.broadcasted_iota(jnp.int32, (rows, rows), 1)
                query_pos = i * rows + lax.broadcasted_iota(jnp.int32, (rows, rows), 0)
                last = packed_all[j, pl.ds(trees + tree, 1), :]
                allowed = (key_pos <= query_pos) & (seg_col[span, :] <= last)
                bias[...] = jnp.where(allowed, 0.0, -2e30)
                for head in range(heads):
                    group = head // per_group
                    cols = slice(head * HEAD, (head + 1) * HEAD)
                    keys = kv_all[j, span, group * HEAD : (group + 1) * HEAD]
                    values = kv_all[
                        j, span, kv_width + group * HEAD : kv_width + (group + 1) * HEAD
                    ]
                    scores = contract_last(q_ref[span, cols], keys) * 0.125 + bias[...]
                    old = tops[span, head : head + 1]
                    top = jnp.maximum(old, jnp.max(scores, axis=1, keepdims=True))
                    weights = jnp.exp(scores - top)
                    shrink = jnp.exp(old - top)
                    tops[span, head : head + 1] = top
                    norms[span, head : head + 1] = norms[span, head : head + 1] * shrink + jnp.sum(
                        weights, axis=1, keepdims=True
                    )
                    sums[span, cols] = sums[span, cols] * shrink + matmul(
                        weights.astype(BF), values
                    )

        @pl.when(d == 0)
        def _():
            pass_on(2)

        @pl.when(d == min(2, contexts - 1))
        def _():
            pass_on(3)

    for head in range(heads):
        cols = slice(head * HEAD, (head + 1) * HEAD)
        o_ref[:, cols] = (sums[:, cols] / norms[:, head : head + 1]).astype(BF)
    lse = tops[...] + jnp.log(norms[...] + jnp.where(norms[...] == 0.0, 1.0, 0.0))
    for tree in range(trees):
        lse_ref[tree] = lse[tree * rows : (tree + 1) * rows].T[: lse_ref.shape[1]]
    relay(1).wait_recv()
    part[:, :half] = matmul(o_ref[...], wout[...]).astype(BF)
    part[:, half:] = matmul(o_ref[...], far_out[...]).astype(BF)

    def consume(row):
        span = pl.ds(row, CHUNK)
        own_x, far_x = halves(x_ref, span, shard)
        own_x = own_x + total[span, :half].astype(F32)
        far_x = far_x + total[span, half:].astype(F32)
        h_ref[span, :half] = own_x
        h_ref[span, half:] = far_x
        inverse = inverse_norm(own_x, far_x)
        own_x = (own_x * inverse * gains[1:2, :]).astype(BF)
        far_x = (far_x * inverse * far_gains[1:2, :]).astype(BF)
        n2_ref[span, :half] = own_x
        n2_ref[span, half:] = far_x
        n2t_ref[:half, span] = own_x.T
        n2t_ref[half:, span] = far_x.T

    def between(c):
        for at in range(2):

            @pl.when(c == at)
            def _():
                pass_on(4 + at)

    sum_over_tensor(part, total, arrived, mine, other, sems, consume, between)
    for m in range(6, count):
        pass_on(m)
    for m in range(2, count):
        relay(m).wait_recv()
    for m in range(count):
        direct(m).wait_send()
        relay(m).wait_send()
    gain_copy.wait_send()

    @pl.loop(0, contexts)
    def _(c):
        @pl.when(c != i)
        def _():
            tell(c, i).wait_send()

        @pl.when((c <= i) & (i < contexts - 1))
        def _():
            lift(c).wait_send()


def front(contexts, trees, x, seg_col, packed, gains, w_qkv, w_out, w_gate, w_up, w_down, both):
    tokens, width = x.shape
    rows = tokens // trees
    cols = w_out.shape[0]
    anywhere = pl.BlockSpec(memory_space=pl.ANY)
    local_memory = pl.BlockSpec(memory_space=pltpu.VMEM)
    shape = jax.ShapeDtypeStruct
    like = [shape(ref.shape, ref.dtype) for ref in (gains, w_qkv, w_out, w_gate, w_up, w_down)]
    dma = pltpu.SemaphoreType.DMA
    return pl.pallas_call(
        functools.partial(front_kernel, contexts, trees),
        out_shape=(
            shape((contexts,) + packed.shape, jnp.int32),
            *like,
            shape((tokens, cols), BF),
            shape((contexts, tokens, both), BF),
            shape((width, tokens), BF),
            shape((tokens, cols), BF),
            shape((trees, 8, rows), F32),
            shape((tokens, width), F32),
            shape((tokens, width), BF),
            shape((width, tokens), BF),
        ),
        in_specs=[local_memory] * 6 + [anywhere] * 3,
        out_specs=(local_memory,) * 4 + (anywhere,) * 3 + (local_memory,) * 8,
        scratch_shapes=[
            pltpu.VMEM((tokens, width), BF),
            pltpu.VMEM((rows, rows), F32),
            pltpu.VMEM((tokens, 128), F32),
            pltpu.VMEM((tokens, 128), F32),
            pltpu.VMEM((tokens, cols), F32),
            pltpu.VMEM((tokens, width), BF),
        ]
        + sum_scratch(tokens, width)[:4]
        + [dma((9,)), dma((9,)), dma((8,)), dma((8,))]
        + [dma((contexts,))] * 4
        + sum_scratch(tokens, width)[4:],
        compiler_params=pltpu.CompilerParams(
            collective_id=2, has_side_effects=True, vmem_limit_bytes=VMEM_LIMIT
        ),
        cost_estimate=COST,
        name="front",
    )(x, seg_col, packed, gains, w_qkv, w_out, w_gate, w_up, w_down)


def after_experts_kernel(
    part, h_ref, teacher_ref, mask_ref, factor_ref,
    y_ref, low_ref, lowt_ref, square_ref, total, arrived, mine, other, *sems
):
    half = h_ref.shape[1] // 2
    shard = lax.axis_index("shard")
    square_ref[...] = jnp.zeros_like(square_ref)

    def consume(row):
        rows = pl.ds(row, CHUNK)
        mask = mask_ref[rows, :]
        factor = factor_ref[...] * mask
        near_t, far_t = halves(teacher_ref, rows, shard)
        near = h_ref[rows, :half] + total[rows, :half].astype(F32)
        far = h_ref[rows, half:] + total[rows, half:].astype(F32)
        put_halves(y_ref, rows, shard, near, far)
        for begin, error in ((0, near - near_t), (half, far - far_t)):
            span = slice(begin, begin + half)
            squares = mask * jnp.sum(error * error, axis=1, keepdims=True)
            square_ref[...] += jnp.sum(squares, axis=0, keepdims=True)
            low = (factor * error).astype(BF)
            low_ref[rows, span] = low
            lowt_ref[span, rows] = low.T

    greet(tensor_peers()[1:])
    sum_over_tensor(part, total, arrived, mine, other, sems, consume)


def after_experts(part, hidden, teacher, mask, factor):
    tokens, width = hidden.shape
    return pl.pallas_call(
        after_experts_kernel,
        out_shape=(
            jax.ShapeDtypeStruct((tokens, width), BF),
            jax.ShapeDtypeStruct((tokens, width), BF),
            jax.ShapeDtypeStruct((width, tokens), BF),
            jax.ShapeDtypeStruct((1, 1), F32),
        ),
        scratch_shapes=sum_scratch(tokens, width),
        compiler_params=pltpu.CompilerParams(
            collective_id=3, has_side_effects=True, vmem_limit_bytes=VMEM_LIMIT
        ),
        cost_estimate=COST,
        name="after_experts",
    )(part, hidden, teacher, mask, factor)


def back_kernel(
    contexts, trees, lag, gains, wqkv, far_qkv, wout, far_out, q_ref, o_ref, lse_ref, packed_all,
    part, h_hbm, gy_hbm, x_hbm, nt_hbm, n2t_hbm, gyt_hbm, grads_hbm, cm_hbm, kv_hbm,
    result, out_hbm, scale_ref, own_hbm, far_hbm, came, up_hbm, down_hbm, part2, dkv_part, dkv_came,
    sums_ring, up_ring, down_ring, came_buf, out_buf, turned, gyt, grads_buf, cm_buf, stage,
    hbuf, chunk_low, chunk_out, my_part, total, arrived, mine, other, other2,
    dat, do_ref, dq_ref, dqs, deltas, bias, kv_buf, dkv_buf, dkv_sum, dkv_add, tile_buf,
    local_sem, ring_sem, ysend, yrecv, usend, urecv, dsend, drecv, store_sem, gsend, grecv, *ar_sems
):
    i = lax.axis_index("context")
    shard = lax.axis_index("shard")
    tokens, width = hbuf.shape
    half = width // 2
    rows = tokens // trees
    units = result.shape[0] // UNIT
    slots = lag * (contexts - 1) + 2
    ff = result.shape[2]
    pairs = grads_hbm.shape[0]
    heads = q_ref.shape[1] // HEAD
    kv_width = kv_buf.shape[1] // 2
    per_group = q_ref.shape[1] // kv_width
    low, near, far = tensor_peers()
    has_left, has_right = i > 0, i < contexts - 1
    right = {"context": lax.rem(i + 1, contexts)}
    left = {"context": lax.rem(i + contexts - 1, contexts)}
    other_shard = {"shard": 1 - shard}
    greet(
        [other_shard, near, far]
        + [{"context": lax.rem(i + c, contexts)} for c in range(1, contexts)]
    )

    def remote(src, dst, send, recv, to):
        return pltpu.make_async_remote_copy(
            src, dst, send, recv, device_id=to, device_id_type=MESH
        )

    def fetch(*moves):
        copies = [
            pltpu.make_async_copy(src, dst, local_sem.at[at]) for at, (src, dst) in enumerate(moves)
        ]
        for copy in copies:
            copy.start()
        for copy in copies:
            copy.wait()


    def slabs(k):
        return pl.ds(k * UNIT, UNIT)

    def exchange(k):
        return remote(
            far_hbm.at[slabs(k)], came.at[slabs(k)], ysend.at[k], yrecv.at[k], other_shard
        )

    def upward(k, ring):
        return remote(
            ring.at[lax.rem(k, slots)], up_hbm.at[slabs(k)], usend.at[k], urecv.at[k], right
        )

    def downward(k, ring):
        return remote(
            ring.at[lax.rem(k, slots)], down_hbm.at[slabs(k)], dsend.at[k], drecv.at[k], left
        )

    def store(k):
        return pltpu.make_async_copy(
            out_buf.at[lax.rem(k, 2)], result.at[slabs(k)], store_sem.at[lax.rem(k, 2)]
        )

    def add_unit(k):
        u, d = k - lag * i, k - lag * (contexts - 1 - i)
        slot, up_slot, down_slot = (lax.rem(jnp.maximum(at, 0), slots) for at in (k, u, d))
        has_new = k < units
        has_up = has_left & (u >= 0) & (u < units)
        has_down = has_right & (d >= 0) & (d < units)

        def load(at, src, dst):
            return pltpu.make_async_copy(src, dst, ring_sem.at[at])

        def new_loads():
            return (
                load(0, own_hbm.at[slabs(k)], sums_ring.at[slot]),
                load(1, came.at[slabs(k)], came_buf),
            )

        def up_load():
            return load(2, up_hbm.at[slabs(u)], up_ring.at[up_slot])

        def down_load():
            return load(3, down_hbm.at[slabs(d)], down_ring.at[down_slot])

        @pl.when(has_new)
        def _():
            @pl.when((k >= slots) & (i == 0))
            def _():
                upward(k - slots, sums_ring).wait_send()

            @pl.when((k >= slots) & (i == contexts - 1))
            def _():
                downward(k - slots, sums_ring).wait_send()

            exchange(k).wait_recv()
            for copy in new_loads():
                copy.start()

        @pl.when(has_up)
        def _():
            @pl.when(has_right & (u >= slots))
            def _():
                upward(u - slots, up_ring).wait_send()

            upward(u, up_ring).wait_recv()
            up_load().start()

        @pl.when(has_down)
        def _():
            @pl.when(has_left & (d >= slots))
            def _():
                downward(d - slots, down_ring).wait_send()

            downward(d, down_ring).wait_recv()
            down_load().start()

        @pl.when(has_new)
        def _():
            for copy in new_loads():
                copy.wait()
            sums_ring[slot] = (sums_ring[slot].astype(F32) + came_buf[...].astype(F32)).astype(BF)

            @pl.when(i == 0)
            def _():
                upward(k, sums_ring).start()

            @pl.when(i == contexts - 1)
            def _():
                downward(k, sums_ring).start()

        @pl.when(has_up)
        def _():
            up_load().wait()
            up_ring[up_slot] = (
                up_ring[up_slot].astype(F32) + sums_ring[up_slot].astype(F32)
            ).astype(BF)

            @pl.when(has_right)
            def _():
                upward(u, up_ring).start()

        @pl.when(has_down)
        def _():
            down_load().wait()
            down_ring[down_slot] = (
                down_ring[down_slot].astype(F32) + sums_ring[down_slot].astype(F32)
            ).astype(BF)

            @pl.when(has_left)
            def _():
                downward(d, down_ring).start()

        e = k - lag * jnp.maximum(i, contexts - 1 - i)

        @pl.when((e >= 0) & (e < units))
        def _():
            out_slot = lax.rem(e, slots)
            here = lax.rem(e, 2)

            @pl.when(e >= 2)
            def _():
                store(e - 2).wait()

            @pl.when(i == 0)
            def _():
                out_buf[here] = down_ring[out_slot]

            @pl.when(i == contexts - 1)
            def _():
                out_buf[here] = up_ring[out_slot]

            @pl.when(has_left & has_right)
            def _():
                out_buf[here] = (
                    up_ring[out_slot].astype(F32)
                    + (down_ring[out_slot].astype(F32) - sums_ring[out_slot].astype(F32))
                ).astype(BF)

            store(e).start()


    def write_slabs(first, number, products):
        for part_index, target in ((0, own_hbm), (1, far_hbm)):
            at = 0
            for left_ref, right_value, order in products:
                block = matmul(
                    left_ref[part_index * half : (part_index + 1) * half, :], right_value
                ).astype(BF)
                for c, place in enumerate(order):
                    stage[part_index, at + place] = block[:, c * ff : (c + 1) * ff]
                at += len(order)
        fetch(
            *(
                (stage.at[p, pl.ds(0, number)], target.at[pl.ds(first, number)])
                for p, target in ((0, own_hbm), (1, far_hbm))
            )
        )
        for c in range(number // UNIT):
            exchange(first // UNIT + c).start()

    def pair_slabs(p):
        fetch((grads_hbm.at[p], grads_buf), (cm_hbm.at[p], cm_buf))
        write_slabs(
            p * 6, 6, ((turned, grads_buf[...], (0, 2, 1, 3)), (gyt, cm_buf[...], (0, 1)))
        )


    chunks = arrived.shape[0]
    low_half = tokens // 2

    def chunk_rows(side, c):
        return pl.ds(pl.multiple_of(side * low_half + c * CHUNK, CHUNK), CHUNK)

    def summing(source, landing, sems):
        send1, recv1, send2, recv2, send3, recv3 = sems

        def give(c):
            return remote(
                source.at[chunk_rows(1 - low, c)], arrived.at[c], send1.at[c], recv1.at[c], near
            )

        def swap(c):
            return remote(mine.at[c], landing.at[c], send2.at[c], recv2.at[c], far)

        def back(c):
            span = chunk_rows(low, c)
            return remote(total.at[span], total.at[span], send3.at[c], recv3.at[c], near)

        def start():
            for c in range(chunks):
                give(c).start()

        def middle():
            fetch(*((source.at[chunk_rows(low, c)], my_part.at[c]) for c in range(chunks)))
            for c in range(chunks):
                give(c).wait_recv()
                mine[c] = (my_part[c].astype(F32) + arrived[c].astype(F32)).astype(BF)
                swap(c).start()

        def finish(c, consume):
            swap(c).wait_recv()
            total[chunk_rows(low, c), :] = (
                mine[c].astype(F32) + landing[c].astype(F32)
            ).astype(BF)
            back(c).start()
            consume(pl.multiple_of(low * low_half + c * CHUNK, CHUNK))

        def finish_other(c, consume):
            back(c).wait_recv()
            consume(pl.multiple_of((1 - low) * low_half + c * CHUNK, CHUNK))

        def drain():
            for c in range(chunks):
                give(c).wait_send()
                swap(c).wait_send()
                back(c).wait_send()

        return start, middle, finish, finish_other, drain

    start1, middle1, finish1, other1, drain1 = summing(part, other, ar_sems[:6])
    start2, middle2, finish2, finish_other2, drain2 = summing(part2, other2, ar_sems[6:])

    def through_second_norm(row):
        span = pl.ds(row, CHUNK)
        fetch((gy_hbm.at[span], chunk_low), (h_hbm.at[span], hbuf.at[span]))
        own_h, far_h = hbuf[span, :half], hbuf[span, half:]
        inverse = inverse_norm(own_h, far_h)
        own_d, far_d, own_scale, far_scale = norm_backward(
            own_h, far_h, inverse, gains[1:2, :], total[span, :].astype(F32)
        )
        scale_ref[1:2, :half] += own_scale
        scale_ref[1:2, half:] += far_scale
        own_d = chunk_low[:, :half].astype(F32) + own_d
        far_d = chunk_low[:, half:].astype(F32) + far_d
        hbuf[span, :half] = own_d
        hbuf[span, half:] = far_d
        own_d = own_d.astype(BF)
        far_d = far_d.astype(BF)
        dat[:half, span] = own_d.T
        dat[half:, span] = far_d.T
        do_ref[span, :] = (
            contract_last(own_d, wout[...]) + contract_last(far_d, far_out[...])
        ).astype(BF)

    def through_first_norm(row):
        span = pl.ds(row, CHUNK)
        fetch((x_hbm.at[span], chunk_low))
        own_x, far_x = halves(chunk_low, slice(None), shard)
        inverse = inverse_norm(own_x, far_x)
        own_d, far_d, own_scale, far_scale = norm_backward(
            own_x, far_x, inverse, gains[0:1, :], total[span, :].astype(F32)
        )
        scale_ref[0:1, :half] += own_scale
        scale_ref[0:1, half:] += far_scale
        put_halves(
            chunk_out, slice(None), shard, hbuf[span, :half] + own_d, hbuf[span, half:] + far_d
        )
        fetch((chunk_out, out_hbm.at[span]))


    def make_deltas():
        @pl.loop(0, trees)
        def _(tree):
            span = pl.ds(pl.multiple_of(tree * rows, rows), rows)
            for head in range(heads):
                cols = slice(head * HEAD, (head + 1) * HEAD)
                product = do_ref[span, cols].astype(F32) * o_ref[span, cols].astype(F32)
                deltas[tree, head] = lax.dot_general(
                    jnp.ones((8, HEAD), F32),
                    product,
                    (((1,), (1,)), ((), ())),
                    precision=lax.Precision.HIGHEST,
                    preferred_element_type=F32,
                )

    def hand(j, tree):
        span = pl.ds(pl.multiple_of(tree * rows, rows), rows)
        return remote(
            dkv_part.at[j, span], dkv_came.at[i, span], gsend.at[j, tree], grecv.at[i, tree],
            {"context": j},
        )

    def taken(c, tree):
        span = pl.ds(pl.multiple_of(tree * rows, rows), rows)
        return remote(
            dkv_part.at[c, span], dkv_came.at[c, span], gsend.at[c, tree], grecv.at[c, tree],
            {"context": c},
        )

    def attention_block(number):
        tree, j = number // contexts, lax.rem(number, contexts)

        @pl.when((number < trees * contexts) & (j <= i))
        def _():
            span = pl.ds(pl.multiple_of(tree * rows, rows), rows)
            fetch((kv_hbm.at[j, span], kv_buf))
            key_pos = j * rows + lax.broadcasted_iota(jnp.int32, (rows, rows), 0)
            query_pos = i * rows + lax.broadcasted_iota(jnp.int32, (rows, rows), 1)
            last = column(packed_all[j].astype(F32).T, trees + tree)
            segment = packed_all[i, pl.ds(tree, 1), :].astype(F32)
            allowed = (key_pos <= query_pos) & (segment <= last)
            bias[...] = jnp.where(allowed, 0.0, -2e30)
            for group in range(heads // per_group):
                keys = kv_buf[:, group * HEAD : (group + 1) * HEAD]
                values = kv_buf[:, kv_width + group * HEAD : kv_width + (group + 1) * HEAD]
                dk = jnp.zeros((rows, HEAD), F32)
                dv = jnp.zeros((rows, HEAD), F32)
                for head in range(group * per_group, (group + 1) * per_group):
                    cols = slice(head * HEAD, (head + 1) * HEAD)
                    queries = q_ref[span, cols]
                    grads = do_ref[span, cols]
                    scores = contract_last(keys, queries) * 0.125 + bias[...]
                    probs = jnp.exp(scores - lse_ref[tree, head : head + 1, :])
                    grad_probs = contract_last(values, grads)
                    grad_scores = (probs * (grad_probs - deltas[tree, head, 0:1, :])).astype(BF)
                    dv = dv + matmul(probs.astype(BF), grads)
                    dk = dk + matmul(grad_scores, queries)
                    dqs[span, cols] += contract_first(grad_scores, keys)
                dkv_buf[:, group * HEAD : (group + 1) * HEAD] = (dk * 0.125).astype(BF)
                dkv_buf[:, kv_width + group * HEAD : kv_width + (group + 1) * HEAD] = dv.astype(BF)

            @pl.when(j == i)
            def _():
                dkv_sum[span, :] = dkv_buf[...].astype(F32)

            @pl.when(j < i)
            def _():
                fetch((dkv_buf, dkv_part.at[j, span]))
                hand(j, tree).start()

    def query_slabs():
        dq_ref[...] = (dqs[...] * 0.125).astype(BF)
        thirds = tuple(range(dq_ref.shape[1] // ff))
        write_slabs(
            pairs * 6, 2 * len(thirds), ((turned, dq_ref[...], thirds), (dat, o_ref[...], thirds))
        )

    def key_value_sum():
        @pl.loop(0, contexts)
        def _(c):
            @pl.when(c > i)
            def _():
                @pl.loop(0, trees)
                def _(tree):
                    taken(c, tree).wait_recv()
                    span = pl.ds(pl.multiple_of(tree * rows, rows), rows)
                    fetch((dkv_came.at[c, span], dkv_add))
                    dkv_sum[span, :] += dkv_add[...].astype(F32)

        grad_kv = dkv_sum[...].astype(BF)
        pieces = tuple(range(grad_kv.shape[1] // ff))
        first = pairs * 6 + 2 * (dq_ref.shape[1] // ff)
        write_slabs(first, len(pieces), ((turned, grad_kv, pieces),))

    def first_norm_parts():
        @pl.loop(0, tokens // CHUNK)
        def _(c):
            span = pl.ds(pl.multiple_of(c * CHUNK, CHUNK), CHUNK)
            grads = jnp.concatenate([dq_ref[span, :], dkv_sum[span, :].astype(BF)], axis=1)
            tile_buf[:, :half] = contract_last(grads, wqkv[...]).astype(BF)
            tile_buf[:, half:] = contract_last(grads, far_qkv[...]).astype(BF)
            fetch((tile_buf, part2.at[span]))

        start2()


    start1()
    fetch((n2t_hbm, turned), (gyt_hbm, gyt))
    scale_ref[...] = jnp.zeros_like(scale_ref)
    dqs[...] = jnp.zeros_like(dqs)
    pair_slabs(0)
    middle1()

    chain = []
    for finish, finish_other, consume in (
        (finish1, other1, through_second_norm), (finish2, finish_other2, through_first_norm),
    ):
        steps = [[functools.partial(finish, 0, consume)]]
        for c in range(chunks):
            steps.append([functools.partial(finish_other, c, consume)])
            if c + 1 < chunks:
                steps[-1].append(functools.partial(finish, c + 1, consume))
        chain.append(steps)
    chain[0][-1].append(make_deltas)
    tasks = {}
    for p in range(1, pairs):
        tasks[3 * p - 3] = [functools.partial(pair_slabs, p)]
    last_pair = 3 * pairs - 6
    at = 0

    def put(acts):
        nonlocal at
        at += 1
        while at in tasks:
            at += 1
        tasks[at] = acts

    for acts in chain[0]:
        put(acts)
    per_step = -(-trees * contexts // 8)

    def attention_step(number):
        @pl.loop(0, per_step)
        def _(step):
            attention_block(number * per_step + step)

    attention_steps = {}
    for number in range(8):
        at += 1
        while at in tasks:
            at += 1
        attention_steps[at] = number
    first_at, last_at = min(attention_steps), max(attention_steps)
    at = max(at, last_pair)
    put([lambda: fetch((nt_hbm, turned)), query_slabs])
    at = max(at, last_at + 3)
    put([key_value_sum])
    put([first_norm_parts])
    put([drain1, middle2])
    for acts in chain[1]:
        put(acts)

    @pl.loop(0, units + lag * (contexts - 1))
    def _(k):
        add_unit(k)
        for when, acts in sorted(tasks.items()):

            @pl.when(k == when)
            def _(acts=acts):
                for act in acts:
                    act()

        number, due = jnp.int32(0), k < 0
        for when, index in attention_steps.items():
            number = jnp.where(k == when, index, number)
            due = due | (k == when)

        @pl.when(due)
        def _():
            attention_step(number)

    drain2()
    for k in (units - 2, units - 1):
        store(k).wait()

    @pl.loop(0, units)
    def _(k):
        exchange(k).wait_send()

        @pl.when((k >= units - slots) & has_right)
        def _():
            upward(k, up_ring).wait_send()

        @pl.when((k >= units - slots) & has_left)
        def _():
            downward(k, down_ring).wait_send()

    @pl.loop(0, contexts)
    def _(c):
        @pl.when(c < i)
        def _():
            @pl.loop(0, trees)
            def _(tree):
                hand(c, tree).wait_send()


def back(
    contexts, trees, gains, w_qkv, far_qkv, w_out, far_out, q, o, lse, packed_all,
    part, hidden, grad_y, x, normed_t, normed_two_t, grad_y_t, grads, middle, kv,
):
    tokens, width = hidden.shape
    half, rows = width // 2, tokens // trees
    pairs, _, four = grads.shape
    ff, cols, both = four // 4, q.shape[1], kv.shape[2]
    count = pairs * 6 + (2 * cols + both) // ff
    units = count // UNIT
    lag = 2 if contexts <= 4 else 1
    slots = lag * (contexts - 1) + 2
    chunks = tokens // 2 // CHUNK
    shape, vmem, dma = jax.ShapeDtypeStruct, pltpu.VMEM, pltpu.SemaphoreType.DMA
    slabs = shape((count, half, ff), BF)
    unit = (UNIT, half, ff)
    piece = vmem((chunks, CHUNK, width), BF)
    anywhere = pl.BlockSpec(memory_space=pl.ANY)
    near_memory = pl.BlockSpec(memory_space=pltpu.VMEM)
    outs = pl.pallas_call(
        functools.partial(back_kernel, contexts, trees, lag),
        out_shape=(
            slabs,
            shape((tokens, width), F32),
            shape((8, width), F32),
            *(slabs,) * 5,
            shape((tokens, width), BF),
            shape(kv.shape, BF),
            shape(kv.shape, BF),
        ),
        in_specs=[near_memory] * 9 + [anywhere] * 10,
        out_specs=(anywhere,) * 2 + (near_memory,) + (anywhere,) * 8,
        scratch_shapes=[
            vmem((slots,) + unit, BF),
            vmem((slots,) + unit, BF),
            vmem((slots,) + unit, BF),
            vmem(unit, BF),
            vmem((2,) + unit, BF),
            vmem((width, tokens), BF),
            vmem((width, tokens), BF),
            vmem((tokens, 4 * ff), BF),
            vmem((tokens, 2 * ff), BF),
            vmem((2, 6, half, ff), BF),
            vmem((tokens, width), F32),
            vmem((CHUNK, width), BF),
            vmem((CHUNK, width), F32),
            piece,
            vmem((tokens, width), BF),
            piece,
            piece,
            piece,
            piece,
            vmem((width, tokens), BF),
            vmem((tokens, cols), BF),
            vmem((tokens, cols), BF),
            vmem((tokens, cols), F32),
            vmem((trees, cols // HEAD, 8, rows), F32),
            vmem((rows, rows), F32),
            vmem((rows, both), BF),
            vmem((rows, both), BF),
            vmem((tokens, both), F32),
            vmem((rows, both), BF),
            vmem((CHUNK, width), BF),
            dma((4,)),
            dma((4,)),
        ]
        + [dma((units,))] * 6
        + [dma((2,)), dma((contexts, trees)), dma((contexts, trees))]
        + [dma((chunks,))] * 12,
        compiler_params=pltpu.CompilerParams(
            collective_id=1, has_side_effects=True, vmem_limit_bytes=60 * 1024 * 1024
        ),
        cost_estimate=COST,
        name="back",
    )(
        gains, w_qkv, far_qkv, w_out, far_out, q, o, lse, packed_all,
        part, hidden, grad_y, x, normed_t, normed_two_t, grad_y_t, grads, middle, kv,
    )
    return outs[:3]


def local(
    states, segments, routes, gates, valid, teacher, attn_gain, w_query, key_matrix, value_matrix,
    w_out, moe_gain, w_gate, w_up, w_down,
):
    shard = lax.axis_index("shard")
    context = lax.axis_index("context")
    shards = lax.axis_size("shard")
    contexts = lax.axis_size("context")
    trees, rows, width = states.shape
    tokens = trees * rows
    half = width // 2
    experts, _, ff = w_gate.shape
    swap = [(a, shards - 1 - a) for a in range(shards)]

    def over_shard(value):
        return lax.ppermute(value, "shard", swap)

    def tied(*values):
        return lax.optimization_barrier(values)

    last = jnp.where(
        segments == 0, 1 << 20, jnp.where(segments % 3 == 1, segments + 2, segments)
    )
    count = jnp.sum(valid.astype(jnp.int32))
    packed = jnp.concatenate([segments, last, jnp.broadcast_to(count, (trees, rows))])
    packed = jnp.pad(packed, ((0, -packed.shape[0] % 8), (0, 0)))
    gains_own = jnp.pad(jnp.stack([attn_gain, moe_gain]), ((0, 6), (0, 0)))
    qkv_own = jnp.concatenate([w_query, key_matrix, value_matrix], axis=1)
    query_cols = w_query.shape[1]
    both = qkv_own.shape[1] - query_cols
    x = states.reshape(tokens, width)
    (
        packed_all, gains_far, qkv_far, out_far, gate_far, up_far, down_far,
        q, kv, normed_t, attended, lse, hidden, normed_two, normed_two_t,
    ) = front(
        contexts, trees, x, segments.reshape(tokens, 1), packed, gains_own, qkv_own, w_out,
        w_gate, w_up, w_down, both,
    )
    gains = jnp.concatenate([gains_own, gains_far], axis=1)
    valid_total = jnp.sum(packed_all[:, 2 * trees, 0]).reshape(1, 1).astype(F32)
    valid_total = valid_total + over_shard(valid_total)
    gate_ws, up_ws, down_ws = (w_gate, gate_far), (w_up, up_far), (w_down, down_far)

    expert_ids = jnp.arange(experts, dtype=jnp.int32)
    combine = jnp.sum(
        gates.reshape(tokens, -1)[..., None]
        * (routes.reshape(tokens, -1)[..., None] == expert_ids).astype(F32),
        axis=1,
    )
    pre, middle, moe_part = experts_forward(normed_two, combine, gate_ws, up_ws, down_ws)
    token_total = tokens * shards * contexts
    result, grad_y, grad_y_t, square = after_experts(
        moe_part,
        hidden,
        teacher.reshape(tokens, width),
        valid.reshape(tokens, 1).astype(F32),
        token_total / valid_total,
    )
    expert_grads, dn_part = experts_backward(grad_y, combine, gate_ws, up_ws, down_ws, pre)
    sums, grad_inputs, grad_scales = back(
        contexts, trees, gains, qkv_own, qkv_far, w_out, out_far, q, attended, lse, packed_all,
        dn_part, hidden, grad_y, x, normed_t, normed_two_t, grad_y_t, expert_grads, middle, kv,
    )

    grad_scales = grad_scales[:2]
    tail = jnp.concatenate([grad_scales[:, :half], jnp.broadcast_to(square, (1, half))])
    tail_far = jnp.concatenate([grad_scales[:, half:], jnp.broadcast_to(square, (1, half))])
    tail = tail + over_shard(tail_far)
    key_cols = key_matrix.shape[1]
    final_query, final_out, final_key, final_value = unpack_attention(sums, query_cols, key_cols)
    tail, sums, final_query = tied(tail, sums, final_query)
    final_gate, final_up, final_down = unpack(sums, experts // 2)
    hop = 1
    while hop < contexts:
        tail = tail + lax.ppermute(tail, "context", [(a, a ^ hop) for a in range(contexts)])
        if hop == 1:
            tail, final_gate = tied(tail, final_gate)
        hop *= 2
    return (
        tail[2, 0] / (valid_total[0, 0] * width),
        result.reshape(trees, rows, width),
        grad_inputs.reshape(trees, rows, width),
        tail[0],
        final_query,
        final_key,
        final_value,
        final_out,
        tail[1],
        final_gate,
        final_up,
        final_down,
    )


def solution(mesh):
    return jax.shard_map(
        local,
        mesh=mesh,
        in_specs=(
            P("shard", "context", None),
            P("shard", "context"),
            P("shard", "context", None),
            P("shard", "context", None),
            P("shard", "context"),
            P("shard", "context", None),
            P("shard"),
            P("shard", "tensor"),
            P("shard", "tensor"),
            P("shard", "tensor"),
            P("tensor", "shard"),
            P("shard"),
            P(None, "shard", "tensor"),
            P(None, "shard", "tensor"),
            P(None, "tensor", "shard"),
        ),
        out_specs=(
            P(),
            P("shard", "context", None),
            P("shard", "context", None),
            P("shard"),
            P("shard", "tensor"),
            P("shard", "tensor"),
            P("shard", "tensor"),
            P("tensor", "shard"),
            P("shard"),
            P(None, "shard", "tensor"),
            P(None, "shard", "tensor"),
            P(None, "tensor", "shard"),
        ),
        check_vma=False,
    )
```

```python
import functools
import math

import jax
import jax.numpy as jnp
from jax import lax
from jax.experimental import pallas as pl
from jax.experimental.pallas import tpu as pltpu
from jax.sharding import PartitionSpec as P

HEAD = 64
EPS = 1e-05
BF = jnp.bfloat16
F32 = jnp.float32
MESH = pl.DeviceIdType.MESH
VMEM_LIMIT = 56 * 1024 * 1024
UNIT = 2
COST = pl.CostEstimate(flops=1, bytes_accessed=1, transcendentals=0)


def matmul(left, right):
    return jnp.dot(left, right, preferred_element_type=F32)


def contract_first(left, right):
    return lax.dot_general(left, right, (((0,), (0,)), ((), ())), preferred_element_type=F32)


def contract_last(left, right):
    return lax.dot_general(left, right, (((1,), (1,)), ((), ())), preferred_element_type=F32)


def stage_weights(gates, ups, downs, wide, tall):
    half, ff = gates[0].shape[1], gates[0].shape[2]
    for part in range(2):
        for a in range(2):
            features = slice(part * half, (part + 1) * half)
            wide[features, 2 * a * ff : (2 * a + 1) * ff] = gates[part][a]
            wide[features, (2 * a + 1) * ff : (2 * a + 2) * ff] = ups[part][a]
            tall[a * ff : (a + 1) * ff, features] = downs[part][a]


def column(block, index):
    lane = lax.broadcasted_iota(jnp.int32, block.shape, 1)
    return jnp.sum(jnp.where(lane == index, block, 0.0), axis=1, keepdims=True)


def experts_forward_kernel(
    n_ref, c_ref, g0, g1, u0, u1, d0, d1, pre_ref, cm_ref, m_ref, wide, tall, acc
):
    step = pl.program_id(0)
    ff = g0.shape[2]
    stage_weights((g0, g1), (u0, u1), (d0, d1), wide, tall)

    @pl.when(step == 0)
    def _():
        acc[...] = jnp.zeros_like(acc)

    hidden = matmul(n_ref[...], wide[...])
    pre_ref[0] = hidden.astype(BF)
    pieces = []
    for a in range(2):
        gate = hidden[:, 2 * a * ff : (2 * a + 1) * ff]
        up = hidden[:, (2 * a + 1) * ff : (2 * a + 2) * ff]
        weight = column(c_ref[...], 2 * step + a)
        pieces.append((weight * (gate * jax.nn.sigmoid(gate) * up)).astype(BF))
    middle = jnp.concatenate(pieces, axis=1)
    cm_ref[0] = middle
    acc[...] += matmul(middle, tall[...])

    @pl.when(step == pl.num_programs(0) - 1)
    def _():
        m_ref[...] = acc[...].astype(BF)


def expert_specs(half, ff):
    return [
        pl.BlockSpec(shape, lambda i: (i, 0, 0))
        for shape in ((2, half, ff),) * 4 + ((2, ff, half),) * 2
    ]


def experts_forward(normed, combine, gates, ups, downs):
    tokens, width = normed.shape
    experts, half, ff = gates[0].shape
    steps = experts // 2
    whole = pl.BlockSpec((tokens, width), lambda i: (0, 0))
    return pl.pallas_call(
        experts_forward_kernel,
        out_shape=(
            jax.ShapeDtypeStruct((steps, tokens, 4 * ff), BF),
            jax.ShapeDtypeStruct((steps, tokens, 2 * ff), BF),
            jax.ShapeDtypeStruct((tokens, width), BF),
        ),
        grid=(steps,),
        in_specs=[whole, pl.BlockSpec((tokens, experts), lambda i: (0, 0))]
        + expert_specs(half, ff),
        out_specs=[
            pl.BlockSpec((1, tokens, 4 * ff), lambda i: (i, 0, 0)),
            pl.BlockSpec((1, tokens, 2 * ff), lambda i: (i, 0, 0)),
            whole,
        ],
        scratch_shapes=[
            pltpu.VMEM((width, 4 * ff), BF),
            pltpu.VMEM((2 * ff, width), BF),
            pltpu.VMEM((tokens, width), F32),
        ],
        compiler_params=pltpu.CompilerParams(vmem_limit_bytes=VMEM_LIMIT),
        cost_estimate=COST,
        name="experts_forward",
    )(normed, combine, *gates, *ups, *downs)


def experts_backward_kernel(
    gy_ref, c_ref, g0, g1, u0, u1, d0, d1, pre_ref, grads_ref, dn_ref, wide, tall, acc
):
    step = pl.program_id(0)
    ff = g0.shape[2]
    stage_weights((g0, g1), (u0, u1), (d0, d1), wide, tall)

    @pl.when(step == 0)
    def _():
        acc[...] = jnp.zeros_like(acc)

    grad_middle = contract_last(gy_ref[...], tall[...])
    for a in range(2):
        gate = pre_ref[0, :, 2 * a * ff : (2 * a + 1) * ff].astype(F32)
        up = pre_ref[0, :, (2 * a + 1) * ff : (2 * a + 2) * ff].astype(F32)
        weight = column(c_ref[...], 2 * step + a)
        gm = weight * grad_middle[:, a * ff : (a + 1) * ff]
        sig = jax.nn.sigmoid(gate)
        grads_ref[0, :, 2 * a * ff : (2 * a + 1) * ff] = (
            gm * up * (sig + gate * sig * (1.0 - sig))
        ).astype(BF)
        grads_ref[0, :, (2 * a + 1) * ff : (2 * a + 2) * ff] = (gm * gate * sig).astype(BF)
    acc[...] += contract_last(grads_ref[0], wide[...])

    @pl.when(step == pl.num_programs(0) - 1)
    def _():
        dn_ref[...] = acc[...].astype(BF)


def experts_backward(grad_y, combine, gates, ups, downs, pre):
    tokens, width = grad_y.shape
    experts, half, ff = gates[0].shape
    steps = experts // 2
    whole = pl.BlockSpec((tokens, width), lambda i: (0, 0))
    by_pair = pl.BlockSpec((1, tokens, 4 * ff), lambda i: (i, 0, 0))
    return pl.pallas_call(
        experts_backward_kernel,
        out_shape=(
            jax.ShapeDtypeStruct((steps, tokens, 4 * ff), BF),
            jax.ShapeDtypeStruct((tokens, width), BF),
        ),
        grid=(steps,),
        in_specs=[whole, pl.BlockSpec((tokens, experts), lambda i: (0, 0))]
        + expert_specs(half, ff)
        + [by_pair],
        out_specs=[by_pair, whole],
        scratch_shapes=[
            pltpu.VMEM((width, 4 * ff), BF),
            pltpu.VMEM((2 * ff, width), BF),
            pltpu.VMEM((tokens, width), F32),
        ],
        compiler_params=pltpu.CompilerParams(vmem_limit_bytes=VMEM_LIMIT),
        cost_estimate=COST,
        name="experts_backward",
    )(grad_y, combine, *gates, *ups, *downs, pre)


def unpack_kernel(slabs_ref, gate_ref, up_ref, down_ref):
    for a in range(2):
        gate_ref[a] = slabs_ref[a].astype(F32)
        up_ref[a] = slabs_ref[2 + a].astype(F32)
        down_ref[a] = slabs_ref[4 + a].astype(F32).T


def unpack(slabs, steps):
    _, half, ff = slabs.shape
    wide = jax.ShapeDtypeStruct((2 * steps, half, ff), F32)
    tall = jax.ShapeDtypeStruct((2 * steps, ff, half), F32)
    return pl.pallas_call(
        unpack_kernel,
        out_shape=(wide, wide, tall),
        grid=(steps,),
        in_specs=[pl.BlockSpec((6, half, ff), lambda i: (i, 0, 0))],
        out_specs=[pl.BlockSpec((2, half, ff), lambda i: (i, 0, 0))] * 2
        + [pl.BlockSpec((2, ff, half), lambda i: (i, 0, 0))],
        compiler_params=pltpu.CompilerParams(vmem_limit_bytes=VMEM_LIMIT),
        cost_estimate=COST,
        name="unpack",
    )(slabs)


def unpack_attention_kernel(slabs_ref, q_ref, out_ref, k_ref, v_ref):
    ff = slabs_ref.shape[2]
    at = 0
    for ref, turn in ((q_ref, False), (out_ref, True), (k_ref, False), (v_ref, False)):
        for c in range(ref.shape[0 if turn else 1] // ff):
            value = slabs_ref[at].astype(F32)
            if turn:
                ref[c * ff : (c + 1) * ff, :] = value.T
            else:
                ref[:, c * ff : (c + 1) * ff] = value
            at += 1


def unpack_attention(slabs, query_cols, key_cols):
    total, rows, ff = slabs.shape
    count = 2 * (query_cols + key_cols) // ff
    shapes = ((rows, query_cols), (query_cols, rows), (rows, key_cols), (rows, key_cols))
    return pl.pallas_call(
        unpack_attention_kernel,
        out_shape=tuple(jax.ShapeDtypeStruct(shape, F32) for shape in shapes),
        grid=(1,),
        in_specs=[pl.BlockSpec((count, rows, ff), lambda i: (total // count - 1, 0, 0))],
        out_specs=[pl.BlockSpec(shape, lambda i: (0, 0)) for shape in shapes],
        compiler_params=pltpu.CompilerParams(vmem_limit_bytes=VMEM_LIMIT),
        cost_estimate=COST,
        name="unpack_attention",
    )(slabs)


def inverse_norm(near, far):
    count = near.shape[1] + far.shape[1]
    squares = jnp.sum(near * near, axis=1, keepdims=True) + jnp.sum(far * far, axis=1, keepdims=True)
    return lax.rsqrt(squares / count + EPS)


def halves(ref, rows, shard):
    half = ref.shape[1] // 2
    own = pl.ds(pl.multiple_of(shard * half, 128), half)
    far = pl.ds(pl.multiple_of((1 - shard) * half, 128), half)
    return ref[rows, own].astype(F32), ref[rows, far].astype(F32)


def put_halves(ref, rows, shard, near, far):
    half = ref.shape[1] // 2
    ref[rows, pl.ds(pl.multiple_of(shard * half, 128), half)] = near.astype(ref.dtype)
    ref[rows, pl.ds(pl.multiple_of((1 - shard) * half, 128), half)] = far.astype(ref.dtype)


def norm_backward(near, far, inverse, gain, grads):
    half = near.shape[1]
    near_scaled = grads[:, :half] * gain[:, :half]
    far_scaled = grads[:, half:] * gain[:, half:]
    along = (
        jnp.sum(near_scaled * near, axis=1, keepdims=True)
        + jnp.sum(far_scaled * far, axis=1, keepdims=True)
    ) / (2 * half)
    cube = inverse * inverse * inverse * along
    return (
        inverse * near_scaled - near * cube,
        inverse * far_scaled - far * cube,
        jnp.sum(grads[:, :half] * near * inverse, axis=0, keepdims=True),
        jnp.sum(grads[:, half:] * far * inverse, axis=0, keepdims=True),
    )


CHUNK = 128


def tensor_peers():
    t = lax.axis_index("tensor")
    low, high = lax.rem(t, 2), lax.rem(t // 2, 2)
    return low, {"tensor": t + 1 - 2 * low}, {"tensor": t + 2 - 4 * high}


def greet(peers):
    barrier = pltpu.get_barrier_semaphore()
    for peer in peers:
        pl.semaphore_signal(barrier, inc=1, device_id=peer, device_id_type=MESH)
    pl.semaphore_wait(barrier, len(peers))


def sum_over_tensor(part, total, arrived, mine, other, sems, consume, between=lambda c: None):
    send1, recv1, send2, recv2, send3, recv3 = sems
    low, near, far = tensor_peers()
    chunks = arrived.shape[0]
    half = chunks * CHUNK

    def rows(side, c):
        return pl.ds(pl.multiple_of(side * half + c * CHUNK, CHUNK), CHUNK)

    def give(c):
        return pltpu.make_async_remote_copy(
            part.at[rows(1 - low, c)], arrived.at[c], send1.at[c], recv1.at[c],
            device_id=near, device_id_type=MESH,
        )

    def swap(c):
        return pltpu.make_async_remote_copy(
            mine.at[c], other.at[c], send2.at[c], recv2.at[c], device_id=far, device_id_type=MESH
        )

    def back(c):
        return pltpu.make_async_remote_copy(
            total.at[rows(low, c)], total.at[rows(low, c)], send3.at[c], recv3.at[c],
            device_id=near, device_id_type=MESH,
        )

    @pl.loop(0, chunks)
    def _(c):
        give(c).start()

    @pl.loop(0, chunks)
    def _(c):
        give(c).wait_recv()
        mine[c] = (part[rows(low, c), :].astype(F32) + arrived[c].astype(F32)).astype(BF)
        swap(c).start()

    @pl.loop(0, chunks)
    def _(c):
        between(c)
        swap(c).wait_recv()
        total[rows(low, c), :] = (mine[c].astype(F32) + other[c].astype(F32)).astype(BF)
        back(c).start()
        consume(pl.multiple_of(low * half + c * CHUNK, CHUNK))
        back(c).wait_recv()
        consume(pl.multiple_of((1 - low) * half + c * CHUNK, CHUNK))

    @pl.loop(0, chunks)
    def _(c):
        give(c).wait_send()
        swap(c).wait_send()
        back(c).wait_send()


def sum_scratch(tokens, width):
    chunks = tokens // 2 // CHUNK
    piece = pltpu.VMEM((chunks, CHUNK, width), BF)
    return [pltpu.VMEM((tokens, width), BF)] + [piece] * 3 + [
        pltpu.SemaphoreType.DMA((chunks,))
    ] * 6


def fill_columns(target, refs):
    at = 0
    for ref in refs:
        target[:, at : at + ref.shape[1]] = ref[...]
        at += ref.shape[1]


def front_kernel(
    contexts, trees, x_ref, seg_ref, valid_ref, gain1_ref, gain2_ref, wq, wk, wv, wout, w_gate, w_up, w_down,
    packed_all, all_gains, far_qkv, far_out, far_gate, far_up, far_down,
    q_ref, kv_out, nt_out, o_ref, lse_ref, h_out, n2_out, n2t_out, count_ref,
    packed, gains, wqkv, far_gains, kv_all, nt_ref, h_ref, n2_ref, n2t_ref,
    normed, bias, tops, norms, sums, part, total, arrived, mine, other,
    ysend, yrecv, rsend, rrecv, psend, precv, ksend, krecv, out_sem, *sems
):
    i = lax.axis_index("context")
    shard = lax.axis_index("shard")
    parity = lax.rem(i, 2)
    tokens, width = x_ref.shape
    half = width // 2
    rows = tokens // trees
    heads = q_ref.shape[1] // HEAD
    kv_width = kv_all.shape[2] // 2
    per_group = q_ref.shape[1] // kv_width
    other_shard = {"shard": 1 - shard}
    partner = {"context": i + 1 - 2 * parity}
    right = {"context": lax.rem(i + 1, contexts)}
    _, near, far = tensor_peers()
    fill_columns(wqkv, (wq, wk, wv))
    segment = seg_ref[...]
    last = jnp.where(
        segment == 0, 1 << 20, jnp.where(lax.rem(segment, 3) == 1, segment + 2, segment)
    )
    packed[...] = jnp.zeros_like(packed)
    packed[0:trees, :] = segment.astype(F32)
    packed[trees : 2 * trees, :] = last.astype(F32)
    counted = jnp.sum(jnp.sum(valid_ref[...].astype(F32), axis=1, keepdims=True), axis=0, keepdims=True)
    gains[...] = jnp.broadcast_to(counted, gains.shape)
    gains[0:1, :] = gain1_ref[...]
    gains[1:2, :] = gain2_ref[...]
    greet(
        [other_shard, near, far]
        + [{"context": lax.rem(i + c, contexts)} for c in range(1, contexts)]
    )

    def half_span(ref, axis):
        size = ref.shape[axis] // 2
        return pl.ds(pl.multiple_of(parity * size, size), size)

    experts = w_gate.shape[0]
    shared = experts // 8
    own_count = (experts - shared) // 2
    moves = [
        (wqkv.at[half_span(wqkv, 0)], far_qkv.at[half_span(wqkv, 0)]),
        (wout.at[:, half_span(wout, 1)], far_out.at[:, half_span(wout, 1)]),
    ]
    first = (own_count + 1) // 2
    for begin, size in (
        (parity * own_count, first),
        (parity * own_count + first, own_count - first),
        (2 * own_count, shared),
    ):
        span = pl.ds(begin, size)
        for source, target in ((w_gate, far_gate), (w_up, far_up), (w_down, far_down)):
            moves.append((source.at[span], target.at[span]))
    relays = len(moves) - 3

    def direct(m):
        source, target = moves[m]
        return pltpu.make_async_remote_copy(
            source, target, ysend.at[m], yrecv.at[m],
            device_id=other_shard, device_id_type=MESH,
        )

    def relay(m):
        target = moves[m][1]
        return pltpu.make_async_remote_copy(
            target, target, rsend.at[m], rrecv.at[m], device_id=partner, device_id_type=MESH
        )

    def pass_on(m):
        direct(m).wait_recv()
        relay(m).start()

    count = len(moves)
    gain_copy = pltpu.make_async_remote_copy(
        gains, far_gains, ysend.at[count], yrecv.at[count],
        device_id=other_shard, device_id_type=MESH,
    )

    def tell(c, slot):
        return pltpu.make_async_remote_copy(
            packed, packed_all.at[slot], psend.at[c], precv.at[slot],
            device_id={"context": c}, device_id_type=MESH,
        )

    def lift(j):
        return pltpu.make_async_remote_copy(
            kv_all.at[j], kv_all.at[j], ksend.at[j], krecv.at[j],
            device_id=right, device_id_type=MESH,
        )

    outs = [
        pltpu.make_async_copy(src, dst, out_sem.at[at])
        for at, (src, dst) in enumerate((
            (nt_ref, nt_out), (kv_all, kv_out), (h_ref, h_out), (n2_ref, n2_out), (n2t_ref, n2t_out),
        ))
    ]
    gain_copy.start()
    for m in range(count):
        direct(m).start()

    gain_copy.wait_recv()
    packed[2 * trees : 2 * trees + 1, :] = gains[2:3, :rows] + far_gains[2:3, :rows]
    packed_all[i] = packed[...]

    @pl.loop(0, contexts)
    def _(c):
        @pl.when(c != i)
        def _():
            tell(c, i).start()

    all_gains[:, :half] = gains[...]
    all_gains[:, half:] = far_gains[...]
    tile = 128

    @pl.loop(0, tokens // tile)
    def _(index):
        span = pl.ds(pl.multiple_of(index * tile, tile), tile)
        own_x, far_x = halves(x_ref, span, shard)
        inverse = inverse_norm(own_x, far_x)
        own_x = (own_x * inverse * gains[0:1, :]).astype(BF)
        far_x = (far_x * inverse * far_gains[0:1, :]).astype(BF)
        normed[span, :half] = own_x
        normed[span, half:] = far_x
        nt_ref[:half, span] = own_x.T
        nt_ref[half:, span] = far_x.T

    outs[0].start()
    pass_on(0)
    pass_on(1)
    relay(0).wait_recv()
    qkv = matmul(normed[:, :half], wqkv[...]) + matmul(normed[:, half:], far_qkv[...])
    q_ref[...] = qkv[:, : q_ref.shape[1]].astype(BF)
    kv_all[i] = qkv[:, q_ref.shape[1] :].astype(BF)

    @pl.when(i < contexts - 1)
    def _():
        lift(i).start()

    tops[...] = jnp.full_like(tops, -1e30)
    norms[...] = jnp.zeros_like(norms)
    sums[...] = jnp.zeros_like(sums)

    @pl.loop(0, contexts)
    def _(c):
        @pl.when(c != i)
        def _():
            tell(i, c).wait_recv()

    pack_t = packed[...].T
    counted = packed_all[0, 2 * trees : 2 * trees + 1, 0:1]
    for c in range(1, contexts):
        counted = counted + packed_all[c, 2 * trees : 2 * trees + 1, 0:1]
    count_ref[...] = counted

    @pl.loop(0, contexts)
    def _(d):
        @pl.when(d <= i)
        def _():
            j = i - d

            @pl.when(d > 0)
            def _():
                lift(j).wait_recv()

                @pl.when(i < contexts - 1)
                def _():
                    lift(j).start()

            @pl.loop(0, trees)
            def _(tree):
                span = pl.ds(pl.multiple_of(tree * rows, rows), rows)
                key_pos = j * rows + lax.broadcasted_iota(jnp.int32, (rows, rows), 1)
                query_pos = i * rows + lax.broadcasted_iota(jnp.int32, (rows, rows), 0)
                last = packed_all[j, pl.ds(trees + tree, 1), :]
                allowed = (key_pos <= query_pos) & (column(pack_t, tree) <= last)
                bias[...] = jnp.where(allowed, 0.0, -2e30)
                for head in range(heads):
                    group = head // per_group
                    cols = slice(head * HEAD, (head + 1) * HEAD)
                    keys = kv_all[j, span, group * HEAD : (group + 1) * HEAD]
                    values = kv_all[
                        j, span, kv_width + group * HEAD : kv_width + (group + 1) * HEAD
                    ]
                    scores = contract_last(q_ref[span, cols], keys) * 0.125 + bias[...]
                    old = tops[span, head : head + 1]
                    top = jnp.maximum(old, jnp.max(scores, axis=1, keepdims=True))
                    weights = jnp.exp(scores - top)
                    shrink = jnp.exp(old - top)
                    tops[span, head : head + 1] = top
                    norms[span, head : head + 1] = norms[span, head : head + 1] * shrink + jnp.sum(
                        weights, axis=1, keepdims=True
                    )
                    sums[span, cols] = sums[span, cols] * shrink + matmul(
                        weights.astype(BF), values
                    )

        @pl.when(d == 0)
        def _():
            pass_on(2)

        @pl.when(d == min(2, contexts - 1))
        def _():
            pass_on(3)

    for head in range(heads):
        cols = slice(head * HEAD, (head + 1) * HEAD)
        o_ref[:, cols] = (sums[:, cols] / norms[:, head : head + 1]).astype(BF)
    lse = tops[...] + jnp.log(norms[...] + jnp.where(norms[...] == 0.0, 1.0, 0.0))
    for tree in range(trees):
        lse_ref[tree] = lse[tree * rows : (tree + 1) * rows].T[: lse_ref.shape[1]]
    outs[1].start()
    relay(1).wait_recv()
    part[:, :half] = matmul(o_ref[...], wout[...]).astype(BF)
    part[:, half:] = matmul(o_ref[...], far_out[...]).astype(BF)

    def consume(row):
        span = pl.ds(row, CHUNK)
        own_x, far_x = halves(x_ref, span, shard)
        own_x = own_x + total[span, :half].astype(F32)
        far_x = far_x + total[span, half:].astype(F32)
        h_ref[span, :half] = own_x
        h_ref[span, half:] = far_x
        inverse = inverse_norm(own_x, far_x)
        own_x = (own_x * inverse * gains[1:2, :]).astype(BF)
        far_x = (far_x * inverse * far_gains[1:2, :]).astype(BF)
        n2_ref[span, :half] = own_x
        n2_ref[span, half:] = far_x
        n2t_ref[:half, span] = own_x.T
        n2t_ref[half:, span] = far_x.T

    chunks = arrived.shape[0]

    def between(c):
        for at in range(chunks):

            @pl.when(c == at)
            def _():
                pass_on(4 + at)

    sum_over_tensor(part, total, arrived, mine, other, sems, consume, between)
    for copy in outs[2:]:
        copy.start()
    for m in range(4 + chunks, relays):
        pass_on(m)
    for m in range(2, relays):
        relay(m).wait_recv()
    for m in range(relays, count):
        direct(m).wait_recv()
    for m in range(count):
        direct(m).wait_send()
        if m < relays:
            relay(m).wait_send()
    gain_copy.wait_send()
    for copy in outs:
        copy.wait()

    @pl.loop(0, contexts)
    def _(c):
        @pl.when(c != i)
        def _():
            tell(c, i).wait_send()

        @pl.when((c <= i) & (i < contexts - 1))
        def _():
            lift(c).wait_send()


def front(
    contexts, trees, x, segments, valid, gain1, gain2, w_query, w_key, w_value, w_out,
    w_gate, w_up, w_down,
):
    tokens, width = x.shape
    half, rows = width // 2, tokens // trees
    cols = w_out.shape[0]
    both = w_key.shape[1] + w_value.shape[1]
    anywhere = pl.BlockSpec(memory_space=pl.ANY)
    near_memory = pl.BlockSpec(memory_space=pltpu.VMEM)
    shape, vmem, dma = jax.ShapeDtypeStruct, pltpu.VMEM, pltpu.SemaphoreType.DMA
    buffers = sum_scratch(tokens, width)
    return pl.pallas_call(
        functools.partial(front_kernel, contexts, trees),
        out_shape=(
            shape((contexts, 8, rows), F32),
            shape((8, width), F32),
            shape((half, cols + both), BF),
            *(shape(ref.shape, BF) for ref in (w_out, w_gate, w_up, w_down)),
            shape((tokens, cols), BF),
            shape((contexts, tokens, both), BF),
            shape((width, tokens), BF),
            shape((tokens, cols), BF),
            shape((trees, 8, rows), F32),
            shape((tokens, width), F32),
            shape((tokens, width), BF),
            shape((width, tokens), BF),
            shape((1, 1), F32),
        ),
        in_specs=[near_memory] * 9 + [anywhere] * 3,
        out_specs=(near_memory,) * 4
        + (anywhere,) * 3
        + (near_memory, anywhere, anywhere, near_memory, near_memory)
        + (anywhere,) * 3
        + (near_memory,),
        scratch_shapes=[
            vmem((8, rows), F32),
            vmem((8, half), F32),
            vmem((half, cols + both), BF),
            vmem((8, half), F32),
            vmem((contexts, tokens, both), BF),
            vmem((width, tokens), BF),
            vmem((tokens, width), F32),
            vmem((tokens, width), BF),
            vmem((width, tokens), BF),
            vmem((tokens, width), BF),
            vmem((rows, rows), F32),
            vmem((tokens, 128), F32),
            vmem((tokens, 128), F32),
            vmem((tokens, cols), F32),
            vmem((tokens, width), BF),
        ]
        + buffers[:4]
        + [dma((12,)), dma((12,)), dma((8,)), dma((8,))]
        + [dma((contexts,))] * 4
        + [dma((5,))]
        + buffers[4:],
        compiler_params=pltpu.CompilerParams(
            collective_id=2, has_side_effects=True, vmem_limit_bytes=60 * 1024 * 1024
        ),
        cost_estimate=COST,
        name="front",
    )(
        x, segments, valid, gain1, gain2, w_query, w_key, w_value, w_out, w_gate, w_up, w_down
    )


def after_experts_kernel(
    token_total, part, h_hbm, teacher_hbm, mask_ref, count_ref,
    y_hbm, low_hbm, lowt_hbm, square_ref,
    h_ref, teacher_ref, y_ref, low_ref, lowt_ref, in_sem, out_sem, total, arrived, mine, other, *sems
):
    tokens, width = h_ref.shape
    half = width // 2
    shard = lax.axis_index("shard")
    loads = [
        pltpu.make_async_copy(h_hbm, h_ref, in_sem.at[0]),
        pltpu.make_async_copy(teacher_hbm, teacher_ref, in_sem.at[1]),
    ]
    for copy in loads:
        copy.start()
    square_ref[...] = jnp.zeros_like(square_ref)

    def stores(row):
        rows = pl.ds(row, CHUNK)
        at = row // CHUNK
        return [
            pltpu.make_async_copy(y_ref.at[rows], y_hbm.at[rows], out_sem.at[0, at]),
            pltpu.make_async_copy(low_ref.at[rows], low_hbm.at[rows], out_sem.at[1, at]),
            pltpu.make_async_copy(lowt_ref.at[:, rows], lowt_hbm.at[:, rows], out_sem.at[2, at]),
        ]

    def consume(row):
        rows = pl.ds(row, CHUNK)
        mask = mask_ref[rows, :]
        factor = token_total / count_ref[...] * mask
        near_t, far_t = halves(teacher_ref, rows, shard)
        near = h_ref[rows, :half] + total[rows, :half].astype(F32)
        far = h_ref[rows, half:] + total[rows, half:].astype(F32)
        put_halves(y_ref, rows, shard, near, far)
        for begin, error in ((0, near - near_t), (half, far - far_t)):
            span = slice(begin, begin + half)
            squares = mask * jnp.sum(error * error, axis=1, keepdims=True)
            square_ref[...] += jnp.sum(squares, axis=0, keepdims=True)
            low = (factor * error).astype(BF)
            low_ref[rows, span] = low
            lowt_ref[span, rows] = low.T
        for copy in stores(row):
            copy.start()

    def between(c):
        @pl.when(c == 0)
        def _():
            for copy in loads:
                copy.wait()

    greet(tensor_peers()[1:])
    sum_over_tensor(part, total, arrived, mine, other, sems, consume, between)

    @pl.loop(0, tokens // CHUNK)
    def _(c):
        for copy in stores(pl.multiple_of(c * CHUNK, CHUNK)):
            copy.wait()


def after_experts(token_total, part, hidden, teacher, mask, count):
    tokens, width = hidden.shape
    shape, vmem, dma = jax.ShapeDtypeStruct, pltpu.VMEM, pltpu.SemaphoreType.DMA
    anywhere = pl.BlockSpec(memory_space=pl.ANY)
    near_memory = pl.BlockSpec(memory_space=pltpu.VMEM)
    return pl.pallas_call(
        functools.partial(after_experts_kernel, token_total),
        out_shape=(
            shape((tokens, width), BF),
            shape((tokens, width), BF),
            shape((width, tokens), BF),
            shape((1, 1), F32),
        ),
        in_specs=[near_memory, anywhere, anywhere, near_memory, near_memory],
        out_specs=(anywhere,) * 3 + (near_memory,),
        scratch_shapes=[
            vmem((tokens, width), F32),
            vmem((tokens, width), BF),
            vmem((tokens, width), BF),
            vmem((tokens, width), BF),
            vmem((width, tokens), BF),
            dma((2,)),
            dma((3, tokens // CHUNK)),
        ]
        + sum_scratch(tokens, width),
        compiler_params=pltpu.CompilerParams(
            collective_id=3, has_side_effects=True, vmem_limit_bytes=VMEM_LIMIT
        ),
        cost_estimate=COST,
        name="after_experts",
    )(part, hidden, teacher, mask, count)


def back_kernel(
    contexts, trees, lag, gains, wq, wk, wv, far_qkv, wout, far_out, q_ref, o_ref, lse_ref, packed_all,
    square_ref, part, h_hbm, gy_hbm, x_hbm, nt_hbm, n2t_hbm, gyt_hbm, grads_hbm, cm_hbm, kv_hbm,
    result, out_hbm, tail_ref, own_hbm, far_hbm, came, up_hbm, down_hbm, part2, dkv_part, dkv_came,
    wqkv, scale_ref, tail_own, tail_far, tail_came, tails,
    sums_ring, up_ring, down_ring, came_buf, out_buf, turned, gyt, grads_buf, cm_buf, stage,
    hbuf, chunk_low, chunk_out, my_part, total, arrived, mine, other, other2,
    dat, do_ref, dq_ref, dqs, deltas, bias, kv_buf, dkv_buf, dkv_sum, dkv_add, tile_buf,
    local_sem, ring_sem, tail_sem, tsend, trecv, ysend, yrecv, usend, urecv, dsend, drecv, store_sem, gsend, grecv, *ar_sems
):
    i = lax.axis_index("context")
    shard = lax.axis_index("shard")
    tokens, width = hbuf.shape
    half = width // 2
    rows = tokens // trees
    units = result.shape[0] // UNIT
    slots = lag * (contexts - 1) + 2
    ff = result.shape[2]
    pairs = grads_hbm.shape[0]
    heads = q_ref.shape[1] // HEAD
    kv_width = kv_buf.shape[1] // 2
    per_group = q_ref.shape[1] // kv_width
    low, near, far = tensor_peers()
    has_left, has_right = i > 0, i < contexts - 1
    right = {"context": lax.rem(i + 1, contexts)}
    left = {"context": lax.rem(i + contexts - 1, contexts)}
    other_shard = {"shard": 1 - shard}
    greet(
        [other_shard, near, far]
        + [{"context": lax.rem(i + c, contexts)} for c in range(1, contexts)]
    )

    def remote(src, dst, send, recv, to):
        return pltpu.make_async_remote_copy(
            src, dst, send, recv, device_id=to, device_id_type=MESH
        )

    def fetch(*moves):
        copies = [
            pltpu.make_async_copy(src, dst, local_sem.at[at]) for at, (src, dst) in enumerate(moves)
        ]
        for copy in copies:
            copy.start()
        for copy in copies:
            copy.wait()


    def slabs(k):
        return pl.ds(k * UNIT, UNIT)

    def exchange(k):
        return remote(
            far_hbm.at[slabs(k)], came.at[slabs(k)], ysend.at[k], yrecv.at[k], other_shard
        )

    def upward(k, ring):
        return remote(
            ring.at[lax.rem(k, slots)], up_hbm.at[slabs(k)], usend.at[k], urecv.at[k], right
        )

    def downward(k, ring):
        return remote(
            ring.at[lax.rem(k, slots)], down_hbm.at[slabs(k)], dsend.at[k], drecv.at[k], left
        )

    def store(k):
        return pltpu.make_async_copy(
            out_buf.at[lax.rem(k, 2)], result.at[slabs(k)], store_sem.at[lax.rem(k, 2)]
        )

    def add_unit(k):
        u, d = k - lag * i, k - lag * (contexts - 1 - i)
        slot, up_slot, down_slot = (lax.rem(jnp.maximum(at, 0), slots) for at in (k, u, d))
        has_new = k < units
        has_up = has_left & (u >= 0) & (u < units)
        has_down = has_right & (d >= 0) & (d < units)

        def load(at, src, dst):
            return pltpu.make_async_copy(src, dst, ring_sem.at[at])

        def new_loads():
            return (
                load(0, own_hbm.at[slabs(k)], sums_ring.at[slot]),
                load(1, came.at[slabs(k)], came_buf),
            )

        def up_load():
            return load(2, up_hbm.at[slabs(u)], up_ring.at[up_slot])

        def down_load():
            return load(3, down_hbm.at[slabs(d)], down_ring.at[down_slot])

        @pl.when(has_new)
        def _():
            @pl.when((k >= slots) & (i == 0))
            def _():
                upward(k - slots, sums_ring).wait_send()

            @pl.when((k >= slots) & (i == contexts - 1))
            def _():
                downward(k - slots, sums_ring).wait_send()

            exchange(k).wait_recv()
            for copy in new_loads():
                copy.start()

        @pl.when(has_up)
        def _():
            @pl.when(has_right & (u >= slots))
            def _():
                upward(u - slots, up_ring).wait_send()

            upward(u, up_ring).wait_recv()
            up_load().start()

        @pl.when(has_down)
        def _():
            @pl.when(has_left & (d >= slots))
            def _():
                downward(d - slots, down_ring).wait_send()

            downward(d, down_ring).wait_recv()
            down_load().start()

        @pl.when(has_new)
        def _():
            for copy in new_loads():
                copy.wait()
            sums_ring[slot] = (sums_ring[slot].astype(F32) + came_buf[...].astype(F32)).astype(BF)

            @pl.when(i == 0)
            def _():
                upward(k, sums_ring).start()

            @pl.when(i == contexts - 1)
            def _():
                downward(k, sums_ring).start()

        @pl.when(has_up)
        def _():
            up_load().wait()
            up_ring[up_slot] = (
                up_ring[up_slot].astype(F32) + sums_ring[up_slot].astype(F32)
            ).astype(BF)

            @pl.when(has_right)
            def _():
                upward(u, up_ring).start()

        @pl.when(has_down)
        def _():
            down_load().wait()
            down_ring[down_slot] = (
                down_ring[down_slot].astype(F32) + sums_ring[down_slot].astype(F32)
            ).astype(BF)

            @pl.when(has_left)
            def _():
                downward(d, down_ring).start()

        e = k - lag * jnp.maximum(i, contexts - 1 - i)

        @pl.when((e >= 0) & (e < units))
        def _():
            out_slot = lax.rem(e, slots)
            here = lax.rem(e, 2)

            @pl.when(e >= 2)
            def _():
                store(e - 2).wait()

            @pl.when(i == 0)
            def _():
                out_buf[here] = down_ring[out_slot]

            @pl.when(i == contexts - 1)
            def _():
                out_buf[here] = up_ring[out_slot]

            @pl.when(has_left & has_right)
            def _():
                out_buf[here] = (
                    up_ring[out_slot].astype(F32)
                    + (down_ring[out_slot].astype(F32) - sums_ring[out_slot].astype(F32))
                ).astype(BF)

            store(e).start()


    def write_slabs(first, number, products):
        for part_index, target in ((0, own_hbm), (1, far_hbm)):
            at = 0
            for left_ref, right_value, order in products:
                block = matmul(
                    left_ref[part_index * half : (part_index + 1) * half, :], right_value
                ).astype(BF)
                for c, place in enumerate(order):
                    stage[part_index, at + place] = block[:, c * ff : (c + 1) * ff]
                at += len(order)
        fetch(
            *(
                (stage.at[p, pl.ds(0, number)], target.at[pl.ds(first, number)])
                for p, target in ((0, own_hbm), (1, far_hbm))
            )
        )
        for c in range(number // UNIT):
            exchange(first // UNIT + c).start()

    def pair_slabs(p):
        fetch((grads_hbm.at[p], grads_buf), (cm_hbm.at[p], cm_buf))
        write_slabs(
            p * 6, 6, ((turned, grads_buf[...], (0, 2, 1, 3)), (gyt, cm_buf[...], (0, 1)))
        )


    chunks = arrived.shape[0]
    low_half = tokens // 2

    def chunk_rows(side, c):
        return pl.ds(pl.multiple_of(side * low_half + c * CHUNK, CHUNK), CHUNK)

    def summing(source, landing, sems):
        send1, recv1, send2, recv2, send3, recv3 = sems

        def give(c):
            return remote(
                source.at[chunk_rows(1 - low, c)], arrived.at[c], send1.at[c], recv1.at[c], near
            )

        def swap(c):
            return remote(mine.at[c], landing.at[c], send2.at[c], recv2.at[c], far)

        def back(c):
            span = chunk_rows(low, c)
            return remote(total.at[span], total.at[span], send3.at[c], recv3.at[c], near)

        def start():
            for c in range(chunks):
                give(c).start()

        def middle():
            fetch(*((source.at[chunk_rows(low, c)], my_part.at[c]) for c in range(chunks)))
            for c in range(chunks):
                give(c).wait_recv()
                mine[c] = (my_part[c].astype(F32) + arrived[c].astype(F32)).astype(BF)
                swap(c).start()

        def finish(c, consume):
            swap(c).wait_recv()
            total[chunk_rows(low, c), :] = (
                mine[c].astype(F32) + landing[c].astype(F32)
            ).astype(BF)
            back(c).start()
            consume(pl.multiple_of(low * low_half + c * CHUNK, CHUNK))

        def finish_other(c, consume):
            back(c).wait_recv()
            consume(pl.multiple_of((1 - low) * low_half + c * CHUNK, CHUNK))

        def drain():
            for c in range(chunks):
                give(c).wait_send()
                swap(c).wait_send()
                back(c).wait_send()

        return start, middle, finish, finish_other, drain

    start1, middle1, finish1, other1, drain1 = summing(part, other, ar_sems[:6])
    start2, middle2, finish2, finish_other2, drain2 = summing(part2, other2, ar_sems[6:])

    def through_second_norm(row):
        span = pl.ds(row, CHUNK)
        fetch((gy_hbm.at[span], chunk_low), (h_hbm.at[span], hbuf.at[span]))
        own_h, far_h = hbuf[span, :half], hbuf[span, half:]
        inverse = inverse_norm(own_h, far_h)
        own_d, far_d, own_scale, far_scale = norm_backward(
            own_h, far_h, inverse, gains[1:2, :], total[span, :].astype(F32)
        )
        scale_ref[1:2, :half] += own_scale
        scale_ref[1:2, half:] += far_scale
        own_d = chunk_low[:, :half].astype(F32) + own_d
        far_d = chunk_low[:, half:].astype(F32) + far_d
        hbuf[span, :half] = own_d
        hbuf[span, half:] = far_d
        own_d = own_d.astype(BF)
        far_d = far_d.astype(BF)
        dat[:half, span] = own_d.T
        dat[half:, span] = far_d.T
        do_ref[span, :] = (
            contract_last(own_d, wout[...]) + contract_last(far_d, far_out[...])
        ).astype(BF)

    def through_first_norm(row):
        span = pl.ds(row, CHUNK)
        fetch((x_hbm.at[span], chunk_low))
        own_x, far_x = halves(chunk_low, slice(None), shard)
        inverse = inverse_norm(own_x, far_x)
        own_d, far_d, own_scale, far_scale = norm_backward(
            own_x, far_x, inverse, gains[0:1, :], total[span, :].astype(F32)
        )
        scale_ref[0:1, :half] += own_scale
        scale_ref[0:1, half:] += far_scale
        put_halves(
            chunk_out, slice(None), shard, hbuf[span, :half] + own_d, hbuf[span, half:] + far_d
        )
        fetch((chunk_out, out_hbm.at[span]))


    def make_deltas():
        @pl.loop(0, trees)
        def _(tree):
            span = pl.ds(pl.multiple_of(tree * rows, rows), rows)
            for head in range(heads):
                cols = slice(head * HEAD, (head + 1) * HEAD)
                product = do_ref[span, cols].astype(F32) * o_ref[span, cols].astype(F32)
                deltas[tree, head] = lax.dot_general(
                    jnp.ones((8, HEAD), F32),
                    product,
                    (((1,), (1,)), ((), ())),
                    precision=lax.Precision.HIGHEST,
                    preferred_element_type=F32,
                )

    def hand(j, tree):
        span = pl.ds(pl.multiple_of(tree * rows, rows), rows)
        return remote(
            dkv_part.at[j, span], dkv_came.at[i, span], gsend.at[j, tree], grecv.at[i, tree],
            {"context": j},
        )

    def taken(c, tree):
        span = pl.ds(pl.multiple_of(tree * rows, rows), rows)
        return remote(
            dkv_part.at[c, span], dkv_came.at[c, span], gsend.at[c, tree], grecv.at[c, tree],
            {"context": c},
        )

    def attention_block(number):
        tree, j = number // contexts, lax.rem(number, contexts)

        @pl.when((number < trees * contexts) & (j <= i))
        def _():
            span = pl.ds(pl.multiple_of(tree * rows, rows), rows)
            fetch((kv_hbm.at[j, span], kv_buf))
            key_pos = j * rows + lax.broadcasted_iota(jnp.int32, (rows, rows), 0)
            query_pos = i * rows + lax.broadcasted_iota(jnp.int32, (rows, rows), 1)
            last = column(packed_all[j].T, trees + tree)
            segment = packed_all[i, pl.ds(tree, 1), :]
            allowed = (key_pos <= query_pos) & (segment <= last)
            bias[...] = jnp.where(allowed, 0.0, -2e30)
            for group in range(heads // per_group):
                keys = kv_buf[:, group * HEAD : (group + 1) * HEAD]
                values = kv_buf[:, kv_width + group * HEAD : kv_width + (group + 1) * HEAD]
                dk = jnp.zeros((rows, HEAD), F32)
                dv = jnp.zeros((rows, HEAD), F32)
                for head in range(group * per_group, (group + 1) * per_group):
                    cols = slice(head * HEAD, (head + 1) * HEAD)
                    queries = q_ref[span, cols]
                    grads = do_ref[span, cols]
                    scores = contract_last(keys, queries) * 0.125 + bias[...]
                    probs = jnp.exp(scores - lse_ref[tree, head : head + 1, :])
                    grad_probs = contract_last(values, grads)
                    grad_scores = (probs * (grad_probs - deltas[tree, head, 0:1, :])).astype(BF)
                    dv = dv + matmul(probs.astype(BF), grads)
                    dk = dk + matmul(grad_scores, queries)
                    dqs[span, cols] += contract_first(grad_scores, keys)
                dkv_buf[:, group * HEAD : (group + 1) * HEAD] = (dk * 0.125).astype(BF)
                dkv_buf[:, kv_width + group * HEAD : kv_width + (group + 1) * HEAD] = dv.astype(BF)

            @pl.when(j == i)
            def _():
                dkv_sum[span, :] = dkv_buf[...].astype(F32)

            @pl.when(j < i)
            def _():
                fetch((dkv_buf, dkv_part.at[j, span]))
                hand(j, tree).start()

    def query_slabs():
        dq_ref[...] = (dqs[...] * 0.125).astype(BF)
        thirds = tuple(range(dq_ref.shape[1] // ff))
        write_slabs(
            pairs * 6, 2 * len(thirds), ((turned, dq_ref[...], thirds), (dat, o_ref[...], thirds))
        )

    def key_value_sum():
        @pl.loop(0, contexts)
        def _(c):
            @pl.when(c > i)
            def _():
                @pl.loop(0, trees)
                def _(tree):
                    taken(c, tree).wait_recv()
                    span = pl.ds(pl.multiple_of(tree * rows, rows), rows)
                    fetch((dkv_came.at[c, span], dkv_add))
                    dkv_sum[span, :] += dkv_add[...].astype(F32)

        grad_kv = dkv_sum[...].astype(BF)
        pieces = tuple(range(grad_kv.shape[1] // ff))
        first = pairs * 6 + 2 * (dq_ref.shape[1] // ff)
        write_slabs(first, len(pieces), ((turned, grad_kv, pieces),))

    def first_norm_parts():
        @pl.loop(0, tokens // CHUNK)
        def _(c):
            span = pl.ds(pl.multiple_of(c * CHUNK, CHUNK), CHUNK)
            grads = jnp.concatenate([dq_ref[span, :], dkv_sum[span, :].astype(BF)], axis=1)
            tile_buf[:, :half] = contract_last(grads, wqkv[...]).astype(BF)
            tile_buf[:, half:] = contract_last(grads, far_qkv[...]).astype(BF)
            fetch((tile_buf, part2.at[span]))

        start2()


    tail_copy = remote(tail_far, tail_came, tail_sem.at[0], tail_sem.at[1], other_shard)

    def tell(c, slot):
        return remote(tails.at[slot], tails.at[slot], tsend.at[c], trecv.at[slot], {"context": c})

    def send_tail():
        for begin, target in ((0, tail_own), (half, tail_far)):
            target[...] = jnp.broadcast_to(square_ref[...], target.shape)
            target[0:2, :] = scale_ref[0:2, begin : begin + half]
        tail_copy.start()

    def tell_tail():
        tail_copy.wait_recv()
        tails[i] = tail_own[...] + tail_came[...]

        @pl.loop(0, contexts)
        def _(c):
            @pl.when(c != i)
            def _():
                tell(c, i).start()


    start1()
    fetch((n2t_hbm, turned), (gyt_hbm, gyt))
    fill_columns(wqkv, (wq, wk, wv))
    scale_ref[...] = jnp.zeros_like(scale_ref)
    dqs[...] = jnp.zeros_like(dqs)
    pair_slabs(0)
    middle1()

    chain = []
    for finish, finish_other, consume in (
        (finish1, other1, through_second_norm), (finish2, finish_other2, through_first_norm),
    ):
        steps = [[functools.partial(finish, 0, consume)]]
        for c in range(chunks):
            steps.append([functools.partial(finish_other, c, consume)])
            if c + 1 < chunks:
                steps[-1].append(functools.partial(finish, c + 1, consume))
        chain.append(steps)
    chain[0][-1].append(make_deltas)
    tasks = {}
    for p in range(1, pairs):
        tasks[3 * p - 3] = [functools.partial(pair_slabs, p)]
    last_pair = 3 * pairs - 6
    at = 0

    def put(acts):
        nonlocal at
        at += 1
        while at in tasks:
            at += 1
        tasks[at] = acts

    for acts in chain[0]:
        put(acts)
    per_step = -(-trees * contexts // 8)

    def attention_step(number):
        @pl.loop(0, per_step)
        def _(step):
            attention_block(number * per_step + step)

    attention_steps = {}
    for number in range(8):
        at += 1
        while at in tasks:
            at += 1
        attention_steps[at] = number
    first_at, last_at = min(attention_steps), max(attention_steps)
    at = max(at, last_pair)
    put([lambda: fetch((nt_hbm, turned)), query_slabs])
    at = max(at, last_at + 3)
    put([key_value_sum])
    put([first_norm_parts])
    put([drain1, middle2])
    for acts in chain[1]:
        put(acts)
    put([send_tail])
    put([tell_tail])
    assert at < units + lag * (contexts - 1)

    @pl.loop(0, units + lag * (contexts - 1))
    def _(k):
        add_unit(k)
        for when, acts in sorted(tasks.items()):

            @pl.when(k == when)
            def _(acts=acts):
                for act in acts:
                    act()

        number, due = jnp.int32(0), k < 0
        for when, index in attention_steps.items():
            number = jnp.where(k == when, index, number)
            due = due | (k == when)

        @pl.when(due)
        def _():
            attention_step(number)

    @pl.loop(0, contexts)
    def _(c):
        @pl.when(c != i)
        def _():
            tell(i, c).wait_recv()
            tell(c, i).wait_send()

    tail_copy.wait_send()
    tail = tails[0]
    for c in range(1, contexts):
        tail = tail + tails[c]
    tail_ref[...] = tail
    drain2()
    for k in (units - 2, units - 1):
        store(k).wait()

    @pl.loop(0, units)
    def _(k):
        exchange(k).wait_send()

        @pl.when((k >= units - slots) & has_right)
        def _():
            upward(k, up_ring).wait_send()

        @pl.when((k >= units - slots) & has_left)
        def _():
            downward(k, down_ring).wait_send()

    @pl.loop(0, contexts)
    def _(c):
        @pl.when(c < i)
        def _():
            @pl.loop(0, trees)
            def _(tree):
                hand(c, tree).wait_send()


def back(
    contexts, trees, gains, w_query, w_key, w_value, far_qkv, w_out, far_out, q, o, lse,
    packed_all, square, part, hidden, grad_y, x, normed_t, normed_two_t, grad_y_t, grads, middle, kv,
):
    tokens, width = hidden.shape
    half, rows = width // 2, tokens // trees
    pairs, _, four = grads.shape
    ff, cols, both = four // 4, q.shape[1], kv.shape[2]
    count = pairs * 6 + (2 * cols + both) // ff
    units = count // UNIT
    lag = 2 if contexts <= 4 else 1
    slots = lag * (contexts - 1) + 2
    chunks = tokens // 2 // CHUNK
    shape, vmem, dma = jax.ShapeDtypeStruct, pltpu.VMEM, pltpu.SemaphoreType.DMA
    slabs = shape((count, half, ff), BF)
    unit = (UNIT, half, ff)
    piece = vmem((chunks, CHUNK, width), BF)
    anywhere = pl.BlockSpec(memory_space=pl.ANY)
    near_memory = pl.BlockSpec(memory_space=pltpu.VMEM)
    outs = pl.pallas_call(
        functools.partial(back_kernel, contexts, trees, lag),
        out_shape=(
            slabs,
            shape((tokens, width), F32),
            shape((8, half), F32),
            *(slabs,) * 5,
            shape((tokens, width), BF),
            shape(kv.shape, BF),
            shape(kv.shape, BF),
        ),
        in_specs=[near_memory] * 12 + [anywhere] * 10,
        out_specs=(anywhere,) * 2 + (near_memory,) + (anywhere,) * 8,
        scratch_shapes=[
            vmem((half, cols + both), BF),
            vmem((8, width), F32),
            vmem((8, half), F32),
            vmem((8, half), F32),
            vmem((8, half), F32),
            vmem((contexts, 8, half), F32),
            vmem((slots,) + unit, BF),
            vmem((slots,) + unit, BF),
            vmem((slots,) + unit, BF),
            vmem(unit, BF),
            vmem((2,) + unit, BF),
            vmem((width, tokens), BF),
            vmem((width, tokens), BF),
            vmem((tokens, 4 * ff), BF),
            vmem((tokens, 2 * ff), BF),
            vmem((2, 6, half, ff), BF),
            vmem((tokens, width), F32),
            vmem((CHUNK, width), BF),
            vmem((CHUNK, width), F32),
            piece,
            vmem((tokens, width), BF),
            piece,
            piece,
            piece,
            piece,
            vmem((width, tokens), BF),
            vmem((tokens, cols), BF),
            vmem((tokens, cols), BF),
            vmem((tokens, cols), F32),
            vmem((trees, cols // HEAD, 8, rows), F32),
            vmem((rows, rows), F32),
            vmem((rows, both), BF),
            vmem((rows, both), BF),
            vmem((tokens, both), F32),
            vmem((rows, both), BF),
            vmem((CHUNK, width), BF),
            dma((4,)),
            dma((4,)),
            dma((2,)),
            dma((contexts,)),
            dma((contexts,)),
        ]
        + [dma((units,))] * 6
        + [dma((2,)), dma((contexts, trees)), dma((contexts, trees))]
        + [dma((chunks,))] * 12,
        compiler_params=pltpu.CompilerParams(
            collective_id=1, has_side_effects=True, vmem_limit_bytes=60 * 1024 * 1024
        ),
        cost_estimate=COST,
        name="back",
    )(
        gains, w_query, w_key, w_value, far_qkv, w_out, far_out, q, o, lse, packed_all,
        square, part, hidden, grad_y, x, normed_t, normed_two_t, grad_y_t, grads, middle, kv,
    )
    return outs[:3]


def local(
    states, segments, routes, gates, valid, teacher, attn_gain, w_query, key_matrix, value_matrix,
    w_out, moe_gain, w_gate, w_up, w_down,
):
    shards = lax.axis_size("shard")
    contexts = lax.axis_size("context")
    trees, rows, width = states.shape
    tokens = trees * rows
    half = width // 2
    experts = w_gate.shape[0]
    x = states.reshape(tokens, width)
    (
        packed_all, gains, qkv_far, out_far, gate_far, up_far, down_far, q, kv, normed_t,
        attended, lse, hidden, normed_two, normed_two_t, count,
    ) = front(
        contexts, trees, x, segments, valid, attn_gain.reshape(1, half), moe_gain.reshape(1, half),
        w_query, key_matrix, value_matrix, w_out, w_gate, w_up, w_down,
    )
    gate_ws, up_ws, down_ws = (w_gate, gate_far), (w_up, up_far), (w_down, down_far)

    expert_ids = jnp.arange(experts, dtype=jnp.int32)
    combine = jnp.sum(
        gates.reshape(tokens, -1)[..., None]
        * (routes.reshape(tokens, -1)[..., None] == expert_ids).astype(F32),
        axis=1,
    )
    pre, middle, moe_part = experts_forward(normed_two, combine, gate_ws, up_ws, down_ws)
    result, grad_y, grad_y_t, square = after_experts(
        float(tokens * shards * contexts),
        moe_part,
        hidden,
        teacher.reshape(tokens, width),
        valid.reshape(tokens, 1).astype(F32),
        count,
    )
    expert_grads, dn_part = experts_backward(grad_y, combine, gate_ws, up_ws, down_ws, pre)
    sums, grad_inputs, tail = back(
        contexts, trees, gains, w_query, key_matrix, value_matrix, qkv_far, w_out, out_far, q,
        attended, lse, packed_all, square, dn_part, hidden, grad_y, x, normed_t, normed_two_t,
        grad_y_t, expert_grads, middle, kv,
    )
    final_query, final_out, final_key, final_value = unpack_attention(
        sums, w_query.shape[1], key_matrix.shape[1]
    )
    final_gate, final_up, final_down = unpack(sums, experts // 2)
    return (
        tail[2, 0] / (count[0, 0] * width),
        result.reshape(trees, rows, width),
        grad_inputs.reshape(trees, rows, width),
        tail[0],
        final_query,
        final_key,
        final_value,
        final_out,
        tail[1],
        final_gate,
        final_up,
        final_down,
    )


def solution(mesh):
    return jax.shard_map(
        local,
        mesh=mesh,
        in_specs=(
            P("shard", "context", None),
            P("shard", "context"),
            P("shard", "context", None),
            P("shard", "context", None),
            P("shard", "context"),
            P("shard", "context", None),
            P("shard"),
            P("shard", "tensor"),
            P("shard", "tensor"),
            P("shard", "tensor"),
            P("tensor", "shard"),
            P("shard"),
            P(None, "shard", "tensor"),
            P(None, "shard", "tensor"),
            P(None, "tensor", "shard"),
        ),
        out_specs=(
            P(),
            P("shard", "context", None),
            P("shard", "context", None),
            P("shard"),
            P("shard", "tensor"),
            P("shard", "tensor"),
            P("shard", "tensor"),
            P("tensor", "shard"),
            P("shard"),
            P(None, "shard", "tensor"),
            P(None, "shard", "tensor"),
            P(None, "tensor", "shard"),
        ),
        check_vma=False,
    )
```

```python
import functools
import math

import jax
import jax.numpy as jnp
from jax import lax
from jax.experimental import pallas as pl
from jax.experimental.pallas import tpu as pltpu
from jax.sharding import PartitionSpec as P

HEAD = 64
EPS = 1e-05
BF = jnp.bfloat16
F32 = jnp.float32
MESH = pl.DeviceIdType.MESH
VMEM_LIMIT = 56 * 1024 * 1024
UNIT = 2
COST = pl.CostEstimate(flops=1, bytes_accessed=1, transcendentals=0)


def matmul(left, right):
    return jnp.dot(left, right, preferred_element_type=F32)


def contract_first(left, right):
    return lax.dot_general(left, right, (((0,), (0,)), ((), ())), preferred_element_type=F32)


def contract_last(left, right):
    return lax.dot_general(left, right, (((1,), (1,)), ((), ())), preferred_element_type=F32)


def column(block, index):
    lane = lax.broadcasted_iota(jnp.int32, block.shape, 1)
    return jnp.sum(jnp.where(lane == index, block, 0.0), axis=1, keepdims=True)


def experts_backward_kernel(
    gy_ref, c_ref, g0, g1, u0, u1, d0, d1, pre_hbm, grads_hbm, dn_ref,
    wide, tall, grads, pre_buf, weight_sem, pre_sem, out_sem,
):
    pairs, tokens = pre_hbm.shape[0], gy_ref.shape[0]
    half, ff = g0.shape[1], g0.shape[2]
    tile = 256

    def weight_loads(p):
        copies = []
        for side, gate, up, down in ((0, g0, u0, d0), (1, g1, u1, d1)):
            features = pl.ds(side * half, half)
            for a in range(2):
                e = 2 * p + a
                for source, target in (
                    (gate, wide.at[features, pl.ds(pl.multiple_of(2 * e * ff, 128), ff)]),
                    (up, wide.at[features, pl.ds(pl.multiple_of((2 * e + 1) * ff, 128), ff)]),
                    (down, tall.at[p, pl.ds(a * ff, ff), features]),
                ):
                    copies.append(
                        pltpu.make_async_copy(
                            source.at[e], target, weight_sem.at[p, len(copies)]
                        )
                    )
        return copies

    def pre_load(p):
        return pltpu.make_async_copy(
            pre_hbm.at[p], pre_buf.at[lax.rem(p, 2)], pre_sem.at[lax.rem(p, 2)]
        )

    def span(p):
        return pl.ds(pl.multiple_of(p * 4 * ff, 128), 4 * ff)

    def store(p):
        return pltpu.make_async_copy(grads.at[:, span(p)], grads_hbm.at[p], out_sem.at[p])

    for copy in weight_loads(0):
        copy.start()
    pre_load(0).start()

    @pl.loop(1, pairs)
    def _(p):
        for copy in weight_loads(p):
            copy.start()

    @pl.loop(0, pairs)
    def _(p):
        @pl.when(p + 1 < pairs)
        def _():
            pre_load(p + 1).start()

        for copy in weight_loads(p):
            copy.wait()
        pre_load(p).wait()
        slot = lax.rem(p, 2)
        grad_middle = contract_last(gy_ref[...], tall[p])
        pieces = []
        for a in range(2):
            gate = pre_buf[slot, :, 2 * a * ff : (2 * a + 1) * ff].astype(F32)
            up = pre_buf[slot, :, (2 * a + 1) * ff : (2 * a + 2) * ff].astype(F32)
            weight = column(c_ref[...], 2 * p + a)
            gm = weight * grad_middle[:, a * ff : (a + 1) * ff]
            sig = jax.nn.sigmoid(gate)
            pieces.append((gm * up * (sig + gate * sig * (1.0 - sig))).astype(BF))
            pieces.append((gm * gate * sig).astype(BF))
        grads[:, span(p)] = jnp.concatenate(pieces, axis=1)
        store(p).start()

    @pl.loop(0, 2 * half // tile)
    def _(index):
        rows = pl.ds(pl.multiple_of(index * tile, tile), tile)
        dn_ref[:, rows] = contract_last(grads[...], wide[rows, :]).astype(BF)

    @pl.loop(0, pairs)
    def _(p):
        store(p).wait()


def experts_backward(grad_y, combine, gates, ups, downs, pre):
    tokens, width = grad_y.shape
    experts, half, ff = gates[0].shape
    pairs = experts // 2
    vmem, dma = pltpu.VMEM, pltpu.SemaphoreType.DMA
    anywhere = pl.BlockSpec(memory_space=pl.ANY)
    near_memory = pl.BlockSpec(memory_space=pltpu.VMEM)
    return pl.pallas_call(
        experts_backward_kernel,
        out_shape=(
            jax.ShapeDtypeStruct((pairs, tokens, 4 * ff), BF),
            jax.ShapeDtypeStruct((tokens, width), BF),
        ),
        in_specs=[near_memory] * 2 + [anywhere] * 7,
        out_specs=(anywhere, near_memory),
        scratch_shapes=[
            vmem((width, 2 * experts * ff), BF),
            vmem((pairs, 2 * ff, width), BF),
            vmem((tokens, 2 * experts * ff), BF),
            vmem((2, tokens, 4 * ff), BF),
            dma((pairs, 12)),
            dma((2,)),
            dma((pairs,)),
        ],
        compiler_params=pltpu.CompilerParams(vmem_limit_bytes=60 * 1024 * 1024),
        cost_estimate=COST,
        name="experts_backward",
    )(grad_y, combine, *gates, *ups, *downs, pre)


def unpack_kernel(slabs_ref, gate_ref, up_ref, down_ref):
    for a in range(2):
        gate_ref[a] = slabs_ref[a].astype(F32)
        up_ref[a] = slabs_ref[2 + a].astype(F32)
        down_ref[a] = slabs_ref[4 + a].T.astype(F32)


def unpack(slabs, steps):
    _, half, ff = slabs.shape
    wide = jax.ShapeDtypeStruct((2 * steps, half, ff), F32)
    tall = jax.ShapeDtypeStruct((2 * steps, ff, half), F32)
    return pl.pallas_call(
        unpack_kernel,
        out_shape=(wide, wide, tall),
        grid=(steps,),
        in_specs=[pl.BlockSpec((6, half, ff), lambda i: (i, 0, 0))],
        out_specs=[pl.BlockSpec((2, half, ff), lambda i: (i, 0, 0))] * 2
        + [pl.BlockSpec((2, ff, half), lambda i: (i, 0, 0))],
        compiler_params=pltpu.CompilerParams(vmem_limit_bytes=VMEM_LIMIT),
        cost_estimate=COST,
        name="unpack",
    )(slabs)


def unpack_attention_kernel(slabs_ref, q_ref, out_ref, k_ref, v_ref):
    ff = slabs_ref.shape[2]
    at = 0
    for ref, turn in ((q_ref, False), (out_ref, True), (k_ref, False), (v_ref, False)):
        for c in range(ref.shape[0 if turn else 1] // ff):
            value = slabs_ref[at].astype(F32)
            if turn:
                ref[c * ff : (c + 1) * ff, :] = value.T
            else:
                ref[:, c * ff : (c + 1) * ff] = value
            at += 1


def unpack_attention(slabs, query_cols, key_cols):
    total, rows, ff = slabs.shape
    count = 2 * (query_cols + key_cols) // ff
    shapes = ((rows, query_cols), (query_cols, rows), (rows, key_cols), (rows, key_cols))
    return pl.pallas_call(
        unpack_attention_kernel,
        out_shape=tuple(jax.ShapeDtypeStruct(shape, F32) for shape in shapes),
        grid=(1,),
        in_specs=[pl.BlockSpec((count, rows, ff), lambda i: (total // count - 1, 0, 0))],
        out_specs=[pl.BlockSpec(shape, lambda i: (0, 0)) for shape in shapes],
        compiler_params=pltpu.CompilerParams(vmem_limit_bytes=VMEM_LIMIT),
        cost_estimate=COST,
        name="unpack_attention",
    )(slabs)


def inverse_norm(near, far):
    count = near.shape[1] + far.shape[1]
    squares = jnp.sum(near * near, axis=1, keepdims=True) + jnp.sum(far * far, axis=1, keepdims=True)
    return lax.rsqrt(squares / count + EPS)


def halves(ref, rows, shard):
    half = ref.shape[1] // 2
    own = pl.ds(pl.multiple_of(shard * half, 128), half)
    far = pl.ds(pl.multiple_of((1 - shard) * half, 128), half)
    return ref[rows, own].astype(F32), ref[rows, far].astype(F32)


def put_halves(ref, rows, shard, near, far):
    half = ref.shape[1] // 2
    ref[rows, pl.ds(pl.multiple_of(shard * half, 128), half)] = near.astype(ref.dtype)
    ref[rows, pl.ds(pl.multiple_of((1 - shard) * half, 128), half)] = far.astype(ref.dtype)


def norm_backward(near, far, inverse, gain, grads):
    half = near.shape[1]
    near_scaled = grads[:, :half] * gain[:, :half]
    far_scaled = grads[:, half:] * gain[:, half:]
    along = (
        jnp.sum(near_scaled * near, axis=1, keepdims=True)
        + jnp.sum(far_scaled * far, axis=1, keepdims=True)
    ) / (2 * half)
    cube = inverse * inverse * inverse * along
    return (
        inverse * near_scaled - near * cube,
        inverse * far_scaled - far * cube,
        jnp.sum(grads[:, :half] * near * inverse, axis=0, keepdims=True),
        jnp.sum(grads[:, half:] * far * inverse, axis=0, keepdims=True),
    )


CHUNK = 128


def tensor_peers():
    t = lax.axis_index("tensor")
    low, high = lax.rem(t, 2), lax.rem(t // 2, 2)
    return low, {"tensor": t + 1 - 2 * low}, {"tensor": t + 2 - 4 * high}


def greet(peers):
    barrier = pltpu.get_barrier_semaphore()
    for peer in peers:
        pl.semaphore_signal(barrier, inc=1, device_id=peer, device_id_type=MESH)
    pl.semaphore_wait(barrier, len(peers))


def sum_over_tensor(part, total, arrived, mine, other, sems, consume, between=lambda c: None):
    send1, recv1, send2, recv2, send3, recv3 = sems
    low, near, far = tensor_peers()
    chunks = arrived.shape[0]
    half = chunks * CHUNK

    def rows(side, c):
        return pl.ds(pl.multiple_of(side * half + c * CHUNK, CHUNK), CHUNK)

    def give(c):
        return pltpu.make_async_remote_copy(
            part.at[rows(1 - low, c)], arrived.at[c], send1.at[c], recv1.at[c],
            device_id=near, device_id_type=MESH,
        )

    def swap(c):
        return pltpu.make_async_remote_copy(
            mine.at[c], other.at[c], send2.at[c], recv2.at[c], device_id=far, device_id_type=MESH
        )

    def back(c):
        return pltpu.make_async_remote_copy(
            total.at[rows(low, c)], total.at[rows(low, c)], send3.at[c], recv3.at[c],
            device_id=near, device_id_type=MESH,
        )

    @pl.loop(0, chunks)
    def _(c):
        give(c).start()

    @pl.loop(0, chunks)
    def _(c):
        give(c).wait_recv()
        mine[c] = (part[rows(low, c), :].astype(F32) + arrived[c].astype(F32)).astype(BF)
        swap(c).start()

    @pl.loop(0, chunks)
    def _(c):
        between(c)
        swap(c).wait_recv()
        total[rows(low, c), :] = (mine[c].astype(F32) + other[c].astype(F32)).astype(BF)
        back(c).start()
        consume(pl.multiple_of(low * half + c * CHUNK, CHUNK))
        back(c).wait_recv()
        consume(pl.multiple_of((1 - low) * half + c * CHUNK, CHUNK))

    @pl.loop(0, chunks)
    def _(c):
        give(c).wait_send()
        swap(c).wait_send()
        back(c).wait_send()


def sum_scratch(tokens, width):
    chunks = tokens // 2 // CHUNK
    piece = pltpu.VMEM((chunks, CHUNK, width), BF)
    return [pltpu.VMEM((tokens, width), BF)] + [piece] * 3 + [
        pltpu.SemaphoreType.DMA((chunks,))
    ] * 6


def fill_columns(target, refs):
    at = 0
    for ref in refs:
        target[:, at : at + ref.shape[1]] = ref[...]
        at += ref.shape[1]


def front_kernel(
    contexts, trees, x_ref, seg_ref, valid_ref, gain1_ref, gain2_ref, wq, wk, wv, wout, w_gate, w_up, w_down,
    packed_all, all_gains, far_qkv, far_out, far_gate, far_up, far_down,
    q_ref, kv_out, nt_out, o_ref, lse_ref, h_out, n2_out, n2t_out, count_ref,
    packed, gains, wqkv, far_gains, kv_all, nt_ref, h_ref, n2_ref, n2t_ref,
    normed, bias, tops, norms, sums, part, total, arrived, mine, other,
    ysend, yrecv, rsend, rrecv, psend, precv, ksend, krecv, out_sem, *sems
):
    i = lax.axis_index("context")
    shard = lax.axis_index("shard")
    parity = lax.rem(i, 2)
    tokens, width = x_ref.shape
    half = width // 2
    rows = tokens // trees
    heads = q_ref.shape[1] // HEAD
    kv_width = kv_all.shape[2] // 2
    per_group = q_ref.shape[1] // kv_width
    other_shard = {"shard": 1 - shard}
    partner = {"context": i + 1 - 2 * parity}
    right = {"context": lax.rem(i + 1, contexts)}
    _, near, far = tensor_peers()
    fill_columns(wqkv, (wq, wk, wv))
    segment = seg_ref[...]
    last = jnp.where(
        segment == 0, 1 << 20, jnp.where(lax.rem(segment, 3) == 1, segment + 2, segment)
    )
    packed[...] = jnp.zeros_like(packed)
    packed[0:trees, :] = segment.astype(F32)
    packed[trees : 2 * trees, :] = last.astype(F32)
    counted = jnp.sum(jnp.sum(valid_ref[...].astype(F32), axis=1, keepdims=True), axis=0, keepdims=True)
    gains[...] = jnp.broadcast_to(counted, gains.shape)
    gains[0:1, :] = gain1_ref[...]
    gains[1:2, :] = gain2_ref[...]
    greet(
        [other_shard, near, far]
        + [{"context": lax.rem(i + c, contexts)} for c in range(1, contexts)]
    )

    def half_span(ref, axis):
        size = ref.shape[axis] // 2
        return pl.ds(pl.multiple_of(parity * size, size), size)

    experts = w_gate.shape[0]
    shared = experts // 8
    own_count = (experts - shared) // 2
    moves = [
        (wqkv.at[half_span(wqkv, 0)], far_qkv.at[half_span(wqkv, 0)]),
        (wout.at[:, half_span(wout, 1)], far_out.at[:, half_span(wout, 1)]),
    ]
    first = (own_count + 1) // 2
    for begin, size in (
        (parity * own_count, first),
        (parity * own_count + first, own_count - first),
        (2 * own_count, shared),
    ):
        span = pl.ds(begin, size)
        for source, target in ((w_gate, far_gate), (w_up, far_up), (w_down, far_down)):
            moves.append((source.at[span], target.at[span]))
    relays = len(moves) - 3

    def direct(m):
        source, target = moves[m]
        return pltpu.make_async_remote_copy(
            source, target, ysend.at[m], yrecv.at[m],
            device_id=other_shard, device_id_type=MESH,
        )

    def relay(m):
        target = moves[m][1]
        return pltpu.make_async_remote_copy(
            target, target, rsend.at[m], rrecv.at[m], device_id=partner, device_id_type=MESH
        )

    def pass_on(m):
        direct(m).wait_recv()
        relay(m).start()

    count = len(moves)
    gain_copy = pltpu.make_async_remote_copy(
        gains, far_gains, ysend.at[count], yrecv.at[count],
        device_id=other_shard, device_id_type=MESH,
    )

    def tell(c, slot):
        return pltpu.make_async_remote_copy(
            packed, packed_all.at[slot], psend.at[c], precv.at[slot],
            device_id={"context": c}, device_id_type=MESH,
        )

    def lift(j):
        return pltpu.make_async_remote_copy(
            kv_all.at[j], kv_all.at[j], ksend.at[j], krecv.at[j],
            device_id=right, device_id_type=MESH,
        )

    outs = [
        pltpu.make_async_copy(src, dst, out_sem.at[at])
        for at, (src, dst) in enumerate((
            (nt_ref, nt_out), (kv_all, kv_out), (h_ref, h_out), (n2_ref, n2_out), (n2t_ref, n2t_out),
        ))
    ]
    gain_copy.start()
    for m in range(count):
        direct(m).start()

    gain_copy.wait_recv()
    packed[2 * trees : 2 * trees + 1, :] = gains[2:3, :rows] + far_gains[2:3, :rows]
    packed_all[i] = packed[...]

    @pl.loop(0, contexts)
    def _(c):
        @pl.when(c != i)
        def _():
            tell(c, i).start()

    all_gains[:, :half] = gains[...]
    all_gains[:, half:] = far_gains[...]
    tile = 128

    @pl.loop(0, tokens // tile)
    def _(index):
        span = pl.ds(pl.multiple_of(index * tile, tile), tile)
        own_x, far_x = halves(x_ref, span, shard)
        inverse = inverse_norm(own_x, far_x)
        own_x = (own_x * inverse * gains[0:1, :]).astype(BF)
        far_x = (far_x * inverse * far_gains[0:1, :]).astype(BF)
        normed[span, :half] = own_x
        normed[span, half:] = far_x
        nt_ref[:half, span] = own_x.T
        nt_ref[half:, span] = far_x.T

    outs[0].start()
    pass_on(0)
    pass_on(1)
    relay(0).wait_recv()
    qkv = matmul(normed[:, :half], wqkv[...]) + matmul(normed[:, half:], far_qkv[...])
    q_ref[...] = qkv[:, : q_ref.shape[1]].astype(BF)
    kv_all[i] = qkv[:, q_ref.shape[1] :].astype(BF)

    @pl.when(i < contexts - 1)
    def _():
        lift(i).start()

    tops[...] = jnp.full_like(tops, -1e30)
    norms[...] = jnp.zeros_like(norms)
    sums[...] = jnp.zeros_like(sums)

    @pl.loop(0, contexts)
    def _(c):
        @pl.when(c != i)
        def _():
            tell(i, c).wait_recv()

    pack_t = packed[...].T
    counted = packed_all[0, 2 * trees : 2 * trees + 1, 0:1]
    for c in range(1, contexts):
        counted = counted + packed_all[c, 2 * trees : 2 * trees + 1, 0:1]
    count_ref[...] = counted

    @pl.loop(0, contexts)
    def _(d):
        @pl.when(d <= i)
        def _():
            j = i - d

            @pl.when(d > 0)
            def _():
                lift(j).wait_recv()

                @pl.when(i < contexts - 1)
                def _():
                    lift(j).start()

            @pl.loop(0, trees)
            def _(tree):
                span = pl.ds(pl.multiple_of(tree * rows, rows), rows)
                key_pos = j * rows + lax.broadcasted_iota(jnp.int32, (rows, rows), 1)
                query_pos = i * rows + lax.broadcasted_iota(jnp.int32, (rows, rows), 0)
                last = packed_all[j, pl.ds(trees + tree, 1), :]
                allowed = (key_pos <= query_pos) & (column(pack_t, tree) <= last)
                bias[...] = jnp.where(allowed, 0.0, -2e30)
                for head in range(heads):
                    group = head // per_group
                    cols = slice(head * HEAD, (head + 1) * HEAD)
                    keys = kv_all[j, span, group * HEAD : (group + 1) * HEAD]
                    values = kv_all[
                        j, span, kv_width + group * HEAD : kv_width + (group + 1) * HEAD
                    ]
                    scores = contract_last(q_ref[span, cols], keys) * 0.125 + bias[...]
                    old = tops[span, head : head + 1]
                    top = jnp.maximum(old, jnp.max(scores, axis=1, keepdims=True))
                    weights = jnp.exp(scores - top)
                    shrink = jnp.exp(old - top)
                    tops[span, head : head + 1] = top
                    norms[span, head : head + 1] = norms[span, head : head + 1] * shrink + jnp.sum(
                        weights, axis=1, keepdims=True
                    )
                    sums[span, cols] = sums[span, cols] * shrink + matmul(
                        weights.astype(BF), values
                    )

        @pl.when(d == 0)
        def _():
            pass_on(2)

        @pl.when(d == min(2, contexts - 1))
        def _():
            pass_on(3)

    for head in range(heads):
        cols = slice(head * HEAD, (head + 1) * HEAD)
        o_ref[:, cols] = (sums[:, cols] / norms[:, head : head + 1]).astype(BF)
    lse = tops[...] + jnp.log(norms[...] + jnp.where(norms[...] == 0.0, 1.0, 0.0))
    for tree in range(trees):
        lse_ref[tree] = lse[tree * rows : (tree + 1) * rows].T[: lse_ref.shape[1]]
    outs[1].start()
    relay(1).wait_recv()
    part[:, :half] = matmul(o_ref[...], wout[...]).astype(BF)
    part[:, half:] = matmul(o_ref[...], far_out[...]).astype(BF)

    def consume(row):
        span = pl.ds(row, CHUNK)
        own_x, far_x = halves(x_ref, span, shard)
        own_x = own_x + total[span, :half].astype(F32)
        far_x = far_x + total[span, half:].astype(F32)
        h_ref[span, :half] = own_x
        h_ref[span, half:] = far_x
        inverse = inverse_norm(own_x, far_x)
        own_x = (own_x * inverse * gains[1:2, :]).astype(BF)
        far_x = (far_x * inverse * far_gains[1:2, :]).astype(BF)
        n2_ref[span, :half] = own_x
        n2_ref[span, half:] = far_x
        n2t_ref[:half, span] = own_x.T
        n2t_ref[half:, span] = far_x.T

    chunks = arrived.shape[0]

    def between(c):
        for at in range(chunks):

            @pl.when(c == at)
            def _():
                pass_on(4 + at)

    sum_over_tensor(part, total, arrived, mine, other, sems, consume, between)
    for copy in outs[2:]:
        copy.start()
    for m in range(4 + chunks, relays):
        pass_on(m)
    for m in range(2, relays):
        relay(m).wait_recv()
    for m in range(relays, count):
        direct(m).wait_recv()
    for m in range(count):
        direct(m).wait_send()
        if m < relays:
            relay(m).wait_send()
    gain_copy.wait_send()
    for copy in outs:
        copy.wait()

    @pl.loop(0, contexts)
    def _(c):
        @pl.when(c != i)
        def _():
            tell(c, i).wait_send()

        @pl.when((c <= i) & (i < contexts - 1))
        def _():
            lift(c).wait_send()


def front(
    contexts, trees, x, segments, valid, gain1, gain2, w_query, w_key, w_value, w_out,
    w_gate, w_up, w_down,
):
    tokens, width = x.shape
    half, rows = width // 2, tokens // trees
    cols = w_out.shape[0]
    both = w_key.shape[1] + w_value.shape[1]
    anywhere = pl.BlockSpec(memory_space=pl.ANY)
    near_memory = pl.BlockSpec(memory_space=pltpu.VMEM)
    shape, vmem, dma = jax.ShapeDtypeStruct, pltpu.VMEM, pltpu.SemaphoreType.DMA
    buffers = sum_scratch(tokens, width)
    return pl.pallas_call(
        functools.partial(front_kernel, contexts, trees),
        out_shape=(
            shape((contexts, 8, rows), F32),
            shape((8, width), F32),
            shape((half, cols + both), BF),
            *(shape(ref.shape, BF) for ref in (w_out, w_gate, w_up, w_down)),
            shape((tokens, cols), BF),
            shape((contexts, tokens, both), BF),
            shape((width, tokens), BF),
            shape((tokens, cols), BF),
            shape((trees, 8, rows), F32),
            shape((tokens, width), F32),
            shape((tokens, width), BF),
            shape((width, tokens), BF),
            shape((1, 1), F32),
        ),
        in_specs=[near_memory] * 9 + [anywhere] * 3,
        out_specs=(near_memory,) * 4
        + (anywhere,) * 3
        + (near_memory, anywhere, anywhere, near_memory, near_memory)
        + (anywhere,) * 3
        + (near_memory,),
        scratch_shapes=[
            vmem((8, rows), F32),
            vmem((8, half), F32),
            vmem((half, cols + both), BF),
            vmem((8, half), F32),
            vmem((contexts, tokens, both), BF),
            vmem((width, tokens), BF),
            vmem((tokens, width), F32),
            vmem((tokens, width), BF),
            vmem((width, tokens), BF),
            vmem((tokens, width), BF),
            vmem((rows, rows), F32),
            vmem((tokens, 128), F32),
            vmem((tokens, 128), F32),
            vmem((tokens, cols), F32),
            vmem((tokens, width), BF),
        ]
        + buffers[:4]
        + [dma((12,)), dma((12,)), dma((8,)), dma((8,))]
        + [dma((contexts,))] * 4
        + [dma((5,))]
        + buffers[4:],
        compiler_params=pltpu.CompilerParams(
            collective_id=2, has_side_effects=True, vmem_limit_bytes=60 * 1024 * 1024
        ),
        cost_estimate=COST,
        name="front",
    )(
        x, segments, valid, gain1, gain2, w_query, w_key, w_value, w_out, w_gate, w_up, w_down
    )


def experts_forward_kernel(
    token_total, n_ref, c_ref, mask_ref, count_ref, g0, g1, u0, u1, d0, d1, h_hbm, teacher_hbm,
    pre_hbm, cm_hbm, y_hbm, low_hbm, lowt_hbm, square_ref,
    wide, tall, pre_buf, cm_all, part, h_ref, teacher_ref, y_ref, low_ref, lowt_ref,
    weight_sem, in_sem, pre_sem, out_sem, total, arrived, mine, other,
    send1, recv1, send2, recv2, send3, recv3,
):
    tokens, width = h_ref.shape
    half = width // 2
    pairs, ff = wide.shape[0], g0.shape[2]
    chunks = arrived.shape[0]
    shard = lax.axis_index("shard")
    low_side, near, far = tensor_peers()
    loads = [
        pltpu.make_async_copy(h_hbm, h_ref, in_sem.at[0]),
        pltpu.make_async_copy(teacher_hbm, teacher_ref, in_sem.at[1]),
    ]

    def weight_loads(p):
        copies = []
        for side, gate, up, down in ((0, g0, u0, d0), (1, g1, u1, d1)):
            features = pl.ds(side * half, half)
            for a in range(2):
                for source, target in (
                    (gate, wide.at[p, features, pl.ds(2 * a * ff, ff)]),
                    (up, wide.at[p, features, pl.ds((2 * a + 1) * ff, ff)]),
                    (down, tall.at[pl.ds((2 * p + a) * ff, ff), features]),
                ):
                    copies.append(
                        pltpu.make_async_copy(
                            source.at[2 * p + a], target, weight_sem.at[p, len(copies)]
                        )
                    )
        return copies

    @pl.loop(0, pairs)
    def _(p):
        for copy in weight_loads(p):
            copy.start()

    for copy in loads:
        copy.start()
    square_ref[...] = jnp.zeros_like(square_ref)
    greet([near, far])

    def rows(side, c):
        return pl.ds(pl.multiple_of((2 * c + side) * CHUNK, CHUNK), CHUNK)

    def both_rows(c):
        return pl.ds(pl.multiple_of(2 * c * CHUNK, 2 * CHUNK), 2 * CHUNK)

    def remote(src, dst, send, recv, to):
        return pltpu.make_async_remote_copy(
            src, dst, send, recv, device_id=to, device_id_type=MESH
        )

    def give(c):
        return remote(part.at[rows(1 - low_side, c)], arrived.at[c], send1.at[c], recv1.at[c], near)

    def swap(c):
        return remote(mine.at[c], other.at[c], send2.at[c], recv2.at[c], far)

    def back_copy(c):
        span = rows(low_side, c)
        return remote(total.at[span], total.at[span], send3.at[c], recv3.at[c], near)

    def kept(c, p):
        slot = lax.rem(p, 2)
        return (
            pltpu.make_async_copy(
                pre_buf.at[slot], pre_hbm.at[p, both_rows(c)], pre_sem.at[slot, 0]
            ),
            pltpu.make_async_copy(
                cm_all.at[:, pl.ds(pl.multiple_of(p * 2 * ff, 128), 2 * ff)],
                cm_hbm.at[p, both_rows(c)],
                pre_sem.at[slot, 1],
            ),
        )

    @pl.loop(0, chunks)
    def _(c):
        span = both_rows(c)

        @pl.loop(0, pairs)
        def _(p):
            @pl.when(c == 0)
            def _():
                for copy in weight_loads(p):
                    copy.wait()

            slot = lax.rem(p, 2)

            @pl.when(p >= 2)
            def _():
                for copy in kept(c, p - 2):
                    copy.wait()

            hidden = matmul(n_ref[span, :], wide[p])
            pre_buf[slot] = hidden.astype(BF)
            pieces = []
            for a in range(2):
                gate = hidden[:, 2 * a * ff : (2 * a + 1) * ff]
                up = hidden[:, (2 * a + 1) * ff : (2 * a + 2) * ff]
                weight = column(c_ref[span, :], 2 * p + a)
                pieces.append((weight * (gate * jax.nn.sigmoid(gate) * up)).astype(BF))
            cm_all[:, pl.ds(pl.multiple_of(p * 2 * ff, 128), 2 * ff)] = jnp.concatenate(
                pieces, axis=1
            )
            for copy in kept(c, p):
                copy.start()

        for p in (pairs - 2, pairs - 1):
            for copy in kept(c, p):
                copy.wait()
        part[span, :] = matmul(cm_all[...], tall[...]).astype(BF)
        give(c).start()
        give(c).wait_recv()
        mine[c] = (part[rows(low_side, c), :].astype(F32) + arrived[c].astype(F32)).astype(BF)
        swap(c).start()

    def stores(at):
        span = pl.ds(pl.multiple_of(at * CHUNK, CHUNK), CHUNK)
        return [
            pltpu.make_async_copy(y_ref.at[span], y_hbm.at[span], out_sem.at[0, at]),
            pltpu.make_async_copy(low_ref.at[span], low_hbm.at[span], out_sem.at[1, at]),
            pltpu.make_async_copy(lowt_ref.at[:, span], lowt_hbm.at[:, span], out_sem.at[2, at]),
        ]

    def consume(side, c):
        span = rows(side, c)
        mask = mask_ref[span, :]
        factor = token_total / count_ref[...] * mask
        near_t, far_t = halves(teacher_ref, span, shard)
        near_y = h_ref[span, :half] + total[span, :half].astype(F32)
        far_y = h_ref[span, half:] + total[span, half:].astype(F32)
        put_halves(y_ref, span, shard, near_y, far_y)
        for begin, error in ((0, near_y - near_t), (half, far_y - far_t)):
            features = slice(begin, begin + half)
            squares = mask * jnp.sum(error * error, axis=1, keepdims=True)
            square_ref[...] += jnp.sum(squares, axis=0, keepdims=True)
            grad = (factor * error).astype(BF)
            low_ref[span, features] = grad
            lowt_ref[features, span] = grad.T
        for copy in stores(2 * c + side):
            copy.start()

    for copy in loads:
        copy.wait()

    @pl.loop(0, chunks)
    def _(c):
        swap(c).wait_recv()
        total[rows(low_side, c), :] = (mine[c].astype(F32) + other[c].astype(F32)).astype(BF)
        back_copy(c).start()
        consume(low_side, c)
        back_copy(c).wait_recv()
        consume(1 - low_side, c)

    @pl.loop(0, chunks)
    def _(c):
        give(c).wait_send()
        swap(c).wait_send()
        back_copy(c).wait_send()
        for side in range(2):
            for copy in stores(2 * c + side):
                copy.wait()


def experts_forward(token_total, normed, combine, mask, count, gates, ups, downs, hidden, teacher):
    tokens, width = hidden.shape
    experts, half, ff = gates[0].shape
    pairs = experts // 2
    shape, vmem, dma = jax.ShapeDtypeStruct, pltpu.VMEM, pltpu.SemaphoreType.DMA
    anywhere = pl.BlockSpec(memory_space=pl.ANY)
    near_memory = pl.BlockSpec(memory_space=pltpu.VMEM)
    return pl.pallas_call(
        functools.partial(experts_forward_kernel, token_total),
        out_shape=(
            shape((pairs, tokens, 4 * ff), BF),
            shape((pairs, tokens, 2 * ff), BF),
            shape((tokens, width), BF),
            shape((tokens, width), BF),
            shape((width, tokens), BF),
            shape((1, 1), F32),
        ),
        in_specs=[near_memory] * 4 + [anywhere] * 8,
        out_specs=(anywhere,) * 5 + (near_memory,),
        scratch_shapes=[
            vmem((pairs, width, 4 * ff), BF),
            vmem((experts * ff, width), BF),
            vmem((2, 2 * CHUNK, 4 * ff), BF),
            vmem((2 * CHUNK, experts * ff), BF),
            vmem((tokens, width), BF),
            vmem((tokens, width), F32),
            vmem((tokens, width), BF),
            vmem((tokens, width), BF),
            vmem((tokens, width), BF),
            vmem((width, tokens), BF),
            dma((pairs, 12)),
            dma((2,)),
            dma((2, 2)),
            dma((3, tokens // CHUNK)),
        ]
        + sum_scratch(tokens, width),
        compiler_params=pltpu.CompilerParams(
            collective_id=3, has_side_effects=True, vmem_limit_bytes=60 * 1024 * 1024
        ),
        cost_estimate=COST,
        name="experts_forward",
    )(normed, combine, mask, count, *gates, *ups, *downs, hidden, teacher)


def back_kernel(
    contexts, trees, lag, gains, wq, wk, wv, far_qkv, wout, far_out, q_ref, o_ref, lse_ref, packed_all,
    square_ref, part, h_hbm, gy_hbm, x_hbm, nt_hbm, n2t_hbm, gyt_hbm, grads_hbm, cm_hbm, kv_hbm,
    result, out_hbm, tail_ref, own_hbm, far_hbm, came, up_hbm, down_hbm, part2, dkv_part, dkv_came,
    wqkv, scale_ref, tail_own, tail_far, tail_came, tails,
    sums_ring, up_ring, down_ring, came_buf, out_buf, turned, gyt, grads_buf, cm_buf, stage,
    hbuf, chunk_low, chunk_out, my_part, total, arrived, mine, other, other2,
    dat, do_ref, dq_ref, dqs, deltas, bias, kv_buf, dkv_buf, dkv_sum, dkv_add, tile_buf,
    local_sem, ring_sem, tail_sem, tsend, trecv, ysend, yrecv, usend, urecv, dsend, drecv, store_sem, gsend, grecv, *ar_sems
):
    i = lax.axis_index("context")
    shard = lax.axis_index("shard")
    tokens, width = hbuf.shape
    half = width // 2
    rows = tokens // trees
    units = result.shape[0] // UNIT
    slots = lag * (contexts - 1) + 2
    ff = result.shape[2]
    pairs = grads_hbm.shape[0]
    heads = q_ref.shape[1] // HEAD
    kv_width = kv_buf.shape[1] // 2
    per_group = q_ref.shape[1] // kv_width
    low, near, far = tensor_peers()
    has_left, has_right = i > 0, i < contexts - 1
    right = {"context": lax.rem(i + 1, contexts)}
    left = {"context": lax.rem(i + contexts - 1, contexts)}
    other_shard = {"shard": 1 - shard}

    def remote(src, dst, send, recv, to):
        return pltpu.make_async_remote_copy(
            src, dst, send, recv, device_id=to, device_id_type=MESH
        )

    def fetch(*moves):
        copies = [
            pltpu.make_async_copy(src, dst, local_sem.at[at]) for at, (src, dst) in enumerate(moves)
        ]
        for copy in copies:
            copy.start()
        for copy in copies:
            copy.wait()


    def slabs(k):
        return pl.ds(k * UNIT, UNIT)

    def exchange(k):
        return remote(
            far_hbm.at[slabs(k)], came.at[slabs(k)], ysend.at[k], yrecv.at[k], other_shard
        )

    def upward(k, ring):
        return remote(
            ring.at[lax.rem(k, slots)], up_hbm.at[slabs(k)], usend.at[k], urecv.at[k], right
        )

    def downward(k, ring):
        return remote(
            ring.at[lax.rem(k, slots)], down_hbm.at[slabs(k)], dsend.at[k], drecv.at[k], left
        )

    def store(k):
        return pltpu.make_async_copy(
            out_buf.at[lax.rem(k, 2)], result.at[slabs(k)], store_sem.at[lax.rem(k, 2)]
        )

    def add_unit(k):
        u, d = k - lag * i, k - lag * (contexts - 1 - i)
        slot, up_slot, down_slot = (lax.rem(jnp.maximum(at, 0), slots) for at in (k, u, d))
        has_new = k < units
        has_up = has_left & (u >= 0) & (u < units)
        has_down = has_right & (d >= 0) & (d < units)

        def load(at, src, dst):
            return pltpu.make_async_copy(src, dst, ring_sem.at[at])

        def new_loads():
            return (
                load(0, own_hbm.at[slabs(k)], sums_ring.at[slot]),
                load(1, came.at[slabs(k)], came_buf),
            )

        def up_load():
            return load(2, up_hbm.at[slabs(u)], up_ring.at[up_slot])

        def down_load():
            return load(3, down_hbm.at[slabs(d)], down_ring.at[down_slot])

        @pl.when(has_new)
        def _():
            @pl.when((k >= slots) & (i == 0))
            def _():
                upward(k - slots, sums_ring).wait_send()

            @pl.when((k >= slots) & (i == contexts - 1))
            def _():
                downward(k - slots, sums_ring).wait_send()

            exchange(k).wait_recv()
            for copy in new_loads():
                copy.start()

        @pl.when(has_up)
        def _():
            @pl.when(has_right & (u >= slots))
            def _():
                upward(u - slots, up_ring).wait_send()

            upward(u, up_ring).wait_recv()
            up_load().start()

        @pl.when(has_down)
        def _():
            @pl.when(has_left & (d >= slots))
            def _():
                downward(d - slots, down_ring).wait_send()

            downward(d, down_ring).wait_recv()
            down_load().start()

        @pl.when(has_new)
        def _():
            for copy in new_loads():
                copy.wait()
            sums_ring[slot] = (sums_ring[slot].astype(F32) + came_buf[...].astype(F32)).astype(BF)

            @pl.when(i == 0)
            def _():
                upward(k, sums_ring).start()

            @pl.when(i == contexts - 1)
            def _():
                downward(k, sums_ring).start()

        @pl.when(has_up)
        def _():
            up_load().wait()
            up_ring[up_slot] = (
                up_ring[up_slot].astype(F32) + sums_ring[up_slot].astype(F32)
            ).astype(BF)

            @pl.when(has_right)
            def _():
                upward(u, up_ring).start()

        @pl.when(has_down)
        def _():
            down_load().wait()
            down_ring[down_slot] = (
                down_ring[down_slot].astype(F32) + sums_ring[down_slot].astype(F32)
            ).astype(BF)

            @pl.when(has_left)
            def _():
                downward(d, down_ring).start()

        e = k - lag * jnp.maximum(i, contexts - 1 - i)

        @pl.when((e >= 0) & (e < units))
        def _():
            out_slot = lax.rem(e, slots)
            here = lax.rem(e, 2)

            @pl.when(e >= 2)
            def _():
                store(e - 2).wait()

            @pl.when(i == 0)
            def _():
                out_buf[here] = down_ring[out_slot]

            @pl.when(i == contexts - 1)
            def _():
                out_buf[here] = up_ring[out_slot]

            @pl.when(has_left & has_right)
            def _():
                out_buf[here] = (
                    up_ring[out_slot].astype(F32)
                    + (down_ring[out_slot].astype(F32) - sums_ring[out_slot].astype(F32))
                ).astype(BF)

            store(e).start()


    def write_slabs(first, number, products, send=True):
        for part_index, target in ((0, own_hbm), (1, far_hbm)):
            at = 0
            for left_ref, right_value, order in products:
                block = matmul(
                    left_ref[part_index * half : (part_index + 1) * half, :], right_value
                ).astype(BF)
                for c, place in enumerate(order):
                    stage[part_index, at + place] = block[:, c * ff : (c + 1) * ff]
                at += len(order)
        fetch(
            *(
                (stage.at[p, pl.ds(0, number)], target.at[pl.ds(first, number)])
                for p, target in ((0, own_hbm), (1, far_hbm))
            )
        )
        if send:
            for c in range(number // UNIT):
                exchange(first // UNIT + c).start()

    def pair_slabs(p, send=True):
        fetch((grads_hbm.at[p], grads_buf), (cm_hbm.at[p], cm_buf))
        write_slabs(
            p * 6, 6, ((turned, grads_buf[...], (0, 2, 1, 3)), (gyt, cm_buf[...], (0, 1))), send
        )


    chunks = arrived.shape[0]
    low_half = tokens // 2

    def chunk_rows(side, c):
        return pl.ds(pl.multiple_of(side * low_half + c * CHUNK, CHUNK), CHUNK)

    def summing(source, landing, sems):
        send1, recv1, send2, recv2, send3, recv3 = sems

        def give(c):
            return remote(
                source.at[chunk_rows(1 - low, c)], arrived.at[c], send1.at[c], recv1.at[c], near
            )

        def swap(c):
            return remote(mine.at[c], landing.at[c], send2.at[c], recv2.at[c], far)

        def back(c):
            span = chunk_rows(low, c)
            return remote(total.at[span], total.at[span], send3.at[c], recv3.at[c], near)

        def start():
            for c in range(chunks):
                give(c).start()

        def middle():
            fetch(*((source.at[chunk_rows(low, c)], my_part.at[c]) for c in range(chunks)))
            for c in range(chunks):
                give(c).wait_recv()
                mine[c] = (my_part[c].astype(F32) + arrived[c].astype(F32)).astype(BF)
                swap(c).start()

        def finish(c, consume):
            swap(c).wait_recv()
            total[chunk_rows(low, c), :] = (
                mine[c].astype(F32) + landing[c].astype(F32)
            ).astype(BF)
            back(c).start()
            consume(pl.multiple_of(low * low_half + c * CHUNK, CHUNK))

        def finish_other(c, consume):
            back(c).wait_recv()
            consume(pl.multiple_of((1 - low) * low_half + c * CHUNK, CHUNK))

        def drain():
            for c in range(chunks):
                give(c).wait_send()
                swap(c).wait_send()
                back(c).wait_send()

        return start, middle, finish, finish_other, drain

    start1, middle1, finish1, other1, drain1 = summing(part, other, ar_sems[:6])
    start2, middle2, finish2, finish_other2, drain2 = summing(part2, other2, ar_sems[6:])

    def through_second_norm(row):
        span = pl.ds(row, CHUNK)
        fetch((gy_hbm.at[span], chunk_low), (h_hbm.at[span], hbuf.at[span]))
        own_h, far_h = hbuf[span, :half], hbuf[span, half:]
        inverse = inverse_norm(own_h, far_h)
        own_d, far_d, own_scale, far_scale = norm_backward(
            own_h, far_h, inverse, gains[1:2, :], total[span, :].astype(F32)
        )
        scale_ref[1:2, :half] += own_scale
        scale_ref[1:2, half:] += far_scale
        own_d = chunk_low[:, :half].astype(F32) + own_d
        far_d = chunk_low[:, half:].astype(F32) + far_d
        hbuf[span, :half] = own_d
        hbuf[span, half:] = far_d
        own_d = own_d.astype(BF)
        far_d = far_d.astype(BF)
        dat[:half, span] = own_d.T
        dat[half:, span] = far_d.T
        do_ref[span, :] = (
            contract_last(own_d, wout[...]) + contract_last(far_d, far_out[...])
        ).astype(BF)

    def through_first_norm(row):
        span = pl.ds(row, CHUNK)
        fetch((x_hbm.at[span], chunk_low))
        own_x, far_x = halves(chunk_low, slice(None), shard)
        inverse = inverse_norm(own_x, far_x)
        own_d, far_d, own_scale, far_scale = norm_backward(
            own_x, far_x, inverse, gains[0:1, :], total[span, :].astype(F32)
        )
        scale_ref[0:1, :half] += own_scale
        scale_ref[0:1, half:] += far_scale
        put_halves(
            chunk_out, slice(None), shard, hbuf[span, :half] + own_d, hbuf[span, half:] + far_d
        )
        fetch((chunk_out, out_hbm.at[span]))


    def make_deltas():
        @pl.loop(0, trees)
        def _(tree):
            span = pl.ds(pl.multiple_of(tree * rows, rows), rows)
            for head in range(heads):
                cols = slice(head * HEAD, (head + 1) * HEAD)
                product = do_ref[span, cols].astype(F32) * o_ref[span, cols].astype(F32)
                deltas[tree, head] = lax.dot_general(
                    jnp.ones((8, HEAD), F32),
                    product,
                    (((1,), (1,)), ((), ())),
                    precision=lax.Precision.HIGHEST,
                    preferred_element_type=F32,
                )

    def hand(j, tree):
        span = pl.ds(pl.multiple_of(tree * rows, rows), rows)
        return remote(
            dkv_part.at[j, span], dkv_came.at[i, span], gsend.at[j, tree], grecv.at[i, tree],
            {"context": j},
        )

    def taken(c, tree):
        span = pl.ds(pl.multiple_of(tree * rows, rows), rows)
        return remote(
            dkv_part.at[c, span], dkv_came.at[c, span], gsend.at[c, tree], grecv.at[c, tree],
            {"context": c},
        )

    def attention_block(number):
        tree, j = number // contexts, lax.rem(number, contexts)

        @pl.when((number < trees * contexts) & (j <= i))
        def _():
            span = pl.ds(pl.multiple_of(tree * rows, rows), rows)
            fetch((kv_hbm.at[j, span], kv_buf))
            key_pos = j * rows + lax.broadcasted_iota(jnp.int32, (rows, rows), 0)
            query_pos = i * rows + lax.broadcasted_iota(jnp.int32, (rows, rows), 1)
            last = column(packed_all[j].T, trees + tree)
            segment = packed_all[i, pl.ds(tree, 1), :]
            allowed = (key_pos <= query_pos) & (segment <= last)
            bias[...] = jnp.where(allowed, 0.0, -2e30)
            for group in range(heads // per_group):
                keys = kv_buf[:, group * HEAD : (group + 1) * HEAD]
                values = kv_buf[:, kv_width + group * HEAD : kv_width + (group + 1) * HEAD]
                dk = jnp.zeros((rows, HEAD), F32)
                dv = jnp.zeros((rows, HEAD), F32)
                for head in range(group * per_group, (group + 1) * per_group):
                    cols = slice(head * HEAD, (head + 1) * HEAD)
                    queries = q_ref[span, cols]
                    grads = do_ref[span, cols]
                    scores = contract_last(keys, queries) * 0.125 + bias[...]
                    probs = jnp.exp(scores - lse_ref[tree, head : head + 1, :])
                    grad_probs = contract_last(values, grads)
                    grad_scores = (probs * (grad_probs - deltas[tree, head, 0:1, :])).astype(BF)
                    dv = dv + matmul(probs.astype(BF), grads)
                    dk = dk + matmul(grad_scores, queries)
                    dqs[span, cols] += contract_first(grad_scores, keys)
                dkv_buf[:, group * HEAD : (group + 1) * HEAD] = (dk * 0.125).astype(BF)
                dkv_buf[:, kv_width + group * HEAD : kv_width + (group + 1) * HEAD] = dv.astype(BF)

            @pl.when(j == i)
            def _():
                dkv_sum[span, :] = dkv_buf[...].astype(F32)

            @pl.when(j < i)
            def _():
                fetch((dkv_buf, dkv_part.at[j, span]))
                hand(j, tree).start()

    def query_slabs():
        dq_ref[...] = (dqs[...] * 0.125).astype(BF)
        thirds = tuple(range(dq_ref.shape[1] // ff))
        write_slabs(
            pairs * 6, 2 * len(thirds), ((turned, dq_ref[...], thirds), (dat, o_ref[...], thirds))
        )

    def key_value_sum():
        @pl.loop(0, contexts)
        def _(c):
            @pl.when(c > i)
            def _():
                @pl.loop(0, trees)
                def _(tree):
                    taken(c, tree).wait_recv()
                    span = pl.ds(pl.multiple_of(tree * rows, rows), rows)
                    fetch((dkv_came.at[c, span], dkv_add))
                    dkv_sum[span, :] += dkv_add[...].astype(F32)

        grad_kv = dkv_sum[...].astype(BF)
        pieces = tuple(range(grad_kv.shape[1] // ff))
        first = pairs * 6 + 2 * (dq_ref.shape[1] // ff)
        write_slabs(first, len(pieces), ((turned, grad_kv, pieces),))

    def first_norm_parts():
        @pl.loop(0, tokens // CHUNK)
        def _(c):
            span = pl.ds(pl.multiple_of(c * CHUNK, CHUNK), CHUNK)
            grads = jnp.concatenate([dq_ref[span, :], dkv_sum[span, :].astype(BF)], axis=1)
            tile_buf[:, :half] = contract_last(grads, wqkv[...]).astype(BF)
            tile_buf[:, half:] = contract_last(grads, far_qkv[...]).astype(BF)
            fetch((tile_buf, part2.at[span]))

        start2()


    tail_copy = remote(tail_far, tail_came, tail_sem.at[0], tail_sem.at[1], other_shard)

    def tell(c, slot):
        return remote(tails.at[slot], tails.at[slot], tsend.at[c], trecv.at[slot], {"context": c})

    def send_tail():
        for begin, target in ((0, tail_own), (half, tail_far)):
            target[...] = jnp.broadcast_to(square_ref[...], target.shape)
            target[0:2, :] = scale_ref[0:2, begin : begin + half]
        tail_copy.start()

    def tell_tail():
        tail_copy.wait_recv()
        tails[i] = tail_own[...] + tail_came[...]

        @pl.loop(0, contexts)
        def _(c):
            @pl.when(c != i)
            def _():
                tell(c, i).start()


    fetch((n2t_hbm, turned), (gyt_hbm, gyt))
    pair_slabs(0, False)
    greet(
        [other_shard, near, far]
        + [{"context": lax.rem(i + c, contexts)} for c in range(1, contexts)]
    )
    for c in range(6 // UNIT):
        exchange(c).start()
    start1()
    fill_columns(wqkv, (wq, wk, wv))
    scale_ref[...] = jnp.zeros_like(scale_ref)
    dqs[...] = jnp.zeros_like(dqs)
    middle1()

    chain = []
    for finish, finish_other, consume in (
        (finish1, other1, through_second_norm), (finish2, finish_other2, through_first_norm),
    ):
        steps = [[functools.partial(finish, 0, consume)]]
        for c in range(chunks):
            steps.append([functools.partial(finish_other, c, consume)])
            if c + 1 < chunks:
                steps[-1].append(functools.partial(finish, c + 1, consume))
        chain.append(steps)
    chain[0][-1].append(make_deltas)
    tasks = {}
    for p in range(1, pairs):
        tasks[3 * p - 3] = [functools.partial(pair_slabs, p)]
    last_pair = 3 * pairs - 6
    at = 0

    def put(acts):
        nonlocal at
        at += 1
        while at in tasks:
            at += 1
        tasks[at] = acts

    for acts in chain[0]:
        put(acts)
    per_step = -(-trees * contexts // 8)

    def attention_step(number):
        @pl.loop(0, per_step)
        def _(step):
            attention_block(number * per_step + step)

    attention_steps = {}
    for number in range(8):
        at += 1
        while at in tasks:
            at += 1
        attention_steps[at] = number
    first_at, last_at = min(attention_steps), max(attention_steps)
    at = max(at, last_pair)
    put([lambda: fetch((nt_hbm, turned)), query_slabs])
    at = max(at, last_at + 3)
    put([key_value_sum])
    put([first_norm_parts])
    put([drain1, middle2])
    for acts in chain[1]:
        put(acts)
    put([send_tail])
    put([tell_tail])
    assert at < units + lag * (contexts - 1)

    @pl.loop(0, units + lag * (contexts - 1))
    def _(k):
        add_unit(k)
        for when, acts in sorted(tasks.items()):

            @pl.when(k == when)
            def _(acts=acts):
                for act in acts:
                    act()

        number, due = jnp.int32(0), k < 0
        for when, index in attention_steps.items():
            number = jnp.where(k == when, index, number)
            due = due | (k == when)

        @pl.when(due)
        def _():
            attention_step(number)

    @pl.loop(0, contexts)
    def _(c):
        @pl.when(c != i)
        def _():
            tell(i, c).wait_recv()
            tell(c, i).wait_send()

    tail_copy.wait_send()
    tail = tails[0]
    for c in range(1, contexts):
        tail = tail + tails[c]
    tail_ref[...] = tail
    drain2()
    for k in (units - 2, units - 1):
        store(k).wait()

    @pl.loop(0, units)
    def _(k):
        exchange(k).wait_send()

        @pl.when((k >= units - slots) & has_right)
        def _():
            upward(k, up_ring).wait_send()

        @pl.when((k >= units - slots) & has_left)
        def _():
            downward(k, down_ring).wait_send()

    @pl.loop(0, contexts)
    def _(c):
        @pl.when(c < i)
        def _():
            @pl.loop(0, trees)
            def _(tree):
                hand(c, tree).wait_send()


def back(
    contexts, trees, gains, w_query, w_key, w_value, far_qkv, w_out, far_out, q, o, lse,
    packed_all, square, part, hidden, grad_y, x, normed_t, normed_two_t, grad_y_t, grads, middle, kv,
):
    tokens, width = hidden.shape
    half, rows = width // 2, tokens // trees
    pairs, _, four = grads.shape
    ff, cols, both = four // 4, q.shape[1], kv.shape[2]
    count = pairs * 6 + (2 * cols + both) // ff
    units = count // UNIT
    lag = 2 if contexts <= 4 else 1
    slots = lag * (contexts - 1) + 2
    chunks = tokens // 2 // CHUNK
    shape, vmem, dma = jax.ShapeDtypeStruct, pltpu.VMEM, pltpu.SemaphoreType.DMA
    slabs = shape((count, half, ff), BF)
    unit = (UNIT, half, ff)
    piece = vmem((chunks, CHUNK, width), BF)
    anywhere = pl.BlockSpec(memory_space=pl.ANY)
    near_memory = pl.BlockSpec(memory_space=pltpu.VMEM)
    outs = pl.pallas_call(
        functools.partial(back_kernel, contexts, trees, lag),
        out_shape=(
            slabs,
            shape((tokens, width), F32),
            shape((8, half), F32),
            *(slabs,) * 5,
            shape((tokens, width), BF),
            shape(kv.shape, BF),
            shape(kv.shape, BF),
        ),
        in_specs=[near_memory] * 12 + [anywhere] * 10,
        out_specs=(anywhere,) * 2 + (near_memory,) + (anywhere,) * 8,
        scratch_shapes=[
            vmem((half, cols + both), BF),
            vmem((8, width), F32),
            vmem((8, half), F32),
            vmem((8, half), F32),
            vmem((8, half), F32),
            vmem((contexts, 8, half), F32),
            vmem((slots,) + unit, BF),
            vmem((slots,) + unit, BF),
            vmem((slots,) + unit, BF),
            vmem(unit, BF),
            vmem((2,) + unit, BF),
            vmem((width, tokens), BF),
            vmem((width, tokens), BF),
            vmem((tokens, 4 * ff), BF),
            vmem((tokens, 2 * ff), BF),
            vmem((2, 6, half, ff), BF),
            vmem((tokens, width), F32),
            vmem((CHUNK, width), BF),
            vmem((CHUNK, width), F32),
            piece,
            vmem((tokens, width), BF),
            piece,
            piece,
            piece,
            piece,
            vmem((width, tokens), BF),
            vmem((tokens, cols), BF),
            vmem((tokens, cols), BF),
            vmem((tokens, cols), F32),
            vmem((trees, cols // HEAD, 8, rows), F32),
            vmem((rows, rows), F32),
            vmem((rows, both), BF),
            vmem((rows, both), BF),
            vmem((tokens, both), F32),
            vmem((rows, both), BF),
            vmem((CHUNK, width), BF),
            dma((4,)),
            dma((4,)),
            dma((2,)),
            dma((contexts,)),
            dma((contexts,)),
        ]
        + [dma((units,))] * 6
        + [dma((2,)), dma((contexts, trees)), dma((contexts, trees))]
        + [dma((chunks,))] * 12,
        compiler_params=pltpu.CompilerParams(
            collective_id=1, has_side_effects=True, vmem_limit_bytes=60 * 1024 * 1024
        ),
        cost_estimate=COST,
        name="back",
    )(
        gains, w_query, w_key, w_value, far_qkv, w_out, far_out, q, o, lse, packed_all,
        square, part, hidden, grad_y, x, normed_t, normed_two_t, grad_y_t, grads, middle, kv,
    )
    return outs[:3]


def local(
    states, segments, routes, gates, valid, teacher, attn_gain, w_query, key_matrix, value_matrix,
    w_out, moe_gain, w_gate, w_up, w_down,
):
    shards = lax.axis_size("shard")
    contexts = lax.axis_size("context")
    trees, rows, width = states.shape
    tokens = trees * rows
    half = width // 2
    experts = w_gate.shape[0]
    x = states.reshape(tokens, width)
    (
        packed_all, gains, qkv_far, out_far, gate_far, up_far, down_far, q, kv, normed_t,
        attended, lse, hidden, normed_two, normed_two_t, count,
    ) = front(
        contexts, trees, x, segments, valid, attn_gain.reshape(1, half), moe_gain.reshape(1, half),
        w_query, key_matrix, value_matrix, w_out, w_gate, w_up, w_down,
    )
    gate_ws, up_ws, down_ws = (w_gate, gate_far), (w_up, up_far), (w_down, down_far)

    expert_ids = jnp.arange(experts, dtype=jnp.int32)
    combine = jnp.sum(
        gates.reshape(tokens, -1)[..., None]
        * (routes.reshape(tokens, -1)[..., None] == expert_ids).astype(F32),
        axis=1,
    )
    pre, middle, result, grad_y, grad_y_t, square = experts_forward(
        float(tokens * shards * contexts),
        normed_two,
        combine,
        valid.reshape(tokens, 1).astype(F32),
        count,
        gate_ws,
        up_ws,
        down_ws,
        hidden,
        teacher.reshape(tokens, width),
    )
    expert_grads, dn_part = experts_backward(grad_y, combine, gate_ws, up_ws, down_ws, pre)
    sums, grad_inputs, tail = back(
        contexts, trees, gains, w_query, key_matrix, value_matrix, qkv_far, w_out, out_far, q,
        attended, lse, packed_all, square, dn_part, hidden, grad_y, x, normed_t, normed_two_t,
        grad_y_t, expert_grads, middle, kv,
    )
    final_query, final_out, final_key, final_value = unpack_attention(
        sums, w_query.shape[1], key_matrix.shape[1]
    )
    final_gate, final_up, final_down = unpack(sums, experts // 2)
    return (
        tail[2, 0] / (count[0, 0] * width),
        result.reshape(trees, rows, width),
        grad_inputs.reshape(trees, rows, width),
        tail[0],
        final_query,
        final_key,
        final_value,
        final_out,
        tail[1],
        final_gate,
        final_up,
        final_down,
    )


def solution(mesh):
    return jax.shard_map(
        local,
        mesh=mesh,
        in_specs=(
            P("shard", "context", None),
            P("shard", "context"),
            P("shard", "context", None),
            P("shard", "context", None),
            P("shard", "context"),
            P("shard", "context", None),
            P("shard"),
            P("shard", "tensor"),
            P("shard", "tensor"),
            P("shard", "tensor"),
            P("tensor", "shard"),
            P("shard"),
            P(None, "shard", "tensor"),
            P(None, "shard", "tensor"),
            P(None, "tensor", "shard"),
        ),
        out_specs=(
            P(),
            P("shard", "context", None),
            P("shard", "context", None),
            P("shard"),
            P("shard", "tensor"),
            P("shard", "tensor"),
            P("shard", "tensor"),
            P("tensor", "shard"),
            P("shard"),
            P(None, "shard", "tensor"),
            P(None, "shard", "tensor"),
            P(None, "tensor", "shard"),
        ),
        check_vma=False,
    )
```

```python
import functools
import math

import jax
import jax.numpy as jnp
from jax import lax
from jax.experimental import pallas as pl
from jax.experimental.pallas import tpu as pltpu
from jax.sharding import PartitionSpec as P

HEAD = 64
EPS = 1e-05
BF = jnp.bfloat16
F32 = jnp.float32
MESH = pl.DeviceIdType.MESH
VMEM_LIMIT = 56 * 1024 * 1024
UNIT = 2
COST = pl.CostEstimate(flops=1, bytes_accessed=1, transcendentals=0)


def matmul(left, right):
    return jnp.dot(left, right, preferred_element_type=F32)


def contract_first(left, right):
    return lax.dot_general(left, right, (((0,), (0,)), ((), ())), preferred_element_type=F32)


def contract_last(left, right):
    return lax.dot_general(left, right, (((1,), (1,)), ((), ())), preferred_element_type=F32)


def column(block, index):
    lane = lax.broadcasted_iota(jnp.int32, block.shape, 1)
    return jnp.sum(jnp.where(lane == index, block, 0.0), axis=1, keepdims=True)


def experts_backward_kernel(
    gy_ref, c_ref, g0, g1, u0, u1, d0, d1, pre_hbm, grads_hbm, dn_ref,
    wide, tall, grads, pre_buf, weight_sem, pre_sem, out_sem,
):
    pairs, tokens = pre_hbm.shape[0], gy_ref.shape[0]
    half, ff = g0.shape[1], g0.shape[2]
    tile = 256

    def weight_loads(p):
        copies = []
        for side, gate, up, down in ((0, g0, u0, d0), (1, g1, u1, d1)):
            features = pl.ds(side * half, half)
            for a in range(2):
                e = 2 * p + a
                for source, target in (
                    (gate, wide.at[features, pl.ds(pl.multiple_of(2 * e * ff, 128), ff)]),
                    (up, wide.at[features, pl.ds(pl.multiple_of((2 * e + 1) * ff, 128), ff)]),
                    (down, tall.at[p, pl.ds(a * ff, ff), features]),
                ):
                    copies.append(
                        pltpu.make_async_copy(
                            source.at[e], target, weight_sem.at[p, len(copies)]
                        )
                    )
        return copies

    def pre_load(p):
        return pltpu.make_async_copy(
            pre_hbm.at[p], pre_buf.at[lax.rem(p, 2)], pre_sem.at[lax.rem(p, 2)]
        )

    def span(p):
        return pl.ds(pl.multiple_of(p * 4 * ff, 128), 4 * ff)

    def store(p):
        return pltpu.make_async_copy(grads.at[:, span(p)], grads_hbm.at[p], out_sem.at[p])

    for copy in weight_loads(0):
        copy.start()
    pre_load(0).start()

    @pl.loop(1, pairs)
    def _(p):
        for copy in weight_loads(p):
            copy.start()

    @pl.loop(0, pairs)
    def _(p):
        @pl.when(p + 1 < pairs)
        def _():
            pre_load(p + 1).start()

        for copy in weight_loads(p):
            copy.wait()
        pre_load(p).wait()
        slot = lax.rem(p, 2)
        grad_middle = contract_last(gy_ref[...], tall[p])
        pieces = []
        for a in range(2):
            gate = pre_buf[slot, :, 2 * a * ff : (2 * a + 1) * ff].astype(F32)
            up = pre_buf[slot, :, (2 * a + 1) * ff : (2 * a + 2) * ff].astype(F32)
            weight = column(c_ref[...], 2 * p + a)
            gm = weight * grad_middle[:, a * ff : (a + 1) * ff]
            sig = jax.nn.sigmoid(gate)
            pieces.append((gm * up * (sig + gate * sig * (1.0 - sig))).astype(BF))
            pieces.append((gm * gate * sig).astype(BF))
        grads[:, span(p)] = jnp.concatenate(pieces, axis=1)
        store(p).start()

    @pl.loop(0, 2 * half // tile)
    def _(index):
        rows = pl.ds(pl.multiple_of(index * tile, tile), tile)
        dn_ref[:, rows] = contract_last(grads[...], wide[rows, :]).astype(BF)

    @pl.loop(0, pairs)
    def _(p):
        store(p).wait()


def experts_backward(grad_y, combine, gates, ups, downs, pre):
    tokens, width = grad_y.shape
    experts, half, ff = gates[0].shape
    pairs = experts // 2
    vmem, dma = pltpu.VMEM, pltpu.SemaphoreType.DMA
    anywhere = pl.BlockSpec(memory_space=pl.ANY)
    near_memory = pl.BlockSpec(memory_space=pltpu.VMEM)
    return pl.pallas_call(
        experts_backward_kernel,
        out_shape=(
            jax.ShapeDtypeStruct((pairs, tokens, 4 * ff), BF),
            jax.ShapeDtypeStruct((tokens, width), BF),
        ),
        in_specs=[near_memory] * 2 + [anywhere] * 7,
        out_specs=(anywhere, near_memory),
        scratch_shapes=[
            vmem((width, 2 * experts * ff), BF),
            vmem((pairs, 2 * ff, width), BF),
            vmem((tokens, 2 * experts * ff), BF),
            vmem((2, tokens, 4 * ff), BF),
            dma((pairs, 12)),
            dma((2,)),
            dma((pairs,)),
        ],
        compiler_params=pltpu.CompilerParams(vmem_limit_bytes=60 * 1024 * 1024),
        cost_estimate=COST,
        name="experts_backward",
    )(grad_y, combine, *gates, *ups, *downs, pre)


def unpack_kernel(slabs_ref, gate_ref, up_ref, down_ref):
    for a in range(2):
        gate_ref[a] = slabs_ref[a].astype(F32)
        up_ref[a] = slabs_ref[2 + a].astype(F32)
        down_ref[a] = slabs_ref[4 + a].T.astype(F32)


def unpack(slabs, steps):
    _, half, ff = slabs.shape
    wide = jax.ShapeDtypeStruct((2 * steps, half, ff), F32)
    tall = jax.ShapeDtypeStruct((2 * steps, ff, half), F32)
    return pl.pallas_call(
        unpack_kernel,
        out_shape=(wide, wide, tall),
        grid=(steps,),
        in_specs=[pl.BlockSpec((6, half, ff), lambda i: (i, 0, 0))],
        out_specs=[pl.BlockSpec((2, half, ff), lambda i: (i, 0, 0))] * 2
        + [pl.BlockSpec((2, ff, half), lambda i: (i, 0, 0))],
        compiler_params=pltpu.CompilerParams(vmem_limit_bytes=VMEM_LIMIT),
        cost_estimate=COST,
        name="unpack",
    )(slabs)


def unpack_attention_kernel(
    width, slabs_ref, tail_ref, count_ref, q_ref, out_ref, k_ref, v_ref, gain1_ref, gain2_ref, loss_ref
):
    gain1_ref[...] = tail_ref[0:1, :].reshape(gain1_ref.shape)
    gain2_ref[...] = tail_ref[1:2, :].reshape(gain2_ref.shape)
    loss_ref[...] = tail_ref[2:3, 0:1] / (count_ref[...] * width)
    ff = slabs_ref.shape[2]
    at = 0
    for ref, turn in ((q_ref, False), (out_ref, True), (k_ref, False), (v_ref, False)):
        for c in range(ref.shape[0 if turn else 1] // ff):
            value = slabs_ref[at].astype(F32)
            if turn:
                ref[c * ff : (c + 1) * ff, :] = value.T
            else:
                ref[:, c * ff : (c + 1) * ff] = value
            at += 1


def unpack_attention(slabs, tail, count, query_cols, key_cols):
    total, rows, ff = slabs.shape
    number = 2 * (query_cols + key_cols) // ff
    shapes = (
        (rows, query_cols), (query_cols, rows), (rows, key_cols), (rows, key_cols),
        (rows,), (rows,), (1, 1),
    )
    return pl.pallas_call(
        functools.partial(unpack_attention_kernel, 2 * rows),
        out_shape=tuple(jax.ShapeDtypeStruct(shape, F32) for shape in shapes),
        grid=(1,),
        in_specs=[
            pl.BlockSpec((number, rows, ff), lambda i: (total // number - 1, 0, 0)),
            pl.BlockSpec(tail.shape, lambda i: (0, 0)),
            pl.BlockSpec((1, 1), lambda i: (0, 0)),
        ],
        out_specs=[
            pl.BlockSpec(shape, (lambda i: (0, 0)) if len(shape) == 2 else (lambda i: (0,)))
            for shape in shapes
        ],
        compiler_params=pltpu.CompilerParams(vmem_limit_bytes=VMEM_LIMIT),
        cost_estimate=COST,
        name="unpack_attention",
    )(slabs, tail, count)


def inverse_norm(near, far):
    count = near.shape[1] + far.shape[1]
    squares = jnp.sum(near * near, axis=1, keepdims=True) + jnp.sum(far * far, axis=1, keepdims=True)
    return lax.rsqrt(squares / count + EPS)


def halves(ref, rows, shard):
    half = ref.shape[1] // 2
    own = pl.ds(pl.multiple_of(shard * half, 128), half)
    far = pl.ds(pl.multiple_of((1 - shard) * half, 128), half)
    return ref[rows, own].astype(F32), ref[rows, far].astype(F32)


def put_halves(ref, rows, shard, near, far):
    half = ref.shape[1] // 2
    ref[rows, pl.ds(pl.multiple_of(shard * half, 128), half)] = near.astype(ref.dtype)
    ref[rows, pl.ds(pl.multiple_of((1 - shard) * half, 128), half)] = far.astype(ref.dtype)


def norm_backward(near, far, inverse, gain, grads):
    half = near.shape[1]
    near_scaled = grads[:, :half] * gain[:, :half]
    far_scaled = grads[:, half:] * gain[:, half:]
    along = (
        jnp.sum(near_scaled * near, axis=1, keepdims=True)
        + jnp.sum(far_scaled * far, axis=1, keepdims=True)
    ) / (2 * half)
    cube = inverse * inverse * inverse * along
    return (
        inverse * near_scaled - near * cube,
        inverse * far_scaled - far * cube,
        jnp.sum(grads[:, :half] * near * inverse, axis=0, keepdims=True),
        jnp.sum(grads[:, half:] * far * inverse, axis=0, keepdims=True),
    )


CHUNK = 128


def tensor_peers():
    t = lax.axis_index("tensor")
    low, high = lax.rem(t, 2), lax.rem(t // 2, 2)
    return low, {"tensor": t + 1 - 2 * low}, {"tensor": t + 2 - 4 * high}


def greet(peers):
    barrier = pltpu.get_barrier_semaphore()
    for peer in peers:
        pl.semaphore_signal(barrier, inc=1, device_id=peer, device_id_type=MESH)
    pl.semaphore_wait(barrier, len(peers))


def sum_over_tensor(part, total, arrived, mine, other, sems, consume, between=lambda c: None):
    send1, recv1, send2, recv2, send3, recv3 = sems
    low, near, far = tensor_peers()
    chunks = arrived.shape[0]
    half = chunks * CHUNK

    def rows(side, c):
        return pl.ds(pl.multiple_of(side * half + c * CHUNK, CHUNK), CHUNK)

    def give(c):
        return pltpu.make_async_remote_copy(
            part.at[rows(1 - low, c)], arrived.at[c], send1.at[c], recv1.at[c],
            device_id=near, device_id_type=MESH,
        )

    def swap(c):
        return pltpu.make_async_remote_copy(
            mine.at[c], other.at[c], send2.at[c], recv2.at[c], device_id=far, device_id_type=MESH
        )

    def back(c):
        return pltpu.make_async_remote_copy(
            total.at[rows(low, c)], total.at[rows(low, c)], send3.at[c], recv3.at[c],
            device_id=near, device_id_type=MESH,
        )

    @pl.loop(0, chunks)
    def _(c):
        give(c).start()

    @pl.loop(0, chunks)
    def _(c):
        give(c).wait_recv()
        mine[c] = (part[rows(low, c), :].astype(F32) + arrived[c].astype(F32)).astype(BF)
        swap(c).start()

    @pl.loop(0, chunks)
    def _(c):
        between(c)
        swap(c).wait_recv()
        total[rows(low, c), :] = (mine[c].astype(F32) + other[c].astype(F32)).astype(BF)
        back(c).start()
        consume(pl.multiple_of(low * half + c * CHUNK, CHUNK))
        back(c).wait_recv()
        consume(pl.multiple_of((1 - low) * half + c * CHUNK, CHUNK))

    @pl.loop(0, chunks)
    def _(c):
        give(c).wait_send()
        swap(c).wait_send()
        back(c).wait_send()


def sum_scratch(tokens, width):
    chunks = tokens // 2 // CHUNK
    piece = pltpu.VMEM((chunks, CHUNK, width), BF)
    return [pltpu.VMEM((tokens, width), BF)] + [piece] * 3 + [
        pltpu.SemaphoreType.DMA((chunks,))
    ] * 6


def fill_columns(target, refs):
    at = 0
    for ref in refs:
        target[:, at : at + ref.shape[1]] = ref[...]
        at += ref.shape[1]


def front_kernel(
    contexts, trees, x_ref, seg_ref, valid_ref, routes_ref, gates_ref, gain1_ref, gain2_ref, wq, wk, wv, wout, w_gate, w_up, w_down,
    packed_all, all_gains, far_qkv, far_out, far_gate, far_up, far_down,
    q_ref, kv_out, nt_out, o_ref, lse_ref, h_out, n2_out, n2t_out, count_ref, c_ref,
    packed, gains, wqkv, far_gains, kv_all, nt_ref, h_ref, n2_ref, n2t_ref,
    normed, bias, tops, norms, sums, part, total, arrived, mine, other,
    ysend, yrecv, rsend, rrecv, psend, precv, ksend, krecv, out_sem, *sems
):
    i = lax.axis_index("context")
    shard = lax.axis_index("shard")
    parity = lax.rem(i, 2)
    tokens, width = x_ref.shape
    half = width // 2
    rows = tokens // trees
    heads = q_ref.shape[1] // HEAD
    kv_width = kv_all.shape[2] // 2
    per_group = q_ref.shape[1] // kv_width
    other_shard = {"shard": 1 - shard}
    partner = {"context": i + 1 - 2 * parity}
    right = {"context": lax.rem(i + 1, contexts)}
    _, near, far = tensor_peers()
    fill_columns(wqkv, (wq, wk, wv))
    segment = seg_ref[...]
    last = jnp.where(
        segment == 0, 1 << 20, jnp.where(lax.rem(segment, 3) == 1, segment + 2, segment)
    )
    packed[...] = jnp.zeros_like(packed)
    packed[0:trees, :] = segment.astype(F32)
    packed[trees : 2 * trees, :] = last.astype(F32)
    packed[2 * trees + 1 : 3 * trees + 1, :] = valid_ref[...].astype(F32)
    counted = jnp.sum(jnp.sum(valid_ref[...].astype(F32), axis=1, keepdims=True), axis=0, keepdims=True)
    gains[...] = jnp.broadcast_to(counted, gains.shape)
    gains[0:1, :] = gain1_ref[...].reshape(1, half)
    gains[1:2, :] = gain2_ref[...].reshape(1, half)
    greet(
        [other_shard, near, far]
        + [{"context": lax.rem(i + c, contexts)} for c in range(1, contexts)]
    )

    def half_span(ref, axis):
        size = ref.shape[axis] // 2
        return pl.ds(pl.multiple_of(parity * size, size), size)

    experts = w_gate.shape[0]
    shared = experts // 8
    own_count = (experts - shared) // 2
    moves = [
        (wqkv.at[half_span(wqkv, 0)], far_qkv.at[half_span(wqkv, 0)]),
        (wout.at[:, half_span(wout, 1)], far_out.at[:, half_span(wout, 1)]),
    ]
    first = (own_count + 1) // 2
    for begin, size in (
        (parity * own_count, first),
        (parity * own_count + first, own_count - first),
        (2 * own_count, shared),
    ):
        span = pl.ds(begin, size)
        for source, target in ((w_gate, far_gate), (w_up, far_up), (w_down, far_down)):
            moves.append((source.at[span], target.at[span]))
    relays = len(moves) - 3

    def direct(m):
        source, target = moves[m]
        return pltpu.make_async_remote_copy(
            source, target, ysend.at[m], yrecv.at[m],
            device_id=other_shard, device_id_type=MESH,
        )

    def relay(m):
        target = moves[m][1]
        return pltpu.make_async_remote_copy(
            target, target, rsend.at[m], rrecv.at[m], device_id=partner, device_id_type=MESH
        )

    def pass_on(m):
        direct(m).wait_recv()
        relay(m).start()

    count = len(moves)
    gain_copy = pltpu.make_async_remote_copy(
        gains, far_gains, ysend.at[count], yrecv.at[count],
        device_id=other_shard, device_id_type=MESH,
    )

    def tell(c, slot):
        return pltpu.make_async_remote_copy(
            packed, packed_all.at[slot], psend.at[c], precv.at[slot],
            device_id={"context": c}, device_id_type=MESH,
        )

    def lift(j):
        return pltpu.make_async_remote_copy(
            kv_all.at[j], kv_all.at[j], ksend.at[j], krecv.at[j],
            device_id=right, device_id_type=MESH,
        )

    outs = [
        pltpu.make_async_copy(src, dst, out_sem.at[at])
        for at, (src, dst) in enumerate((
            (nt_ref, nt_out), (kv_all, kv_out), (h_ref, h_out), (n2_ref, n2_out), (n2t_ref, n2t_out),
        ))
    ]
    gain_copy.start()
    for m in range(count):
        direct(m).start()

    gain_copy.wait_recv()
    packed[2 * trees : 2 * trees + 1, :] = gains[2:3, :rows] + far_gains[2:3, :rows]
    packed_all[i] = packed[...]

    @pl.loop(0, contexts)
    def _(c):
        @pl.when(c != i)
        def _():
            tell(c, i).start()

    all_gains[:, :half] = gains[...]
    all_gains[:, half:] = far_gains[...]
    tile = 128

    @pl.loop(0, tokens // tile)
    def _(index):
        span = pl.ds(pl.multiple_of(index * tile, tile), tile)
        own_x, far_x = halves(x_ref, span, shard)
        inverse = inverse_norm(own_x, far_x)
        own_x = (own_x * inverse * gains[0:1, :]).astype(BF)
        far_x = (far_x * inverse * far_gains[0:1, :]).astype(BF)
        normed[span, :half] = own_x
        normed[span, half:] = far_x
        nt_ref[:half, span] = own_x.T
        nt_ref[half:, span] = far_x.T

    outs[0].start()
    pack_t = packed[...].T
    lane = lax.broadcasted_iota(jnp.int32, (rows, c_ref.shape[1]), 1).astype(F32)
    for tree in range(trees):
        weights = jnp.where(lane == float(experts), column(pack_t, 2 * trees + 1 + tree), 0.0)
        routes = routes_ref[tree].astype(F32).T
        gates = gates_ref[tree].T
        for at in range(routes.shape[1]):
            weights = weights + jnp.where(
                routes[:, at : at + 1] == lane, gates[:, at : at + 1], 0.0
            )
        c_ref[tree * rows : (tree + 1) * rows, :] = weights
    pass_on(0)
    pass_on(1)
    relay(0).wait_recv()
    qkv = matmul(normed[:, :half], wqkv[...]) + matmul(normed[:, half:], far_qkv[...])
    q_ref[...] = qkv[:, : q_ref.shape[1]].astype(BF)
    kv_all[i] = qkv[:, q_ref.shape[1] :].astype(BF)

    @pl.when(i < contexts - 1)
    def _():
        lift(i).start()

    tops[...] = jnp.full_like(tops, -1e30)
    norms[...] = jnp.zeros_like(norms)
    sums[...] = jnp.zeros_like(sums)

    @pl.loop(0, contexts)
    def _(c):
        @pl.when(c != i)
        def _():
            tell(i, c).wait_recv()

    counted = packed_all[0, 2 * trees : 2 * trees + 1, 0:1]
    for c in range(1, contexts):
        counted = counted + packed_all[c, 2 * trees : 2 * trees + 1, 0:1]
    count_ref[...] = counted

    @pl.loop(0, contexts)
    def _(d):
        @pl.when(d <= i)
        def _():
            j = i - d

            @pl.when(d > 0)
            def _():
                lift(j).wait_recv()

                @pl.when(i < contexts - 1)
                def _():
                    lift(j).start()

            @pl.loop(0, trees)
            def _(tree):
                span = pl.ds(pl.multiple_of(tree * rows, rows), rows)
                key_pos = j * rows + lax.broadcasted_iota(jnp.int32, (rows, rows), 1)
                query_pos = i * rows + lax.broadcasted_iota(jnp.int32, (rows, rows), 0)
                last = packed_all[j, pl.ds(trees + tree, 1), :]
                allowed = (key_pos <= query_pos) & (column(pack_t, tree) <= last)
                bias[...] = jnp.where(allowed, 0.0, -2e30)
                for head in range(heads):
                    group = head // per_group
                    cols = slice(head * HEAD, (head + 1) * HEAD)
                    keys = kv_all[j, span, group * HEAD : (group + 1) * HEAD]
                    values = kv_all[
                        j, span, kv_width + group * HEAD : kv_width + (group + 1) * HEAD
                    ]
                    scores = contract_last(q_ref[span, cols], keys) * 0.125 + bias[...]
                    old = tops[span, head : head + 1]
                    top = jnp.maximum(old, jnp.max(scores, axis=1, keepdims=True))
                    weights = jnp.exp(scores - top)
                    shrink = jnp.exp(old - top)
                    tops[span, head : head + 1] = top
                    norms[span, head : head + 1] = norms[span, head : head + 1] * shrink + jnp.sum(
                        weights, axis=1, keepdims=True
                    )
                    sums[span, cols] = sums[span, cols] * shrink + matmul(
                        weights.astype(BF), values
                    )

        @pl.when(d == 0)
        def _():
            pass_on(2)

        @pl.when(d == min(2, contexts - 1))
        def _():
            pass_on(3)

    for head in range(heads):
        cols = slice(head * HEAD, (head + 1) * HEAD)
        o_ref[:, cols] = (sums[:, cols] / norms[:, head : head + 1]).astype(BF)
    lse = tops[...] + jnp.log(norms[...] + jnp.where(norms[...] == 0.0, 1.0, 0.0))
    for tree in range(trees):
        lse_ref[tree] = lse[tree * rows : (tree + 1) * rows].T[: lse_ref.shape[1]]
    outs[1].start()
    relay(1).wait_recv()
    part[:, :half] = matmul(o_ref[...], wout[...]).astype(BF)
    part[:, half:] = matmul(o_ref[...], far_out[...]).astype(BF)

    def consume(row):
        span = pl.ds(row, CHUNK)
        own_x, far_x = halves(x_ref, span, shard)
        own_x = own_x + total[span, :half].astype(F32)
        far_x = far_x + total[span, half:].astype(F32)
        h_ref[span, :half] = own_x
        h_ref[span, half:] = far_x
        inverse = inverse_norm(own_x, far_x)
        own_x = (own_x * inverse * gains[1:2, :]).astype(BF)
        far_x = (far_x * inverse * far_gains[1:2, :]).astype(BF)
        n2_ref[span, :half] = own_x
        n2_ref[span, half:] = far_x
        n2t_ref[:half, span] = own_x.T
        n2t_ref[half:, span] = far_x.T

    chunks = arrived.shape[0]

    def between(c):
        for at in range(chunks):

            @pl.when(c == at)
            def _():
                pass_on(4 + at)

    sum_over_tensor(part, total, arrived, mine, other, sems, consume, between)
    for copy in outs[2:]:
        copy.start()
    for m in range(4 + chunks, relays):
        pass_on(m)
    for m in range(2, relays):
        relay(m).wait_recv()
    for m in range(relays, count):
        direct(m).wait_recv()
    for m in range(count):
        direct(m).wait_send()
        if m < relays:
            relay(m).wait_send()
    gain_copy.wait_send()
    for copy in outs:
        copy.wait()

    @pl.loop(0, contexts)
    def _(c):
        @pl.when(c != i)
        def _():
            tell(c, i).wait_send()

        @pl.when((c <= i) & (i < contexts - 1))
        def _():
            lift(c).wait_send()


def front(
    contexts, trees, x, segments, valid, routes, gates, gain1, gain2, w_query, w_key, w_value,
    w_out, w_gate, w_up, w_down,
):
    tokens, width = x.shape
    half, rows = width // 2, tokens // trees
    cols = w_out.shape[0]
    both = w_key.shape[1] + w_value.shape[1]
    anywhere = pl.BlockSpec(memory_space=pl.ANY)
    near_memory = pl.BlockSpec(memory_space=pltpu.VMEM)
    shape, vmem, dma = jax.ShapeDtypeStruct, pltpu.VMEM, pltpu.SemaphoreType.DMA
    buffers = sum_scratch(tokens, width)
    return pl.pallas_call(
        functools.partial(front_kernel, contexts, trees),
        out_shape=(
            shape((contexts, 8, rows), F32),
            shape((8, width), F32),
            shape((half, cols + both), BF),
            *(shape(ref.shape, BF) for ref in (w_out, w_gate, w_up, w_down)),
            shape((tokens, cols), BF),
            shape((contexts, tokens, both), BF),
            shape((width, tokens), BF),
            shape((tokens, cols), BF),
            shape((trees, 8, rows), F32),
            shape((tokens, width), F32),
            shape((tokens, width), BF),
            shape((width, tokens), BF),
            shape((1, 1), F32),
            shape((tokens, 128), F32),
        ),
        in_specs=[near_memory] * 11 + [anywhere] * 3,
        out_specs=(near_memory,) * 4
        + (anywhere,) * 3
        + (near_memory, anywhere, anywhere, near_memory, near_memory)
        + (anywhere,) * 3
        + (near_memory,) * 2,
        scratch_shapes=[
            vmem((8, rows), F32),
            vmem((8, half), F32),
            vmem((half, cols + both), BF),
            vmem((8, half), F32),
            vmem((contexts, tokens, both), BF),
            vmem((width, tokens), BF),
            vmem((tokens, width), F32),
            vmem((tokens, width), BF),
            vmem((width, tokens), BF),
            vmem((tokens, width), BF),
            vmem((rows, rows), F32),
            vmem((tokens, 128), F32),
            vmem((tokens, 128), F32),
            vmem((tokens, cols), F32),
            vmem((tokens, width), BF),
        ]
        + buffers[:4]
        + [dma((12,)), dma((12,)), dma((8,)), dma((8,))]
        + [dma((contexts,))] * 4
        + [dma((5,))]
        + buffers[4:],
        compiler_params=pltpu.CompilerParams(
            collective_id=2, has_side_effects=True, vmem_limit_bytes=60 * 1024 * 1024
        ),
        cost_estimate=COST,
        name="front",
    )(
        x, segments, valid, routes, gates, gain1, gain2, w_query, w_key, w_value, w_out,
        w_gate, w_up, w_down,
    )


def experts_forward_kernel(
    token_total, n_ref, c_ref, count_ref, g0, g1, u0, u1, d0, d1, h_hbm, teacher_hbm,
    pre_hbm, cm_hbm, y_hbm, low_hbm, lowt_hbm, square_ref,
    wide, tall, pre_buf, cm_all, part, h_ref, teacher_ref, y_ref, low_ref, lowt_ref,
    weight_sem, in_sem, pre_sem, out_sem, total, arrived, mine, other,
    send1, recv1, send2, recv2, send3, recv3,
):
    tokens, width = h_ref.shape
    half = width // 2
    pairs, ff = wide.shape[0], g0.shape[2]
    chunks = arrived.shape[0]
    shard = lax.axis_index("shard")
    low_side, near, far = tensor_peers()
    loads = [
        pltpu.make_async_copy(h_hbm, h_ref, in_sem.at[0]),
        pltpu.make_async_copy(teacher_hbm, teacher_ref, in_sem.at[1]),
    ]

    def weight_loads(p):
        copies = []
        for side, gate, up, down in ((0, g0, u0, d0), (1, g1, u1, d1)):
            features = pl.ds(side * half, half)
            for a in range(2):
                for source, target in (
                    (gate, wide.at[p, features, pl.ds(2 * a * ff, ff)]),
                    (up, wide.at[p, features, pl.ds((2 * a + 1) * ff, ff)]),
                    (down, tall.at[pl.ds((2 * p + a) * ff, ff), features]),
                ):
                    copies.append(
                        pltpu.make_async_copy(
                            source.at[2 * p + a], target, weight_sem.at[p, len(copies)]
                        )
                    )
        return copies

    @pl.loop(0, pairs)
    def _(p):
        for copy in weight_loads(p):
            copy.start()

    for copy in loads:
        copy.start()
    square_ref[...] = jnp.zeros_like(square_ref)
    greet([near, far])

    def rows(side, c):
        return pl.ds(pl.multiple_of((2 * c + side) * CHUNK, CHUNK), CHUNK)

    def both_rows(c):
        return pl.ds(pl.multiple_of(2 * c * CHUNK, 2 * CHUNK), 2 * CHUNK)

    def remote(src, dst, send, recv, to):
        return pltpu.make_async_remote_copy(
            src, dst, send, recv, device_id=to, device_id_type=MESH
        )

    def give(c):
        return remote(part.at[rows(1 - low_side, c)], arrived.at[c], send1.at[c], recv1.at[c], near)

    def swap(c):
        return remote(mine.at[c], other.at[c], send2.at[c], recv2.at[c], far)

    def back_copy(c):
        span = rows(low_side, c)
        return remote(total.at[span], total.at[span], send3.at[c], recv3.at[c], near)

    def kept(c, p):
        slot = lax.rem(p, 2)
        return (
            pltpu.make_async_copy(
                pre_buf.at[slot], pre_hbm.at[p, both_rows(c)], pre_sem.at[slot, 0]
            ),
            pltpu.make_async_copy(
                cm_all.at[:, pl.ds(pl.multiple_of(p * 2 * ff, 128), 2 * ff)],
                cm_hbm.at[p, both_rows(c)],
                pre_sem.at[slot, 1],
            ),
        )

    @pl.loop(0, chunks)
    def _(c):
        span = both_rows(c)

        @pl.loop(0, pairs)
        def _(p):
            @pl.when(c == 0)
            def _():
                for copy in weight_loads(p):
                    copy.wait()

            slot = lax.rem(p, 2)

            @pl.when(p >= 2)
            def _():
                for copy in kept(c, p - 2):
                    copy.wait()

            hidden = matmul(n_ref[span, :], wide[p])
            pre_buf[slot] = hidden.astype(BF)
            pieces = []
            for a in range(2):
                gate = hidden[:, 2 * a * ff : (2 * a + 1) * ff]
                up = hidden[:, (2 * a + 1) * ff : (2 * a + 2) * ff]
                weight = column(c_ref[span, :], 2 * p + a)
                pieces.append((weight * (gate * jax.nn.sigmoid(gate) * up)).astype(BF))
            cm_all[:, pl.ds(pl.multiple_of(p * 2 * ff, 128), 2 * ff)] = jnp.concatenate(
                pieces, axis=1
            )
            for copy in kept(c, p):
                copy.start()

        for p in (pairs - 2, pairs - 1):
            for copy in kept(c, p):
                copy.wait()
        part[span, :] = matmul(cm_all[...], tall[...]).astype(BF)
        give(c).start()
        give(c).wait_recv()
        mine[c] = (part[rows(low_side, c), :].astype(F32) + arrived[c].astype(F32)).astype(BF)
        swap(c).start()

    def stores(at):
        span = pl.ds(pl.multiple_of(at * CHUNK, CHUNK), CHUNK)
        return [
            pltpu.make_async_copy(y_ref.at[span], y_hbm.at[span], out_sem.at[0, at]),
            pltpu.make_async_copy(low_ref.at[span], low_hbm.at[span], out_sem.at[1, at]),
            pltpu.make_async_copy(lowt_ref.at[:, span], lowt_hbm.at[:, span], out_sem.at[2, at]),
        ]

    def consume(side, c):
        span = rows(side, c)
        mask = column(c_ref[span, :], 2 * pairs)
        factor = token_total / count_ref[...] * mask
        near_t, far_t = halves(teacher_ref, span, shard)
        near_y = h_ref[span, :half] + total[span, :half].astype(F32)
        far_y = h_ref[span, half:] + total[span, half:].astype(F32)
        put_halves(y_ref, span, shard, near_y, far_y)
        for begin, error in ((0, near_y - near_t), (half, far_y - far_t)):
            features = slice(begin, begin + half)
            squares = mask * jnp.sum(error * error, axis=1, keepdims=True)
            square_ref[...] += jnp.sum(squares, axis=0, keepdims=True)
            grad = (factor * error).astype(BF)
            low_ref[span, features] = grad
            lowt_ref[features, span] = grad.T
        for copy in stores(2 * c + side):
            copy.start()

    for copy in loads:
        copy.wait()

    @pl.loop(0, chunks)
    def _(c):
        swap(c).wait_recv()
        total[rows(low_side, c), :] = (mine[c].astype(F32) + other[c].astype(F32)).astype(BF)
        back_copy(c).start()
        consume(low_side, c)
        back_copy(c).wait_recv()
        consume(1 - low_side, c)

    @pl.loop(0, chunks)
    def _(c):
        give(c).wait_send()
        swap(c).wait_send()
        back_copy(c).wait_send()
        for side in range(2):
            for copy in stores(2 * c + side):
                copy.wait()


def experts_forward(token_total, normed, combine, count, gates, ups, downs, hidden, teacher):
    tokens, width = hidden.shape
    experts, half, ff = gates[0].shape
    pairs = experts // 2
    shape, vmem, dma = jax.ShapeDtypeStruct, pltpu.VMEM, pltpu.SemaphoreType.DMA
    anywhere = pl.BlockSpec(memory_space=pl.ANY)
    near_memory = pl.BlockSpec(memory_space=pltpu.VMEM)
    return pl.pallas_call(
        functools.partial(experts_forward_kernel, token_total),
        out_shape=(
            shape((pairs, tokens, 4 * ff), BF),
            shape((pairs, tokens, 2 * ff), BF),
            shape((tokens, width), BF),
            shape((tokens, width), BF),
            shape((width, tokens), BF),
            shape((1, 1), F32),
        ),
        in_specs=[near_memory] * 3 + [anywhere] * 8,
        out_specs=(anywhere,) * 5 + (near_memory,),
        scratch_shapes=[
            vmem((pairs, width, 4 * ff), BF),
            vmem((experts * ff, width), BF),
            vmem((2, 2 * CHUNK, 4 * ff), BF),
            vmem((2 * CHUNK, experts * ff), BF),
            vmem((tokens, width), BF),
            vmem((tokens, width), F32),
            vmem((tokens, width), BF),
            vmem((tokens, width), BF),
            vmem((tokens, width), BF),
            vmem((width, tokens), BF),
            dma((pairs, 12)),
            dma((2,)),
            dma((2, 2)),
            dma((3, tokens // CHUNK)),
        ]
        + sum_scratch(tokens, width),
        compiler_params=pltpu.CompilerParams(
            collective_id=3, has_side_effects=True, vmem_limit_bytes=60 * 1024 * 1024
        ),
        cost_estimate=COST,
        name="experts_forward",
    )(normed, combine, count, *gates, *ups, *downs, hidden, teacher)


def back_kernel(
    contexts, trees, lag, gains, wq, wk, wv, far_qkv, wout, far_out, q_ref, o_ref, lse_ref, packed_all,
    square_ref, part, h_hbm, gy_hbm, x_hbm, nt_hbm, n2t_hbm, gyt_hbm, grads_hbm, cm_hbm, kv_hbm,
    result, out_hbm, tail_ref, own_hbm, far_hbm, came, up_hbm, down_hbm, part2, dkv_part, dkv_came,
    wqkv, scale_ref, tail_own, tail_far, tail_came, tails,
    sums_ring, up_ring, down_ring, came_buf, out_buf, turned, gyt, grads_buf, cm_buf, stage,
    hbuf, chunk_low, chunk_out, my_part, total, arrived, mine, other, other2,
    dat, do_ref, dq_ref, dqs, deltas, bias, kv_buf, dkv_buf, dkv_sum, dkv_add, tile_buf,
    local_sem, ring_sem, tail_sem, tsend, trecv, ysend, yrecv, usend, urecv, dsend, drecv, store_sem, gsend, grecv, *ar_sems
):
    i = lax.axis_index("context")
    shard = lax.axis_index("shard")
    tokens, width = hbuf.shape
    half = width // 2
    rows = tokens // trees
    units = result.shape[0] // UNIT
    slots = lag * (contexts - 1) + 2
    ff = result.shape[2]
    pairs = grads_hbm.shape[0]
    heads = q_ref.shape[1] // HEAD
    kv_width = kv_buf.shape[1] // 2
    per_group = q_ref.shape[1] // kv_width
    low, near, far = tensor_peers()
    has_left, has_right = i > 0, i < contexts - 1
    right = {"context": lax.rem(i + 1, contexts)}
    left = {"context": lax.rem(i + contexts - 1, contexts)}
    other_shard = {"shard": 1 - shard}

    def remote(src, dst, send, recv, to):
        return pltpu.make_async_remote_copy(
            src, dst, send, recv, device_id=to, device_id_type=MESH
        )

    def fetch(*moves):
        copies = [
            pltpu.make_async_copy(src, dst, local_sem.at[at]) for at, (src, dst) in enumerate(moves)
        ]
        for copy in copies:
            copy.start()
        for copy in copies:
            copy.wait()


    def slabs(k):
        return pl.ds(k * UNIT, UNIT)

    def exchange(k):
        return remote(
            far_hbm.at[slabs(k)], came.at[slabs(k)], ysend.at[k], yrecv.at[k], other_shard
        )

    def upward(k, ring):
        return remote(
            ring.at[lax.rem(k, slots)], up_hbm.at[slabs(k)], usend.at[k], urecv.at[k], right
        )

    def downward(k, ring):
        return remote(
            ring.at[lax.rem(k, slots)], down_hbm.at[slabs(k)], dsend.at[k], drecv.at[k], left
        )

    def store(k):
        return pltpu.make_async_copy(
            out_buf.at[lax.rem(k, 2)], result.at[slabs(k)], store_sem.at[lax.rem(k, 2)]
        )

    def add_unit(k):
        u, d = k - lag * i, k - lag * (contexts - 1 - i)
        slot, up_slot, down_slot = (lax.rem(jnp.maximum(at, 0), slots) for at in (k, u, d))
        has_new = k < units
        has_up = has_left & (u >= 0) & (u < units)
        has_down = has_right & (d >= 0) & (d < units)

        def load(at, src, dst):
            return pltpu.make_async_copy(src, dst, ring_sem.at[at])

        def new_loads():
            return (
                load(0, own_hbm.at[slabs(k)], sums_ring.at[slot]),
                load(1, came.at[slabs(k)], came_buf),
            )

        def up_load():
            return load(2, up_hbm.at[slabs(u)], up_ring.at[up_slot])

        def down_load():
            return load(3, down_hbm.at[slabs(d)], down_ring.at[down_slot])

        @pl.when(has_new)
        def _():
            @pl.when((k >= slots) & (i == 0))
            def _():
                upward(k - slots, sums_ring).wait_send()

            @pl.when((k >= slots) & (i == contexts - 1))
            def _():
                downward(k - slots, sums_ring).wait_send()

            exchange(k).wait_recv()
            for copy in new_loads():
                copy.start()

        @pl.when(has_up)
        def _():
            @pl.when(has_right & (u >= slots))
            def _():
                upward(u - slots, up_ring).wait_send()

            upward(u, up_ring).wait_recv()
            up_load().start()

        @pl.when(has_down)
        def _():
            @pl.when(has_left & (d >= slots))
            def _():
                downward(d - slots, down_ring).wait_send()

            downward(d, down_ring).wait_recv()
            down_load().start()

        @pl.when(has_new)
        def _():
            for copy in new_loads():
                copy.wait()
            sums_ring[slot] = (sums_ring[slot].astype(F32) + came_buf[...].astype(F32)).astype(BF)

            @pl.when(i == 0)
            def _():
                upward(k, sums_ring).start()

            @pl.when(i == contexts - 1)
            def _():
                downward(k, sums_ring).start()

        @pl.when(has_up)
        def _():
            up_load().wait()
            up_ring[up_slot] = (
                up_ring[up_slot].astype(F32) + sums_ring[up_slot].astype(F32)
            ).astype(BF)

            @pl.when(has_right)
            def _():
                upward(u, up_ring).start()

        @pl.when(has_down)
        def _():
            down_load().wait()
            down_ring[down_slot] = (
                down_ring[down_slot].astype(F32) + sums_ring[down_slot].astype(F32)
            ).astype(BF)

            @pl.when(has_left)
            def _():
                downward(d, down_ring).start()

        e = k - lag * jnp.maximum(i, contexts - 1 - i)

        @pl.when((e >= 0) & (e < units))
        def _():
            out_slot = lax.rem(e, slots)
            here = lax.rem(e, 2)

            @pl.when(e >= 2)
            def _():
                store(e - 2).wait()

            @pl.when(i == 0)
            def _():
                out_buf[here] = down_ring[out_slot]

            @pl.when(i == contexts - 1)
            def _():
                out_buf[here] = up_ring[out_slot]

            @pl.when(has_left & has_right)
            def _():
                out_buf[here] = (
                    up_ring[out_slot].astype(F32)
                    + (down_ring[out_slot].astype(F32) - sums_ring[out_slot].astype(F32))
                ).astype(BF)

            store(e).start()


    def write_slabs(first, number, products, send=True):
        for part_index, target in ((0, own_hbm), (1, far_hbm)):
            at = 0
            for left_ref, right_value, order in products:
                block = matmul(
                    left_ref[part_index * half : (part_index + 1) * half, :], right_value
                ).astype(BF)
                for c, place in enumerate(order):
                    stage[part_index, at + place] = block[:, c * ff : (c + 1) * ff]
                at += len(order)
        fetch(
            *(
                (stage.at[p, pl.ds(0, number)], target.at[pl.ds(first, number)])
                for p, target in ((0, own_hbm), (1, far_hbm))
            )
        )
        if send:
            for c in range(number // UNIT):
                exchange(first // UNIT + c).start()

    def pair_slabs(p, send=True):
        fetch((grads_hbm.at[p], grads_buf), (cm_hbm.at[p], cm_buf))
        write_slabs(
            p * 6, 6, ((turned, grads_buf[...], (0, 2, 1, 3)), (gyt, cm_buf[...], (0, 1))), send
        )


    chunks = arrived.shape[0]
    low_half = tokens // 2

    def chunk_rows(side, c):
        return pl.ds(pl.multiple_of(side * low_half + c * CHUNK, CHUNK), CHUNK)

    def summing(source, landing, sems):
        send1, recv1, send2, recv2, send3, recv3 = sems

        def give(c):
            return remote(
                source.at[chunk_rows(1 - low, c)], arrived.at[c], send1.at[c], recv1.at[c], near
            )

        def swap(c):
            return remote(mine.at[c], landing.at[c], send2.at[c], recv2.at[c], far)

        def back(c):
            span = chunk_rows(low, c)
            return remote(total.at[span], total.at[span], send3.at[c], recv3.at[c], near)

        def start():
            for c in range(chunks):
                give(c).start()

        def middle():
            fetch(*((source.at[chunk_rows(low, c)], my_part.at[c]) for c in range(chunks)))
            for c in range(chunks):
                give(c).wait_recv()
                mine[c] = (my_part[c].astype(F32) + arrived[c].astype(F32)).astype(BF)
                swap(c).start()

        def finish(c, consume):
            swap(c).wait_recv()
            total[chunk_rows(low, c), :] = (
                mine[c].astype(F32) + landing[c].astype(F32)
            ).astype(BF)
            back(c).start()
            consume(pl.multiple_of(low * low_half + c * CHUNK, CHUNK))

        def finish_other(c, consume):
            back(c).wait_recv()
            consume(pl.multiple_of((1 - low) * low_half + c * CHUNK, CHUNK))

        def drain():
            for c in range(chunks):
                give(c).wait_send()
                swap(c).wait_send()
                back(c).wait_send()

        return start, middle, finish, finish_other, drain

    start1, middle1, finish1, other1, drain1 = summing(part, other, ar_sems[:6])
    start2, middle2, finish2, finish_other2, drain2 = summing(part2, other2, ar_sems[6:])

    def through_second_norm(row):
        span = pl.ds(row, CHUNK)
        fetch((gy_hbm.at[span], chunk_low), (h_hbm.at[span], hbuf.at[span]))
        own_h, far_h = hbuf[span, :half], hbuf[span, half:]
        inverse = inverse_norm(own_h, far_h)
        own_d, far_d, own_scale, far_scale = norm_backward(
            own_h, far_h, inverse, gains[1:2, :], total[span, :].astype(F32)
        )
        scale_ref[1:2, :half] += own_scale
        scale_ref[1:2, half:] += far_scale
        own_d = chunk_low[:, :half].astype(F32) + own_d
        far_d = chunk_low[:, half:].astype(F32) + far_d
        hbuf[span, :half] = own_d
        hbuf[span, half:] = far_d
        own_d = own_d.astype(BF)
        far_d = far_d.astype(BF)
        dat[:half, span] = own_d.T
        dat[half:, span] = far_d.T
        do_ref[span, :] = (
            contract_last(own_d, wout[...]) + contract_last(far_d, far_out[...])
        ).astype(BF)

    def through_first_norm(row):
        span = pl.ds(row, CHUNK)
        fetch((x_hbm.at[span], chunk_low))
        own_x, far_x = halves(chunk_low, slice(None), shard)
        inverse = inverse_norm(own_x, far_x)
        own_d, far_d, own_scale, far_scale = norm_backward(
            own_x, far_x, inverse, gains[0:1, :], total[span, :].astype(F32)
        )
        scale_ref[0:1, :half] += own_scale
        scale_ref[0:1, half:] += far_scale
        put_halves(
            chunk_out, slice(None), shard, hbuf[span, :half] + own_d, hbuf[span, half:] + far_d
        )
        fetch((chunk_out, out_hbm.at[span]))


    def make_deltas():
        @pl.loop(0, trees)
        def _(tree):
            span = pl.ds(pl.multiple_of(tree * rows, rows), rows)
            for head in range(heads):
                cols = slice(head * HEAD, (head + 1) * HEAD)
                product = do_ref[span, cols].astype(F32) * o_ref[span, cols].astype(F32)
                deltas[tree, head] = lax.dot_general(
                    jnp.ones((8, HEAD), F32),
                    product,
                    (((1,), (1,)), ((), ())),
                    precision=lax.Precision.HIGHEST,
                    preferred_element_type=F32,
                )

    def hand(j, tree):
        span = pl.ds(pl.multiple_of(tree * rows, rows), rows)
        return remote(
            dkv_part.at[j, span], dkv_came.at[i, span], gsend.at[j, tree], grecv.at[i, tree],
            {"context": j},
        )

    def taken(c, tree):
        span = pl.ds(pl.multiple_of(tree * rows, rows), rows)
        return remote(
            dkv_part.at[c, span], dkv_came.at[c, span], gsend.at[c, tree], grecv.at[c, tree],
            {"context": c},
        )

    def attention_block(number):
        tree, j = number // contexts, lax.rem(number, contexts)

        @pl.when((number < trees * contexts) & (j <= i))
        def _():
            span = pl.ds(pl.multiple_of(tree * rows, rows), rows)
            fetch((kv_hbm.at[j, span], kv_buf))
            key_pos = j * rows + lax.broadcasted_iota(jnp.int32, (rows, rows), 0)
            query_pos = i * rows + lax.broadcasted_iota(jnp.int32, (rows, rows), 1)
            last = column(packed_all[j].T, trees + tree)
            segment = packed_all[i, pl.ds(tree, 1), :]
            allowed = (key_pos <= query_pos) & (segment <= last)
            bias[...] = jnp.where(allowed, 0.0, -2e30)
            for group in range(heads // per_group):
                keys = kv_buf[:, group * HEAD : (group + 1) * HEAD]
                values = kv_buf[:, kv_width + group * HEAD : kv_width + (group + 1) * HEAD]
                dk = jnp.zeros((rows, HEAD), F32)
                dv = jnp.zeros((rows, HEAD), F32)
                for head in range(group * per_group, (group + 1) * per_group):
                    cols = slice(head * HEAD, (head + 1) * HEAD)
                    queries = q_ref[span, cols]
                    grads = do_ref[span, cols]
                    scores = contract_last(keys, queries) * 0.125 + bias[...]
                    probs = jnp.exp(scores - lse_ref[tree, head : head + 1, :])
                    grad_probs = contract_last(values, grads)
                    grad_scores = (probs * (grad_probs - deltas[tree, head, 0:1, :])).astype(BF)
                    dv = dv + matmul(probs.astype(BF), grads)
                    dk = dk + matmul(grad_scores, queries)
                    dqs[span, cols] += contract_first(grad_scores, keys)
                dkv_buf[:, group * HEAD : (group + 1) * HEAD] = (dk * 0.125).astype(BF)
                dkv_buf[:, kv_width + group * HEAD : kv_width + (group + 1) * HEAD] = dv.astype(BF)

            @pl.when(j == i)
            def _():
                dkv_sum[span, :] = dkv_buf[...].astype(F32)

            @pl.when(j < i)
            def _():
                fetch((dkv_buf, dkv_part.at[j, span]))
                hand(j, tree).start()

    def query_slabs():
        dq_ref[...] = (dqs[...] * 0.125).astype(BF)
        thirds = tuple(range(dq_ref.shape[1] // ff))
        write_slabs(
            pairs * 6, 2 * len(thirds), ((turned, dq_ref[...], thirds), (dat, o_ref[...], thirds))
        )

    def key_value_sum():
        @pl.loop(0, contexts)
        def _(c):
            @pl.when(c > i)
            def _():
                @pl.loop(0, trees)
                def _(tree):
                    taken(c, tree).wait_recv()
                    span = pl.ds(pl.multiple_of(tree * rows, rows), rows)
                    fetch((dkv_came.at[c, span], dkv_add))
                    dkv_sum[span, :] += dkv_add[...].astype(F32)

        grad_kv = dkv_sum[...].astype(BF)
        pieces = tuple(range(grad_kv.shape[1] // ff))
        first = pairs * 6 + 2 * (dq_ref.shape[1] // ff)
        write_slabs(first, len(pieces), ((turned, grad_kv, pieces),))

    def first_norm_parts():
        @pl.loop(0, tokens // CHUNK)
        def _(c):
            span = pl.ds(pl.multiple_of(c * CHUNK, CHUNK), CHUNK)
            grads = jnp.concatenate([dq_ref[span, :], dkv_sum[span, :].astype(BF)], axis=1)
            tile_buf[:, :half] = contract_last(grads, wqkv[...]).astype(BF)
            tile_buf[:, half:] = contract_last(grads, far_qkv[...]).astype(BF)
            fetch((tile_buf, part2.at[span]))

        start2()


    tail_copy = remote(tail_far, tail_came, tail_sem.at[0], tail_sem.at[1], other_shard)

    def tell(c, slot):
        return remote(tails.at[slot], tails.at[slot], tsend.at[c], trecv.at[slot], {"context": c})

    def send_tail():
        for begin, target in ((0, tail_own), (half, tail_far)):
            target[...] = jnp.broadcast_to(square_ref[...], target.shape)
            target[0:2, :] = scale_ref[0:2, begin : begin + half]
        tail_copy.start()

    def tell_tail():
        tail_copy.wait_recv()
        tails[i] = tail_own[...] + tail_came[...]

        @pl.loop(0, contexts)
        def _(c):
            @pl.when(c != i)
            def _():
                tell(c, i).start()


    fetch((n2t_hbm, turned), (gyt_hbm, gyt))
    pair_slabs(0, False)
    greet(
        [other_shard, near, far]
        + [{"context": lax.rem(i + c, contexts)} for c in range(1, contexts)]
    )
    for c in range(6 // UNIT):
        exchange(c).start()
    start1()
    fill_columns(wqkv, (wq, wk, wv))
    scale_ref[...] = jnp.zeros_like(scale_ref)
    dqs[...] = jnp.zeros_like(dqs)
    middle1()

    chain = []
    for finish, finish_other, consume in (
        (finish1, other1, through_second_norm), (finish2, finish_other2, through_first_norm),
    ):
        steps = [[functools.partial(finish, 0, consume)]]
        for c in range(chunks):
            steps.append([functools.partial(finish_other, c, consume)])
            if c + 1 < chunks:
                steps[-1].append(functools.partial(finish, c + 1, consume))
        chain.append(steps)
    chain[0][-1].append(make_deltas)
    tasks = {}
    for p in range(1, pairs):
        tasks[3 * p - 3] = [functools.partial(pair_slabs, p)]
    last_pair = 3 * pairs - 6
    at = 0

    def put(acts):
        nonlocal at
        at += 1
        while at in tasks:
            at += 1
        tasks[at] = acts

    for acts in chain[0]:
        put(acts)
    per_step = -(-trees * contexts // 8)

    def attention_step(number):
        @pl.loop(0, per_step)
        def _(step):
            attention_block(number * per_step + step)

    attention_steps = {}
    for number in range(8):
        at += 1
        while at in tasks:
            at += 1
        attention_steps[at] = number
    first_at, last_at = min(attention_steps), max(attention_steps)
    at = max(at, last_pair)
    put([lambda: fetch((nt_hbm, turned)), query_slabs])
    at = max(at, last_at + 3)
    put([key_value_sum])
    put([first_norm_parts])
    put([drain1, middle2])
    for acts in chain[1]:
        put(acts)
    put([send_tail])
    put([tell_tail])
    assert at < units + lag * (contexts - 1)

    @pl.loop(0, units + lag * (contexts - 1))
    def _(k):
        add_unit(k)
        for when, acts in sorted(tasks.items()):

            @pl.when(k == when)
            def _(acts=acts):
                for act in acts:
                    act()

        number, due = jnp.int32(0), k < 0
        for when, index in attention_steps.items():
            number = jnp.where(k == when, index, number)
            due = due | (k == when)

        @pl.when(due)
        def _():
            attention_step(number)

    @pl.loop(0, contexts)
    def _(c):
        @pl.when(c != i)
        def _():
            tell(i, c).wait_recv()
            tell(c, i).wait_send()

    tail_copy.wait_send()
    tail = tails[0]
    for c in range(1, contexts):
        tail = tail + tails[c]
    tail_ref[...] = tail
    drain2()
    for k in (units - 2, units - 1):
        store(k).wait()

    @pl.loop(0, units)
    def _(k):
        exchange(k).wait_send()

        @pl.when((k >= units - slots) & has_right)
        def _():
            upward(k, up_ring).wait_send()

        @pl.when((k >= units - slots) & has_left)
        def _():
            downward(k, down_ring).wait_send()

    @pl.loop(0, contexts)
    def _(c):
        @pl.when(c < i)
        def _():
            @pl.loop(0, trees)
            def _(tree):
                hand(c, tree).wait_send()


def back(
    contexts, trees, gains, w_query, w_key, w_value, far_qkv, w_out, far_out, q, o, lse,
    packed_all, square, part, hidden, grad_y, x, normed_t, normed_two_t, grad_y_t, grads, middle, kv,
):
    tokens, width = hidden.shape
    half, rows = width // 2, tokens // trees
    pairs, _, four = grads.shape
    ff, cols, both = four // 4, q.shape[1], kv.shape[2]
    count = pairs * 6 + (2 * cols + both) // ff
    units = count // UNIT
    lag = 2 if contexts <= 4 else 1
    slots = lag * (contexts - 1) + 2
    chunks = tokens // 2 // CHUNK
    shape, vmem, dma = jax.ShapeDtypeStruct, pltpu.VMEM, pltpu.SemaphoreType.DMA
    slabs = shape((count, half, ff), BF)
    unit = (UNIT, half, ff)
    piece = vmem((chunks, CHUNK, width), BF)
    anywhere = pl.BlockSpec(memory_space=pl.ANY)
    near_memory = pl.BlockSpec(memory_space=pltpu.VMEM)
    outs = pl.pallas_call(
        functools.partial(back_kernel, contexts, trees, lag),
        out_shape=(
            slabs,
            shape((tokens, width), F32),
            shape((8, half), F32),
            *(slabs,) * 5,
            shape((tokens, width), BF),
            shape(kv.shape, BF),
            shape(kv.shape, BF),
        ),
        in_specs=[near_memory] * 12 + [anywhere] * 10,
        out_specs=(anywhere,) * 2 + (near_memory,) + (anywhere,) * 8,
        scratch_shapes=[
            vmem((half, cols + both), BF),
            vmem((8, width), F32),
            vmem((8, half), F32),
            vmem((8, half), F32),
            vmem((8, half), F32),
            vmem((contexts, 8, half), F32),
            vmem((slots,) + unit, BF),
            vmem((slots,) + unit, BF),
            vmem((slots,) + unit, BF),
            vmem(unit, BF),
            vmem((2,) + unit, BF),
            vmem((width, tokens), BF),
            vmem((width, tokens), BF),
            vmem((tokens, 4 * ff), BF),
            vmem((tokens, 2 * ff), BF),
            vmem((2, 6, half, ff), BF),
            vmem((tokens, width), F32),
            vmem((CHUNK, width), BF),
            vmem((CHUNK, width), F32),
            piece,
            vmem((tokens, width), BF),
            piece,
            piece,
            piece,
            piece,
            vmem((width, tokens), BF),
            vmem((tokens, cols), BF),
            vmem((tokens, cols), BF),
            vmem((tokens, cols), F32),
            vmem((trees, cols // HEAD, 8, rows), F32),
            vmem((rows, rows), F32),
            vmem((rows, both), BF),
            vmem((rows, both), BF),
            vmem((tokens, both), F32),
            vmem((rows, both), BF),
            vmem((CHUNK, width), BF),
            dma((4,)),
            dma((4,)),
            dma((2,)),
            dma((contexts,)),
            dma((contexts,)),
        ]
        + [dma((units,))] * 6
        + [dma((2,)), dma((contexts, trees)), dma((contexts, trees))]
        + [dma((chunks,))] * 12,
        compiler_params=pltpu.CompilerParams(
            collective_id=1, has_side_effects=True, vmem_limit_bytes=60 * 1024 * 1024
        ),
        cost_estimate=COST,
        name="back",
    )(
        gains, w_query, w_key, w_value, far_qkv, w_out, far_out, q, o, lse, packed_all,
        square, part, hidden, grad_y, x, normed_t, normed_two_t, grad_y_t, grads, middle, kv,
    )
    return outs[:3]


def local(
    states, segments, routes, gates, valid, teacher, attn_gain, w_query, key_matrix, value_matrix,
    w_out, moe_gain, w_gate, w_up, w_down,
):
    shards = lax.axis_size("shard")
    contexts = lax.axis_size("context")
    trees, rows, width = states.shape
    tokens = trees * rows
    half = width // 2
    experts = w_gate.shape[0]
    x = states.reshape(tokens, width)
    (
        packed_all, gains, qkv_far, out_far, gate_far, up_far, down_far, q, kv, normed_t,
        attended, lse, hidden, normed_two, normed_two_t, count, combine,
    ) = front(
        contexts, trees, x, segments, valid, routes.transpose(0, 2, 1), gates.transpose(0, 2, 1),
        attn_gain, moe_gain, w_query, key_matrix, value_matrix, w_out, w_gate, w_up, w_down,
    )
    gate_ws, up_ws, down_ws = (w_gate, gate_far), (w_up, up_far), (w_down, down_far)

    pre, middle, result, grad_y, grad_y_t, square = experts_forward(
        float(tokens * shards * contexts),
        normed_two,
        combine,
        count,
        gate_ws,
        up_ws,
        down_ws,
        hidden,
        teacher.reshape(tokens, width),
    )
    expert_grads, dn_part = experts_backward(grad_y, combine, gate_ws, up_ws, down_ws, pre)
    sums, grad_inputs, tail = back(
        contexts, trees, gains, w_query, key_matrix, value_matrix, qkv_far, w_out, out_far, q,
        attended, lse, packed_all, square, dn_part, hidden, grad_y, x, normed_t, normed_two_t,
        grad_y_t, expert_grads, middle, kv,
    )
    final_query, final_out, final_key, final_value, final_gain1, final_gain2, loss = (
        unpack_attention(sums, tail, count, w_query.shape[1], key_matrix.shape[1])
    )
    final_gate, final_up, final_down = unpack(sums, experts // 2)
    return (
        loss[0, 0],
        result.reshape(trees, rows, width),
        grad_inputs.reshape(trees, rows, width),
        final_gain1,
        final_query,
        final_key,
        final_value,
        final_out,
        final_gain2,
        final_gate,
        final_up,
        final_down,
    )


def solution(mesh):
    return jax.shard_map(
        local,
        mesh=mesh,
        in_specs=(
            P("shard", "context", None),
            P("shard", "context"),
            P("shard", "context", None),
            P("shard", "context", None),
            P("shard", "context"),
            P("shard", "context", None),
            P("shard"),
            P("shard", "tensor"),
            P("shard", "tensor"),
            P("shard", "tensor"),
            P("tensor", "shard"),
            P("shard"),
            P(None, "shard", "tensor"),
            P(None, "shard", "tensor"),
            P(None, "tensor", "shard"),
        ),
        out_specs=(
            P(),
            P("shard", "context", None),
            P("shard", "context", None),
            P("shard"),
            P("shard", "tensor"),
            P("shard", "tensor"),
            P("shard", "tensor"),
            P("tensor", "shard"),
            P("shard"),
            P(None, "shard", "tensor"),
            P(None, "shard", "tensor"),
            P(None, "tensor", "shard"),
        ),
        check_vma=False,
    )
```

```python
import functools
import math

import jax
import jax.numpy as jnp
from jax import lax
from jax.experimental import pallas as pl
from jax.experimental.pallas import tpu as pltpu
from jax.sharding import PartitionSpec as P

HEAD = 64
EPS = 1e-05
BF = jnp.bfloat16
F32 = jnp.float32
MESH = pl.DeviceIdType.MESH
VMEM_LIMIT = 56 * 1024 * 1024
UNIT = 2
COST = pl.CostEstimate(flops=1, bytes_accessed=1, transcendentals=0)


def matmul(left, right):
    return jnp.dot(left, right, preferred_element_type=F32)


def contract_first(left, right):
    return lax.dot_general(left, right, (((0,), (0,)), ((), ())), preferred_element_type=F32)


def contract_last(left, right):
    return lax.dot_general(left, right, (((1,), (1,)), ((), ())), preferred_element_type=F32)


def column(block, index):
    lane = lax.broadcasted_iota(jnp.int32, block.shape, 1)
    return jnp.sum(jnp.where(lane == index, block, 0.0), axis=1, keepdims=True)


def experts_backward_kernel(
    gy_ref, c_ref, g0, g1, u0, u1, d0, d1, pre_hbm, grads_hbm, dn_ref,
    wide, tall, grads, pre_buf, weight_sem, pre_sem, out_sem,
):
    pairs, tokens = pre_hbm.shape[0], gy_ref.shape[0]
    half, ff = g0.shape[1], g0.shape[2]
    tile = 256

    def weight_loads(p):
        copies = []
        for side, gate, up, down in ((0, g0, u0, d0), (1, g1, u1, d1)):
            features = pl.ds(side * half, half)
            for a in range(2):
                e = 2 * p + a
                for source, target in (
                    (gate, wide.at[features, pl.ds(pl.multiple_of(2 * e * ff, 128), ff)]),
                    (up, wide.at[features, pl.ds(pl.multiple_of((2 * e + 1) * ff, 128), ff)]),
                    (down, tall.at[p, pl.ds(a * ff, ff), features]),
                ):
                    copies.append(
                        pltpu.make_async_copy(
                            source.at[e], target, weight_sem.at[p, len(copies)]
                        )
                    )
        return copies

    def pre_load(p):
        return pltpu.make_async_copy(
            pre_hbm.at[p], pre_buf.at[lax.rem(p, 2)], pre_sem.at[lax.rem(p, 2)]
        )

    def span(p):
        return pl.ds(pl.multiple_of(p * 4 * ff, 128), 4 * ff)

    def store(p):
        return pltpu.make_async_copy(grads.at[:, span(p)], grads_hbm.at[p], out_sem.at[p])

    for copy in weight_loads(0):
        copy.start()
    pre_load(0).start()

    @pl.loop(1, pairs)
    def _(p):
        for copy in weight_loads(p):
            copy.start()

    @pl.loop(0, pairs)
    def _(p):
        @pl.when(p + 1 < pairs)
        def _():
            pre_load(p + 1).start()

        for copy in weight_loads(p):
            copy.wait()
        pre_load(p).wait()
        slot = lax.rem(p, 2)
        grad_middle = contract_last(gy_ref[...], tall[p])
        pieces = []
        for a in range(2):
            gate = pre_buf[slot, :, 2 * a * ff : (2 * a + 1) * ff].astype(F32)
            up = pre_buf[slot, :, (2 * a + 1) * ff : (2 * a + 2) * ff].astype(F32)
            weight = column(c_ref[...], 2 * p + a)
            gm = weight * grad_middle[:, a * ff : (a + 1) * ff]
            sig = jax.nn.sigmoid(gate)
            pieces.append((gm * up * (sig + gate * sig * (1.0 - sig))).astype(BF))
            pieces.append((gm * gate * sig).astype(BF))
        grads[:, span(p)] = jnp.concatenate(pieces, axis=1)
        store(p).start()

    @pl.loop(0, 2 * half // tile)
    def _(index):
        rows = pl.ds(pl.multiple_of(index * tile, tile), tile)
        dn_ref[:, rows] = contract_last(grads[...], wide[rows, :]).astype(BF)

    @pl.loop(0, pairs)
    def _(p):
        store(p).wait()


def experts_backward(grad_y, combine, gates, ups, downs, pre):
    tokens, width = grad_y.shape
    experts, half, ff = gates[0].shape
    pairs = experts // 2
    vmem, dma = pltpu.VMEM, pltpu.SemaphoreType.DMA
    anywhere = pl.BlockSpec(memory_space=pl.ANY)
    near_memory = pl.BlockSpec(memory_space=pltpu.VMEM)
    return pl.pallas_call(
        experts_backward_kernel,
        out_shape=(
            jax.ShapeDtypeStruct((pairs, tokens, 4 * ff), BF),
            jax.ShapeDtypeStruct((tokens, width), BF),
        ),
        in_specs=[near_memory] * 2 + [anywhere] * 7,
        out_specs=(anywhere, near_memory),
        scratch_shapes=[
            vmem((width, 2 * experts * ff), BF),
            vmem((pairs, 2 * ff, width), BF),
            vmem((tokens, 2 * experts * ff), BF),
            vmem((2, tokens, 4 * ff), BF),
            dma((pairs, 12)),
            dma((2,)),
            dma((pairs,)),
        ],
        compiler_params=pltpu.CompilerParams(vmem_limit_bytes=60 * 1024 * 1024),
        cost_estimate=COST,
        name="experts_backward",
    )(grad_y, combine, *gates, *ups, *downs, pre)


def unpack_kernel(slabs_ref, gate_ref, up_ref, down_ref):
    for a in range(2):
        gate_ref[a] = slabs_ref[a].astype(F32)
        up_ref[a] = slabs_ref[2 + a].astype(F32)
        down_ref[a] = slabs_ref[4 + a].T.astype(F32)


def unpack(slabs, steps):
    _, half, ff = slabs.shape
    wide = jax.ShapeDtypeStruct((2 * steps, half, ff), F32)
    tall = jax.ShapeDtypeStruct((2 * steps, ff, half), F32)
    return pl.pallas_call(
        unpack_kernel,
        out_shape=(wide, wide, tall),
        grid=(steps,),
        in_specs=[pl.BlockSpec((6, half, ff), lambda i: (i, 0, 0))],
        out_specs=[pl.BlockSpec((2, half, ff), lambda i: (i, 0, 0))] * 2
        + [pl.BlockSpec((2, ff, half), lambda i: (i, 0, 0))],
        compiler_params=pltpu.CompilerParams(vmem_limit_bytes=VMEM_LIMIT),
        cost_estimate=COST,
        name="unpack",
    )(slabs)


def unpack_attention_kernel(
    width, slabs_ref, tail_ref, count_ref, q_ref, out_ref, k_ref, v_ref, gain1_ref, gain2_ref, loss_ref
):
    gain1_ref[...] = tail_ref[0:1, :].reshape(gain1_ref.shape)
    gain2_ref[...] = tail_ref[1:2, :].reshape(gain2_ref.shape)
    loss_ref[...] = tail_ref[2:3, 0:1] / (count_ref[...] * width)
    ff = slabs_ref.shape[2]
    at = 0
    for ref, turn in ((q_ref, False), (out_ref, True), (k_ref, False), (v_ref, False)):
        for c in range(ref.shape[0 if turn else 1] // ff):
            value = slabs_ref[at].astype(F32)
            if turn:
                ref[c * ff : (c + 1) * ff, :] = value.T
            else:
                ref[:, c * ff : (c + 1) * ff] = value
            at += 1


def unpack_attention(slabs, tail, count, query_cols, key_cols):
    total, rows, ff = slabs.shape
    number = 2 * (query_cols + key_cols) // ff
    shapes = (
        (rows, query_cols), (query_cols, rows), (rows, key_cols), (rows, key_cols),
        (rows,), (rows,), (1, 1),
    )
    return pl.pallas_call(
        functools.partial(unpack_attention_kernel, 2 * rows),
        out_shape=tuple(jax.ShapeDtypeStruct(shape, F32) for shape in shapes),
        grid=(1,),
        in_specs=[
            pl.BlockSpec((number, rows, ff), lambda i: (total // number - 1, 0, 0)),
            pl.BlockSpec(tail.shape, lambda i: (0, 0)),
            pl.BlockSpec((1, 1), lambda i: (0, 0)),
        ],
        out_specs=[
            pl.BlockSpec(shape, (lambda i: (0, 0)) if len(shape) == 2 else (lambda i: (0,)))
            for shape in shapes
        ],
        compiler_params=pltpu.CompilerParams(vmem_limit_bytes=VMEM_LIMIT),
        cost_estimate=COST,
        name="unpack_attention",
    )(slabs, tail, count)


def inverse_norm(near, far):
    count = near.shape[1] + far.shape[1]
    squares = jnp.sum(near * near, axis=1, keepdims=True) + jnp.sum(far * far, axis=1, keepdims=True)
    return lax.rsqrt(squares / count + EPS)


def halves(ref, rows, shard):
    half = ref.shape[1] // 2
    own = pl.ds(pl.multiple_of(shard * half, 128), half)
    far = pl.ds(pl.multiple_of((1 - shard) * half, 128), half)
    return ref[rows, own].astype(F32), ref[rows, far].astype(F32)


def put_halves(ref, rows, shard, near, far):
    half = ref.shape[1] // 2
    ref[rows, pl.ds(pl.multiple_of(shard * half, 128), half)] = near.astype(ref.dtype)
    ref[rows, pl.ds(pl.multiple_of((1 - shard) * half, 128), half)] = far.astype(ref.dtype)


def norm_backward(near, far, inverse, gain, grads):
    half = near.shape[1]
    near_scaled = grads[:, :half] * gain[:, :half]
    far_scaled = grads[:, half:] * gain[:, half:]
    along = (
        jnp.sum(near_scaled * near, axis=1, keepdims=True)
        + jnp.sum(far_scaled * far, axis=1, keepdims=True)
    ) / (2 * half)
    cube = inverse * inverse * inverse * along
    return (
        inverse * near_scaled - near * cube,
        inverse * far_scaled - far * cube,
        jnp.sum(grads[:, :half] * near * inverse, axis=0, keepdims=True),
        jnp.sum(grads[:, half:] * far * inverse, axis=0, keepdims=True),
    )


CHUNK = 128


def tensor_peers():
    t = lax.axis_index("tensor")
    low, high = lax.rem(t, 2), lax.rem(t // 2, 2)
    return low, {"tensor": t + 1 - 2 * low}, {"tensor": t + 2 - 4 * high}


def greet(peers):
    barrier = pltpu.get_barrier_semaphore()
    for peer in peers:
        pl.semaphore_signal(barrier, inc=1, device_id=peer, device_id_type=MESH)
    pl.semaphore_wait(barrier, len(peers))


def sum_over_tensor(part, total, arrived, mine, other, sems, consume, between=lambda c: None):
    send1, recv1, send2, recv2, send3, recv3 = sems
    low, near, far = tensor_peers()
    chunks = arrived.shape[0]
    half = chunks * CHUNK

    def rows(side, c):
        return pl.ds(pl.multiple_of(side * half + c * CHUNK, CHUNK), CHUNK)

    def give(c):
        return pltpu.make_async_remote_copy(
            part.at[rows(1 - low, c)], arrived.at[c], send1.at[c], recv1.at[c],
            device_id=near, device_id_type=MESH,
        )

    def swap(c):
        return pltpu.make_async_remote_copy(
            mine.at[c], other.at[c], send2.at[c], recv2.at[c], device_id=far, device_id_type=MESH
        )

    def back(c):
        return pltpu.make_async_remote_copy(
            total.at[rows(low, c)], total.at[rows(low, c)], send3.at[c], recv3.at[c],
            device_id=near, device_id_type=MESH,
        )

    @pl.loop(0, chunks)
    def _(c):
        give(c).start()

    @pl.loop(0, chunks)
    def _(c):
        give(c).wait_recv()
        mine[c] = (part[rows(low, c), :].astype(F32) + arrived[c].astype(F32)).astype(BF)
        swap(c).start()

    @pl.loop(0, chunks)
    def _(c):
        between(c)
        swap(c).wait_recv()
        total[rows(low, c), :] = (mine[c].astype(F32) + other[c].astype(F32)).astype(BF)
        back(c).start()
        consume(pl.multiple_of(low * half + c * CHUNK, CHUNK))
        back(c).wait_recv()
        consume(pl.multiple_of((1 - low) * half + c * CHUNK, CHUNK))

    @pl.loop(0, chunks)
    def _(c):
        give(c).wait_send()
        swap(c).wait_send()
        back(c).wait_send()


def sum_scratch(tokens, width):
    chunks = tokens // 2 // CHUNK
    piece = pltpu.VMEM((chunks, CHUNK, width), BF)
    return [pltpu.VMEM((tokens, width), BF)] + [piece] * 3 + [
        pltpu.SemaphoreType.DMA((chunks,))
    ] * 6


def fill_columns(target, refs):
    at = 0
    for ref in refs:
        target[:, at : at + ref.shape[1]] = ref[...]
        at += ref.shape[1]


def front_kernel(
    contexts, trees, x_ref, seg_ref, valid_ref, routes_ref, gates_ref, gain1_ref, gain2_ref, wq, wk, wv, wout, w_gate, w_up, w_down,
    packed_all, all_gains, far_qkv, far_out, far_gate, far_up, far_down,
    q_ref, kv_out, nt_out, o_ref, lse_ref, h_out, n2_out, n2t_out, count_ref, c_ref,
    packed, gains, wqkv, far_gains, kv_all, nt_ref, h_ref, n2_ref, n2t_ref,
    normed, bias, tops, norms, sums, part, total, arrived, mine, other,
    ysend, yrecv, rsend, rrecv, psend, precv, ksend, krecv, out_sem, *sems
):
    i = lax.axis_index("context")
    shard = lax.axis_index("shard")
    parity = lax.rem(i, 2)
    tokens, width = x_ref.shape
    half = width // 2
    rows = tokens // trees
    heads = q_ref.shape[1] // HEAD
    kv_width = kv_all.shape[2] // 2
    per_group = q_ref.shape[1] // kv_width
    other_shard = {"shard": 1 - shard}
    partner = {"context": i + 1 - 2 * parity}
    right = {"context": lax.rem(i + 1, contexts)}
    _, near, far = tensor_peers()
    fill_columns(wqkv, (wq, wk, wv))
    segment = seg_ref[...]
    last = jnp.where(
        segment == 0, 1 << 20, jnp.where(lax.rem(segment, 3) == 1, segment + 2, segment)
    )
    packed[...] = jnp.zeros_like(packed)
    packed[0:trees, :] = segment.astype(F32)
    packed[trees : 2 * trees, :] = last.astype(F32)
    packed[2 * trees + 1 : 3 * trees + 1, :] = valid_ref[...].astype(F32)
    counted = jnp.sum(jnp.sum(valid_ref[...].astype(F32), axis=1, keepdims=True), axis=0, keepdims=True)
    gains[...] = jnp.broadcast_to(counted, gains.shape)
    gains[0:1, :] = gain1_ref[...].reshape(1, half)
    gains[1:2, :] = gain2_ref[...].reshape(1, half)
    greet(
        [other_shard, near, far]
        + [{"context": lax.rem(i + c, contexts)} for c in range(1, contexts)]
    )

    def half_span(ref, axis):
        size = ref.shape[axis] // 2
        return pl.ds(pl.multiple_of(parity * size, size), size)

    experts = w_gate.shape[0]
    shared = experts // 8
    own_count = (experts - shared) // 2
    moves = [
        (wqkv.at[half_span(wqkv, 0)], far_qkv.at[half_span(wqkv, 0)]),
        (wout.at[:, half_span(wout, 1)], far_out.at[:, half_span(wout, 1)]),
    ]
    first = (own_count + 1) // 2
    for begin, size in (
        (parity * own_count, first),
        (parity * own_count + first, own_count - first),
        (2 * own_count, shared),
    ):
        span = pl.ds(begin, size)
        for source, target in ((w_gate, far_gate), (w_up, far_up), (w_down, far_down)):
            moves.append((source.at[span], target.at[span]))
    relays = len(moves) - 3

    def direct(m):
        source, target = moves[m]
        return pltpu.make_async_remote_copy(
            source, target, ysend.at[m], yrecv.at[m],
            device_id=other_shard, device_id_type=MESH,
        )

    def relay(m):
        target = moves[m][1]
        return pltpu.make_async_remote_copy(
            target, target, rsend.at[m], rrecv.at[m], device_id=partner, device_id_type=MESH
        )

    def pass_on(m):
        direct(m).wait_recv()
        relay(m).start()

    count = len(moves)
    gain_copy = pltpu.make_async_remote_copy(
        gains, far_gains, ysend.at[count], yrecv.at[count],
        device_id=other_shard, device_id_type=MESH,
    )

    def tell(c, slot):
        return pltpu.make_async_remote_copy(
            packed, packed_all.at[slot], psend.at[c], precv.at[slot],
            device_id={"context": c}, device_id_type=MESH,
        )

    def lift(j):
        return pltpu.make_async_remote_copy(
            kv_all.at[j], kv_all.at[j], ksend.at[j], krecv.at[j],
            device_id=right, device_id_type=MESH,
        )

    outs = [
        pltpu.make_async_copy(src, dst, out_sem.at[at])
        for at, (src, dst) in enumerate((
            (nt_ref, nt_out), (kv_all, kv_out), (h_ref, h_out), (n2_ref, n2_out), (n2t_ref, n2t_out),
        ))
    ]
    gain_copy.start()
    for m in range(count):
        direct(m).start()

    gain_copy.wait_recv()
    packed[2 * trees : 2 * trees + 1, :] = gains[2:3, :rows] + far_gains[2:3, :rows]
    packed_all[i] = packed[...]

    @pl.loop(0, contexts)
    def _(c):
        @pl.when(c != i)
        def _():
            tell(c, i).start()

    all_gains[:, :half] = gains[...]
    all_gains[:, half:] = far_gains[...]
    tile = 128

    @pl.loop(0, tokens // tile)
    def _(index):
        span = pl.ds(pl.multiple_of(index * tile, tile), tile)
        own_x, far_x = halves(x_ref, span, shard)
        inverse = inverse_norm(own_x, far_x)
        own_x = (own_x * inverse * gains[0:1, :]).astype(BF)
        far_x = (far_x * inverse * far_gains[0:1, :]).astype(BF)
        normed[span, :half] = own_x
        normed[span, half:] = far_x
        nt_ref[:half, span] = own_x.T
        nt_ref[half:, span] = far_x.T

    outs[0].start()
    pack_t = packed[...].T
    lane = lax.broadcasted_iota(jnp.int32, (rows, c_ref.shape[1]), 1).astype(F32)
    for tree in range(trees):
        weights = jnp.where(lane == float(experts), column(pack_t, 2 * trees + 1 + tree), 0.0)
        routes = routes_ref[tree].astype(F32).T
        gates = gates_ref[tree].T
        for at in range(routes.shape[1]):
            weights = weights + jnp.where(
                routes[:, at : at + 1] == lane, gates[:, at : at + 1], 0.0
            )
        c_ref[tree * rows : (tree + 1) * rows, :] = weights
    pass_on(0)
    pass_on(1)
    relay(0).wait_recv()
    qkv = matmul(normed[:, :half], wqkv[...]) + matmul(normed[:, half:], far_qkv[...])
    q_ref[...] = qkv[:, : q_ref.shape[1]].astype(BF)
    kv_all[i] = qkv[:, q_ref.shape[1] :].astype(BF)

    @pl.when(i < contexts - 1)
    def _():
        lift(i).start()

    tops[...] = jnp.full_like(tops, -1e30)
    norms[...] = jnp.zeros_like(norms)
    sums[...] = jnp.zeros_like(sums)

    @pl.loop(0, contexts)
    def _(c):
        @pl.when(c != i)
        def _():
            tell(i, c).wait_recv()

    counted = packed_all[0, 2 * trees : 2 * trees + 1, 0:1]
    for c in range(1, contexts):
        counted = counted + packed_all[c, 2 * trees : 2 * trees + 1, 0:1]
    count_ref[...] = counted

    @pl.loop(0, contexts)
    def _(d):
        @pl.when(d <= i)
        def _():
            j = i - d

            @pl.when(d > 0)
            def _():
                lift(j).wait_recv()

                @pl.when(i < contexts - 1)
                def _():
                    lift(j).start()

            @pl.loop(0, trees)
            def _(tree):
                span = pl.ds(pl.multiple_of(tree * rows, rows), rows)
                key_pos = j * rows + lax.broadcasted_iota(jnp.int32, (rows, rows), 1)
                query_pos = i * rows + lax.broadcasted_iota(jnp.int32, (rows, rows), 0)
                last = packed_all[j, pl.ds(trees + tree, 1), :]
                allowed = (key_pos <= query_pos) & (column(pack_t, tree) <= last)
                bias[...] = jnp.where(allowed, 0.0, -2e30)
                for head in range(heads):
                    group = head // per_group
                    cols = slice(head * HEAD, (head + 1) * HEAD)
                    keys = kv_all[j, span, group * HEAD : (group + 1) * HEAD]
                    values = kv_all[
                        j, span, kv_width + group * HEAD : kv_width + (group + 1) * HEAD
                    ]
                    scores = contract_last(q_ref[span, cols], keys) * 0.125 + bias[...]
                    old = tops[span, head : head + 1]
                    top = jnp.maximum(old, jnp.max(scores, axis=1, keepdims=True))
                    weights = jnp.exp(scores - top)
                    shrink = jnp.exp(old - top)
                    tops[span, head : head + 1] = top
                    norms[span, head : head + 1] = norms[span, head : head + 1] * shrink + jnp.sum(
                        weights, axis=1, keepdims=True
                    )
                    sums[span, cols] = sums[span, cols] * shrink + matmul(
                        weights.astype(BF), values
                    )

        @pl.when(d == 0)
        def _():
            pass_on(2)

        @pl.when(d == min(2, contexts - 1))
        def _():
            pass_on(3)

    for head in range(heads):
        cols = slice(head * HEAD, (head + 1) * HEAD)
        o_ref[:, cols] = (sums[:, cols] / norms[:, head : head + 1]).astype(BF)
    lse = tops[...] + jnp.log(norms[...] + jnp.where(norms[...] == 0.0, 1.0, 0.0))
    for tree in range(trees):
        lse_ref[tree] = lse[tree * rows : (tree + 1) * rows].T[: lse_ref.shape[1]]
    outs[1].start()
    relay(1).wait_recv()
    part[:, :half] = matmul(o_ref[...], wout[...]).astype(BF)
    part[:, half:] = matmul(o_ref[...], far_out[...]).astype(BF)

    def consume(row):
        span = pl.ds(row, CHUNK)
        own_x, far_x = halves(x_ref, span, shard)
        own_x = own_x + total[span, :half].astype(F32)
        far_x = far_x + total[span, half:].astype(F32)
        h_ref[span, :half] = own_x
        h_ref[span, half:] = far_x
        inverse = inverse_norm(own_x, far_x)
        own_x = (own_x * inverse * gains[1:2, :]).astype(BF)
        far_x = (far_x * inverse * far_gains[1:2, :]).astype(BF)
        n2_ref[span, :half] = own_x
        n2_ref[span, half:] = far_x
        n2t_ref[:half, span] = own_x.T
        n2t_ref[half:, span] = far_x.T

    chunks = arrived.shape[0]

    def between(c):
        for at in range(chunks):

            @pl.when(c == at)
            def _():
                pass_on(4 + at)

    sum_over_tensor(part, total, arrived, mine, other, sems, consume, between)
    for copy in outs[2:]:
        copy.start()
    for m in range(4 + chunks, relays):
        pass_on(m)
    for m in range(2, relays):
        relay(m).wait_recv()
    for m in range(relays, count):
        direct(m).wait_recv()
    for m in range(count):
        direct(m).wait_send()
        if m < relays:
            relay(m).wait_send()
    gain_copy.wait_send()
    for copy in outs:
        copy.wait()

    @pl.loop(0, contexts)
    def _(c):
        @pl.when(c != i)
        def _():
            tell(c, i).wait_send()

        @pl.when((c <= i) & (i < contexts - 1))
        def _():
            lift(c).wait_send()


def front(
    contexts, trees, x, segments, valid, routes, gates, gain1, gain2, w_query, w_key, w_value,
    w_out, w_gate, w_up, w_down,
):
    tokens, width = x.shape
    half, rows = width // 2, tokens // trees
    cols = w_out.shape[0]
    both = w_key.shape[1] + w_value.shape[1]
    anywhere = pl.BlockSpec(memory_space=pl.ANY)
    near_memory = pl.BlockSpec(memory_space=pltpu.VMEM)
    shape, vmem, dma = jax.ShapeDtypeStruct, pltpu.VMEM, pltpu.SemaphoreType.DMA
    buffers = sum_scratch(tokens, width)
    return pl.pallas_call(
        functools.partial(front_kernel, contexts, trees),
        out_shape=(
            shape((contexts, 8, rows), F32),
            shape((8, width), F32),
            shape((half, cols + both), BF),
            *(shape(ref.shape, BF) for ref in (w_out, w_gate, w_up, w_down)),
            shape((tokens, cols), BF),
            shape((contexts, tokens, both), BF),
            shape((width, tokens), BF),
            shape((tokens, cols), BF),
            shape((trees, 8, rows), F32),
            shape((tokens, width), F32),
            shape((tokens, width), BF),
            shape((width, tokens), BF),
            shape((1, 1), F32),
            shape((tokens, 128), F32),
        ),
        in_specs=[near_memory] * 11 + [anywhere] * 3,
        out_specs=(near_memory,) * 4
        + (anywhere,) * 3
        + (near_memory, anywhere, anywhere, near_memory, near_memory)
        + (anywhere,) * 3
        + (near_memory,) * 2,
        scratch_shapes=[
            vmem((8, rows), F32),
            vmem((8, half), F32),
            vmem((half, cols + both), BF),
            vmem((8, half), F32),
            vmem((contexts, tokens, both), BF),
            vmem((width, tokens), BF),
            vmem((tokens, width), F32),
            vmem((tokens, width), BF),
            vmem((width, tokens), BF),
            vmem((tokens, width), BF),
            vmem((rows, rows), F32),
            vmem((tokens, 128), F32),
            vmem((tokens, 128), F32),
            vmem((tokens, cols), F32),
            vmem((tokens, width), BF),
        ]
        + buffers[:4]
        + [dma((12,)), dma((12,)), dma((8,)), dma((8,))]
        + [dma((contexts,))] * 4
        + [dma((5,))]
        + buffers[4:],
        compiler_params=pltpu.CompilerParams(
            collective_id=2, has_side_effects=True, vmem_limit_bytes=60 * 1024 * 1024
        ),
        cost_estimate=COST,
        name="front",
    )(
        x, segments, valid, routes, gates, gain1, gain2, w_query, w_key, w_value, w_out,
        w_gate, w_up, w_down,
    )


def experts_forward_kernel(
    token_total, n_ref, c_ref, count_ref, g0, g1, u0, u1, d0, d1, h_hbm, teacher_hbm,
    pre_hbm, cm_hbm, y_hbm, low_hbm, lowt_hbm, square_ref,
    wide, tall, pre_buf, cm_all, part, h_ref, teacher_ref, y_ref, low_ref, lowt_ref,
    weight_sem, in_sem, pre_sem, out_sem, total, arrived, mine, other,
    send1, recv1, send2, recv2, send3, recv3,
):
    tokens, width = h_ref.shape
    half = width // 2
    pairs, ff = wide.shape[0], g0.shape[2]
    chunks = arrived.shape[0]
    shard = lax.axis_index("shard")
    low_side, near, far = tensor_peers()
    loads = [
        pltpu.make_async_copy(h_hbm, h_ref, in_sem.at[0]),
        pltpu.make_async_copy(teacher_hbm, teacher_ref, in_sem.at[1]),
    ]

    def weight_loads(p):
        copies = []
        for side, gate, up, down in ((0, g0, u0, d0), (1, g1, u1, d1)):
            features = pl.ds(side * half, half)
            for a in range(2):
                for source, target in (
                    (gate, wide.at[p, features, pl.ds(2 * a * ff, ff)]),
                    (up, wide.at[p, features, pl.ds((2 * a + 1) * ff, ff)]),
                    (down, tall.at[pl.ds((2 * p + a) * ff, ff), features]),
                ):
                    copies.append(
                        pltpu.make_async_copy(
                            source.at[2 * p + a], target, weight_sem.at[p, len(copies)]
                        )
                    )
        return copies

    @pl.loop(0, pairs)
    def _(p):
        for copy in weight_loads(p):
            copy.start()

    for copy in loads:
        copy.start()
    square_ref[...] = jnp.zeros_like(square_ref)
    greet([near, far])

    def rows(side, c):
        return pl.ds(pl.multiple_of((2 * c + side) * CHUNK, CHUNK), CHUNK)

    def both_rows(c):
        return pl.ds(pl.multiple_of(2 * c * CHUNK, 2 * CHUNK), 2 * CHUNK)

    def remote(src, dst, send, recv, to):
        return pltpu.make_async_remote_copy(
            src, dst, send, recv, device_id=to, device_id_type=MESH
        )

    def give(c):
        return remote(part.at[rows(1 - low_side, c)], arrived.at[c], send1.at[c], recv1.at[c], near)

    def swap(c):
        return remote(mine.at[c], other.at[c], send2.at[c], recv2.at[c], far)

    def back_copy(c):
        span = rows(low_side, c)
        return remote(total.at[span], total.at[span], send3.at[c], recv3.at[c], near)

    def kept(c, p):
        slot = lax.rem(p, 2)
        return (
            pltpu.make_async_copy(
                pre_buf.at[slot], pre_hbm.at[p, both_rows(c)], pre_sem.at[slot, 0]
            ),
            pltpu.make_async_copy(
                cm_all.at[:, pl.ds(pl.multiple_of(p * 2 * ff, 128), 2 * ff)],
                cm_hbm.at[p, both_rows(c)],
                pre_sem.at[slot, 1],
            ),
        )

    @pl.loop(0, chunks)
    def _(c):
        span = both_rows(c)

        @pl.loop(0, pairs)
        def _(p):
            @pl.when(c == 0)
            def _():
                for copy in weight_loads(p):
                    copy.wait()

            slot = lax.rem(p, 2)

            @pl.when(p >= 2)
            def _():
                for copy in kept(c, p - 2):
                    copy.wait()

            hidden = matmul(n_ref[span, :], wide[p])
            pre_buf[slot] = hidden.astype(BF)
            pieces = []
            for a in range(2):
                gate = hidden[:, 2 * a * ff : (2 * a + 1) * ff]
                up = hidden[:, (2 * a + 1) * ff : (2 * a + 2) * ff]
                weight = column(c_ref[span, :], 2 * p + a)
                pieces.append((weight * (gate * jax.nn.sigmoid(gate) * up)).astype(BF))
            cm_all[:, pl.ds(pl.multiple_of(p * 2 * ff, 128), 2 * ff)] = jnp.concatenate(
                pieces, axis=1
            )
            for copy in kept(c, p):
                copy.start()

        for p in (pairs - 2, pairs - 1):
            for copy in kept(c, p):
                copy.wait()
        part[span, :] = matmul(cm_all[...], tall[...]).astype(BF)
        give(c).start()
        give(c).wait_recv()
        mine[c] = (part[rows(low_side, c), :].astype(F32) + arrived[c].astype(F32)).astype(BF)
        swap(c).start()

    def stores(at):
        span = pl.ds(pl.multiple_of(at * CHUNK, CHUNK), CHUNK)
        return [
            pltpu.make_async_copy(y_ref.at[span], y_hbm.at[span], out_sem.at[0, at]),
            pltpu.make_async_copy(low_ref.at[span], low_hbm.at[span], out_sem.at[1, at]),
            pltpu.make_async_copy(lowt_ref.at[:, span], lowt_hbm.at[:, span], out_sem.at[2, at]),
        ]

    def consume(side, c):
        span = rows(side, c)
        mask = column(c_ref[span, :], 2 * pairs)
        factor = token_total / count_ref[...] * mask
        near_t, far_t = halves(teacher_ref, span, shard)
        near_y = h_ref[span, :half] + total[span, :half].astype(F32)
        far_y = h_ref[span, half:] + total[span, half:].astype(F32)
        put_halves(y_ref, span, shard, near_y, far_y)
        for begin, error in ((0, near_y - near_t), (half, far_y - far_t)):
            features = slice(begin, begin + half)
            squares = mask * jnp.sum(error * error, axis=1, keepdims=True)
            square_ref[...] += jnp.sum(squares, axis=0, keepdims=True)
            grad = (factor * error).astype(BF)
            low_ref[span, features] = grad
            lowt_ref[features, span] = grad.T
        for copy in stores(2 * c + side):
            copy.start()

    for copy in loads:
        copy.wait()

    @pl.loop(0, chunks)
    def _(c):
        swap(c).wait_recv()
        total[rows(low_side, c), :] = (mine[c].astype(F32) + other[c].astype(F32)).astype(BF)
        back_copy(c).start()
        consume(low_side, c)
        back_copy(c).wait_recv()
        consume(1 - low_side, c)

    @pl.loop(0, chunks)
    def _(c):
        give(c).wait_send()
        swap(c).wait_send()
        back_copy(c).wait_send()
        for side in range(2):
            for copy in stores(2 * c + side):
                copy.wait()


def experts_forward(token_total, normed, combine, count, gates, ups, downs, hidden, teacher):
    tokens, width = hidden.shape
    experts, half, ff = gates[0].shape
    pairs = experts // 2
    shape, vmem, dma = jax.ShapeDtypeStruct, pltpu.VMEM, pltpu.SemaphoreType.DMA
    anywhere = pl.BlockSpec(memory_space=pl.ANY)
    near_memory = pl.BlockSpec(memory_space=pltpu.VMEM)
    return pl.pallas_call(
        functools.partial(experts_forward_kernel, token_total),
        out_shape=(
            shape((pairs, tokens, 4 * ff), BF),
            shape((pairs, tokens, 2 * ff), BF),
            shape((tokens, width), BF),
            shape((tokens, width), BF),
            shape((width, tokens), BF),
            shape((1, 1), F32),
        ),
        in_specs=[near_memory] * 3 + [anywhere] * 8,
        out_specs=(anywhere,) * 5 + (near_memory,),
        scratch_shapes=[
            vmem((pairs, width, 4 * ff), BF),
            vmem((experts * ff, width), BF),
            vmem((2, 2 * CHUNK, 4 * ff), BF),
            vmem((2 * CHUNK, experts * ff), BF),
            vmem((tokens, width), BF),
            vmem((tokens, width), F32),
            vmem((tokens, width), BF),
            vmem((tokens, width), BF),
            vmem((tokens, width), BF),
            vmem((width, tokens), BF),
            dma((pairs, 12)),
            dma((2,)),
            dma((2, 2)),
            dma((3, tokens // CHUNK)),
        ]
        + sum_scratch(tokens, width),
        compiler_params=pltpu.CompilerParams(
            collective_id=3, has_side_effects=True, vmem_limit_bytes=60 * 1024 * 1024
        ),
        cost_estimate=COST,
        name="experts_forward",
    )(normed, combine, count, *gates, *ups, *downs, hidden, teacher)


def back_kernel(
    contexts, trees, lag, gains, wq, wk, wv, far_qkv, wout, far_out, q_ref, o_ref, lse_ref, packed_all,
    square_ref, part, h_hbm, gy_hbm, x_hbm, nt_hbm, n2t_hbm, gyt_hbm, grads_hbm, cm_hbm, kv_hbm,
    result, out_hbm, tail_ref, own_hbm, far_hbm, came, up_hbm, down_hbm, part2, dkv_part, dkv_came, dkv_pair,
    wqkv, scale_ref, tail_own, tail_far, tail_came, tails,
    sums_ring, up_ring, down_ring, came_buf, out_buf, turned, gyt, grads_buf, cm_buf, stage,
    hbuf, chunk_low, chunk_out, my_part, total, arrived, mine, other, other2,
    dat, do_ref, dq_ref, dqs, deltas, bias, kv_buf, dkv_buf, dkv_sum, dkv_add, tile_buf,
    local_sem, ring_sem, pair_recv, tail_sem, tsend, trecv, ysend, yrecv, usend, urecv, dsend, drecv, store_sem, gsend, grecv, *ar_sems
):
    i = lax.axis_index("context")
    shard = lax.axis_index("shard")
    tokens, width = hbuf.shape
    half = width // 2
    rows = tokens // trees
    units = result.shape[0] // UNIT
    slots = lag * (contexts - 1) + 2
    ff = result.shape[2]
    pairs = grads_hbm.shape[0]
    heads = q_ref.shape[1] // HEAD
    kv_width = kv_buf.shape[1] // 2
    per_group = q_ref.shape[1] // kv_width
    low, near, far = tensor_peers()
    has_left, has_right = i > 0, i < contexts - 1
    right = {"context": lax.rem(i + 1, contexts)}
    left = {"context": lax.rem(i + contexts - 1, contexts)}
    other_shard = {"shard": 1 - shard}

    def remote(src, dst, send, recv, to):
        return pltpu.make_async_remote_copy(
            src, dst, send, recv, device_id=to, device_id_type=MESH
        )

    def fetch(*moves):
        copies = [
            pltpu.make_async_copy(src, dst, local_sem.at[at]) for at, (src, dst) in enumerate(moves)
        ]
        for copy in copies:
            copy.start()
        for copy in copies:
            copy.wait()


    def slabs(k):
        return pl.ds(k * UNIT, UNIT)

    def exchange(k):
        return remote(
            far_hbm.at[slabs(k)], came.at[slabs(k)], ysend.at[k], yrecv.at[k], other_shard
        )

    def upward(k, ring):
        return remote(
            ring.at[lax.rem(k, slots)], up_hbm.at[slabs(k)], usend.at[k], urecv.at[k], right
        )

    def downward(k, ring):
        return remote(
            ring.at[lax.rem(k, slots)], down_hbm.at[slabs(k)], dsend.at[k], drecv.at[k], left
        )

    def store(k):
        return pltpu.make_async_copy(
            out_buf.at[lax.rem(k, 2)], result.at[slabs(k)], store_sem.at[lax.rem(k, 2)]
        )

    def add_unit(k):
        u, d = k - lag * i, k - lag * (contexts - 1 - i)
        slot, up_slot, down_slot = (lax.rem(jnp.maximum(at, 0), slots) for at in (k, u, d))
        has_new = k < units
        has_up = has_left & (u >= 0) & (u < units)
        has_down = has_right & (d >= 0) & (d < units)

        def load(at, src, dst):
            return pltpu.make_async_copy(src, dst, ring_sem.at[at])

        def new_loads():
            return (
                load(0, own_hbm.at[slabs(k)], sums_ring.at[slot]),
                load(1, came.at[slabs(k)], came_buf),
            )

        def up_load():
            return load(2, up_hbm.at[slabs(u)], up_ring.at[up_slot])

        def down_load():
            return load(3, down_hbm.at[slabs(d)], down_ring.at[down_slot])

        @pl.when(has_new)
        def _():
            @pl.when((k >= slots) & (i == 0))
            def _():
                upward(k - slots, sums_ring).wait_send()

            @pl.when((k >= slots) & (i == contexts - 1))
            def _():
                downward(k - slots, sums_ring).wait_send()

            exchange(k).wait_recv()
            for copy in new_loads():
                copy.start()

        @pl.when(has_up)
        def _():
            @pl.when(has_right & (u >= slots))
            def _():
                upward(u - slots, up_ring).wait_send()

            upward(u, up_ring).wait_recv()
            up_load().start()

        @pl.when(has_down)
        def _():
            @pl.when(has_left & (d >= slots))
            def _():
                downward(d - slots, down_ring).wait_send()

            downward(d, down_ring).wait_recv()
            down_load().start()

        @pl.when(has_new)
        def _():
            for copy in new_loads():
                copy.wait()
            sums_ring[slot] = (sums_ring[slot].astype(F32) + came_buf[...].astype(F32)).astype(BF)

            @pl.when(i == 0)
            def _():
                upward(k, sums_ring).start()

            @pl.when(i == contexts - 1)
            def _():
                downward(k, sums_ring).start()

        @pl.when(has_up)
        def _():
            up_load().wait()
            up_ring[up_slot] = (
                up_ring[up_slot].astype(F32) + sums_ring[up_slot].astype(F32)
            ).astype(BF)

            @pl.when(has_right)
            def _():
                upward(u, up_ring).start()

        @pl.when(has_down)
        def _():
            down_load().wait()
            down_ring[down_slot] = (
                down_ring[down_slot].astype(F32) + sums_ring[down_slot].astype(F32)
            ).astype(BF)

            @pl.when(has_left)
            def _():
                downward(d, down_ring).start()

        e = k - lag * jnp.maximum(i, contexts - 1 - i)

        @pl.when((e >= 0) & (e < units))
        def _():
            out_slot = lax.rem(e, slots)
            here = lax.rem(e, 2)

            @pl.when(e >= 2)
            def _():
                store(e - 2).wait()

            @pl.when(i == 0)
            def _():
                out_buf[here] = down_ring[out_slot]

            @pl.when(i == contexts - 1)
            def _():
                out_buf[here] = up_ring[out_slot]

            @pl.when(has_left & has_right)
            def _():
                out_buf[here] = (
                    up_ring[out_slot].astype(F32)
                    + (down_ring[out_slot].astype(F32) - sums_ring[out_slot].astype(F32))
                ).astype(BF)

            store(e).start()


    def write_slabs(first, number, products, send=True):
        for part_index, target in ((0, own_hbm), (1, far_hbm)):
            at = 0
            for left_ref, right_value, order in products:
                block = matmul(
                    left_ref[part_index * half : (part_index + 1) * half, :], right_value
                ).astype(BF)
                for c, place in enumerate(order):
                    stage[part_index, at + place] = block[:, c * ff : (c + 1) * ff]
                at += len(order)
        fetch(
            *(
                (stage.at[p, pl.ds(0, number)], target.at[pl.ds(first, number)])
                for p, target in ((0, own_hbm), (1, far_hbm))
            )
        )
        if send:
            for c in range(number // UNIT):
                exchange(first // UNIT + c).start()

    def pair_slabs(p, send=True):
        fetch((grads_hbm.at[p], grads_buf), (cm_hbm.at[p], cm_buf))
        write_slabs(
            p * 6, 6, ((turned, grads_buf[...], (0, 2, 1, 3)), (gyt, cm_buf[...], (0, 1))), send
        )


    chunks = arrived.shape[0]
    low_half = tokens // 2

    def chunk_rows(side, c):
        return pl.ds(pl.multiple_of(side * low_half + c * CHUNK, CHUNK), CHUNK)

    def summing(source, landing, sems):
        send1, recv1, send2, recv2, send3, recv3 = sems

        def give(c):
            return remote(
                source.at[chunk_rows(1 - low, c)], arrived.at[c], send1.at[c], recv1.at[c], near
            )

        def swap(c):
            return remote(mine.at[c], landing.at[c], send2.at[c], recv2.at[c], far)

        def back(c):
            span = chunk_rows(low, c)
            return remote(total.at[span], total.at[span], send3.at[c], recv3.at[c], near)

        def start():
            for c in range(chunks):
                give(c).start()

        def middle():
            fetch(*((source.at[chunk_rows(low, c)], my_part.at[c]) for c in range(chunks)))
            for c in range(chunks):
                give(c).wait_recv()
                mine[c] = (my_part[c].astype(F32) + arrived[c].astype(F32)).astype(BF)
                swap(c).start()

        def finish(c, consume):
            swap(c).wait_recv()
            total[chunk_rows(low, c), :] = (
                mine[c].astype(F32) + landing[c].astype(F32)
            ).astype(BF)
            back(c).start()
            consume(pl.multiple_of(low * low_half + c * CHUNK, CHUNK))

        def finish_other(c, consume):
            back(c).wait_recv()
            consume(pl.multiple_of((1 - low) * low_half + c * CHUNK, CHUNK))

        def drain():
            for c in range(chunks):
                give(c).wait_send()
                swap(c).wait_send()
                back(c).wait_send()

        return start, middle, finish, finish_other, drain

    start1, middle1, finish1, other1, drain1 = summing(part, other, ar_sems[:6])
    start2, middle2, finish2, finish_other2, drain2 = summing(part2, other2, ar_sems[6:])

    def through_second_norm(row):
        span = pl.ds(row, CHUNK)
        fetch((gy_hbm.at[span], chunk_low), (h_hbm.at[span], hbuf.at[span]))
        own_h, far_h = hbuf[span, :half], hbuf[span, half:]
        inverse = inverse_norm(own_h, far_h)
        own_d, far_d, own_scale, far_scale = norm_backward(
            own_h, far_h, inverse, gains[1:2, :], total[span, :].astype(F32)
        )
        scale_ref[1:2, :half] += own_scale
        scale_ref[1:2, half:] += far_scale
        own_d = chunk_low[:, :half].astype(F32) + own_d
        far_d = chunk_low[:, half:].astype(F32) + far_d
        hbuf[span, :half] = own_d
        hbuf[span, half:] = far_d
        own_d = own_d.astype(BF)
        far_d = far_d.astype(BF)
        dat[:half, span] = own_d.T
        dat[half:, span] = far_d.T
        do_ref[span, :] = (
            contract_last(own_d, wout[...]) + contract_last(far_d, far_out[...])
        ).astype(BF)

    def through_first_norm(row):
        span = pl.ds(row, CHUNK)
        fetch((x_hbm.at[span], chunk_low))
        own_x, far_x = halves(chunk_low, slice(None), shard)
        inverse = inverse_norm(own_x, far_x)
        own_d, far_d, own_scale, far_scale = norm_backward(
            own_x, far_x, inverse, gains[0:1, :], total[span, :].astype(F32)
        )
        scale_ref[0:1, :half] += own_scale
        scale_ref[0:1, half:] += far_scale
        put_halves(
            chunk_out, slice(None), shard, hbuf[span, :half] + own_d, hbuf[span, half:] + far_d
        )
        fetch((chunk_out, out_hbm.at[span]))


    def make_deltas():
        @pl.loop(0, trees)
        def _(tree):
            span = pl.ds(pl.multiple_of(tree * rows, rows), rows)
            for head in range(heads):
                cols = slice(head * HEAD, (head + 1) * HEAD)
                product = do_ref[span, cols].astype(F32) * o_ref[span, cols].astype(F32)
                deltas[tree, head] = lax.dot_general(
                    jnp.ones((8, HEAD), F32),
                    product,
                    (((1,), (1,)), ((), ())),
                    precision=lax.Precision.HIGHEST,
                    preferred_element_type=F32,
                )

    def hand(j, tree):
        span = pl.ds(pl.multiple_of(tree * rows, rows), rows)
        return remote(
            dkv_part.at[j, span], dkv_came.at[i, span], gsend.at[j, tree], grecv.at[i, tree],
            {"context": j},
        )

    odd = lax.rem(i, 2) == 1

    def hand_to_pair(j, tree):
        span = pl.ds(pl.multiple_of(tree * rows, rows), rows)
        return remote(
            dkv_part.at[j, span], dkv_pair.at[j, span], gsend.at[j, tree], pair_recv.at[j, tree],
            left,
        )

    def merge_block(number):
        tree, j = number // contexts, lax.rem(number, contexts)

        @pl.when((number < trees * contexts) & (j < i) & (lax.rem(i, 2) == 0))
        def _():
            span = pl.ds(pl.multiple_of(tree * rows, rows), rows)
            hand_to_pair(j, tree).wait_recv()
            fetch((dkv_pair.at[j, span], dkv_add), (dkv_part.at[j, span], dkv_buf))
            dkv_buf[...] = (dkv_buf[...].astype(F32) + dkv_add[...].astype(F32)).astype(BF)
            fetch((dkv_buf, dkv_part.at[j, span]))
            hand(j, tree).start()

    def taken(c, tree):
        span = pl.ds(pl.multiple_of(tree * rows, rows), rows)
        return remote(
            dkv_part.at[c, span], dkv_came.at[c, span], gsend.at[c, tree], grecv.at[c, tree],
            {"context": c},
        )

    def attention_block(number):
        tree, j = number // contexts, lax.rem(number, contexts)

        @pl.when((number < trees * contexts) & (j <= i))
        def _():
            span = pl.ds(pl.multiple_of(tree * rows, rows), rows)
            fetch((kv_hbm.at[j, span], kv_buf))
            key_pos = j * rows + lax.broadcasted_iota(jnp.int32, (rows, rows), 0)
            query_pos = i * rows + lax.broadcasted_iota(jnp.int32, (rows, rows), 1)
            last = column(packed_all[j].T, trees + tree)
            segment = packed_all[i, pl.ds(tree, 1), :]
            allowed = (key_pos <= query_pos) & (segment <= last)
            bias[...] = jnp.where(allowed, 0.0, -2e30)
            for group in range(heads // per_group):
                keys = kv_buf[:, group * HEAD : (group + 1) * HEAD]
                values = kv_buf[:, kv_width + group * HEAD : kv_width + (group + 1) * HEAD]
                dk = jnp.zeros((rows, HEAD), F32)
                dv = jnp.zeros((rows, HEAD), F32)
                for head in range(group * per_group, (group + 1) * per_group):
                    cols = slice(head * HEAD, (head + 1) * HEAD)
                    queries = q_ref[span, cols]
                    grads = do_ref[span, cols]
                    scores = contract_last(keys, queries) * 0.125 + bias[...]
                    probs = jnp.exp(scores - lse_ref[tree, head : head + 1, :])
                    grad_probs = contract_last(values, grads)
                    grad_scores = (probs * (grad_probs - deltas[tree, head, 0:1, :])).astype(BF)
                    dv = dv + matmul(probs.astype(BF), grads)
                    dk = dk + matmul(grad_scores, queries)
                    dqs[span, cols] += contract_first(grad_scores, keys)
                dkv_buf[:, group * HEAD : (group + 1) * HEAD] = (dk * 0.125).astype(BF)
                dkv_buf[:, kv_width + group * HEAD : kv_width + (group + 1) * HEAD] = dv.astype(BF)

            @pl.when(j == i)
            def _():
                dkv_sum[span, :] = dkv_buf[...].astype(F32)

            @pl.when(j < i)
            def _():
                fetch((dkv_buf, dkv_part.at[j, span]))

                @pl.when(odd & (j == i - 1))
                def _():
                    hand(j, tree).start()

                @pl.when(odd & (j < i - 1))
                def _():
                    hand_to_pair(j, tree).start()

    def query_slabs():
        dq_ref[...] = (dqs[...] * 0.125).astype(BF)
        thirds = tuple(range(dq_ref.shape[1] // ff))
        write_slabs(
            pairs * 6, 2 * len(thirds), ((turned, dq_ref[...], thirds), (dat, o_ref[...], thirds))
        )

    def key_value_sum():
        @pl.loop(0, contexts)
        def _(c):
            @pl.when((c > i) & ((lax.rem(c, 2) == 0) | ((c == i + 1) & (lax.rem(i, 2) == 0))))
            def _():
                @pl.loop(0, trees)
                def _(tree):
                    taken(c, tree).wait_recv()
                    span = pl.ds(pl.multiple_of(tree * rows, rows), rows)
                    fetch((dkv_came.at[c, span], dkv_add))
                    dkv_sum[span, :] += dkv_add[...].astype(F32)

        grad_kv = dkv_sum[...].astype(BF)
        pieces = tuple(range(grad_kv.shape[1] // ff))
        first = pairs * 6 + 2 * (dq_ref.shape[1] // ff)
        write_slabs(first, len(pieces), ((turned, grad_kv, pieces),))

    def first_norm_parts():
        @pl.loop(0, tokens // CHUNK)
        def _(c):
            span = pl.ds(pl.multiple_of(c * CHUNK, CHUNK), CHUNK)
            grads = jnp.concatenate([dq_ref[span, :], dkv_sum[span, :].astype(BF)], axis=1)
            tile_buf[:, :half] = contract_last(grads, wqkv[...]).astype(BF)
            tile_buf[:, half:] = contract_last(grads, far_qkv[...]).astype(BF)
            fetch((tile_buf, part2.at[span]))

        start2()


    tail_copy = remote(tail_far, tail_came, tail_sem.at[0], tail_sem.at[1], other_shard)

    def tell(c, slot):
        return remote(tails.at[slot], tails.at[slot], tsend.at[c], trecv.at[slot], {"context": c})

    def send_tail():
        for begin, target in ((0, tail_own), (half, tail_far)):
            target[...] = jnp.broadcast_to(square_ref[...], target.shape)
            target[0:2, :] = scale_ref[0:2, begin : begin + half]
        tail_copy.start()

    def tell_tail():
        tail_copy.wait_recv()
        tails[i] = tail_own[...] + tail_came[...]

        @pl.loop(0, contexts)
        def _(c):
            @pl.when(c != i)
            def _():
                tell(c, i).start()


    fetch((n2t_hbm, turned), (gyt_hbm, gyt))
    pair_slabs(0, False)
    greet(
        [other_shard, near, far]
        + [{"context": lax.rem(i + c, contexts)} for c in range(1, contexts)]
    )
    for c in range(6 // UNIT):
        exchange(c).start()
    start1()
    fill_columns(wqkv, (wq, wk, wv))
    scale_ref[...] = jnp.zeros_like(scale_ref)
    dqs[...] = jnp.zeros_like(dqs)
    middle1()

    chain = []
    for finish, finish_other, consume in (
        (finish1, other1, through_second_norm), (finish2, finish_other2, through_first_norm),
    ):
        steps = [[functools.partial(finish, 0, consume)]]
        for c in range(chunks):
            steps.append([functools.partial(finish_other, c, consume)])
            if c + 1 < chunks:
                steps[-1].append(functools.partial(finish, c + 1, consume))
        chain.append(steps)
    chain[0][-1].append(make_deltas)
    tasks = {}
    for p in range(1, pairs):
        tasks[3 * p - 3] = [functools.partial(pair_slabs, p)]
    last_pair = 3 * pairs - 6
    at = 0

    def put(acts):
        nonlocal at
        at += 1
        while at in tasks:
            at += 1
        tasks[at] = acts

    for acts in chain[0]:
        put(acts)
    per_step = -(-trees * contexts // 8)

    def attention_step(number):
        @pl.loop(0, per_step)
        def _(step):
            attention_block(number * per_step + step)

    attention_steps = {}
    for number in range(8):
        at += 1
        while at in tasks:
            at += 1
        attention_steps[at] = number
    first_at, last_at = min(attention_steps), max(attention_steps)
    at = max(at, last_pair)
    put([lambda: fetch((nt_hbm, turned)), query_slabs])
    at = max(at, last_at + 6)
    put([key_value_sum])
    put([first_norm_parts])
    put([drain1, middle2])
    for acts in chain[1]:
        put(acts)
    put([send_tail])
    put([tell_tail])
    assert at < units + lag * (contexts - 1)

    @pl.loop(0, units + lag * (contexts - 1))
    def _(k):
        add_unit(k)
        for when, acts in sorted(tasks.items()):

            @pl.when(k == when)
            def _(acts=acts):
                for act in acts:
                    act()

        number, due = jnp.int32(0), k < 0
        for when, index in attention_steps.items():
            number = jnp.where(k == when, index, number)
            due = due | (k == when)

        @pl.when(due)
        def _():
            attention_step(number)

        number, due = jnp.int32(0), k < 0
        for when, index in attention_steps.items():
            number = jnp.where(k == when + 3, index, number)
            due = due | (k == when + 3)

        @pl.when(due)
        def _():
            @pl.loop(0, per_step)
            def _(step):
                merge_block(number * per_step + step)

    @pl.loop(0, contexts)
    def _(c):
        @pl.when(c != i)
        def _():
            tell(i, c).wait_recv()
            tell(c, i).wait_send()

    tail_copy.wait_send()
    tail = tails[0]
    for c in range(1, contexts):
        tail = tail + tails[c]
    tail_ref[...] = tail
    drain2()
    for k in (units - 2, units - 1):
        store(k).wait()

    @pl.loop(0, units)
    def _(k):
        exchange(k).wait_send()

        @pl.when((k >= units - slots) & has_right)
        def _():
            upward(k, up_ring).wait_send()

        @pl.when((k >= units - slots) & has_left)
        def _():
            downward(k, down_ring).wait_send()

    @pl.loop(0, contexts)
    def _(c):
        @pl.when(c < i)
        def _():
            @pl.loop(0, trees)
            def _(tree):
                hand(c, tree).wait_send()


def back(
    contexts, trees, gains, w_query, w_key, w_value, far_qkv, w_out, far_out, q, o, lse,
    packed_all, square, part, hidden, grad_y, x, normed_t, normed_two_t, grad_y_t, grads, middle, kv,
):
    tokens, width = hidden.shape
    half, rows = width // 2, tokens // trees
    pairs, _, four = grads.shape
    ff, cols, both = four // 4, q.shape[1], kv.shape[2]
    count = pairs * 6 + (2 * cols + both) // ff
    units = count // UNIT
    lag = 2 if contexts <= 4 else 1
    slots = lag * (contexts - 1) + 2
    chunks = tokens // 2 // CHUNK
    shape, vmem, dma = jax.ShapeDtypeStruct, pltpu.VMEM, pltpu.SemaphoreType.DMA
    slabs = shape((count, half, ff), BF)
    unit = (UNIT, half, ff)
    piece = vmem((chunks, CHUNK, width), BF)
    anywhere = pl.BlockSpec(memory_space=pl.ANY)
    near_memory = pl.BlockSpec(memory_space=pltpu.VMEM)
    outs = pl.pallas_call(
        functools.partial(back_kernel, contexts, trees, lag),
        out_shape=(
            slabs,
            shape((tokens, width), F32),
            shape((8, half), F32),
            *(slabs,) * 5,
            shape((tokens, width), BF),
            shape(kv.shape, BF),
            shape(kv.shape, BF),
            shape(kv.shape, BF),
        ),
        in_specs=[near_memory] * 12 + [anywhere] * 10,
        out_specs=(anywhere,) * 2 + (near_memory,) + (anywhere,) * 9,
        scratch_shapes=[
            vmem((half, cols + both), BF),
            vmem((8, width), F32),
            vmem((8, half), F32),
            vmem((8, half), F32),
            vmem((8, half), F32),
            vmem((contexts, 8, half), F32),
            vmem((slots,) + unit, BF),
            vmem((slots,) + unit, BF),
            vmem((slots,) + unit, BF),
            vmem(unit, BF),
            vmem((2,) + unit, BF),
            vmem((width, tokens), BF),
            vmem((width, tokens), BF),
            vmem((tokens, 4 * ff), BF),
            vmem((tokens, 2 * ff), BF),
            vmem((2, 6, half, ff), BF),
            vmem((tokens, width), F32),
            vmem((CHUNK, width), BF),
            vmem((CHUNK, width), F32),
            piece,
            vmem((tokens, width), BF),
            piece,
            piece,
            piece,
            piece,
            vmem((width, tokens), BF),
            vmem((tokens, cols), BF),
            vmem((tokens, cols), BF),
            vmem((tokens, cols), F32),
            vmem((trees, cols // HEAD, 8, rows), F32),
            vmem((rows, rows), F32),
            vmem((rows, both), BF),
            vmem((rows, both), BF),
            vmem((tokens, both), F32),
            vmem((rows, both), BF),
            vmem((CHUNK, width), BF),
            dma((4,)),
            dma((4,)),
            dma((contexts, trees)),
            dma((2,)),
            dma((contexts,)),
            dma((contexts,)),
        ]
        + [dma((units,))] * 6
        + [dma((2,)), dma((contexts, trees)), dma((contexts, trees))]
        + [dma((chunks,))] * 12,
        compiler_params=pltpu.CompilerParams(
            collective_id=1, has_side_effects=True, vmem_limit_bytes=60 * 1024 * 1024
        ),
        cost_estimate=COST,
        name="back",
    )(
        gains, w_query, w_key, w_value, far_qkv, w_out, far_out, q, o, lse, packed_all,
        square, part, hidden, grad_y, x, normed_t, normed_two_t, grad_y_t, grads, middle, kv,
    )
    return outs[:3]


def local(
    states, segments, routes, gates, valid, teacher, attn_gain, w_query, key_matrix, value_matrix,
    w_out, moe_gain, w_gate, w_up, w_down,
):
    shards = lax.axis_size("shard")
    contexts = lax.axis_size("context")
    trees, rows, width = states.shape
    tokens = trees * rows
    half = width // 2
    experts = w_gate.shape[0]
    x = states.reshape(tokens, width)
    (
        packed_all, gains, qkv_far, out_far, gate_far, up_far, down_far, q, kv, normed_t,
        attended, lse, hidden, normed_two, normed_two_t, count, combine,
    ) = front(
        contexts, trees, x, segments, valid, routes.transpose(0, 2, 1), gates.transpose(0, 2, 1),
        attn_gain, moe_gain, w_query, key_matrix, value_matrix, w_out, w_gate, w_up, w_down,
    )
    gate_ws, up_ws, down_ws = (w_gate, gate_far), (w_up, up_far), (w_down, down_far)

    pre, middle, result, grad_y, grad_y_t, square = experts_forward(
        float(tokens * shards * contexts),
        normed_two,
        combine,
        count,
        gate_ws,
        up_ws,
        down_ws,
        hidden,
        teacher.reshape(tokens, width),
    )
    expert_grads, dn_part = experts_backward(grad_y, combine, gate_ws, up_ws, down_ws, pre)
    sums, grad_inputs, tail = back(
        contexts, trees, gains, w_query, key_matrix, value_matrix, qkv_far, w_out, out_far, q,
        attended, lse, packed_all, square, dn_part, hidden, grad_y, x, normed_t, normed_two_t,
        grad_y_t, expert_grads, middle, kv,
    )
    final_query, final_out, final_key, final_value, final_gain1, final_gain2, loss = (
        unpack_attention(sums, tail, count, w_query.shape[1], key_matrix.shape[1])
    )
    final_gate, final_up, final_down = unpack(sums, experts // 2)
    return (
        loss[0, 0],
        result.reshape(trees, rows, width),
        grad_inputs.reshape(trees, rows, width),
        final_gain1,
        final_query,
        final_key,
        final_value,
        final_out,
        final_gain2,
        final_gate,
        final_up,
        final_down,
    )


def solution(mesh):
    return jax.shard_map(
        local,
        mesh=mesh,
        in_specs=(
            P("shard", "context", None),
            P("shard", "context"),
            P("shard", "context", None),
            P("shard", "context", None),
            P("shard", "context"),
            P("shard", "context", None),
            P("shard"),
            P("shard", "tensor"),
            P("shard", "tensor"),
            P("shard", "tensor"),
            P("tensor", "shard"),
            P("shard"),
            P(None, "shard", "tensor"),
            P(None, "shard", "tensor"),
            P(None, "tensor", "shard"),
        ),
        out_specs=(
            P(),
            P("shard", "context", None),
            P("shard", "context", None),
            P("shard"),
            P("shard", "tensor"),
            P("shard", "tensor"),
            P("shard", "tensor"),
            P("tensor", "shard"),
            P("shard"),
            P(None, "shard", "tensor"),
            P(None, "shard", "tensor"),
            P(None, "tensor", "shard"),
        ),
        check_vma=False,
    )
```

```python
import functools
import math

import jax
import jax.numpy as jnp
from jax import lax
from jax.experimental import pallas as pl
from jax.experimental.pallas import tpu as pltpu
from jax.sharding import PartitionSpec as P

HEAD = 64
EPS = 1e-05
BF = jnp.bfloat16
F32 = jnp.float32
MESH = pl.DeviceIdType.MESH
VMEM_LIMIT = 56 * 1024 * 1024
UNIT = 2
COST = pl.CostEstimate(flops=1, bytes_accessed=1, transcendentals=0)


def matmul(left, right):
    return jnp.dot(left, right, preferred_element_type=F32)


def contract_first(left, right):
    return lax.dot_general(left, right, (((0,), (0,)), ((), ())), preferred_element_type=F32)


def contract_last(left, right):
    return lax.dot_general(left, right, (((1,), (1,)), ((), ())), preferred_element_type=F32)


def column(block, index):
    lane = lax.broadcasted_iota(jnp.int32, block.shape, 1)
    return jnp.sum(jnp.where(lane == index, block, 0.0), axis=1, keepdims=True)


def experts_backward_kernel(
    gy_ref, c_ref, g0, g1, u0, u1, d0, d1, pre_hbm, y_hbm, grads_hbm, dn_ref, y_out,
    wide, tall, grads, pre_buf, y_buf, weight_sem, pre_sem, out_sem, y_sem,
):
    pairs, tokens = pre_hbm.shape[0], gy_ref.shape[0]
    half, ff = g0.shape[1], g0.shape[2]
    tile = 256

    def weight_loads(p):
        copies = []
        for side, gate, up, down in ((0, g0, u0, d0), (1, g1, u1, d1)):
            features = pl.ds(side * half, half)
            for a in range(2):
                e = 2 * p + a
                for source, target in (
                    (gate, wide.at[features, pl.ds(pl.multiple_of(2 * e * ff, 128), ff)]),
                    (up, wide.at[features, pl.ds(pl.multiple_of((2 * e + 1) * ff, 128), ff)]),
                    (down, tall.at[p, pl.ds(a * ff, ff), features]),
                ):
                    copies.append(
                        pltpu.make_async_copy(
                            source.at[e], target, weight_sem.at[p, len(copies)]
                        )
                    )
        return copies

    def pre_load(p):
        return pltpu.make_async_copy(
            pre_hbm.at[p], pre_buf.at[lax.rem(p, 2)], pre_sem.at[lax.rem(p, 2)]
        )

    def span(p):
        return pl.ds(pl.multiple_of(p * 4 * ff, 128), 4 * ff)

    def store(p):
        return pltpu.make_async_copy(grads.at[:, span(p)], grads_hbm.at[p], out_sem.at[p])

    for copy in weight_loads(0):
        copy.start()
    pre_load(0).start()

    @pl.loop(1, pairs)
    def _(p):
        for copy in weight_loads(p):
            copy.start()

    y_load = pltpu.make_async_copy(y_hbm, y_buf, y_sem.at[0])
    y_store = pltpu.make_async_copy(y_buf, y_out, y_sem.at[1])
    y_load.start()

    @pl.loop(0, pairs)
    def _(p):
        @pl.when(p + 1 < pairs)
        def _():
            pre_load(p + 1).start()

        for copy in weight_loads(p):
            copy.wait()
        pre_load(p).wait()
        slot = lax.rem(p, 2)
        grad_middle = contract_last(gy_ref[...], tall[p])
        pieces = []
        for a in range(2):
            gate = pre_buf[slot, :, 2 * a * ff : (2 * a + 1) * ff].astype(F32)
            up = pre_buf[slot, :, (2 * a + 1) * ff : (2 * a + 2) * ff].astype(F32)
            weight = column(c_ref[...], 2 * p + a)
            gm = weight * grad_middle[:, a * ff : (a + 1) * ff]
            sig = jax.nn.sigmoid(gate)
            pieces.append((gm * up * (sig + gate * sig * (1.0 - sig))).astype(BF))
            pieces.append((gm * gate * sig).astype(BF))
        grads[:, span(p)] = jnp.concatenate(pieces, axis=1)
        store(p).start()

    y_load.wait()
    y_store.start()

    @pl.loop(0, 2 * half // tile)
    def _(index):
        rows = pl.ds(pl.multiple_of(index * tile, tile), tile)
        dn_ref[:, rows] = contract_last(grads[...], wide[rows, :]).astype(BF)

    @pl.loop(0, pairs)
    def _(p):
        store(p).wait()

    y_store.wait()


def experts_backward(grad_y, combine, gates, ups, downs, pre, result):
    tokens, width = grad_y.shape
    experts, half, ff = gates[0].shape
    pairs = experts // 2
    vmem, dma = pltpu.VMEM, pltpu.SemaphoreType.DMA
    anywhere = pl.BlockSpec(memory_space=pl.ANY)
    near_memory = pl.BlockSpec(memory_space=pltpu.VMEM)
    return pl.pallas_call(
        experts_backward_kernel,
        out_shape=(
            jax.ShapeDtypeStruct((pairs, tokens, 4 * ff), BF),
            jax.ShapeDtypeStruct((tokens, width), BF),
            jax.ShapeDtypeStruct(result.shape, BF),
        ),
        in_specs=[near_memory] * 2 + [anywhere] * 8,
        out_specs=(anywhere, near_memory, anywhere),
        scratch_shapes=[
            vmem((width, 2 * experts * ff), BF),
            vmem((pairs, 2 * ff, width), BF),
            vmem((tokens, 2 * experts * ff), BF),
            vmem((2, tokens, 4 * ff), BF),
            vmem(result.shape, BF),
            dma((pairs, 12)),
            dma((2,)),
            dma((pairs,)),
            dma((2,)),
        ],
        compiler_params=pltpu.CompilerParams(vmem_limit_bytes=60 * 1024 * 1024),
        cost_estimate=COST,
        name="experts_backward",
    )(grad_y, combine, *gates, *ups, *downs, pre, result)


def unpack_kernel(slabs_ref, gate_ref, up_ref, down_ref):
    for a in range(2):
        gate_ref[a] = slabs_ref[a].astype(F32)
        up_ref[a] = slabs_ref[2 + a].astype(F32)
        down_ref[a] = slabs_ref[4 + a].T.astype(F32)


def unpack(slabs, steps):
    _, half, ff = slabs.shape
    wide = jax.ShapeDtypeStruct((2 * steps, half, ff), F32)
    tall = jax.ShapeDtypeStruct((2 * steps, ff, half), F32)
    return pl.pallas_call(
        unpack_kernel,
        out_shape=(wide, wide, tall),
        grid=(steps,),
        in_specs=[pl.BlockSpec((6, half, ff), lambda i: (i, 0, 0))],
        out_specs=[pl.BlockSpec((2, half, ff), lambda i: (i, 0, 0))] * 2
        + [pl.BlockSpec((2, ff, half), lambda i: (i, 0, 0))],
        compiler_params=pltpu.CompilerParams(vmem_limit_bytes=VMEM_LIMIT),
        cost_estimate=COST,
        name="unpack",
    )(slabs)


def unpack_attention_kernel(
    width, slabs_ref, tail_ref, count_ref, q_ref, out_ref, k_ref, v_ref, gain1_ref, gain2_ref, loss_ref
):
    gain1_ref[...] = tail_ref[0:1, :].reshape(gain1_ref.shape)
    gain2_ref[...] = tail_ref[1:2, :].reshape(gain2_ref.shape)
    loss_ref[...] = tail_ref[2:3, 0:1] / (count_ref[...] * width)
    ff = slabs_ref.shape[2]
    at = 0
    for ref, turn in ((q_ref, False), (out_ref, True), (k_ref, False), (v_ref, False)):
        for c in range(ref.shape[0 if turn else 1] // ff):
            value = slabs_ref[at].astype(F32)
            if turn:
                ref[c * ff : (c + 1) * ff, :] = value.T
            else:
                ref[:, c * ff : (c + 1) * ff] = value
            at += 1


def unpack_attention(slabs, tail, count, query_cols, key_cols):
    total, rows, ff = slabs.shape
    number = 2 * (query_cols + key_cols) // ff
    shapes = (
        (rows, query_cols), (query_cols, rows), (rows, key_cols), (rows, key_cols),
        (rows,), (rows,), (1, 1),
    )
    return pl.pallas_call(
        functools.partial(unpack_attention_kernel, 2 * rows),
        out_shape=tuple(jax.ShapeDtypeStruct(shape, F32) for shape in shapes),
        grid=(1,),
        in_specs=[
            pl.BlockSpec((number, rows, ff), lambda i: (total // number - 1, 0, 0)),
            pl.BlockSpec(tail.shape, lambda i: (0, 0)),
            pl.BlockSpec((1, 1), lambda i: (0, 0)),
        ],
        out_specs=[
            pl.BlockSpec(shape, (lambda i: (0, 0)) if len(shape) == 2 else (lambda i: (0,)))
            for shape in shapes
        ],
        compiler_params=pltpu.CompilerParams(vmem_limit_bytes=VMEM_LIMIT),
        cost_estimate=COST,
        name="unpack_attention",
    )(slabs, tail, count)


def inverse_norm(near, far):
    count = near.shape[1] + far.shape[1]
    squares = jnp.sum(near * near, axis=1, keepdims=True) + jnp.sum(far * far, axis=1, keepdims=True)
    return lax.rsqrt(squares / count + EPS)


def halves(ref, rows, shard):
    half = ref.shape[1] // 2
    own = pl.ds(pl.multiple_of(shard * half, 128), half)
    far = pl.ds(pl.multiple_of((1 - shard) * half, 128), half)
    return ref[rows, own].astype(F32), ref[rows, far].astype(F32)


def put_halves(ref, rows, shard, near, far):
    half = ref.shape[1] // 2
    ref[rows, pl.ds(pl.multiple_of(shard * half, 128), half)] = near.astype(ref.dtype)
    ref[rows, pl.ds(pl.multiple_of((1 - shard) * half, 128), half)] = far.astype(ref.dtype)


def norm_backward(near, far, inverse, gain, grads):
    half = near.shape[1]
    near_scaled = grads[:, :half] * gain[:, :half]
    far_scaled = grads[:, half:] * gain[:, half:]
    along = (
        jnp.sum(near_scaled * near, axis=1, keepdims=True)
        + jnp.sum(far_scaled * far, axis=1, keepdims=True)
    ) / (2 * half)
    cube = inverse * inverse * inverse * along
    return (
        inverse * near_scaled - near * cube,
        inverse * far_scaled - far * cube,
        jnp.sum(grads[:, :half] * near * inverse, axis=0, keepdims=True),
        jnp.sum(grads[:, half:] * far * inverse, axis=0, keepdims=True),
    )


CHUNK = 128


def tensor_peers():
    t = lax.axis_index("tensor")
    low, high = lax.rem(t, 2), lax.rem(t // 2, 2)
    return low, {"tensor": t + 1 - 2 * low}, {"tensor": t + 2 - 4 * high}


def greet(peers):
    barrier = pltpu.get_barrier_semaphore()
    for peer in peers:
        pl.semaphore_signal(barrier, inc=1, device_id=peer, device_id_type=MESH)
    pl.semaphore_wait(barrier, len(peers))


def sum_over_tensor(part, total, arrived, mine, other, sems, consume, between=lambda c: None):
    send1, recv1, send2, recv2, send3, recv3 = sems
    low, near, far = tensor_peers()
    chunks = arrived.shape[0]
    half = chunks * CHUNK

    def rows(side, c):
        return pl.ds(pl.multiple_of(side * half + c * CHUNK, CHUNK), CHUNK)

    def give(c):
        return pltpu.make_async_remote_copy(
            part.at[rows(1 - low, c)], arrived.at[c], send1.at[c], recv1.at[c],
            device_id=near, device_id_type=MESH,
        )

    def swap(c):
        return pltpu.make_async_remote_copy(
            mine.at[c], other.at[c], send2.at[c], recv2.at[c], device_id=far, device_id_type=MESH
        )

    def back(c):
        return pltpu.make_async_remote_copy(
            total.at[rows(low, c)], total.at[rows(low, c)], send3.at[c], recv3.at[c],
            device_id=near, device_id_type=MESH,
        )

    @pl.loop(0, chunks)
    def _(c):
        give(c).start()

    @pl.loop(0, chunks)
    def _(c):
        give(c).wait_recv()
        mine[c] = (part[rows(low, c), :].astype(F32) + arrived[c].astype(F32)).astype(BF)
        swap(c).start()

    @pl.loop(0, chunks)
    def _(c):
        between(c)
        swap(c).wait_recv()
        total[rows(low, c), :] = (mine[c].astype(F32) + other[c].astype(F32)).astype(BF)
        back(c).start()
        consume(pl.multiple_of(low * half + c * CHUNK, CHUNK))
        back(c).wait_recv()
        consume(pl.multiple_of((1 - low) * half + c * CHUNK, CHUNK))

    @pl.loop(0, chunks)
    def _(c):
        give(c).wait_send()
        swap(c).wait_send()
        back(c).wait_send()


def sum_scratch(tokens, width):
    chunks = tokens // 2 // CHUNK
    piece = pltpu.VMEM((chunks, CHUNK, width), BF)
    return [pltpu.VMEM((tokens, width), BF)] + [piece] * 3 + [
        pltpu.SemaphoreType.DMA((chunks,))
    ] * 6


def fill_columns(target, refs):
    at = 0
    for ref in refs:
        target[:, at : at + ref.shape[1]] = ref[...]
        at += ref.shape[1]


def front_kernel(
    contexts, trees, x_ref, seg_ref, valid_ref, routes_ref, gates_ref, gain1_ref, gain2_ref, wq, wk, wv, wout, w_gate, w_up, w_down,
    packed_all, all_gains, far_qkv, far_out, far_gate, far_up, far_down,
    q_ref, kv_out, nt_out, o_ref, lse_ref, h_out, n2_out, n2t_out, count_ref, c_ref,
    packed, gains, wqkv, far_gains, kv_all, nt_ref, h_ref, n2_ref, n2t_ref,
    normed, bias, tops, norms, sums, part, total, arrived, mine, other,
    ysend, yrecv, rsend, rrecv, psend, precv, ksend, krecv, out_sem, *sems
):
    i = lax.axis_index("context")
    shard = lax.axis_index("shard")
    parity = lax.rem(i, 2)
    tokens, width = x_ref.shape
    half = width // 2
    rows = tokens // trees
    heads = q_ref.shape[1] // HEAD
    kv_width = kv_all.shape[2] // 2
    per_group = q_ref.shape[1] // kv_width
    other_shard = {"shard": 1 - shard}
    partner = {"context": i + 1 - 2 * parity}
    right = {"context": lax.rem(i + 1, contexts)}
    _, near, far = tensor_peers()
    fill_columns(wqkv, (wq, wk, wv))
    segment = seg_ref[...]
    last = jnp.where(
        segment == 0, 1 << 20, jnp.where(lax.rem(segment, 3) == 1, segment + 2, segment)
    )
    packed[...] = jnp.zeros_like(packed)
    packed[0:trees, :] = segment.astype(F32)
    packed[trees : 2 * trees, :] = last.astype(F32)
    packed[2 * trees + 1 : 3 * trees + 1, :] = valid_ref[...].astype(F32)
    counted = jnp.sum(jnp.sum(valid_ref[...].astype(F32), axis=1, keepdims=True), axis=0, keepdims=True)
    gains[...] = jnp.broadcast_to(counted, gains.shape)
    gains[0:1, :] = gain1_ref[...].reshape(1, half)
    gains[1:2, :] = gain2_ref[...].reshape(1, half)
    greet(
        [other_shard, near, far]
        + [{"context": lax.rem(i + c, contexts)} for c in range(1, contexts)]
    )

    def half_span(ref, axis):
        size = ref.shape[axis] // 2
        return pl.ds(pl.multiple_of(parity * size, size), size)

    experts = w_gate.shape[0]
    shared = experts // 8
    own_count = (experts - shared) // 2
    moves = [
        (wqkv.at[half_span(wqkv, 0)], far_qkv.at[half_span(wqkv, 0)]),
        (wout.at[:, half_span(wout, 1)], far_out.at[:, half_span(wout, 1)]),
    ]
    first = (own_count + 1) // 2
    for begin, size in (
        (parity * own_count, first),
        (parity * own_count + first, own_count - first),
        (2 * own_count, shared),
    ):
        span = pl.ds(begin, size)
        for source, target in ((w_gate, far_gate), (w_up, far_up), (w_down, far_down)):
            moves.append((source.at[span], target.at[span]))
    relays = len(moves) - 3

    def direct(m):
        source, target = moves[m]
        return pltpu.make_async_remote_copy(
            source, target, ysend.at[m], yrecv.at[m],
            device_id=other_shard, device_id_type=MESH,
        )

    def relay(m):
        target = moves[m][1]
        return pltpu.make_async_remote_copy(
            target, target, rsend.at[m], rrecv.at[m], device_id=partner, device_id_type=MESH
        )

    def pass_on(m):
        direct(m).wait_recv()
        relay(m).start()

    count = len(moves)
    gain_copy = pltpu.make_async_remote_copy(
        gains, far_gains, ysend.at[count], yrecv.at[count],
        device_id=other_shard, device_id_type=MESH,
    )

    def tell(c, slot):
        return pltpu.make_async_remote_copy(
            packed, packed_all.at[slot], psend.at[c], precv.at[slot],
            device_id={"context": c}, device_id_type=MESH,
        )

    def lift(j):
        return pltpu.make_async_remote_copy(
            kv_all.at[j], kv_all.at[j], ksend.at[j], krecv.at[j],
            device_id=right, device_id_type=MESH,
        )

    outs = [
        pltpu.make_async_copy(src, dst, out_sem.at[at])
        for at, (src, dst) in enumerate((
            (nt_ref, nt_out), (kv_all, kv_out), (h_ref, h_out), (n2_ref, n2_out), (n2t_ref, n2t_out),
        ))
    ]
    gain_copy.start()
    for m in range(count):
        direct(m).start()

    gain_copy.wait_recv()
    packed[2 * trees : 2 * trees + 1, :] = gains[2:3, :rows] + far_gains[2:3, :rows]
    packed_all[i] = packed[...]

    @pl.loop(0, contexts)
    def _(c):
        @pl.when(c != i)
        def _():
            tell(c, i).start()

    all_gains[:, :half] = gains[...]
    all_gains[:, half:] = far_gains[...]
    tile = 128

    @pl.loop(0, tokens // tile)
    def _(index):
        span = pl.ds(pl.multiple_of(index * tile, tile), tile)
        own_x, far_x = halves(x_ref, span, shard)
        inverse = inverse_norm(own_x, far_x)
        own_x = (own_x * inverse * gains[0:1, :]).astype(BF)
        far_x = (far_x * inverse * far_gains[0:1, :]).astype(BF)
        normed[span, :half] = own_x
        normed[span, half:] = far_x
        nt_ref[:half, span] = own_x.T
        nt_ref[half:, span] = far_x.T

    outs[0].start()
    pack_t = packed[...].T
    lane = lax.broadcasted_iota(jnp.int32, (rows, c_ref.shape[1]), 1).astype(F32)
    for tree in range(trees):
        weights = jnp.where(lane == float(experts), column(pack_t, 2 * trees + 1 + tree), 0.0)
        routes = routes_ref[tree].astype(F32).T
        gates = gates_ref[tree].T
        for at in range(routes.shape[1]):
            weights = weights + jnp.where(
                routes[:, at : at + 1] == lane, gates[:, at : at + 1], 0.0
            )
        c_ref[tree * rows : (tree + 1) * rows, :] = weights
    pass_on(0)
    pass_on(1)
    relay(0).wait_recv()
    qkv = matmul(normed[:, :half], wqkv[...]) + matmul(normed[:, half:], far_qkv[...])
    q_ref[...] = qkv[:, : q_ref.shape[1]].astype(BF)
    kv_all[i] = qkv[:, q_ref.shape[1] :].astype(BF)

    @pl.when(i < contexts - 1)
    def _():
        lift(i).start()

    tops[...] = jnp.full_like(tops, -1e30)
    norms[...] = jnp.zeros_like(norms)
    sums[...] = jnp.zeros_like(sums)

    @pl.loop(0, contexts)
    def _(c):
        @pl.when(c != i)
        def _():
            tell(i, c).wait_recv()

    counted = packed_all[0, 2 * trees : 2 * trees + 1, 0:1]
    for c in range(1, contexts):
        counted = counted + packed_all[c, 2 * trees : 2 * trees + 1, 0:1]
    count_ref[...] = counted

    @pl.loop(0, contexts)
    def _(d):
        @pl.when(d <= i)
        def _():
            j = i - d

            @pl.when(d > 0)
            def _():
                lift(j).wait_recv()

                @pl.when(i < contexts - 1)
                def _():
                    lift(j).start()

            @pl.loop(0, trees)
            def _(tree):
                span = pl.ds(pl.multiple_of(tree * rows, rows), rows)
                key_pos = j * rows + lax.broadcasted_iota(jnp.int32, (rows, rows), 1)
                query_pos = i * rows + lax.broadcasted_iota(jnp.int32, (rows, rows), 0)
                last = packed_all[j, pl.ds(trees + tree, 1), :]
                allowed = (key_pos <= query_pos) & (column(pack_t, tree) <= last)
                bias[...] = jnp.where(allowed, 0.0, -2e30)
                for head in range(heads):
                    group = head // per_group
                    cols = slice(head * HEAD, (head + 1) * HEAD)
                    keys = kv_all[j, span, group * HEAD : (group + 1) * HEAD]
                    values = kv_all[
                        j, span, kv_width + group * HEAD : kv_width + (group + 1) * HEAD
                    ]
                    scores = contract_last(q_ref[span, cols], keys) * 0.125 + bias[...]
                    old = tops[span, head : head + 1]
                    top = jnp.maximum(old, jnp.max(scores, axis=1, keepdims=True))
                    weights = jnp.exp(scores - top)
                    shrink = jnp.exp(old - top)
                    tops[span, head : head + 1] = top
                    norms[span, head : head + 1] = norms[span, head : head + 1] * shrink + jnp.sum(
                        weights, axis=1, keepdims=True
                    )
                    sums[span, cols] = sums[span, cols] * shrink + matmul(
                        weights.astype(BF), values
                    )

        @pl.when(d == 0)
        def _():
            pass_on(2)

        @pl.when(d == min(2, contexts - 1))
        def _():
            pass_on(3)

    for head in range(heads):
        cols = slice(head * HEAD, (head + 1) * HEAD)
        o_ref[:, cols] = (sums[:, cols] / norms[:, head : head + 1]).astype(BF)
    lse = tops[...] + jnp.log(norms[...] + jnp.where(norms[...] == 0.0, 1.0, 0.0))
    for tree in range(trees):
        lse_ref[tree] = lse[tree * rows : (tree + 1) * rows].T[: lse_ref.shape[1]]
    outs[1].start()
    relay(1).wait_recv()
    part[:, :half] = matmul(o_ref[...], wout[...]).astype(BF)
    part[:, half:] = matmul(o_ref[...], far_out[...]).astype(BF)

    def consume(row):
        span = pl.ds(row, CHUNK)
        own_x, far_x = halves(x_ref, span, shard)
        own_x = own_x + total[span, :half].astype(F32)
        far_x = far_x + total[span, half:].astype(F32)
        h_ref[span, :half] = own_x
        h_ref[span, half:] = far_x
        inverse = inverse_norm(own_x, far_x)
        own_x = (own_x * inverse * gains[1:2, :]).astype(BF)
        far_x = (far_x * inverse * far_gains[1:2, :]).astype(BF)
        n2_ref[span, :half] = own_x
        n2_ref[span, half:] = far_x
        n2t_ref[:half, span] = own_x.T
        n2t_ref[half:, span] = far_x.T

    chunks = arrived.shape[0]

    def between(c):
        for at in range(chunks):

            @pl.when(c == at)
            def _():
                pass_on(4 + at)

    sum_over_tensor(part, total, arrived, mine, other, sems, consume, between)
    for copy in outs[2:]:
        copy.start()
    for m in range(4 + chunks, relays):
        pass_on(m)
    for m in range(2, relays):
        relay(m).wait_recv()
    for m in range(relays, count):
        direct(m).wait_recv()
    for m in range(count):
        direct(m).wait_send()
        if m < relays:
            relay(m).wait_send()
    gain_copy.wait_send()
    for copy in outs:
        copy.wait()

    @pl.loop(0, contexts)
    def _(c):
        @pl.when(c != i)
        def _():
            tell(c, i).wait_send()

        @pl.when((c <= i) & (i < contexts - 1))
        def _():
            lift(c).wait_send()


def front(
    contexts, trees, x, segments, valid, routes, gates, gain1, gain2, w_query, w_key, w_value,
    w_out, w_gate, w_up, w_down,
):
    tokens, width = x.shape
    half, rows = width // 2, tokens // trees
    cols = w_out.shape[0]
    both = w_key.shape[1] + w_value.shape[1]
    anywhere = pl.BlockSpec(memory_space=pl.ANY)
    near_memory = pl.BlockSpec(memory_space=pltpu.VMEM)
    shape, vmem, dma = jax.ShapeDtypeStruct, pltpu.VMEM, pltpu.SemaphoreType.DMA
    buffers = sum_scratch(tokens, width)
    return pl.pallas_call(
        functools.partial(front_kernel, contexts, trees),
        out_shape=(
            shape((contexts, 8, rows), F32),
            shape((8, width), F32),
            shape((half, cols + both), BF),
            *(shape(ref.shape, BF) for ref in (w_out, w_gate, w_up, w_down)),
            shape((tokens, cols), BF),
            shape((contexts, tokens, both), BF),
            shape((width, tokens), BF),
            shape((tokens, cols), BF),
            shape((trees, 8, rows), F32),
            shape((tokens, width), F32),
            shape((tokens, width), BF),
            shape((width, tokens), BF),
            shape((1, 1), F32),
            shape((tokens, 128), F32),
        ),
        in_specs=[near_memory] * 11 + [anywhere] * 3,
        out_specs=(near_memory,) * 4
        + (anywhere,) * 3
        + (near_memory, anywhere, anywhere, near_memory, near_memory)
        + (anywhere,) * 3
        + (near_memory,) * 2,
        scratch_shapes=[
            vmem((8, rows), F32),
            vmem((8, half), F32),
            vmem((half, cols + both), BF),
            vmem((8, half), F32),
            vmem((contexts, tokens, both), BF),
            vmem((width, tokens), BF),
            vmem((tokens, width), F32),
            vmem((tokens, width), BF),
            vmem((width, tokens), BF),
            vmem((tokens, width), BF),
            vmem((rows, rows), F32),
            vmem((tokens, 128), F32),
            vmem((tokens, 128), F32),
            vmem((tokens, cols), F32),
            vmem((tokens, width), BF),
        ]
        + buffers[:4]
        + [dma((12,)), dma((12,)), dma((8,)), dma((8,))]
        + [dma((contexts,))] * 4
        + [dma((5,))]
        + buffers[4:],
        compiler_params=pltpu.CompilerParams(
            collective_id=2, has_side_effects=True, vmem_limit_bytes=60 * 1024 * 1024
        ),
        cost_estimate=COST,
        name="front",
    )(
        x, segments, valid, routes, gates, gain1, gain2, w_query, w_key, w_value, w_out,
        w_gate, w_up, w_down,
    )


def experts_forward_kernel(
    token_total, n_ref, c_ref, count_ref, g0, g1, u0, u1, d0, d1, h_hbm, teacher_hbm,
    pre_hbm, cm_hbm, y_hbm, low_hbm, lowt_hbm, square_ref,
    wide, tall, pre_buf, cm_all, part, h_ref, teacher_ref, y_ref, low_ref, lowt_ref,
    weight_sem, in_sem, pre_sem, out_sem, total, arrived, mine, other,
    send1, recv1, send2, recv2, send3, recv3,
):
    tokens, width = h_ref.shape
    half = width // 2
    pairs, ff = wide.shape[0], g0.shape[2]
    chunks = arrived.shape[0]
    shard = lax.axis_index("shard")
    low_side, near, far = tensor_peers()
    loads = [
        pltpu.make_async_copy(h_hbm, h_ref, in_sem.at[0]),
        pltpu.make_async_copy(teacher_hbm, teacher_ref, in_sem.at[1]),
    ]

    def weight_loads(p):
        copies = []
        for side, gate, up, down in ((0, g0, u0, d0), (1, g1, u1, d1)):
            features = pl.ds(side * half, half)
            for a in range(2):
                for source, target in (
                    (gate, wide.at[p, features, pl.ds(2 * a * ff, ff)]),
                    (up, wide.at[p, features, pl.ds((2 * a + 1) * ff, ff)]),
                    (down, tall.at[pl.ds((2 * p + a) * ff, ff), features]),
                ):
                    copies.append(
                        pltpu.make_async_copy(
                            source.at[2 * p + a], target, weight_sem.at[p, len(copies)]
                        )
                    )
        return copies

    @pl.loop(0, pairs)
    def _(p):
        for copy in weight_loads(p):
            copy.start()

    for copy in loads:
        copy.start()
    square_ref[...] = jnp.zeros_like(square_ref)
    greet([near, far])

    def rows(side, c):
        return pl.ds(pl.multiple_of((2 * c + side) * CHUNK, CHUNK), CHUNK)

    def both_rows(c):
        return pl.ds(pl.multiple_of(2 * c * CHUNK, 2 * CHUNK), 2 * CHUNK)

    def remote(src, dst, send, recv, to):
        return pltpu.make_async_remote_copy(
            src, dst, send, recv, device_id=to, device_id_type=MESH
        )

    def give(c):
        return remote(part.at[rows(1 - low_side, c)], arrived.at[c], send1.at[c], recv1.at[c], near)

    def swap(c):
        return remote(mine.at[c], other.at[c], send2.at[c], recv2.at[c], far)

    def back_copy(c):
        span = rows(low_side, c)
        return remote(total.at[span], total.at[span], send3.at[c], recv3.at[c], near)

    def kept(c, p):
        slot = lax.rem(p, 2)
        return (
            pltpu.make_async_copy(
                pre_buf.at[slot], pre_hbm.at[p, both_rows(c)], pre_sem.at[slot, 0]
            ),
            pltpu.make_async_copy(
                cm_all.at[:, pl.ds(pl.multiple_of(p * 2 * ff, 128), 2 * ff)],
                cm_hbm.at[p, both_rows(c)],
                pre_sem.at[slot, 1],
            ),
        )

    @pl.loop(0, chunks)
    def _(c):
        span = both_rows(c)

        @pl.loop(0, pairs)
        def _(p):
            @pl.when(c == 0)
            def _():
                for copy in weight_loads(p):
                    copy.wait()

            slot = lax.rem(p, 2)

            @pl.when(p >= 2)
            def _():
                for copy in kept(c, p - 2):
                    copy.wait()

            hidden = matmul(n_ref[span, :], wide[p])
            pre_buf[slot] = hidden.astype(BF)
            pieces = []
            for a in range(2):
                gate = hidden[:, 2 * a * ff : (2 * a + 1) * ff]
                up = hidden[:, (2 * a + 1) * ff : (2 * a + 2) * ff]
                weight = column(c_ref[span, :], 2 * p + a)
                pieces.append((weight * (gate * jax.nn.sigmoid(gate) * up)).astype(BF))
            cm_all[:, pl.ds(pl.multiple_of(p * 2 * ff, 128), 2 * ff)] = jnp.concatenate(
                pieces, axis=1
            )
            for copy in kept(c, p):
                copy.start()

        for p in (pairs - 2, pairs - 1):
            for copy in kept(c, p):
                copy.wait()
        part[span, :] = matmul(cm_all[...], tall[...]).astype(BF)
        give(c).start()
        give(c).wait_recv()
        mine[c] = (part[rows(low_side, c), :].astype(F32) + arrived[c].astype(F32)).astype(BF)
        swap(c).start()

    def stores(at):
        span = pl.ds(pl.multiple_of(at * CHUNK, CHUNK), CHUNK)
        return [
            pltpu.make_async_copy(y_ref.at[span], y_hbm.at[span], out_sem.at[0, at]),
            pltpu.make_async_copy(low_ref.at[span], low_hbm.at[span], out_sem.at[1, at]),
            pltpu.make_async_copy(lowt_ref.at[:, span], lowt_hbm.at[:, span], out_sem.at[2, at]),
        ]

    def consume(side, c):
        span = rows(side, c)
        mask = column(c_ref[span, :], 2 * pairs)
        factor = token_total / count_ref[...] * mask
        near_t, far_t = halves(teacher_ref, span, shard)
        near_y = h_ref[span, :half] + total[span, :half].astype(F32)
        far_y = h_ref[span, half:] + total[span, half:].astype(F32)
        put_halves(y_ref, span, shard, near_y, far_y)
        for begin, error in ((0, near_y - near_t), (half, far_y - far_t)):
            features = slice(begin, begin + half)
            squares = mask * jnp.sum(error * error, axis=1, keepdims=True)
            square_ref[...] += jnp.sum(squares, axis=0, keepdims=True)
            grad = (factor * error).astype(BF)
            low_ref[span, features] = grad
            lowt_ref[features, span] = grad.T
        for copy in stores(2 * c + side):
            copy.start()

    for copy in loads:
        copy.wait()

    @pl.loop(0, chunks)
    def _(c):
        swap(c).wait_recv()
        total[rows(low_side, c), :] = (mine[c].astype(F32) + other[c].astype(F32)).astype(BF)
        back_copy(c).start()
        consume(low_side, c)
        back_copy(c).wait_recv()
        consume(1 - low_side, c)

    @pl.loop(0, chunks)
    def _(c):
        give(c).wait_send()
        swap(c).wait_send()
        back_copy(c).wait_send()
        for side in range(2):
            for copy in stores(2 * c + side):
                copy.wait()


def experts_forward(token_total, normed, combine, count, gates, ups, downs, hidden, teacher):
    tokens, width = hidden.shape
    experts, half, ff = gates[0].shape
    pairs = experts // 2
    shape, vmem, dma = jax.ShapeDtypeStruct, pltpu.VMEM, pltpu.SemaphoreType.DMA
    anywhere = pl.BlockSpec(memory_space=pl.ANY)
    near_memory = pl.BlockSpec(memory_space=pltpu.VMEM)
    return pl.pallas_call(
        functools.partial(experts_forward_kernel, token_total),
        out_shape=(
            shape((pairs, tokens, 4 * ff), BF),
            shape((pairs, tokens, 2 * ff), BF),
            shape((tokens, width), BF),
            shape((tokens, width), BF),
            shape((width, tokens), BF),
            shape((1, 1), F32),
        ),
        in_specs=[near_memory] * 3 + [anywhere] * 8,
        out_specs=(anywhere,) * 5 + (near_memory,),
        scratch_shapes=[
            vmem((pairs, width, 4 * ff), BF),
            vmem((experts * ff, width), BF),
            vmem((2, 2 * CHUNK, 4 * ff), BF),
            vmem((2 * CHUNK, experts * ff), BF),
            vmem((tokens, width), BF),
            vmem((tokens, width), F32),
            vmem((tokens, width), BF),
            vmem((tokens, width), BF),
            vmem((tokens, width), BF),
            vmem((width, tokens), BF),
            dma((pairs, 12)),
            dma((2,)),
            dma((2, 2)),
            dma((3, tokens // CHUNK)),
        ]
        + sum_scratch(tokens, width),
        compiler_params=pltpu.CompilerParams(
            collective_id=3, has_side_effects=True, vmem_limit_bytes=60 * 1024 * 1024
        ),
        cost_estimate=COST,
        name="experts_forward",
    )(normed, combine, count, *gates, *ups, *downs, hidden, teacher)


def back_kernel(
    contexts, trees, lag, gains, wq, wk, wv, far_qkv, wout, far_out, q_ref, o_ref, lse_ref, packed_all,
    square_ref, part, h_hbm, gy_hbm, x_hbm, nt_hbm, n2t_hbm, gyt_hbm, grads_hbm, cm_hbm, kv_hbm,
    result, out_hbm, tail_ref, own_hbm, far_hbm, came, up_hbm, down_hbm, part2, dkv_part, dkv_came, dkv_pair,
    wqkv, scale_ref, tail_own, tail_far, tail_came, tails,
    sums_ring, up_ring, down_ring, came_buf, out_buf, turned, gyt, grads_buf, cm_buf, stage,
    hbuf, chunk_low, chunk_out, my_part, total, arrived, mine, other, other2,
    dat, do_ref, dq_ref, dqs, deltas, bias, kv_buf, dkv_buf, dkv_sum, dkv_add, tile_buf,
    local_sem, ring_sem, pair_recv, tail_sem, tsend, trecv, ysend, yrecv, usend, urecv, dsend, drecv, store_sem, gsend, grecv, *ar_sems
):
    i = lax.axis_index("context")
    shard = lax.axis_index("shard")
    tokens, width = hbuf.shape
    half = width // 2
    rows = tokens // trees
    units = result.shape[0] // UNIT
    slots = lag * (contexts - 1) + 2
    ff = result.shape[2]
    pairs = grads_hbm.shape[0]
    heads = q_ref.shape[1] // HEAD
    kv_width = kv_buf.shape[1] // 2
    per_group = q_ref.shape[1] // kv_width
    low, near, far = tensor_peers()
    has_left, has_right = i > 0, i < contexts - 1
    right = {"context": lax.rem(i + 1, contexts)}
    left = {"context": lax.rem(i + contexts - 1, contexts)}
    other_shard = {"shard": 1 - shard}

    def remote(src, dst, send, recv, to):
        return pltpu.make_async_remote_copy(
            src, dst, send, recv, device_id=to, device_id_type=MESH
        )

    def fetch(*moves):
        copies = [
            pltpu.make_async_copy(src, dst, local_sem.at[at]) for at, (src, dst) in enumerate(moves)
        ]
        for copy in copies:
            copy.start()
        for copy in copies:
            copy.wait()


    def slabs(k):
        return pl.ds(k * UNIT, UNIT)

    def exchange(k):
        return remote(
            far_hbm.at[slabs(k)], came.at[slabs(k)], ysend.at[k], yrecv.at[k], other_shard
        )

    def upward(k, ring):
        return remote(
            ring.at[lax.rem(k, slots)], up_hbm.at[slabs(k)], usend.at[k], urecv.at[k], right
        )

    def downward(k, ring):
        return remote(
            ring.at[lax.rem(k, slots)], down_hbm.at[slabs(k)], dsend.at[k], drecv.at[k], left
        )

    def store(k):
        return pltpu.make_async_copy(
            out_buf.at[lax.rem(k, 2)], result.at[slabs(k)], store_sem.at[lax.rem(k, 2)]
        )

    def add_unit(k):
        u, d = k - lag * i, k - lag * (contexts - 1 - i)
        slot, up_slot, down_slot = (lax.rem(jnp.maximum(at, 0), slots) for at in (k, u, d))
        has_new = k < units
        has_up = has_left & (u >= 0) & (u < units)
        has_down = has_right & (d >= 0) & (d < units)

        def load(at, src, dst):
            return pltpu.make_async_copy(src, dst, ring_sem.at[at])

        def new_loads():
            return (
                load(0, own_hbm.at[slabs(k)], sums_ring.at[slot]),
                load(1, came.at[slabs(k)], came_buf),
            )

        def up_load():
            return load(2, up_hbm.at[slabs(u)], up_ring.at[up_slot])

        def down_load():
            return load(3, down_hbm.at[slabs(d)], down_ring.at[down_slot])

        @pl.when(has_new)
        def _():
            @pl.when((k >= slots) & (i == 0))
            def _():
                upward(k - slots, sums_ring).wait_send()

            @pl.when((k >= slots) & (i == contexts - 1))
            def _():
                downward(k - slots, sums_ring).wait_send()

            exchange(k).wait_recv()
            for copy in new_loads():
                copy.start()

        @pl.when(has_up)
        def _():
            @pl.when(has_right & (u >= slots))
            def _():
                upward(u - slots, up_ring).wait_send()

            upward(u, up_ring).wait_recv()
            up_load().start()

        @pl.when(has_down)
        def _():
            @pl.when(has_left & (d >= slots))
            def _():
                downward(d - slots, down_ring).wait_send()

            downward(d, down_ring).wait_recv()
            down_load().start()

        @pl.when(has_new)
        def _():
            for copy in new_loads():
                copy.wait()
            sums_ring[slot] = (sums_ring[slot].astype(F32) + came_buf[...].astype(F32)).astype(BF)

            @pl.when(i == 0)
            def _():
                upward(k, sums_ring).start()

            @pl.when(i == contexts - 1)
            def _():
                downward(k, sums_ring).start()

        @pl.when(has_up)
        def _():
            up_load().wait()
            up_ring[up_slot] = (
                up_ring[up_slot].astype(F32) + sums_ring[up_slot].astype(F32)
            ).astype(BF)

            @pl.when(has_right)
            def _():
                upward(u, up_ring).start()

        @pl.when(has_down)
        def _():
            down_load().wait()
            down_ring[down_slot] = (
                down_ring[down_slot].astype(F32) + sums_ring[down_slot].astype(F32)
            ).astype(BF)

            @pl.when(has_left)
            def _():
                downward(d, down_ring).start()

        e = k - lag * jnp.maximum(i, contexts - 1 - i)

        @pl.when((e >= 0) & (e < units))
        def _():
            out_slot = lax.rem(e, slots)
            here = lax.rem(e, 2)

            @pl.when(e >= 2)
            def _():
                store(e - 2).wait()

            @pl.when(i == 0)
            def _():
                out_buf[here] = down_ring[out_slot]

            @pl.when(i == contexts - 1)
            def _():
                out_buf[here] = up_ring[out_slot]

            @pl.when(has_left & has_right)
            def _():
                out_buf[here] = (
                    up_ring[out_slot].astype(F32)
                    + (down_ring[out_slot].astype(F32) - sums_ring[out_slot].astype(F32))
                ).astype(BF)

            store(e).start()


    def write_slabs(first, number, products, send=True):
        for part_index, target in ((0, own_hbm), (1, far_hbm)):
            at = 0
            for left_ref, right_value, order in products:
                block = matmul(
                    left_ref[part_index * half : (part_index + 1) * half, :], right_value
                ).astype(BF)
                for c, place in enumerate(order):
                    stage[part_index, at + place] = block[:, c * ff : (c + 1) * ff]
                at += len(order)
        fetch(
            *(
                (stage.at[p, pl.ds(0, number)], target.at[pl.ds(first, number)])
                for p, target in ((0, own_hbm), (1, far_hbm))
            )
        )
        if send:
            for c in range(number // UNIT):
                exchange(first // UNIT + c).start()

    def pair_slabs(p, send=True):
        if send:
            fetch((grads_hbm.at[p], grads_buf), (cm_hbm.at[p], cm_buf))
        write_slabs(
            p * 6, 6, ((turned, grads_buf[...], (0, 2, 1, 3)), (gyt, cm_buf[...], (0, 1))), send
        )


    chunks = arrived.shape[0]
    low_half = tokens // 2

    def chunk_rows(side, c):
        return pl.ds(pl.multiple_of(side * low_half + c * CHUNK, CHUNK), CHUNK)

    def summing(source, landing, sems):
        send1, recv1, send2, recv2, send3, recv3 = sems

        def give(c):
            return remote(
                source.at[chunk_rows(1 - low, c)], arrived.at[c], send1.at[c], recv1.at[c], near
            )

        def swap(c):
            return remote(mine.at[c], landing.at[c], send2.at[c], recv2.at[c], far)

        def back(c):
            span = chunk_rows(low, c)
            return remote(total.at[span], total.at[span], send3.at[c], recv3.at[c], near)

        def start():
            for c in range(chunks):
                give(c).start()

        def middle():
            fetch(*((source.at[chunk_rows(low, c)], my_part.at[c]) for c in range(chunks)))
            for c in range(chunks):
                give(c).wait_recv()
                mine[c] = (my_part[c].astype(F32) + arrived[c].astype(F32)).astype(BF)
                swap(c).start()

        def finish(c, consume):
            swap(c).wait_recv()
            total[chunk_rows(low, c), :] = (
                mine[c].astype(F32) + landing[c].astype(F32)
            ).astype(BF)
            back(c).start()
            consume(pl.multiple_of(low * low_half + c * CHUNK, CHUNK))

        def finish_other(c, consume):
            back(c).wait_recv()
            consume(pl.multiple_of((1 - low) * low_half + c * CHUNK, CHUNK))

        def drain():
            for c in range(chunks):
                give(c).wait_send()
                swap(c).wait_send()
                back(c).wait_send()

        return start, middle, finish, finish_other, drain

    start1, middle1, finish1, other1, drain1 = summing(part, other, ar_sems[:6])
    start2, middle2, finish2, finish_other2, drain2 = summing(part2, other2, ar_sems[6:])

    def through_second_norm(row):
        span = pl.ds(row, CHUNK)
        fetch((gy_hbm.at[span], chunk_low), (h_hbm.at[span], hbuf.at[span]))
        own_h, far_h = hbuf[span, :half], hbuf[span, half:]
        inverse = inverse_norm(own_h, far_h)
        own_d, far_d, own_scale, far_scale = norm_backward(
            own_h, far_h, inverse, gains[1:2, :], total[span, :].astype(F32)
        )
        scale_ref[1:2, :half] += own_scale
        scale_ref[1:2, half:] += far_scale
        own_d = chunk_low[:, :half].astype(F32) + own_d
        far_d = chunk_low[:, half:].astype(F32) + far_d
        hbuf[span, :half] = own_d
        hbuf[span, half:] = far_d
        own_d = own_d.astype(BF)
        far_d = far_d.astype(BF)
        dat[:half, span] = own_d.T
        dat[half:, span] = far_d.T
        do_ref[span, :] = (
            contract_last(own_d, wout[...]) + contract_last(far_d, far_out[...])
        ).astype(BF)

    def through_first_norm(row):
        span = pl.ds(row, CHUNK)
        fetch((x_hbm.at[span], chunk_low))
        own_x, far_x = halves(chunk_low, slice(None), shard)
        inverse = inverse_norm(own_x, far_x)
        own_d, far_d, own_scale, far_scale = norm_backward(
            own_x, far_x, inverse, gains[0:1, :], total[span, :].astype(F32)
        )
        scale_ref[0:1, :half] += own_scale
        scale_ref[0:1, half:] += far_scale
        put_halves(
            chunk_out, slice(None), shard, hbuf[span, :half] + own_d, hbuf[span, half:] + far_d
        )
        fetch((chunk_out, out_hbm.at[span]))


    def make_deltas():
        @pl.loop(0, trees)
        def _(tree):
            span = pl.ds(pl.multiple_of(tree * rows, rows), rows)
            for head in range(heads):
                cols = slice(head * HEAD, (head + 1) * HEAD)
                product = do_ref[span, cols].astype(F32) * o_ref[span, cols].astype(F32)
                deltas[tree, head] = lax.dot_general(
                    jnp.ones((8, HEAD), F32),
                    product,
                    (((1,), (1,)), ((), ())),
                    precision=lax.Precision.HIGHEST,
                    preferred_element_type=F32,
                )

    def hand(j, tree):
        span = pl.ds(pl.multiple_of(tree * rows, rows), rows)
        return remote(
            dkv_part.at[j, span], dkv_came.at[i, span], gsend.at[j, tree], grecv.at[i, tree],
            {"context": j},
        )

    odd = lax.rem(i, 2) == 1

    def hand_to_pair(j, tree):
        span = pl.ds(pl.multiple_of(tree * rows, rows), rows)
        return remote(
            dkv_part.at[j, span], dkv_pair.at[j, span], gsend.at[j, tree], pair_recv.at[j, tree],
            left,
        )

    def merge_block(number):
        tree, j = number // contexts, lax.rem(number, contexts)

        @pl.when((number < trees * contexts) & (j < i) & (lax.rem(i, 2) == 0))
        def _():
            span = pl.ds(pl.multiple_of(tree * rows, rows), rows)
            hand_to_pair(j, tree).wait_recv()
            fetch((dkv_pair.at[j, span], dkv_add), (dkv_part.at[j, span], dkv_buf))
            dkv_buf[...] = (dkv_buf[...].astype(F32) + dkv_add[...].astype(F32)).astype(BF)
            fetch((dkv_buf, dkv_part.at[j, span]))
            hand(j, tree).start()

    def taken(c, tree):
        span = pl.ds(pl.multiple_of(tree * rows, rows), rows)
        return remote(
            dkv_part.at[c, span], dkv_came.at[c, span], gsend.at[c, tree], grecv.at[c, tree],
            {"context": c},
        )

    def attention_block(number):
        tree, j = number // contexts, lax.rem(number, contexts)

        @pl.when((number < trees * contexts) & (j <= i))
        def _():
            span = pl.ds(pl.multiple_of(tree * rows, rows), rows)
            fetch((kv_hbm.at[j, span], kv_buf))
            key_pos = j * rows + lax.broadcasted_iota(jnp.int32, (rows, rows), 0)
            query_pos = i * rows + lax.broadcasted_iota(jnp.int32, (rows, rows), 1)
            last = column(packed_all[j].T, trees + tree)
            segment = packed_all[i, pl.ds(tree, 1), :]
            allowed = (key_pos <= query_pos) & (segment <= last)
            bias[...] = jnp.where(allowed, 0.0, -2e30)
            for group in range(heads // per_group):
                keys = kv_buf[:, group * HEAD : (group + 1) * HEAD]
                values = kv_buf[:, kv_width + group * HEAD : kv_width + (group + 1) * HEAD]
                dk = jnp.zeros((rows, HEAD), F32)
                dv = jnp.zeros((rows, HEAD), F32)
                for head in range(group * per_group, (group + 1) * per_group):
                    cols = slice(head * HEAD, (head + 1) * HEAD)
                    queries = q_ref[span, cols]
                    grads = do_ref[span, cols]
                    scores = contract_last(keys, queries) * 0.125 + bias[...]
                    probs = jnp.exp(scores - lse_ref[tree, head : head + 1, :])
                    grad_probs = contract_last(values, grads)
                    grad_scores = (probs * (grad_probs - deltas[tree, head, 0:1, :])).astype(BF)
                    dv = dv + matmul(probs.astype(BF), grads)
                    dk = dk + matmul(grad_scores, queries)
                    dqs[span, cols] += contract_first(grad_scores, keys)
                dkv_buf[:, group * HEAD : (group + 1) * HEAD] = (dk * 0.125).astype(BF)
                dkv_buf[:, kv_width + group * HEAD : kv_width + (group + 1) * HEAD] = dv.astype(BF)

            @pl.when(j == i)
            def _():
                dkv_sum[span, :] = dkv_buf[...].astype(F32)

            @pl.when(j < i)
            def _():
                fetch((dkv_buf, dkv_part.at[j, span]))

                @pl.when(odd & (j == i - 1))
                def _():
                    hand(j, tree).start()

                @pl.when(odd & (j < i - 1))
                def _():
                    hand_to_pair(j, tree).start()

    def query_slabs():
        dq_ref[...] = (dqs[...] * 0.125).astype(BF)
        thirds = tuple(range(dq_ref.shape[1] // ff))
        write_slabs(
            pairs * 6, 2 * len(thirds), ((turned, dq_ref[...], thirds), (dat, o_ref[...], thirds))
        )

    def key_value_sum():
        @pl.loop(0, contexts)
        def _(c):
            @pl.when((c > i) & ((lax.rem(c, 2) == 0) | ((c == i + 1) & (lax.rem(i, 2) == 0))))
            def _():
                @pl.loop(0, trees)
                def _(tree):
                    taken(c, tree).wait_recv()
                    span = pl.ds(pl.multiple_of(tree * rows, rows), rows)
                    fetch((dkv_came.at[c, span], dkv_add))
                    dkv_sum[span, :] += dkv_add[...].astype(F32)

        grad_kv = dkv_sum[...].astype(BF)
        pieces = tuple(range(grad_kv.shape[1] // ff))
        first = pairs * 6 + 2 * (dq_ref.shape[1] // ff)
        write_slabs(first, len(pieces), ((turned, grad_kv, pieces),))

    def first_norm_parts():
        @pl.loop(0, tokens // CHUNK)
        def _(c):
            span = pl.ds(pl.multiple_of(c * CHUNK, CHUNK), CHUNK)
            grads = jnp.concatenate([dq_ref[span, :], dkv_sum[span, :].astype(BF)], axis=1)
            tile_buf[:, :half] = contract_last(grads, wqkv[...]).astype(BF)
            tile_buf[:, half:] = contract_last(grads, far_qkv[...]).astype(BF)
            fetch((tile_buf, part2.at[span]))

        start2()


    tail_copy = remote(tail_far, tail_came, tail_sem.at[0], tail_sem.at[1], other_shard)

    def tell(c, slot):
        return remote(tails.at[slot], tails.at[slot], tsend.at[c], trecv.at[slot], {"context": c})

    def send_tail():
        for begin, target in ((0, tail_own), (half, tail_far)):
            target[...] = jnp.broadcast_to(square_ref[...], target.shape)
            target[0:2, :] = scale_ref[0:2, begin : begin + half]
        tail_copy.start()

    def tell_tail():
        tail_copy.wait_recv()
        tails[i] = tail_own[...] + tail_came[...]

        @pl.loop(0, contexts)
        def _(c):
            @pl.when(c != i)
            def _():
                tell(c, i).start()


    fetch(
        (n2t_hbm, turned), (gyt_hbm, gyt), (grads_hbm.at[0], grads_buf), (cm_hbm.at[0], cm_buf)
    )
    pair_slabs(0, False)
    greet(
        [other_shard, near, far]
        + [{"context": lax.rem(i + c, contexts)} for c in range(1, contexts)]
    )
    for c in range(6 // UNIT):
        exchange(c).start()
    start1()
    fill_columns(wqkv, (wq, wk, wv))
    scale_ref[...] = jnp.zeros_like(scale_ref)
    dqs[...] = jnp.zeros_like(dqs)
    middle1()

    chain = []
    for finish, finish_other, consume in (
        (finish1, other1, through_second_norm), (finish2, finish_other2, through_first_norm),
    ):
        steps = [[functools.partial(finish, 0, consume)]]
        for c in range(chunks):
            steps.append([functools.partial(finish_other, c, consume)])
            if c + 1 < chunks:
                steps[-1].append(functools.partial(finish, c + 1, consume))
        chain.append(steps)
    chain[0][-1].append(make_deltas)
    tasks = {}
    for p in range(1, pairs):
        tasks[3 * p - 3] = [functools.partial(pair_slabs, p)]
    last_pair = 3 * pairs - 6
    at = 0

    def put(acts):
        nonlocal at
        at += 1
        while at in tasks:
            at += 1
        tasks[at] = acts

    for acts in chain[0]:
        put(acts)
    per_step = -(-trees * contexts // 8)

    def attention_step(number):
        @pl.loop(0, per_step)
        def _(step):
            attention_block(number * per_step + step)

    attention_steps = {}
    for number in range(8):
        at += 1
        while at in tasks:
            at += 1
        attention_steps[at] = number
    first_at, last_at = min(attention_steps), max(attention_steps)
    at = max(at, last_pair)
    put([lambda: fetch((nt_hbm, turned)), query_slabs])
    at = max(at, last_at + 6)
    put([key_value_sum])
    put([first_norm_parts])
    put([drain1, middle2])
    for acts in chain[1]:
        put(acts)
    put([send_tail])
    put([tell_tail])
    assert at < units + lag * (contexts - 1)

    @pl.loop(0, units + lag * (contexts - 1))
    def _(k):
        add_unit(k)
        for when, acts in sorted(tasks.items()):

            @pl.when(k == when)
            def _(acts=acts):
                for act in acts:
                    act()

        number, due = jnp.int32(0), k < 0
        for when, index in attention_steps.items():
            number = jnp.where(k == when, index, number)
            due = due | (k == when)

        @pl.when(due)
        def _():
            attention_step(number)

        number, due = jnp.int32(0), k < 0
        for when, index in attention_steps.items():
            number = jnp.where(k == when + 3, index, number)
            due = due | (k == when + 3)

        @pl.when(due)
        def _():
            @pl.loop(0, per_step)
            def _(step):
                merge_block(number * per_step + step)

    @pl.loop(0, contexts)
    def _(c):
        @pl.when(c != i)
        def _():
            tell(i, c).wait_recv()
            tell(c, i).wait_send()

    tail_copy.wait_send()
    tail = tails[0]
    for c in range(1, contexts):
        tail = tail + tails[c]
    tail_ref[...] = tail
    drain2()
    for k in (units - 2, units - 1):
        store(k).wait()

    @pl.loop(0, units)
    def _(k):
        exchange(k).wait_send()

        @pl.when((k >= units - slots) & has_right)
        def _():
            upward(k, up_ring).wait_send()

        @pl.when((k >= units - slots) & has_left)
        def _():
            downward(k, down_ring).wait_send()

    @pl.loop(0, contexts)
    def _(c):
        @pl.when(c < i)
        def _():
            @pl.loop(0, trees)
            def _(tree):
                hand(c, tree).wait_send()


def back(
    contexts, trees, gains, w_query, w_key, w_value, far_qkv, w_out, far_out, q, o, lse,
    packed_all, square, part, hidden, grad_y, x, normed_t, normed_two_t, grad_y_t, grads, middle, kv,
):
    tokens, width = hidden.shape
    half, rows = width // 2, tokens // trees
    pairs, _, four = grads.shape
    ff, cols, both = four // 4, q.shape[1], kv.shape[2]
    count = pairs * 6 + (2 * cols + both) // ff
    units = count // UNIT
    lag = 2 if contexts <= 4 else 1
    slots = lag * (contexts - 1) + 2
    chunks = tokens // 2 // CHUNK
    shape, vmem, dma = jax.ShapeDtypeStruct, pltpu.VMEM, pltpu.SemaphoreType.DMA
    slabs = shape((count, half, ff), BF)
    unit = (UNIT, half, ff)
    piece = vmem((chunks, CHUNK, width), BF)
    anywhere = pl.BlockSpec(memory_space=pl.ANY)
    near_memory = pl.BlockSpec(memory_space=pltpu.VMEM)
    outs = pl.pallas_call(
        functools.partial(back_kernel, contexts, trees, lag),
        out_shape=(
            slabs,
            shape((tokens, width), F32),
            shape((8, half), F32),
            *(slabs,) * 5,
            shape((tokens, width), BF),
            shape(kv.shape, BF),
            shape(kv.shape, BF),
            shape(kv.shape, BF),
        ),
        in_specs=[near_memory] * 12 + [anywhere] * 10,
        out_specs=(anywhere,) * 2 + (near_memory,) + (anywhere,) * 9,
        scratch_shapes=[
            vmem((half, cols + both), BF),
            vmem((8, width), F32),
            vmem((8, half), F32),
            vmem((8, half), F32),
            vmem((8, half), F32),
            vmem((contexts, 8, half), F32),
            vmem((slots,) + unit, BF),
            vmem((slots,) + unit, BF),
            vmem((slots,) + unit, BF),
            vmem(unit, BF),
            vmem((2,) + unit, BF),
            vmem((width, tokens), BF),
            vmem((width, tokens), BF),
            vmem((tokens, 4 * ff), BF),
            vmem((tokens, 2 * ff), BF),
            vmem((2, 6, half, ff), BF),
            vmem((tokens, width), F32),
            vmem((CHUNK, width), BF),
            vmem((CHUNK, width), F32),
            piece,
            vmem((tokens, width), BF),
            piece,
            piece,
            piece,
            piece,
            vmem((width, tokens), BF),
            vmem((tokens, cols), BF),
            vmem((tokens, cols), BF),
            vmem((tokens, cols), F32),
            vmem((trees, cols // HEAD, 8, rows), F32),
            vmem((rows, rows), F32),
            vmem((rows, both), BF),
            vmem((rows, both), BF),
            vmem((tokens, both), F32),
            vmem((rows, both), BF),
            vmem((CHUNK, width), BF),
            dma((4,)),
            dma((4,)),
            dma((contexts, trees)),
            dma((2,)),
            dma((contexts,)),
            dma((contexts,)),
        ]
        + [dma((units,))] * 6
        + [dma((2,)), dma((contexts, trees)), dma((contexts, trees))]
        + [dma((chunks,))] * 12,
        compiler_params=pltpu.CompilerParams(
            collective_id=1, has_side_effects=True, vmem_limit_bytes=60 * 1024 * 1024
        ),
        cost_estimate=COST,
        name="back",
    )(
        gains, w_query, w_key, w_value, far_qkv, w_out, far_out, q, o, lse, packed_all,
        square, part, hidden, grad_y, x, normed_t, normed_two_t, grad_y_t, grads, middle, kv,
    )
    return outs[:3]


def local(
    states, segments, routes, gates, valid, teacher, attn_gain, w_query, key_matrix, value_matrix,
    w_out, moe_gain, w_gate, w_up, w_down,
):
    shards = lax.axis_size("shard")
    contexts = lax.axis_size("context")
    trees, rows, width = states.shape
    tokens = trees * rows
    half = width // 2
    experts = w_gate.shape[0]
    x = states.reshape(tokens, width)
    (
        packed_all, gains, qkv_far, out_far, gate_far, up_far, down_far, q, kv, normed_t,
        attended, lse, hidden, normed_two, normed_two_t, count, combine,
    ) = front(
        contexts, trees, x, segments, valid, routes.transpose(0, 2, 1), gates.transpose(0, 2, 1),
        attn_gain, moe_gain, w_query, key_matrix, value_matrix, w_out, w_gate, w_up, w_down,
    )
    gate_ws, up_ws, down_ws = (w_gate, gate_far), (w_up, up_far), (w_down, down_far)

    pre, middle, result, grad_y, grad_y_t, square = experts_forward(
        float(tokens * shards * contexts),
        normed_two,
        combine,
        count,
        gate_ws,
        up_ws,
        down_ws,
        hidden,
        teacher.reshape(tokens, width),
    )
    expert_grads, dn_part, result = experts_backward(
        grad_y, combine, gate_ws, up_ws, down_ws, pre, result
    )
    sums, grad_inputs, tail = back(
        contexts, trees, gains, w_query, key_matrix, value_matrix, qkv_far, w_out, out_far, q,
        attended, lse, packed_all, square, dn_part, hidden, grad_y, x, normed_t, normed_two_t,
        grad_y_t, expert_grads, middle, kv,
    )
    final_query, final_out, final_key, final_value, final_gain1, final_gain2, loss = (
        unpack_attention(sums, tail, count, w_query.shape[1], key_matrix.shape[1])
    )
    final_gate, final_up, final_down = unpack(sums, experts // 2)
    return (
        loss[0, 0],
        result.reshape(trees, rows, width),
        grad_inputs.reshape(trees, rows, width),
        final_gain1,
        final_query,
        final_key,
        final_value,
        final_out,
        final_gain2,
        final_gate,
        final_up,
        final_down,
    )


def solution(mesh):
    return jax.shard_map(
        local,
        mesh=mesh,
        in_specs=(
            P("shard", "context", None),
            P("shard", "context"),
            P("shard", "context", None),
            P("shard", "context", None),
            P("shard", "context"),
            P("shard", "context", None),
            P("shard"),
            P("shard", "tensor"),
            P("shard", "tensor"),
            P("shard", "tensor"),
            P("tensor", "shard"),
            P("shard"),
            P(None, "shard", "tensor"),
            P(None, "shard", "tensor"),
            P(None, "tensor", "shard"),
        ),
        out_specs=(
            P(),
            P("shard", "context", None),
            P("shard", "context", None),
            P("shard"),
            P("shard", "tensor"),
            P("shard", "tensor"),
            P("shard", "tensor"),
            P("tensor", "shard"),
            P("shard"),
            P(None, "shard", "tensor"),
            P(None, "shard", "tensor"),
            P(None, "tensor", "shard"),
        ),
        check_vma=False,
    )
```
